32 devices in a mesh: ha: 16 (over z, x, core), col: 2 (over y).
Axes of the slice: x: 2, y: 2, z: 4, core: 2. Of those that a mesh axis runs over, the one named last changes fastest.
Arguments:
- input_a: bfloat16 [1, 16, 48, 512], P(None, 'ha', None, 'col'), may hold values from -6 to 6
- input_b: bfloat16 [1, 16, 72, 512], P(None, 'ha', None, 'col'), may hold values from -6 to 6
- skip_a: bfloat16 [1, 32, 96, 512], P(None, 'ha', None, 'col'), may hold values from -6 to 6
- skip_b: bfloat16 [1, 32, 144, 512], P(None, 'ha', None, 'col'), may hold values from -6 to 6
- labels_a: int32 [1, 32, 96], P(None, 'ha'), may hold values from 0 to 1
- labels_b: int32 [1, 32, 144], P(None, 'ha'), may hold values from 0 to 1
- valid_a: int32 [1, 32, 96], P(None, 'ha'), may hold values from 0 to 1
- valid_b: int32 [1, 32, 144], P(None, 'ha'), may hold values from 0 to 1
- w_enter: float32 [3, 3, 512, 1024], P(None, None, 'ha', 'col'), may hold values from -0.09375 to 0.09375
- moment_enter: float32 [3, 3, 512, 1024], P(None, None, 'ha', 'col'), may hold values from -0.00010681152 to 0.00010681152
- square_enter: float32 [3, 3, 512, 1024], P(None, None, 'ha', 'col'), may hold values from 2.1152344e-10 to 8.4609375e-10
- w_middle: float32 [3, 3, 1024, 1024], P(None, None, 'ha', 'col'), may hold values from -0.0625 to 0.0625
- moment_middle: float32 [3, 3, 1024, 1024], P(None, None, 'ha', 'col'), may hold values from -0.00010681152 to 0.00010681152
- square_middle: float32 [3, 3, 1024, 1024], P(None, None, 'ha', 'col'), may hold values from 2.1152344e-10 to 8.4609375e-10
- w_upward: float32 [2, 2, 1024, 512], P(None, None, 'ha', 'col'), may hold values from -0.1875 to 0.1875
- moment_upward: float32 [2, 2, 1024, 512], P(None, None, 'ha', 'col'), may hold values from -0.00012207031 to 0.00012207031
- square_upward: float32 [2, 2, 1024, 512], P(None, None, 'ha', 'col'), may hold values from 3.2819011e-10 to 1.3127605e-09
- w_merge: float32 [3, 3, 1024, 512], P(None, None, 'ha', 'col'), may hold values from -0.0625 to 0.0625
- moment_merge: float32 [3, 3, 1024, 512], P(None, None, 'ha', 'col'), may hold values from -0.00036621094 to 0.00036621094
- square_merge: float32 [3, 3, 1024, 512], P(None, None, 'ha', 'col'), may hold values from 2.8710938e-09 to 1.1484375e-08
- w_head: float32 [512, 2], P('col'), may hold values from -0.5 to 0.5
- moment_head: float32 [512, 2], P('col'), may hold values from -0.02734375 to 0.02734375
- square_head: float32 [512, 2], P('col'), may hold values from 6.510417e-06 to 0.00026041668
Outputs:
- enter_master: float32 [3, 3, 512, 1024], P(None, None, 'ha', 'col')
- enter_moment: float32 [3, 3, 512, 1024], P(None, None, 'ha', 'col')
- enter_square: float32 [3, 3, 512, 1024], P(None, None, 'ha', 'col')
- enter_copy: bfloat16 [3, 3, 512, 1024], P(None, None, 'ha', 'col')
- middle_master: float32 [3, 3, 1024, 1024], P(None, None, 'ha', 'col')
- middle_moment: float32 [3, 3, 1024, 1024], P(None, None, 'ha', 'col')
- middle_square: float32 [3, 3, 1024, 1024], P(None, None, 'ha', 'col')
- middle_copy: bfloat16 [3, 3, 1024, 1024], P(None, None, 'ha', 'col')
- upward_master: float32 [2, 2, 1024, 512], P(None, None, 'ha', 'col')
- upward_moment: float32 [2, 2, 1024, 512], P(None, None, 'ha', 'col')
- upward_square: float32 [2, 2, 1024, 512], P(None, None, 'ha', 'col')
- upward_copy: bfloat16 [2, 2, 1024, 512], P(None, None, 'ha', 'col')
- merge_master: float32 [3, 3, 1024, 512], P(None, None, 'ha', 'col')
- merge_moment: float32 [3, 3, 1024, 512], P(None, None, 'ha', 'col')
- merge_square: float32 [3, 3, 1024, 512], P(None, None, 'ha', 'col')
- merge_copy: bfloat16 [3, 3, 1024, 512], P(None, None, 'ha', 'col')
- head_master: float32 [512, 2], P('col')
- head_moment: float32 [512, 2], P('col')
- head_square: float32 [512, 2], P('col')
- head_copy: bfloat16 [512, 2], P('col')
- loss_sum: float32 [], replicated
- label_total: float32 [], replicated
The draws below stay inside these ranges and needn't reach their ends.
All inputs are finite; a program needn't handle non-finite values.
Results may differ from the reference program's by a relative error of at most 0.025.
Values may be sent and summed in bfloat16 or wider, within the bound.
A program may use at most 192 MiB of HBM per device.

```python
import math
import jax
import jax.numpy as jnp
from jax import lax

CIN = 512
CMID = 1024
CUP = 512
CLASSES = 2
IMG_A = 1
IMG_B = 1
WID_A = 48
WID_B = 72
STEP = 10
HGT = 16
NPIX = 7680


def rising(key, images, height, width):
    drawn = jax.random.randint(key, (images, height, width), 0, 4 * height)
    level = jnp.arange(height, dtype=jnp.int32)[None, :, None]
    return (drawn < height + 2 * level).astype(jnp.int32)


def draw_valid_a(key, part):
    key = jax.random.fold_in(key, 11)
    return rising(key, IMG_A, 2 * HGT, 2 * WID_A)


def draw_valid_b(key, part):
    key = jax.random.fold_in(key, 23)
    return rising(key, IMG_B, 2 * HGT, 2 * WID_B)


def plant(entries, own_key, least, top_value):
    spot = [jax.random.randint(jax.random.fold_in(own_key, axis), (), 0, length) for axis, length in enumerate(entries.shape)]
    longest = entries.shape.index(max(entries.shape))
    next_to = spot[:longest] + [(spot[longest] + 1) % entries.shape[longest]] + spot[longest + 1:]
    return entries.at[tuple(spot)].set(least).at[tuple(next_to)].set(top_value)


def shard_levels(stream_key, extent, pieces, low, high):
    def one(axis_at, parts):
        steps = jax.random.uniform(jax.random.fold_in(jax.random.fold_in(stream_key, 6), axis_at), (parts,), jnp.float32, low / len(pieces), high / len(pieces))
        return jnp.repeat(jnp.exp(steps), extent[axis_at] // parts).reshape((-1,) + (1,) * (len(extent) - axis_at - 1))

    level = one(*pieces[0])
    for cut in pieces[1:]:
        level = level * one(*cut)
    return level


def centred(key, extent, scale, reach, pieces=(), kind=jnp.bfloat16):
    array = jax.random.normal(key, extent, jnp.float32) * scale
    if len(pieces) > 0:
        array = shard_levels(key, extent, pieces, -0.22, 0.18) * array
    return jnp.clip(array, min=-reach, max=reach).astype(kind)


def setup_inputs(seed: int = 0) -> dict:
    seeds = jax.random.split(jax.random.key(seed), 24)
    return {
        "input_a": centred(seeds[0], (IMG_A, HGT, WID_A, CIN), 1.0, 6.0, ((1, 16), (3, 2))),
        "input_b": centred(seeds[1], (IMG_B, HGT, WID_B, CIN), 1.0, 6.0, ((1, 16), (3, 2))),
        "skip_a": centred(seeds[2], (IMG_A, 2 * HGT, 2 * WID_A, CUP), 1.0, 6.0, ((1, 16), (3, 2))),
        "skip_b": centred(seeds[3], (IMG_B, 2 * HGT, 2 * WID_B, CUP), 1.0, 6.0, ((1, 16), (3, 2))),
        "labels_a": plant(jax.random.randint(seeds[4], (IMG_A, 2 * HGT, 2 * WID_A), 0, CLASSES), jax.random.fold_in(seeds[4], 1), 0, CLASSES - 1).astype(jnp.int32),
        "labels_b": plant(jax.random.randint(seeds[5], (IMG_B, 2 * HGT, 2 * WID_B), 0, CLASSES), jax.random.fold_in(seeds[5], 1), 0, CLASSES - 1).astype(jnp.int32),
        "valid_a": draw_valid_a(jax.random.fold_in(seeds[23], 71), 0),
        "valid_b": draw_valid_b(jax.random.fold_in(seeds[23], 71), 0),
        "w_enter": centred(seeds[8], (3, 3, CIN, CMID), (9 * CIN) ** -0.5, 0.09375, ((2, 16), (3, 2)), jnp.float32),
        "moment_enter": centred(seeds[9], (3, 3, CIN, CMID), (0.11 * 0.0057 / NPIX ** 0.5), 0.00010681152, ((2, 16), (3, 2)), jnp.float32),
        "square_enter": jnp.clip(jnp.exp(math.log(8.460937506171717e-10) - 1.3862944 * jax.random.uniform(seeds[10], (3, 3, CIN, CMID), jnp.float32) ** shard_levels(seeds[10], (3, 3, CIN, CMID), ((2, 16), (3, 2)), -0.2, 0.2)), 2.1152343765429293e-10, 8.460937506171717e-10),
        "w_middle": centred(seeds[11], (3, 3, CMID, CMID), (9 * CMID) ** -0.5, 0.0625, ((2, 16), (3, 2)), jnp.float32),
        "moment_middle": centred(seeds[12], (3, 3, CMID, CMID), (0.11 * 0.0057 / NPIX ** 0.5), 0.00010681152, ((2, 16), (3, 2)), jnp.float32),
        "square_middle": jnp.clip(jnp.exp(math.log(8.460937506171717e-10) - 1.3862944 * jax.random.uniform(seeds[13], (3, 3, CMID, CMID), jnp.float32) ** shard_levels(seeds[13], (3, 3, CMID, CMID), ((2, 16), (3, 2)), -0.2, 0.2)), 2.1152343765429293e-10, 8.460937506171717e-10),
        "w_upward": centred(seeds[14], (2, 2, CMID, CUP), CMID ** -0.5, 0.1875, ((2, 16), (3, 2)), jnp.float32),
        "moment_upward": centred(seeds[15], (2, 2, CMID, CUP), (0.11 * 0.0071 / NPIX ** 0.5), 0.00012207031, ((2, 16), (3, 2)), jnp.float32),
        "square_upward": jnp.clip(jnp.exp(math.log(1.3127604558960115e-09) - 1.3862944 * jax.random.uniform(seeds[16], (2, 2, CMID, CUP), jnp.float32) ** shard_levels(seeds[16], (2, 2, CMID, CUP), ((2, 16), (3, 2)), -0.2, 0.2)), 3.281901139740029e-10, 1.3127604558960115e-09),
        "w_merge": centred(seeds[17], (3, 3, 2 * CUP, CUP), (18 * CUP) ** -0.5, 0.0625, ((2, 16), (3, 2)), jnp.float32),
        "moment_merge": centred(seeds[18], (3, 3, 2 * CUP, CUP), (0.11 * 0.021 / NPIX ** 0.5), 0.00036621094, ((2, 16), (3, 2)), jnp.float32),
        "square_merge": jnp.clip(jnp.exp(math.log(1.1484375228576482e-08) - 1.3862944 * jax.random.uniform(seeds[19], (3, 3, 2 * CUP, CUP), jnp.float32) ** shard_levels(seeds[19], (3, 3, 2 * CUP, CUP), ((2, 16), (3, 2)), -0.2, 0.2)), 2.8710938071441205e-09, 1.1484375228576482e-08),
        "w_head": centred(seeds[20], (CUP, CLASSES), (CUP // 4) ** -0.5, 0.5, ((0, 2),), jnp.float32),
        "moment_head": centred(seeds[21], (CUP, CLASSES), (0.17 / NPIX ** 0.5), 0.02734375, ((0, 2),), jnp.float32),
        "square_head": jnp.clip(jnp.exp(math.log(0.00026041668) - 3.6888795 * jax.random.uniform(seeds[22], (CUP, CLASSES), jnp.float32) ** shard_levels(seeds[22], (CUP, CLASSES), ((0, 2),), -0.2, 0.2)), 6.510416824312415e-06, 0.00026041668),
    }


@jax.custom_vjp
def low(v):
    return lax.optimization_barrier(v.astype(jnp.bfloat16)).astype(jnp.float32)

@jax.custom_vjp
def low_back(v):
    return v

def low_keep(v):
    return (low(v), None)

def low_pass(kept, grad):
    return (grad,)

def back_keep(v):
    return (v, None)

def back_low(kept, grad):
    return (low(grad),)
low.defvjp(low_keep, low_pass)
low_back.defvjp(back_keep, back_low)
PRECISE = lax.Precision.HIGHEST
NUMBERS = ('NHWC', 'HWIO', 'NHWC')
BETA_ONE = 0.9
BETA_TWO = 0.95
RATE = 0.08
DECAY = 0.1
EPSILON = 1e-08

def convolve(values, weight):
    return lax.conv_general_dilated(values, weight, (1, 1), ((1, 1), (1, 1)), dimension_numbers=NUMBERS, precision=PRECISE)

def upsample(values, weight):
    product = jnp.einsum('nhwc,abcd->nhawbd', values, weight, precision=PRECISE)
    return product.reshape(product.shape[0], 2 * product.shape[1], 2 * product.shape[3], product.shape[5])

def focal(logits, labels, usable):
    logprob = jax.nn.log_softmax(logits, axis=-1)
    picked = jnp.where(labels == 1, logprob[..., 1], logprob[..., 0])
    chance = jnp.exp(picked)
    return jnp.sum(usable.astype(logits.dtype) * (-(1.0 - chance) ** 2 * picked))

def branch(picture, skipped, labels, usable, copies):
    enter, middle, upward, merge, head = copies
    pre_one = low_back(convolve(picture, enter))
    act_one = low(jax.nn.gelu(pre_one))
    pre_two = low_back(convolve(act_one, middle))
    act_two = low(jax.nn.gelu(pre_two))
    raised = low(low_back(upsample(act_two, upward)))
    joined = jnp.concatenate([raised, skipped], axis=-1)
    pre_three = low_back(convolve(joined, merge))
    act_three = low(jax.nn.gelu(pre_three))
    logits = low_back(jnp.einsum('nhwc,ck->nhwk', act_three, head, precision=PRECISE))
    return focal(logits, labels, usable)

def adamw(master, moment, square, gradient):
    moment_new = BETA_ONE * moment + (1.0 - BETA_ONE) * gradient
    square_new = BETA_TWO * square + (1.0 - BETA_TWO) * gradient * gradient
    fixed_moment = moment_new / (1.0 - BETA_ONE ** STEP)
    fixed_square = square_new / (1.0 - BETA_TWO ** STEP)
    master_new = master - RATE * (fixed_moment / (jnp.sqrt(fixed_square) + EPSILON) + DECAY * master)
    return (master_new, moment_new, square_new, master_new.astype(jnp.bfloat16))

def reference(input_a, input_b, skip_a, skip_b, labels_a, labels_b, valid_a, valid_b, w_enter, moment_enter, square_enter, w_middle, moment_middle, square_middle, w_upward, moment_upward, square_upward, w_merge, moment_merge, square_merge, w_head, moment_head, square_head):
    labelled = jnp.sum(valid_a.astype(jnp.float32)) + jnp.sum(valid_b.astype(jnp.float32))
    dataset = ((input_a.astype(jnp.float32), skip_a.astype(jnp.float32), labels_a, valid_a), (input_b.astype(jnp.float32), skip_b.astype(jnp.float32), labels_b, valid_b))
    masters = (w_enter, w_middle, w_upward, w_merge, w_head)

    def mean_loss(weights):
        copies = tuple((low(weight) for weight in weights))
        running = jnp.zeros((), jnp.float32)
        for picture, skipped, labels, usable in dataset:
            running = running + branch(picture, skipped, labels, usable, copies)
        return (running / labelled, running)
    loss_mean, pull, loss_total = jax.vjp(mean_loss, masters, has_aux=True)
    gradients = pull(jnp.ones_like(loss_mean))[0]
    moments = (moment_enter, moment_middle, moment_upward, moment_merge, moment_head)
    squares = (square_enter, square_middle, square_upward, square_merge, square_head)
    results = []
    for index in range(5):
        results.extend(adamw(masters[index], moments[index], squares[index], gradients[index]))
    return (results[0], results[1], results[2], results[3], results[4], results[5], results[6], results[7], results[8], results[9], results[10], results[11], results[12], results[13], results[14], results[15], results[16], results[17], results[18], results[19], loss_total, labelled)
```

```python
import jax
import jax.numpy as jnp
from jax import lax
from jax.experimental import pallas as pl
from jax.experimental.pallas import tpu as pltpu
from jax.sharding import PartitionSpec as P

STEP = 10


NUMBERS = ("NHWC", "HWIO", "NHWC")
BETA_ONE = 0.9
BETA_TWO = 0.95
RATE = 0.08
DECAY = 0.1
EPSILON = 1e-08


def extended(cells, sides, width):
    for axis, dim in sides:
        count = lax.axis_size(axis)
        ends = count - 1
        head = lax.slice_in_dim(cells, 0, width, axis=dim)
        tail = lax.slice_in_dim(cells, cells.shape[dim] - width, cells.shape[dim], axis=dim)
        cells = jnp.concatenate(
            [
                lax.ppermute(tail, axis, [(i, (i + 1) % count) for i in range(ends)]),
                cells,
                lax.ppermute(head, axis, [((i + 1) % count, i) for i in range(ends)]),
            ],
            axis=dim,
        )
    return cells


def shortened(value):

    def short(part):
        return part.astype(jnp.bfloat16) if part.dtype == jnp.float32 else part

    return jax.tree.map(short, value)


def convolve_rows(padded, weight):
    return lax.conv_general_dilated(
        padded,
        weight,
        (1, 1),
        ((0, 0), (1, 1)),
        dimension_numbers=NUMBERS,
        preferred_element_type=jnp.float32,
    )


def flipped(weight):
    return jnp.transpose(weight[::-1, ::-1], (0, 1, 3, 2))


def upsample(values, weight):
    product = jnp.einsum("nhwc,abcd->nhawbd", values, weight, preferred_element_type=jnp.float32)
    return product.reshape(
        product.shape[0], 2 * product.shape[1], 2 * product.shape[3], product.shape[5]
    )


def split_pixels(upstream):
    return upstream.reshape(
        upstream.shape[0], upstream.shape[1] // 2, 2, upstream.shape[2] // 2, 2, upstream.shape[3]
    )


def upsample_back(upstream, weight):
    return jnp.einsum(
        "nhawbd,abcd->nhwc", split_pixels(upstream), weight, preferred_element_type=jnp.float32
    )


def upsample_weight(values, upstream):
    return jnp.einsum(
        "nhwc,nhawbd->abcd", values, split_pixels(upstream), preferred_element_type=jnp.float32
    )


def tap_grads(padded, upstream):
    wide = jnp.pad(padded, ((0, 0), (0, 0), (1, 1), (0, 0)))
    height, across = (upstream.shape[1], upstream.shape[2])
    stacked = []
    for row_tap in range(3):
        tapline = []
        for col_tap in range(3):
            window = wide[:, row_tap : row_tap + height, col_tap : col_tap + across, :]
            tapline.append(
                jnp.einsum("nhwc,nhwd->cd", window, upstream, preferred_element_type=jnp.float32)
            )
        stacked.append(jnp.stack(tapline))
    return jnp.stack(stacked)


def alternate(weight, groups):
    dims = weight.shape
    shaped = weight.reshape(dims[0], dims[1], 2, groups, dims[2] // (2 * groups), dims[3])
    return shaped.transpose(0, 1, 3, 2, 4, 5).reshape(dims)


def deinterleave(weight, groups):
    dims = weight.shape
    shaped = weight.reshape(dims[0], dims[1], groups, 2, dims[2] // (2 * groups), dims[3])
    return shaped.transpose(0, 1, 3, 2, 4, 5).reshape(dims)


def gelu_back(pre_act, upstream):
    return jax.vjp(jax.nn.gelu, pre_act)[1](upstream)[0]


def focal(logits, labels, usable):
    logprob = jax.nn.log_softmax(logits, axis=-1)
    picked = jnp.where(labels == 1, logprob[..., 1], logprob[..., 0])
    chance = jnp.exp(picked)
    return jnp.sum(usable.astype(jnp.float32) * (-((1.0 - chance) ** 2) * picked))


def loss_terms(logits, labels, usable, labelled):
    running, pull = jax.vjp(lambda values: focal(values, labels, usable), logits)
    return (running, pull(1.0 / labelled)[0])


def gather_channels(values):
    return lax.all_gather(values, "col", axis=3, tiled=True)


def spread_back(partial_value):
    return lax.psum_scatter(partial_value, "col", scatter_dimension=3, tiled=True)


def conv_forward(local, weight):
    padded = extended(local, (("ha", 1),), 1)
    whole = gather_channels(padded)
    return (convolve_rows(whole, weight), whole)


def up_forward(local, weight):
    whole = gather_channels(local)
    return (upsample(whole, weight), whole)


def conv_weight_grad(kept, upstream):
    return tap_grads(kept, upstream)


def up_weight_grad(kept, upstream):
    return upsample_weight(kept, upstream)


def backward_weights(merge_up, upward, middle):
    return (flipped(merge_up), upward, flipped(middle))


def conv_input_grad(back_weight, upstream):
    padded = extended(shortened(upstream), (("ha", 1),), 1).astype(upstream.dtype)
    return spread_back(convolve_rows(padded, back_weight))


def up_input_grad(back_weight, upstream):
    return spread_back(upsample_back(upstream, back_weight))


def forward_pass(picture, skipped, copies):
    enter, middle, upward, merge_mixed, back_merge, back_upward, back_middle, head_copy = copies
    pre_one, kept_one = conv_forward(picture, enter)
    act_one = jax.nn.gelu(pre_one).astype(jnp.bfloat16)
    pre_two, kept_two = conv_forward(act_one, middle)
    act_two = jax.nn.gelu(pre_two).astype(jnp.bfloat16)
    raised, kept_up = up_forward(act_two, upward)
    joined = jnp.concatenate([raised.astype(jnp.bfloat16), skipped], axis=3)
    pre_three, kept_three = conv_forward(joined, merge_mixed)
    act_three = jax.nn.gelu(pre_three).astype(jnp.bfloat16)
    partial_value = jnp.einsum(
        "nhwc,ck->nhwk", act_three, head_copy, preferred_element_type=jnp.float32
    )
    return (
        partial_value,
        (pre_one, kept_one, pre_two, kept_two, kept_up, pre_three, kept_three, act_three),
    )


def backward_pass(saved, dlogits, copies):
    enter, middle, upward, merge_mixed, back_merge, back_upward, back_middle, head_copy = copies
    pre_one, kept_one, pre_two, kept_two, kept_up, pre_three, kept_three, act_three = saved
    back_three = jnp.einsum("nhwk,ck->nhwc", dlogits, head_copy, preferred_element_type=jnp.float32)
    grad_head = jnp.einsum("nhwc,nhwk->ck", act_three, dlogits, preferred_element_type=jnp.float32)
    grad_three = gelu_back(pre_three, back_three).astype(jnp.bfloat16)
    grad_merge = conv_weight_grad(kept_three, grad_three)
    d_raised = conv_input_grad(back_merge, grad_three).astype(jnp.bfloat16)
    grad_upward = up_weight_grad(kept_up, d_raised)
    back_two = up_input_grad(back_upward, d_raised)
    grad_two = gelu_back(pre_two, back_two).astype(jnp.bfloat16)
    grad_middle = conv_weight_grad(kept_two, grad_two)
    back_one = conv_input_grad(back_middle, grad_two)
    grad_one = gelu_back(pre_one, back_one).astype(jnp.bfloat16)
    grad_enter = conv_weight_grad(kept_one, grad_one)
    return (grad_enter, grad_middle, grad_upward, grad_merge, grad_head)


def adamw(master, moment, square, gradient):
    moment_new = BETA_ONE * moment + (1.0 - BETA_ONE) * gradient
    square_new = BETA_TWO * square + (1.0 - BETA_TWO) * gradient * gradient
    fixed_moment = moment_new / (1.0 - BETA_ONE**STEP)
    fixed_square = square_new / (1.0 - BETA_TWO**STEP)
    master_new = master - RATE * (
        fixed_moment / (jnp.sqrt(fixed_square) + EPSILON) + DECAY * master
    )
    return (master_new, moment_new, square_new, master_new.astype(jnp.bfloat16))


def own_rows(summed, local):
    return lax.dynamic_slice_in_dim(
        summed, lax.axis_index("ha") * local.shape[2], local.shape[2], 2
    )


def body(
    input_a,
    input_b,
    skip_a,
    skip_b,
    labels_a,
    labels_b,
    valid_a,
    valid_b,
    w_enter,
    moment_enter,
    square_enter,
    w_middle,
    moment_middle,
    square_middle,
    w_upward,
    moment_upward,
    square_upward,
    w_merge,
    moment_merge,
    square_merge,
    w_head,
    moment_head,
    square_head,
):
    groups = lax.axis_size("col")
    enter, middle, upward, merge = (
        lax.all_gather(w_enter.astype(jnp.bfloat16), "ha", axis=2, tiled=True),
        lax.all_gather(w_middle.astype(jnp.bfloat16), "ha", axis=2, tiled=True),
        lax.all_gather(w_upward.astype(jnp.bfloat16), "ha", axis=2, tiled=True),
        lax.all_gather(w_merge.astype(jnp.bfloat16), "ha", axis=2, tiled=True),
    )
    head_low = w_head.astype(jnp.bfloat16)
    merge_up = merge[:, :, : merge.shape[2] // 2]
    back_merge, back_upward, back_middle = backward_weights(merge_up, upward, middle)
    copies = (
        enter,
        middle,
        upward,
        alternate(merge, groups),
        back_merge,
        back_upward,
        back_middle,
        head_low,
    )
    labelled = lax.psum(
        jnp.sum(valid_a.astype(jnp.float32)) + jnp.sum(valid_b.astype(jnp.float32)), "ha"
    )
    partial_a, saved_a = forward_pass(input_a, skip_a, copies)
    partial_b, saved_b = forward_pass(input_b, skip_b, copies)
    logits_a, logits_b = lax.psum((partial_a, partial_b), "col")
    loss_a, dlogits_a = loss_terms(logits_a, labels_a, valid_a, labelled)
    loss_b, dlogits_b = loss_terms(logits_b, labels_b, valid_b, labelled)
    grads_a = backward_pass(saved_a, dlogits_a.astype(jnp.bfloat16), copies)
    grads_b = backward_pass(saved_b, dlogits_b.astype(jnp.bfloat16), copies)
    local_enter = grads_a[0] + grads_b[0]
    local_middle = grads_a[1] + grads_b[1]
    local_upward = grads_a[2] + grads_b[2]
    local_merge = deinterleave(grads_a[3] + grads_b[3], groups)
    local_head = grads_a[4] + grads_b[4]
    local_loss = loss_a + loss_b
    full_enter, full_middle, full_upward, full_merge, head_total, loss_total = (
        lax.psum(local_enter.astype(jnp.bfloat16), "ha").astype(jnp.float32),
        lax.psum(local_middle.astype(jnp.bfloat16), "ha").astype(jnp.float32),
        lax.psum(local_upward.astype(jnp.bfloat16), "ha").astype(jnp.float32),
        lax.psum(local_merge.astype(jnp.bfloat16), "ha").astype(jnp.float32),
        lax.psum(local_head.astype(jnp.bfloat16), "ha").astype(jnp.float32),
        lax.psum(local_loss.astype(jnp.bfloat16), "ha").astype(jnp.float32),
    )
    grad_enter = own_rows(full_enter, w_enter)
    grad_middle = own_rows(full_middle, w_middle)
    grad_upward = own_rows(full_upward, w_upward)
    grad_merge = own_rows(full_merge, w_merge)
    enter_out = adamw(w_enter, moment_enter, square_enter, grad_enter)
    middle_out = adamw(w_middle, moment_middle, square_middle, grad_middle)
    upward_out = adamw(w_upward, moment_upward, square_upward, grad_upward)
    merge_out = adamw(w_merge, moment_merge, square_merge, grad_merge)
    head_out = adamw(w_head, moment_head, square_head, head_total)
    return (
        enter_out[0],
        enter_out[1],
        enter_out[2],
        enter_out[3],
        middle_out[0],
        middle_out[1],
        middle_out[2],
        middle_out[3],
        upward_out[0],
        upward_out[1],
        upward_out[2],
        upward_out[3],
        merge_out[0],
        merge_out[1],
        merge_out[2],
        merge_out[3],
        head_out[0],
        head_out[1],
        head_out[2],
        head_out[3],
        loss_total,
        labelled,
    )


BF = jnp.bfloat16
F32 = jnp.float32
MESH = pl.DeviceIdType.MESH
LANE = 128
PI_PART = 0.7978845608028654
CUBE = 0.044715


def gelu_value(v):
    return 0.5 * v * (1.0 + jnp.tanh(PI_PART * (v + CUBE * (v * v * v))))


def gelu_slope(v):
    bent = jnp.tanh(PI_PART * (v + CUBE * (v * v * v)))
    inner = PI_PART * (1.0 + 3.0 * CUBE * (v * v))
    return 0.5 * (1.0 + bent) + 0.5 * v * (1.0 - bent * bent) * inner


def dot_nn(lhs, rhs):
    return lax.dot_general(lhs, rhs, (((1,), (0,)), ((), ())), preferred_element_type=F32)


def dot_nt(lhs, rhs):
    return lax.dot_general(lhs, rhs, (((1,), (1,)), ((), ())), preferred_element_type=F32)


def span(at, size):
    return pl.ds(pl.multiple_of(at * size, size), size)


SCRATCH = (
    ("IN", (8, 2, 128, 128), BF),
    ("SK", (4, 64, 512), BF),
    ("LB", (16, 8, 128), F32),
    ("W1", (9, 128, 128), BF),
    ("W2", (9, 128, 256), BF),
    ("WU", (16, 64, 256), BF),
    ("W3", (9, 128, 512), BF),
    ("W1T", (128, 1152), BF),
    ("W2T", (256, 1152), BF),
    ("WUT", (256, 1024), BF),
    ("W3T", (512, 1152), BF),
    ("X1", (1152, 2048), BF),
    ("X2", (1152, 2048), BF),
    ("X3", (1152, 2048), BF),
    ("P1", (4, 32, 2048), F32),
    ("P1b", (4, 32, 2048), BF),
    ("R1", (3, 32, 2048), BF),
    ("A1", (4, 32, 2048), BF),
    ("P2b", (128, 2048), BF),
    ("T2", (128, 2048), BF),
    ("S2b", (4, 128, 512), BF),
    ("R2", (3, 128, 512), BF),
    ("pre2", (128, 512), F32),
    ("A2", (8, 128, 512), BF),
    ("J", (2, 4, 128, 768), BF),
    ("P3b", (4, 64, 2048), BF),
    ("T3", (4, 64, 2048), BF),
    ("S3b", (4, 64, 2048), BF),
    ("R3", (3, 64, 2048), BF),
    ("pre3", (64, 2048), F32),
    ("act3", (64, 2048), BF),
    ("LG", (8, 32, 128), F32),
    ("LBL", (32, 128), F32),
    ("DL", (32, 128), F32),
    ("G3", (8, 64, 2048), BF),
    ("Z", (1152, 2048), F32),
    ("HS", (2, 2, 64, 128), F32),
    ("HR", (2, 2, 64, 128), F32),
    ("DB", (4, 64, 128), F32),
    ("DR", (256, 512), BF),
    ("P8", (128, 2048), F32),
    ("P7b", (4, 128, 512), BF),
    ("T7", (4, 128, 512), BF),
    ("S7b", (4, 128, 512), BF),
    ("R7", (3, 128, 512), BF),
    ("G2", (2, 128, 2048), BF),
    ("P8b", (4, 32, 2048), BF),
    ("R8", (3, 32, 2048), BF),
    ("G1", (4, 32, 2048), BF),
    ("GW3", (9, 128, 512), BF),
    ("GWU", (16, 64, 256), BF),
    ("GW2", (9, 128, 256), BF),
    ("GW1", (9, 128, 128), BF),
    ("RG3", (4, 9, 64, 256), BF),
    ("RGU", (16, 64, 256), BF),
    ("RG2", (9, 64, 512), BF),
    ("RG1", (9, 32, 512), BF),
    ("HD", (16, 8, 128), F32),
)
COPIES = 176


def fused(widths, *refs):
    wa, wb = widths
    inT, skT, lab, head, w1, w2, wu, w3, g1o, g2o, guo, g3o, hdo = refs[:13]
    m = {name: ref for (name, _, _), ref in zip(SCRATCH, refs[13:-2])}
    send_sem, recv_sem = refs[-2:]
    h, y = lax.axis_index("ha"), lax.axis_index("col")
    z, x, e = lax.div(h, 4), lax.rem(lax.div(h, 2), 2), lax.rem(h, 2)
    q = 2 * y + x
    s = 2 * q + e
    twin = h + 1 - 2 * e
    started = []
    count = [0]

    def ha(z_, x_, e_):
        return 4 * z_ + 2 * x_ + e_

    def remote(src, dst, h2, y2, sem_s, sem_r):
        return pltpu.make_async_remote_copy(
            src_ref=src,
            dst_ref=dst,
            send_sem=send_sem.at[sem_s],
            recv_sem=recv_sem.at[sem_r],
            device_id={"ha": h2, "col": y2},
            device_id_type=MESH,
        )

    def push(src, dst, h2, y2):
        n = count[0]
        count[0] += 1
        copy = remote(src, dst, h2, y2, n, n)
        copy.start()
        started.append((copy, None))
        return copy

    def reserve(n):
        base = count[0]
        count[0] += n
        return base

    def hand(src, dst, h2, y2, sem_s, sem_r):
        same = jnp.logical_and(h2 == h, y2 == y)
        away = jnp.logical_not(same)
        copy = remote(src, dst, h2, y2, sem_s, sem_r)

        @pl.when(same)
        def _():
            pltpu.make_async_copy(src, dst, recv_sem.at[sem_r]).start()

        @pl.when(away)
        def _():
            copy.start()

        started.append((copy, away))

    def landed(dst, sem_r):
        remote(dst, dst, twin, y, sem_r, sem_r).wait_recv()

    lanes = lax.broadcasted_iota(jnp.int32, (1, LANE), 1)
    left_ok = jnp.logical_and(jnp.logical_and(lanes != 0, lanes != wa), lanes < wa + wb)
    right_ok = jnp.logical_and(lanes != wa - 1, lanes < wa + wb - 1)

    def from_left(v):
        return jnp.where(left_ok, pltpu.roll(v, 1, 1), 0.0)

    def from_right(v):
        return jnp.where(right_ok, pltpu.roll(v, LANE - 1, 1), 0.0)

    J, HR = m["J"], m["HR"]

    @pl.when(z == 0)
    def _():
        J[1, 1:3, :, 0:128] = jnp.zeros((2, 128, 128), BF)
        HR[0] = jnp.zeros((2, 64, 128), F32)

    @pl.when(z == 3)
    def _():
        J[0, 1:3, :, 640:768] = jnp.zeros((2, 128, 128), BF)
        HR[1] = jnp.zeros((2, 64, 128), F32)

    IN, LB = m["IN"], m["LB"]
    in_copies = []
    for dz in range(4):
        for dx in range(2):
            if dz == 0 and dx == 0:
                continue
            zt = lax.rem(z + dz, 4)
            xt = lax.rem(x + dx, 2)
            in_copies.append(
                push(inT.at[span(xt, 128)], IN.at[2 * z + x, e], ha(zt, xt, e), y)
            )
    IN[2 * z + x, e] = inT[span(x, 128), :]

    W1, W2, WU, W3 = m["W1"], m["W2"], m["WU"], m["W3"]
    b1 = reserve(4)
    for i in range(4):
        hand(
            w1.at[:, :, i * 128 : i * 128 + 128],
            W1.at[:, span(2 * x + e, 32), :],
            ha(2 * y + i // 2, lax.rem(z, 2), i % 2),
            lax.div(z, 2),
            b1 + i,
            b1 + 2 * x + e,
        )
    lab_copies = []
    LB[h] = lab[...]
    for d in range(1, 16):
        lab_copies.append(push(lab, LB.at[h], lax.rem(h + d, 16), y))

    for copy in in_copies:
        copy.wait_recv()
    twin_in = push(IN.at[:, e], IN.at[:, e], twin, y)

    b2 = reserve(2)
    for i in range(2):
        hand(
            w2.at[:, :, i * 256 : i * 256 + 256],
            W2.at[:, span(e, 64), :],
            ha(z, i, x),
            y,
            b2 + i,
            b2 + e,
        )
    SK = m["SK"]
    sk_copies = []
    slot = 2 * x + e
    for d in range(1, 4):
        other = lax.rem(slot + d, 4)
        sk_copies.append(push(skT.at[other], SK.at[slot], 4 * z + other, y))
    SK[slot] = skT[slot]
    bu_copies = []
    for d in range(1, 16):
        ht = lax.rem(h + d, 16)
        bu_copies.append(push(wu.at[lax.rem(ht, 4)], WU.at[h], ht, y))
    WU[h] = wu[slot]
    b3 = reserve(4)
    for i in range(4):
        hand(
            w3,
            W3.at[:, span(lax.div(z, 2), 64), span(y, 256)],
            ha(i, x, e),
            lax.rem(z, 2),
            b3 + i,
            b3 + 2 * lax.div(z, 2) + y,
        )

    def patches(block, out):
        def one(i, carry):
            low = block(i)
            v = low.astype(F32)
            kinds = (from_left(v).astype(BF), low, from_right(v).astype(BF))
            for di in (-1, 0, 1):
                row = lax.rem(i - di + 16, 16)
                for dj in range(3):
                    tap = (di + 1) * 3 + dj
                    out[tap * 128 : tap * 128 + 128, span(row, 128)] = kinds[dj]
            return carry

        lax.fori_loop(0, 16, one, 0)
        zero = jnp.zeros((384, 128), BF)
        out[0:384, 0:128] = zero
        out[768:1152, 1920:2048] = zero

    def transposed(weight, out, rows):
        for t in range(weight.shape[0]):
            out[:, t * rows : t * rows + rows] = weight[t].T

    for j in range(4):
        landed(W1.at[:, 32 * j : 32 * j + 32, :], b1 + j)
    transposed(W1, m["W1T"], 128)
    twin_in.wait_recv()
    X1, X2, X3 = m["X1"], m["X2"], m["X3"]
    patches(lambda i: IN[lax.div(i, 2), lax.rem(i, 2)], X1)
    P1, P1b, R1, A1 = m["P1"], m["P1b"], m["R1"], m["A1"]

    def conv_one(n, carry):
        cols = span(n, 512)
        total = dot_nn(m["W1T"][...], X1[:, cols]).reshape(4, 32, 512)
        P1[:, :, cols] = total
        P1b[:, :, cols] = total.astype(BF)
        return carry

    lax.fori_loop(0, 4, conv_one, 0)

    def to_plane(d):
        there = lax.rem(q + d, 4)
        return there, ha(z, lax.rem(there, 2), e), lax.div(there, 2)

    def scatter(source, slots):
        copies = []
        for d in range(1, 4):
            there, h2, y2 = to_plane(d)
            copies.append(push(source.at[there], slots.at[d - 1], h2, y2))
        return copies

    def gather_four(buf):
        copies = []
        for d in range(1, 4):
            _, h2, y2 = to_plane(d)
            copies.append(push(buf.at[q], buf.at[q], h2, y2))
        return copies

    def gather_plane(buf):
        copies = []
        for d in range(1, 4):
            _, h2, y2 = to_plane(d)
            copies.append(push(buf.at[s], buf.at[s], h2, y2))
        last = [push(buf.at[s], buf.at[s], twin, y)]
        for d in range(1, 4):
            copies[d - 1].wait_recv()
            came = 2 * lax.rem(q + 4 - d, 4) + e
            last.append(push(buf.at[came], buf.at[came], twin, y))
        return last

    def arrive(copies):
        for copy in copies:
            copy.wait_recv()

    arrive(scatter(P1b, R1))

    def act_one(n, carry):
        cols = span(n, 512)
        total = P1[q, :, cols] + R1[0, :, cols].astype(F32)
        total = total + R1[1, :, cols].astype(F32) + R1[2, :, cols].astype(F32)
        P1[q, :, cols] = total
        A1[q, :, cols] = gelu_value(total).astype(BF)
        return carry

    lax.fori_loop(0, 4, act_one, 0)
    wait_one = gather_four(A1)
    for j in range(2):
        landed(W2.at[:, 64 * j : 64 * j + 64, :], b2 + j)
    transposed(W2, m["W2T"], 128)
    arrive(wait_one)

    patches(lambda i: A1[:, :, span(i, 128)].reshape(128, 128), X2)
    Z, P2b, T2, S2b, R2 = m["Z"], m["P2b"], m["T2"], m["S2b"], m["R2"]

    def conv_two(n, carry):
        cols = span(n, 512)
        Z[0:256, cols] = dot_nn(m["W2T"][...], X2[:, cols])
        P2b[:, cols] = Z[span(1 - e, 128), cols].astype(BF)
        return carry

    lax.fori_loop(0, 4, conv_two, 0)
    arrive([push(P2b, T2, twin, y)])

    def pair_two(n, carry):
        cols = span(n, 512)
        total = Z[span(e, 128), cols] + T2[:, cols].astype(F32)
        Z[span(e, 128), cols] = total
        S2b[n] = total.astype(BF)
        return carry

    lax.fori_loop(0, 4, pair_two, 0)
    two = []
    for d in range(1, 4):
        zt = lax.rem(z + d, 4)
        two.append(push(S2b.at[zt], R2.at[d - 1], ha(zt, x, e), y))
    for d in range(1, 16):
        bu_copies[d - 1].wait_recv()
    for t in range(8):
        m["WUT"][:, t * 128 : t * 128 + 128] = WU[2 * t : 2 * t + 2].reshape(128, 256).T
    arrive(two)
    pre2, A2 = m["pre2"], m["A2"]
    total = Z[span(e, 128), span(z, 512)] + R2[0].astype(F32)
    total = total + R2[1].astype(F32) + R2[2].astype(F32)
    pre2[...] = total
    A2[s] = gelu_value(total).astype(BF)
    wait_two = gather_plane(A2)
    for copy in sk_copies:
        copy.wait_recv()
    for a in range(2):
        for b in range(2):
            p = 2 * a + b
            for i in range(4):
                J[a, 1 + b, 64:128, 128 + 128 * i : 256 + 128 * i] = SK[i, :, p * 128 : p * 128 + 128]
    arrive(wait_two)

    for p in range(4):
        plane = dot_nn(m["WUT"][p * 64 : p * 64 + 64, :], A2[...].reshape(1024, 512))
        J[p // 2, 1 + p % 2, 0:64, 128:640] = plane.astype(BF)

    def fringe(part, up, down, send_down, keep_down, send_up, keep_up):
        below = remote(send_down, keep_down, lax.rem(h + 4, 16), y, down, down)
        above = remote(send_up, keep_up, lax.rem(h + 12, 16), y, up, up)

        @pl.when(z < 3)
        def _():
            below.start()

        @pl.when(z > 0)
        def _():
            above.start()

        started.append((below, z < 3))
        started.append((above, z > 0))

        def wait():
            @pl.when(z > 0)
            def _():
                below.wait_recv()

            @pl.when(z < 3)
            def _():
                above.wait_recv()

        return wait

    bj = reserve(2)
    fringe(
        None,
        bj,
        bj + 1,
        J.at[1, 1:3, :, 512:640],
        J.at[1, 1:3, :, 0:128],
        J.at[0, 1:3, :, 128:256],
        J.at[0, 1:3, :, 640:768],
    )()
    for a in range(2):
        for i in range(1 - a, 6 - a):
            at = slice(i * 128, i * 128 + 128)
            J[a, 0, :, at] = from_left(J[a, 2, :, at].astype(F32)).astype(BF)
            J[a, 3, :, at] = from_right(J[a, 1, :, at].astype(F32)).astype(BF)
    for a in range(2):
        for b in range(2):
            p = 2 * a + b
            for da in range(3):
                up, di = (a + da - 1) % 2, (a + da - 1) // 2
                for db in range(3):
                    tap = da * 3 + db
                    X3[tap * 128 : tap * 128 + 128, p * 512 : p * 512 + 512] = J[
                        up, b + db, :, (1 + di) * 128 : (5 + di) * 128
                    ]

    for j in range(4):
        t, half = j // 2, j % 2
        landed(W3.at[:, 64 * t : 64 * t + 64, 256 * half : 256 * half + 256], b3 + j)
    transposed(W3, m["W3T"], 128)
    P3b, T3, S3b, R3 = m["P3b"], m["T3"], m["S3b"], m["R3"]

    def conv_three(n, carry):
        cols = span(n, 256)
        Z[0:512, cols] = dot_nn(m["W3T"][...], X3[:, cols])
        for k in range(4):
            P3b[k, :, cols] = Z[span(2 * k + 1 - e, 64), cols].astype(BF)
        return carry

    lax.fori_loop(0, 8, conv_three, 0)
    arrive([push(P3b, T3, twin, y)])

    def pair_three(n, carry):
        cols = span(n, 512)
        for k in range(4):
            total = Z[span(2 * k + e, 64), cols] + T3[k, :, cols].astype(F32)
            Z[span(2 * k + e, 64), cols] = total
            S3b[k, :, cols] = total.astype(BF)
        return carry

    lax.fori_loop(0, 4, pair_three, 0)
    arrive(scatter(S3b, R3))
    pre3, act3, LG = m["pre3"], m["act3"], m["LG"]
    wide = (64, LANE)
    h0 = jnp.broadcast_to(head[:, 0:1], wide)
    h1 = jnp.broadcast_to(head[:, 1:2], wide)
    for b in range(16):
        cols = slice(b * 128, b * 128 + 128)
        total = Z[span(s, 64), cols] + R3[0, :, cols].astype(F32)
        total = total + R3[1, :, cols].astype(F32) + R3[2, :, cols].astype(F32)
        pre3[:, cols] = total
        act = gelu_value(total).astype(BF)
        act3[:, cols] = act
        act = act.astype(F32)
        LG[s, b : b + 1, :] = jnp.sum(act * h0, axis=0, keepdims=True)
        LG[s, 16 + b : 17 + b, :] = jnp.sum(act * h1, axis=0, keepdims=True)
    wait_logits = gather_plane(LG)
    for copy in lab_copies:
        copy.wait_recv()
    LBL = m["LBL"]
    for p in range(4):
        for i in range(4):
            LBL[p * 4 + i : p * 4 + i + 1, :] = LB[4 * z + i, p : p + 1, :]
            LBL[16 + p * 4 + i : 17 + p * 4 + i, :] = LB[4 * z + i, 4 + p : 5 + p, :]
    every = jnp.sum(LB[...], axis=0)
    labelled = jnp.sum(jnp.sum(every[4:8, :], axis=0, keepdims=True), axis=1, keepdims=True)
    arrive(wait_logits)

    logits = LG[0]
    for k in range(1, 8):
        logits = logits + LG[k]
    zero, one = logits[0:16, :], logits[16:32, :]
    picks, usable = LBL[0:16, :] > 0.5, LBL[16:32, :]
    top = jnp.maximum(zero, one)
    lse = top + jnp.log(jnp.exp(zero - top) + jnp.exp(one - top))
    logp = jnp.where(picks, one, zero) - lse
    rest = jnp.exp(jnp.where(picks, zero, one) - lse)
    chance = jnp.exp(logp)
    gap = 1.0 - chance
    terms = usable * (-(gap * gap) * logp)
    slope = (2.0 * gap * chance * logp - gap * gap) * usable / labelled
    own, other = slope * gap, -slope * rest
    DL = m["DL"]
    DL[0:16, :] = jnp.where(picks, other, own).astype(BF).astype(F32)
    DL[16:32, :] = jnp.where(picks, own, other).astype(BF).astype(F32)
    loss = jnp.sum(jnp.sum(terms, axis=0, keepdims=True), axis=1, keepdims=True)
    G3, HD = m["G3"], m["HD"]
    sum0 = jnp.zeros(wide, F32)
    sum1 = jnp.zeros(wide, F32)
    for b in range(16):
        cols = slice(b * 128, b * 128 + 128)
        d0 = jnp.broadcast_to(DL[b : b + 1, :], wide)
        d1 = jnp.broadcast_to(DL[16 + b : 17 + b, :], wide)
        G3[s, :, cols] = ((h0 * d0 + h1 * d1) * gelu_slope(pre3[:, cols])).astype(BF)
        act = act3[:, cols].astype(F32)
        sum0 = sum0 + act * d0
        sum1 = sum1 + act * d1
    wait_g3 = gather_plane(G3)
    side = lax.broadcasted_iota(jnp.int32, wide, 1)
    sum0 = jnp.sum(sum0, axis=1, keepdims=True)
    sum1 = jnp.sum(sum1, axis=1, keepdims=True)
    tile = jnp.where(side == 0, sum0, jnp.where(side == 1, sum1, 0.0))
    HD[h, 0:8, 0:64] = tile.T[0:8, :]
    HD[h, 2:3, 0:64] = jnp.broadcast_to(loss, (1, 64))
    hd_copies = []
    for d in range(1, 16):
        hd_copies.append(push(HD.at[h], HD.at[h], lax.rem(h + d, 16), y))
    arrive(wait_g3)

    HS, DB, DR = m["HS"], m["DB"], m["DR"]

    def back_three(n, carry):
        cols = span(n, 256)
        Z[0:576, cols] = dot_nn(
            W3[:, 0:64, :].reshape(576, 512), G3[:, :, cols].reshape(512, 256)
        )
        return carry

    lax.fori_loop(0, 8, back_three, 0)
    ways = (((0, 0, 0), (1, -1, 0), (1, 1, 1)), ((0, -1, -1), (0, 1, 0), (1, 0, 0)))

    def raised_block(a, b, i):
        straight, bent = [], []
        for ao, da, di in ways[a]:
            io = i - di
            if io < 0 or io > 3 or (i < 0 or i > 3) and di == 0:
                continue
            for bo, db, dj in ways[b]:
                tap = (da + 1) * 3 + db + 1
                at = ((2 * ao + bo) * 4 + io) * 128
                (straight if dj == 0 else bent).append(Z[tap * 64 : tap * 64 + 64, at : at + 128])
        turned = sum(bent[1:], bent[0])
        turned = from_left(turned) if b == 0 else from_right(turned)
        return sum(straight, turned)

    for b in range(2):
        HS[0, b] = raised_block(0, b, 4)
        HS[1, b] = raised_block(1, b, -1)
    bh = reserve(2)
    wait_fringe = fringe(None, bh, bh + 1, HS.at[0], HR.at[0], HS.at[1], HR.at[1])
    for a in range(2):
        for b in range(2):
            p = 2 * a + b
            for i in range(4):
                block = raised_block(a, b, i)
                if i == 3 * a:
                    DB[p] = block
                else:
                    DR[p * 64 : p * 64 + 64, i * 128 : i * 128 + 128] = block.astype(BF)
    wait_fringe()
    for a in range(2):
        for b in range(2):
            p = 2 * a + b
            DR[p * 64 : p * 64 + 64, a * 384 : a * 384 + 128] = (DB[p] + HR[a, b]).astype(BF)

    P7b, T7, S7b, R7 = m["P7b"], m["T7"], m["S7b"], m["R7"]

    def back_up(k, carry):
        Z[span(k, 128), 0:512] = dot_nn(WU[pl.ds(2 * k, 2)].reshape(128, 256), DR[...])
        return carry

    lax.fori_loop(0, 8, back_up, 0)
    for k in range(4):
        P7b[k] = Z[span(2 * k + 1 - e, 128), 0:512].astype(BF)
    wait_pair = push(P7b, T7, twin, y)

    GW3, GWU, GW2, GW1 = m["GW3"], m["GWU"], m["GW2"], m["GW1"]
    RG3, RGU, RG2, RG1 = m["RG3"], m["RGU"], m["RG2"], m["RG1"]

    def pair_seven():
        for k in range(4):
            total = Z[span(2 * k + e, 128), 0:512] + T7[k].astype(F32)
            Z[span(2 * k + e, 128), 0:512] = total
            S7b[k] = total.astype(BF)

    wait_pair.wait_recv()
    pair_seven()
    wait_seven = scatter(S7b, R7)

    def grad_three(t, carry):
        GW3[t] = dot_nt(X3[span(t, 128), :], G3[...].reshape(512, 2048)).astype(BF)
        return carry

    lax.fori_loop(0, 9, grad_three, 0)

    def grad_up(k, carry):
        GWU[pl.ds(2 * k, 2)] = dot_nt(A2[k], DR[...]).astype(BF).reshape(2, 64, 256)
        return carry

    lax.fori_loop(0, 8, grad_up, 0)
    arrive(wait_seven)
    G2 = m["G2"]
    total = Z[span(s, 128), 0:512] + R7[0].astype(F32)
    total = total + R7[1].astype(F32) + R7[2].astype(F32)
    G2[e, :, span(z, 512)] = (total * gelu_slope(pre2[...])).astype(BF)
    mine = G2.at[e, :, span(z, 512)]
    g2_copies = []
    for d in range(1, 4):
        zt = lax.rem(z + d, 4)
        g2_copies.append(push(mine, mine, ha(zt, x, e), y))
    g2_last = [push(mine, mine, twin, y)]
    for d in range(1, 4):
        g2_copies[d - 1].wait_recv()
        came = G2.at[e, :, span(lax.rem(z + 4 - d, 4), 512)]
        g2_last.append(push(came, came, twin, y))

    bg3 = reserve(4)
    for j in range(4):
        t, half = j // 2, j % 2
        hand(
            GW3.at[:, 64 * t : 64 * t + 64, 256 * half : 256 * half + 256],
            RG3.at[z],
            ha(2 * t + y, x, e),
            half,
            bg3 + j,
            bg3 + z,
        )
    gu_copies = []
    for d in range(1, 16):
        ht = lax.rem(h + d, 16)
        gu_copies.append(push(GWU.at[ht], RGU.at[h], ht, y))
    RGU[h] = GWU[h]
    arrive(g2_last)

    def back_two(n, carry):
        cols = span(n, 256)
        Z[:, cols] = dot_nn(W2[...].reshape(1152, 256), G2[:, :, cols].reshape(256, 256))
        return carry

    lax.fori_loop(0, 8, back_two, 0)
    P8b, R8, G1 = m["P8b"], m["R8"], m["G1"]
    P8 = m["P8"]

    def fold(i, carry):
        sums = []
        for dj in range(3):
            part = None
            for di in range(3):
                row = i - (di - 1)
                inside = jnp.logical_and(row >= 0, row <= 15)
                row = jnp.clip(row, 0, 15)
                tap = di * 3 + dj
                block = jnp.where(inside, Z[tap * 128 : tap * 128 + 128, span(row, 128)], 0.0)
                part = block if part is None else part + block
            sums.append(part)
        total = sums[1] + from_right(sums[0]) + from_left(sums[2])
        P8[:, span(i, 128)] = total
        P8b[:, :, span(i, 128)] = total.reshape(4, 32, 128).astype(BF)
        return carry

    lax.fori_loop(0, 16, fold, 0)
    wait_eight = scatter(P8b, R8)

    def grad_two(t, carry):
        GW2[t] = dot_nt(X2[span(t, 128), :], G2[...].reshape(256, 2048)).astype(BF)
        return carry

    lax.fori_loop(0, 9, grad_two, 0)
    arrive(wait_eight)

    def act_back(n, carry):
        cols = span(n, 512)
        total = P8[span(q, 32), cols] + R8[0, :, cols].astype(F32)
        total = total + R8[1, :, cols].astype(F32) + R8[2, :, cols].astype(F32)
        G1[q, :, cols] = (total * gelu_slope(P1[q, :, cols])).astype(BF)
        return carry

    lax.fori_loop(0, 4, act_back, 0)
    wait_g1 = gather_four(G1)
    bg2 = reserve(2)
    for j in range(2):
        hand(
            GW2.at[:, 64 * j : 64 * j + 64, :],
            RG2.at[:, :, span(x, 256)],
            ha(z, e, j),
            y,
            bg2 + j,
            bg2 + x,
        )
    arrive(wait_g1)

    def grad_one(t, carry):
        GW1[t] = dot_nt(X1[span(t, 128), :], G1[...].reshape(128, 2048)).astype(BF)
        return carry

    lax.fori_loop(0, 9, grad_one, 0)
    bg1 = reserve(4)
    r_low = 2 * lax.rem(z, 2) + e
    for j in range(4):
        hand(
            GW1.at[:, 32 * j : 32 * j + 32, :],
            RG1.at[:, :, span(r_low, 128)],
            ha(q, j // 2, j % 2),
            lax.div(z, 2),
            bg1 + j,
            bg1 + r_low,
        )

    for copy in hd_copies:
        copy.wait_recv()
    for j in range(4):
        hdo[j] = HD[j] + HD[4 + j] + HD[8 + j] + HD[12 + j]
    hdo[4] = jnp.broadcast_to(labelled, (8, 128))
    for k in range(4):
        landed(RG3.at[k], bg3 + k)
    for t in range(9):
        g3o[t] = (RG3[0, t].astype(F32) + RG3[1, t].astype(F32)) + (
            RG3[2, t].astype(F32) + RG3[3, t].astype(F32)
        )
    for copy in gu_copies:
        copy.wait_recv()
    for k in range(4):
        guo[k] = (RGU[k].astype(F32) + RGU[4 + k].astype(F32)) + (
            RGU[8 + k].astype(F32) + RGU[12 + k].astype(F32)
        )
    for k in range(2):
        landed(RG2.at[:, :, 256 * k : 256 * k + 256], bg2 + k)
    g2o[...] = RG2[...]
    for k in range(4):
        landed(RG1.at[:, :, 128 * k : 128 * k + 128], bg1 + k)
    g1o[...] = RG1[...]
    for copy, when in started:
        if when is None:
            copy.wait_send()
        else:
            pl.when(when)(copy.wait_send)


def parity_planes(rows):
    _, two, across, chans = rows.shape
    split = rows.reshape(two, across // 2, 2, chans)
    return split.transpose(3, 0, 2, 1)


def lane_blocks(first, second):
    free = LANE - first.shape[-1] - second.shape[-1]
    both = jnp.concatenate([first, second], axis=-1)
    return jnp.pad(both, [(0, 0)] * (both.ndim - 1) + [(0, free)])


def resident_body(
    input_a,
    input_b,
    skip_a,
    skip_b,
    labels_a,
    labels_b,
    valid_a,
    valid_b,
    w_enter,
    moment_enter,
    square_enter,
    w_middle,
    moment_middle,
    square_middle,
    w_upward,
    moment_upward,
    square_upward,
    w_merge,
    moment_merge,
    square_merge,
    w_head,
    moment_head,
    square_head,
):
    slot = lax.rem(lax.axis_index("ha"), 4)
    pixels = lane_blocks(input_a[0, 0].T, input_b[0, 0].T)
    skips = lane_blocks(parity_planes(skip_a), parity_planes(skip_b)).reshape(4, 64, 512)
    marks = jnp.concatenate(
        [
            lane_blocks(parity_planes(one[..., None]), parity_planes(two[..., None])).reshape(4, LANE)
            for one, two in ((labels_a, labels_b), (valid_a, valid_b))
        ]
    ).astype(F32)
    head_low = w_head.astype(BF).astype(F32)
    head_own = jnp.pad(lax.dynamic_slice_in_dim(head_low, slot * 64, 64, 0), ((0, 0), (0, 126)))
    upward = w_upward.astype(BF).reshape(4, 64, 4, 64).transpose(2, 1, 0, 3).reshape(4, 64, 256)
    vmem = pl.BlockSpec(memory_space=pltpu.VMEM)
    g1, g2, gu, g3, hd = pl.pallas_call(
        lambda *refs: fused((input_a.shape[2], input_b.shape[2]), *refs),
        out_shape=(
            jax.ShapeDtypeStruct((9, 32, 512), BF),
            jax.ShapeDtypeStruct((9, 64, 512), BF),
            jax.ShapeDtypeStruct((4, 64, 256), F32),
            jax.ShapeDtypeStruct((9, 64, 256), F32),
            jax.ShapeDtypeStruct((5, 8, 128), F32),
        ),
        in_specs=[vmem] * 8,
        out_specs=[vmem] * 5,
        scratch_shapes=[pltpu.VMEM(shape, kind) for _, shape, kind in SCRATCH]
        + [pltpu.SemaphoreType.DMA((COPIES,)), pltpu.SemaphoreType.DMA((COPIES,))],
        compiler_params=pltpu.CompilerParams(
            has_side_effects=True, vmem_limit_bytes=60 * 1024 * 1024
        ),
    )(
        pixels,
        skips,
        marks,
        head_own,
        w_enter.astype(BF).reshape(9, 32, 512),
        w_middle.astype(BF).reshape(9, 64, 512),
        upward,
        w_merge.astype(BF).reshape(9, 64, 256),
    )
    grad_enter = g1.astype(F32).reshape(w_enter.shape)
    grad_middle = g2.astype(F32).reshape(w_middle.shape)
    grad_upward = gu.reshape(4, 64, 4, 64).transpose(2, 1, 0, 3).reshape(w_upward.shape)
    grad_merge = g3.reshape(w_merge.shape)
    grad_head = hd[0:4, 0:2, 0:64].transpose(0, 2, 1).reshape(w_head.shape)
    return (
        *adamw(w_enter, moment_enter, square_enter, grad_enter),
        *adamw(w_middle, moment_middle, square_middle, grad_middle),
        *adamw(w_upward, moment_upward, square_upward, grad_upward),
        *adamw(w_merge, moment_merge, square_merge, grad_merge),
        *adamw(w_head, moment_head, square_head, grad_head),
        hd[0, 2, 0],
        hd[4, 0, 0],
    )


def chosen(*args):
    input_a, input_b, skip_a = args[0], args[1], args[2]
    w_enter, w_middle, w_upward, w_merge = args[8], args[11], args[14], args[17]
    fits = (
        lax.axis_size("ha") == 16
        and lax.axis_size("col") == 2
        and input_a.shape[:2] == (1, 1)
        and input_b.shape[:2] == (1, 1)
        and input_a.shape[3] == 256
        and skip_a.shape[3] == 256
        and input_a.shape[2] + input_b.shape[2] <= LANE
        and w_enter.shape == (3, 3, 32, 512)
        and w_middle.shape == (3, 3, 64, 512)
        and w_upward.shape == (2, 2, 64, 256)
        and w_merge.shape == (3, 3, 64, 256)
    )
    return resident_body(*args) if fits else body(*args)


def solution(mesh):
    placed = (
        P(None, "ha", None, "col"),
        P(None, "ha", None, "col"),
        P(None, "ha", None, "col"),
        P(None, "ha", None, "col"),
        P(None, "ha", None),
        P(None, "ha", None),
        P(None, "ha", None),
        P(None, "ha", None),
        P(None, None, "ha", "col"),
        P(None, None, "ha", "col"),
        P(None, None, "ha", "col"),
        P(None, None, "ha", "col"),
        P(None, None, "ha", "col"),
        P(None, None, "ha", "col"),
        P(None, None, "ha", "col"),
        P(None, None, "ha", "col"),
        P(None, None, "ha", "col"),
        P(None, None, "ha", "col"),
        P(None, None, "ha", "col"),
        P(None, None, "ha", "col"),
        P("col", None),
        P("col", None),
        P("col", None),
    )
    return jax.shard_map(
        chosen,
        mesh=mesh,
        in_specs=placed,
        out_specs=(
            P(None, None, "ha", "col"),
            P(None, None, "ha", "col"),
            P(None, None, "ha", "col"),
            P(None, None, "ha", "col"),
            P(None, None, "ha", "col"),
            P(None, None, "ha", "col"),
            P(None, None, "ha", "col"),
            P(None, None, "ha", "col"),
            P(None, None, "ha", "col"),
            P(None, None, "ha", "col"),
            P(None, None, "ha", "col"),
            P(None, None, "ha", "col"),
            P(None, None, "ha", "col"),
            P(None, None, "ha", "col"),
            P(None, None, "ha", "col"),
            P(None, None, "ha", "col"),
            P("col", None),
            P("col", None),
            P("col", None),
            P("col", None),
            P(),
            P(),
        ),
        check_vma=False,
    )
```

```python
import jax
import jax.numpy as jnp
from jax import lax
from jax.experimental import pallas as pl
from jax.experimental.pallas import tpu as pltpu
from jax.sharding import PartitionSpec as P

STEP = 10


NUMBERS = ("NHWC", "HWIO", "NHWC")
BETA_ONE = 0.9
BETA_TWO = 0.95
RATE = 0.08
DECAY = 0.1
EPSILON = 1e-08


def extended(cells, sides, width):
    for axis, dim in sides:
        count = lax.axis_size(axis)
        ends = count - 1
        head = lax.slice_in_dim(cells, 0, width, axis=dim)
        tail = lax.slice_in_dim(cells, cells.shape[dim] - width, cells.shape[dim], axis=dim)
        cells = jnp.concatenate(
            [
                lax.ppermute(tail, axis, [(i, (i + 1) % count) for i in range(ends)]),
                cells,
                lax.ppermute(head, axis, [((i + 1) % count, i) for i in range(ends)]),
            ],
            axis=dim,
        )
    return cells


def shortened(value):

    def short(part):
        return part.astype(jnp.bfloat16) if part.dtype == jnp.float32 else part

    return jax.tree.map(short, value)


def convolve_rows(padded, weight):
    return lax.conv_general_dilated(
        padded,
        weight,
        (1, 1),
        ((0, 0), (1, 1)),
        dimension_numbers=NUMBERS,
        preferred_element_type=jnp.float32,
    )


def flipped(weight):
    return jnp.transpose(weight[::-1, ::-1], (0, 1, 3, 2))


def upsample(values, weight):
    product = jnp.einsum("nhwc,abcd->nhawbd", values, weight, preferred_element_type=jnp.float32)
    return product.reshape(
        product.shape[0], 2 * product.shape[1], 2 * product.shape[3], product.shape[5]
    )


def split_pixels(upstream):
    return upstream.reshape(
        upstream.shape[0], upstream.shape[1] // 2, 2, upstream.shape[2] // 2, 2, upstream.shape[3]
    )


def upsample_back(upstream, weight):
    return jnp.einsum(
        "nhawbd,abcd->nhwc", split_pixels(upstream), weight, preferred_element_type=jnp.float32
    )


def upsample_weight(values, upstream):
    return jnp.einsum(
        "nhwc,nhawbd->abcd", values, split_pixels(upstream), preferred_element_type=jnp.float32
    )


def tap_grads(padded, upstream):
    wide = jnp.pad(padded, ((0, 0), (0, 0), (1, 1), (0, 0)))
    height, across = (upstream.shape[1], upstream.shape[2])
    stacked = []
    for row_tap in range(3):
        tapline = []
        for col_tap in range(3):
            window = wide[:, row_tap : row_tap + height, col_tap : col_tap + across, :]
            tapline.append(
                jnp.einsum("nhwc,nhwd->cd", window, upstream, preferred_element_type=jnp.float32)
            )
        stacked.append(jnp.stack(tapline))
    return jnp.stack(stacked)


def alternate(weight, groups):
    dims = weight.shape
    shaped = weight.reshape(dims[0], dims[1], 2, groups, dims[2] // (2 * groups), dims[3])
    return shaped.transpose(0, 1, 3, 2, 4, 5).reshape(dims)


def deinterleave(weight, groups):
    dims = weight.shape
    shaped = weight.reshape(dims[0], dims[1], groups, 2, dims[2] // (2 * groups), dims[3])
    return shaped.transpose(0, 1, 3, 2, 4, 5).reshape(dims)


def gelu_back(pre_act, upstream):
    return jax.vjp(jax.nn.gelu, pre_act)[1](upstream)[0]


def focal(logits, labels, usable):
    logprob = jax.nn.log_softmax(logits, axis=-1)
    picked = jnp.where(labels == 1, logprob[..., 1], logprob[..., 0])
    chance = jnp.exp(picked)
    return jnp.sum(usable.astype(jnp.float32) * (-((1.0 - chance) ** 2) * picked))


def loss_terms(logits, labels, usable, labelled):
    running, pull = jax.vjp(lambda values: focal(values, labels, usable), logits)
    return (running, pull(1.0 / labelled)[0])


def gather_channels(values):
    return lax.all_gather(values, "col", axis=3, tiled=True)


def spread_back(partial_value):
    return lax.psum_scatter(partial_value, "col", scatter_dimension=3, tiled=True)


def conv_forward(local, weight):
    padded = extended(local, (("ha", 1),), 1)
    whole = gather_channels(padded)
    return (convolve_rows(whole, weight), whole)


def up_forward(local, weight):
    whole = gather_channels(local)
    return (upsample(whole, weight), whole)


def conv_weight_grad(kept, upstream):
    return tap_grads(kept, upstream)


def up_weight_grad(kept, upstream):
    return upsample_weight(kept, upstream)


def backward_weights(merge_up, upward, middle):
    return (flipped(merge_up), upward, flipped(middle))


def conv_input_grad(back_weight, upstream):
    padded = extended(shortened(upstream), (("ha", 1),), 1).astype(upstream.dtype)
    return spread_back(convolve_rows(padded, back_weight))


def up_input_grad(back_weight, upstream):
    return spread_back(upsample_back(upstream, back_weight))


def forward_pass(picture, skipped, copies):
    enter, middle, upward, merge_mixed, back_merge, back_upward, back_middle, head_copy = copies
    pre_one, kept_one = conv_forward(picture, enter)
    act_one = jax.nn.gelu(pre_one).astype(jnp.bfloat16)
    pre_two, kept_two = conv_forward(act_one, middle)
    act_two = jax.nn.gelu(pre_two).astype(jnp.bfloat16)
    raised, kept_up = up_forward(act_two, upward)
    joined = jnp.concatenate([raised.astype(jnp.bfloat16), skipped], axis=3)
    pre_three, kept_three = conv_forward(joined, merge_mixed)
    act_three = jax.nn.gelu(pre_three).astype(jnp.bfloat16)
    partial_value = jnp.einsum(
        "nhwc,ck->nhwk", act_three, head_copy, preferred_element_type=jnp.float32
    )
    return (
        partial_value,
        (pre_one, kept_one, pre_two, kept_two, kept_up, pre_three, kept_three, act_three),
    )


def backward_pass(saved, dlogits, copies):
    enter, middle, upward, merge_mixed, back_merge, back_upward, back_middle, head_copy = copies
    pre_one, kept_one, pre_two, kept_two, kept_up, pre_three, kept_three, act_three = saved
    back_three = jnp.einsum("nhwk,ck->nhwc", dlogits, head_copy, preferred_element_type=jnp.float32)
    grad_head = jnp.einsum("nhwc,nhwk->ck", act_three, dlogits, preferred_element_type=jnp.float32)
    grad_three = gelu_back(pre_three, back_three).astype(jnp.bfloat16)
    grad_merge = conv_weight_grad(kept_three, grad_three)
    d_raised = conv_input_grad(back_merge, grad_three).astype(jnp.bfloat16)
    grad_upward = up_weight_grad(kept_up, d_raised)
    back_two = up_input_grad(back_upward, d_raised)
    grad_two = gelu_back(pre_two, back_two).astype(jnp.bfloat16)
    grad_middle = conv_weight_grad(kept_two, grad_two)
    back_one = conv_input_grad(back_middle, grad_two)
    grad_one = gelu_back(pre_one, back_one).astype(jnp.bfloat16)
    grad_enter = conv_weight_grad(kept_one, grad_one)
    return (grad_enter, grad_middle, grad_upward, grad_merge, grad_head)


def adamw(master, moment, square, gradient):
    moment_new = BETA_ONE * moment + (1.0 - BETA_ONE) * gradient
    square_new = BETA_TWO * square + (1.0 - BETA_TWO) * gradient * gradient
    fixed_moment = moment_new / (1.0 - BETA_ONE**STEP)
    fixed_square = square_new / (1.0 - BETA_TWO**STEP)
    master_new = master - RATE * (
        fixed_moment / (jnp.sqrt(fixed_square) + EPSILON) + DECAY * master
    )
    return (master_new, moment_new, square_new, master_new.astype(jnp.bfloat16))


def own_rows(summed, local):
    return lax.dynamic_slice_in_dim(
        summed, lax.axis_index("ha") * local.shape[2], local.shape[2], 2
    )


def body(
    input_a,
    input_b,
    skip_a,
    skip_b,
    labels_a,
    labels_b,
    valid_a,
    valid_b,
    w_enter,
    moment_enter,
    square_enter,
    w_middle,
    moment_middle,
    square_middle,
    w_upward,
    moment_upward,
    square_upward,
    w_merge,
    moment_merge,
    square_merge,
    w_head,
    moment_head,
    square_head,
):
    groups = lax.axis_size("col")
    enter, middle, upward, merge = (
        lax.all_gather(w_enter.astype(jnp.bfloat16), "ha", axis=2, tiled=True),
        lax.all_gather(w_middle.astype(jnp.bfloat16), "ha", axis=2, tiled=True),
        lax.all_gather(w_upward.astype(jnp.bfloat16), "ha", axis=2, tiled=True),
        lax.all_gather(w_merge.astype(jnp.bfloat16), "ha", axis=2, tiled=True),
    )
    head_low = w_head.astype(jnp.bfloat16)
    merge_up = merge[:, :, : merge.shape[2] // 2]
    back_merge, back_upward, back_middle = backward_weights(merge_up, upward, middle)
    copies = (
        enter,
        middle,
        upward,
        alternate(merge, groups),
        back_merge,
        back_upward,
        back_middle,
        head_low,
    )
    labelled = lax.psum(
        jnp.sum(valid_a.astype(jnp.float32)) + jnp.sum(valid_b.astype(jnp.float32)), "ha"
    )
    partial_a, saved_a = forward_pass(input_a, skip_a, copies)
    partial_b, saved_b = forward_pass(input_b, skip_b, copies)
    logits_a, logits_b = lax.psum((partial_a, partial_b), "col")
    loss_a, dlogits_a = loss_terms(logits_a, labels_a, valid_a, labelled)
    loss_b, dlogits_b = loss_terms(logits_b, labels_b, valid_b, labelled)
    grads_a = backward_pass(saved_a, dlogits_a.astype(jnp.bfloat16), copies)
    grads_b = backward_pass(saved_b, dlogits_b.astype(jnp.bfloat16), copies)
    local_enter = grads_a[0] + grads_b[0]
    local_middle = grads_a[1] + grads_b[1]
    local_upward = grads_a[2] + grads_b[2]
    local_merge = deinterleave(grads_a[3] + grads_b[3], groups)
    local_head = grads_a[4] + grads_b[4]
    local_loss = loss_a + loss_b
    full_enter, full_middle, full_upward, full_merge, head_total, loss_total = (
        lax.psum(local_enter.astype(jnp.bfloat16), "ha").astype(jnp.float32),
        lax.psum(local_middle.astype(jnp.bfloat16), "ha").astype(jnp.float32),
        lax.psum(local_upward.astype(jnp.bfloat16), "ha").astype(jnp.float32),
        lax.psum(local_merge.astype(jnp.bfloat16), "ha").astype(jnp.float32),
        lax.psum(local_head.astype(jnp.bfloat16), "ha").astype(jnp.float32),
        lax.psum(local_loss.astype(jnp.bfloat16), "ha").astype(jnp.float32),
    )
    grad_enter = own_rows(full_enter, w_enter)
    grad_middle = own_rows(full_middle, w_middle)
    grad_upward = own_rows(full_upward, w_upward)
    grad_merge = own_rows(full_merge, w_merge)
    enter_out = adamw(w_enter, moment_enter, square_enter, grad_enter)
    middle_out = adamw(w_middle, moment_middle, square_middle, grad_middle)
    upward_out = adamw(w_upward, moment_upward, square_upward, grad_upward)
    merge_out = adamw(w_merge, moment_merge, square_merge, grad_merge)
    head_out = adamw(w_head, moment_head, square_head, head_total)
    return (
        enter_out[0],
        enter_out[1],
        enter_out[2],
        enter_out[3],
        middle_out[0],
        middle_out[1],
        middle_out[2],
        middle_out[3],
        upward_out[0],
        upward_out[1],
        upward_out[2],
        upward_out[3],
        merge_out[0],
        merge_out[1],
        merge_out[2],
        merge_out[3],
        head_out[0],
        head_out[1],
        head_out[2],
        head_out[3],
        loss_total,
        labelled,
    )


BF = jnp.bfloat16
F32 = jnp.float32
MESH = pl.DeviceIdType.MESH
LANE = 128
PI_PART = 0.7978845608028654
CUBE = 0.044715


def gelu_value(v):
    return 0.5 * v * (1.0 + jnp.tanh(PI_PART * (v + CUBE * (v * v * v))))


def gelu_slope(v):
    bent = jnp.tanh(PI_PART * (v + CUBE * (v * v * v)))
    inner = PI_PART * (1.0 + 3.0 * CUBE * (v * v))
    return 0.5 * (1.0 + bent) + 0.5 * v * (1.0 - bent * bent) * inner


def dot_nn(lhs, rhs):
    return lax.dot_general(lhs, rhs, (((1,), (0,)), ((), ())), preferred_element_type=F32)


def dot_nt(lhs, rhs):
    return lax.dot_general(lhs, rhs, (((1,), (1,)), ((), ())), preferred_element_type=F32)


def span(at, size):
    return pl.ds(pl.multiple_of(at * size, size), size)


SCRATCH = (
    ("inT", (2, 4, 32, 128), BF),
    ("skT", (4, 64, 512), BF),
    ("lab", (8, 128), F32),
    ("flat", (4, 256, 128), F32),
    ("w1", (9, 32, 512), BF),
    ("w2", (9, 64, 512), BF),
    ("wu", (4, 64, 256), BF),
    ("w3", (9, 64, 256), BF),
    ("IN", (8, 2, 4, 32, 128), BF),
    ("SK", (4, 64, 512), BF),
    ("LB", (16, 8, 128), F32),
    ("W1", (9, 128, 128), BF),
    ("W2", (9, 128, 256), BF),
    ("WU", (16, 64, 256), BF),
    ("W3", (9, 128, 512), BF),
    ("W1T", (128, 1152), BF),
    ("W2T", (256, 1152), BF),
    ("WUT", (256, 1024), BF),
    ("W3T", (512, 1152), BF),
    ("X", (1152, 2048), BF),
    ("P1", (4, 32, 2048), F32),
    ("P1b", (4, 32, 2048), BF),
    ("R1", (3, 32, 2048), BF),
    ("A1", (4, 32, 2048), BF),
    ("P2b", (128, 2048), BF),
    ("T2", (128, 2048), BF),
    ("S2b", (4, 128, 512), BF),
    ("R2", (3, 128, 512), BF),
    ("pre2", (128, 512), F32),
    ("A2", (8, 128, 512), BF),
    ("J", (2, 4, 128, 768), BF),
    ("P3b", (4, 64, 2048), BF),
    ("T3", (4, 64, 2048), BF),
    ("S3b", (4, 64, 2048), BF),
    ("R3", (3, 64, 2048), BF),
    ("pre3", (64, 2048), F32),
    ("act3", (64, 2048), BF),
    ("LG", (8, 32, 128), F32),
    ("LBL", (32, 128), F32),
    ("DL", (32, 128), F32),
    ("G3", (8, 64, 2048), BF),
    ("Z", (1152, 2048), F32),
    ("HS", (2, 2, 64, 128), F32),
    ("HR", (2, 2, 64, 128), F32),
    ("DB", (4, 64, 128), F32),
    ("DR", (256, 512), BF),
    ("P8", (128, 2048), F32),
    ("P7b", (4, 128, 512), BF),
    ("T7", (4, 128, 512), BF),
    ("S7b", (4, 128, 512), BF),
    ("R7", (3, 128, 512), BF),
    ("G2", (2, 128, 2048), BF),
    ("P8b", (4, 32, 2048), BF),
    ("R8", (3, 32, 2048), BF),
    ("G1", (4, 32, 2048), BF),
    ("GW3", (9, 128, 512), BF),
    ("GWU", (16, 64, 256), BF),
    ("GW2", (9, 128, 256), BF),
    ("GW1", (9, 128, 128), BF),
    ("RG3", (4, 9, 64, 256), BF),
    ("RGU", (16, 64, 256), BF),
    ("RG2", (9, 64, 512), BF),
    ("RG1", (9, 32, 512), BF),
    ("HD", (16, 8, 128), F32),
)
COPIES = 176


def fused(widths, *refs):
    wa, wb = widths
    rows_a, rows_b, skip_a, skip_b, marks_a, marks_b, f1, f2, fu, f3, fh = refs[:11]
    g1o, g2o, guo, g3o, hdo = refs[11:16]
    m = {name: ref for (name, _, _), ref in zip(SCRATCH, refs[16:-2])}
    send_sem, recv_sem = refs[-2:]
    h, y = lax.axis_index("ha"), lax.axis_index("col")
    z, x, e = lax.div(h, 4), lax.rem(lax.div(h, 2), 2), lax.rem(h, 2)
    q = 2 * y + x
    s = 2 * q + e
    twin = h + 1 - 2 * e
    started = []
    count = [0]

    def ha(z_, x_, e_):
        return 4 * z_ + 2 * x_ + e_

    def remote(src, dst, h2, y2, sem_s, sem_r):
        return pltpu.make_async_remote_copy(
            src_ref=src,
            dst_ref=dst,
            send_sem=send_sem.at[sem_s],
            recv_sem=recv_sem.at[sem_r],
            device_id={"ha": h2, "col": y2},
            device_id_type=MESH,
        )

    def push(src, dst, h2, y2):
        n = count[0]
        count[0] += 1
        copy = remote(src, dst, h2, y2, n, n)
        copy.start()
        started.append((copy, None))
        return copy

    def reserve(n):
        base = count[0]
        count[0] += n
        return base

    def hand(src, dst, h2, y2, sem_s, sem_r):
        same = jnp.logical_and(h2 == h, y2 == y)
        away = jnp.logical_not(same)
        copy = remote(src, dst, h2, y2, sem_s, sem_r)

        @pl.when(same)
        def _():
            pltpu.make_async_copy(src, dst, recv_sem.at[sem_r]).start()

        @pl.when(away)
        def _():
            copy.start()

        started.append((copy, away))

    def landed(dst, sem_r):
        remote(dst, dst, twin, y, sem_r, sem_r).wait_recv()

    lanes = lax.broadcasted_iota(jnp.int32, (1, LANE), 1)
    left_ok = jnp.logical_and(jnp.logical_and(lanes != 0, lanes != wa), lanes < wa + wb)
    right_ok = jnp.logical_and(lanes != wa - 1, lanes < wa + wb - 1)

    def from_left(v):
        return jnp.where(left_ok, pltpu.roll(v, 1, 1), 0.0)

    def from_right(v):
        return jnp.where(right_ok, pltpu.roll(v, LANE - 1, 1), 0.0)

    J, HR = m["J"], m["HR"]

    @pl.when(z == 0)
    def _():
        J[1, 1:3, :, 0:128] = jnp.zeros((2, 128, 128), BF)
        HR[0] = jnp.zeros((2, 64, 128), F32)

    @pl.when(z == 3)
    def _():
        J[0, 1:3, :, 640:768] = jnp.zeros((2, 128, 128), BF)
        HR[1] = jnp.zeros((2, 64, 128), F32)

    inT, skT, lab, flat = m["inT"], m["skT"], m["lab"], m["flat"]
    w1, w2, wu, w3 = m["w1"], m["w2"], m["wu"], m["w3"]
    wide_a, wide_b = 2 * wa, 2 * wb
    for c in range(2):
        half = slice(c * 128, c * 128 + 128)
        flat[c, 96:128, :] = jnp.zeros((32, 128), F32)
        flat[c, 0:wa, :] = rows_a[:, half].astype(F32)
        flat[c, wa : wa + wb, :] = rows_b[:, half].astype(F32)
        inT[c] = flat[c, 0:128, :].T.astype(BF).reshape(4, 32, 128)
    w1[...] = f1[...].astype(BF)
    place = lax.broadcasted_iota(jnp.int32, (256, LANE), 0)
    lane = lax.broadcasted_iota(jnp.int32, (256, LANE), 1)
    spread = jnp.zeros((8, 256), F32)
    spread = spread + jnp.pad(marks_a[...].astype(F32), ((0, 0), (0, 256 - wide_a)))
    spread = spread + jnp.concatenate(
        [
            jnp.zeros((8, wide_a), F32),
            marks_b[...].astype(F32),
            jnp.zeros((8, 256 - wide_a - wide_b), F32),
        ],
        axis=1,
    )
    for b in range(2):
        pick = jnp.where(place == 2 * lane + b, 1.0, 0.0)
        planes = dot_nn(spread.astype(BF), pick.astype(BF))
        for a in range(2):
            lab[2 * a + b : 2 * a + b + 1, :] = planes[a : a + 1, :]
            lab[4 + 2 * a + b : 5 + 2 * a + b, :] = planes[2 + a : 3 + a, :]

    IN, LB = m["IN"], m["LB"]
    in_copies = []
    for dz in range(4):
        zt = lax.rem(z + dz, 4)
        for d in range(4):
            if dz == 0 and d == 0:
                continue
            there = lax.rem(2 * x + y + d, 4)
            in_copies.append(
                push(
                    inT.at[:, there],
                    IN.at[2 * z + x, e, pl.ds(2 * y, 2)],
                    ha(zt, lax.div(there, 2), e),
                    lax.rem(there, 2),
                )
            )
    IN[2 * z + x, e, pl.ds(2 * y, 2)] = inT[:, 2 * x + y]

    W1, W2, WU, W3 = m["W1"], m["W2"], m["WU"], m["W3"]
    b1 = reserve(4)
    for i in range(4):
        hand(
            w1.at[:, :, i * 128 : i * 128 + 128],
            W1.at[:, span(z, 32), :],
            ha(2 * y + i // 2, x, i % 2),
            e,
            b1 + i,
            b1 + z,
        )
    lab_copies = []
    LB[h] = lab[...]
    for d in range(1, 16):
        lab_copies.append(push(lab, LB.at[h], lax.rem(h + d, 16), y))

    for copy in in_copies:
        copy.wait_recv()
    twin_in = push(IN.at[:, e], IN.at[:, e], twin, y)

    w2[...] = f2[...].astype(BF)
    w3[...] = f3[...].astype(BF)
    for k in range(4):
        wu[k] = jnp.concatenate([fu[p, :, k * 64 : k * 64 + 64] for p in range(4)], axis=1).astype(BF)
    for a in range(2):
        for c in range(2):
            half = slice(c * 128, c * 128 + 128)
            buf = flat.at[2 * a + c]
            buf[224:256, :] = jnp.zeros((32, 128), F32)
            buf[0:wide_a, :] = skip_a[a, :, half].astype(F32)
            buf[wide_a : wide_a + wide_b, :] = skip_b[a, :, half].astype(F32)
            for b in range(2):
                p = 2 * a + b
                plane = buf[pl.ds(b, 128, stride=2), :]
                skT[2 * c : 2 * c + 2, :, p * 128 : p * 128 + 128] = plane.T.astype(BF).reshape(2, 64, 128)
    b2 = reserve(2)
    for i in range(2):
        hand(
            w2.at[:, :, i * 256 : i * 256 + 256],
            W2.at[:, span(e, 64), :],
            ha(z, i, x),
            y,
            b2 + i,
            b2 + e,
        )
    SK = m["SK"]
    sk_copies = []
    slot = 2 * x + e
    for d in range(1, 4):
        other = lax.rem(slot + d, 4)
        sk_copies.append(push(skT.at[other], SK.at[slot], 4 * z + other, y))
    SK[slot] = skT[slot]
    bu_copies = []
    for d in range(1, 16):
        ht = lax.rem(h + d, 16)
        bu_copies.append(push(wu.at[lax.rem(ht, 4)], WU.at[h], ht, y))
    WU[h] = wu[slot]
    b3 = reserve(4)
    for i in range(4):
        hand(
            w3,
            W3.at[:, span(lax.div(z, 2), 64), span(y, 256)],
            ha(i, x, e),
            lax.rem(z, 2),
            b3 + i,
            b3 + 2 * lax.div(z, 2) + y,
        )

    def patches(block, out):
        def one(i, carry):
            low = block(i)
            v = low.astype(F32)
            kinds = (from_left(v).astype(BF), low, from_right(v).astype(BF))
            for di in (-1, 0, 1):
                row = lax.rem(i - di + 16, 16)
                for dj in range(3):
                    tap = (di + 1) * 3 + dj
                    out[tap * 128 : tap * 128 + 128, span(row, 128)] = kinds[dj]
            return carry

        lax.fori_loop(0, 16, one, 0)
        zero = jnp.zeros((384, 128), BF)
        out[0:384, 0:128] = zero
        out[768:1152, 1920:2048] = zero

    def transposed(weight, out, rows):
        for t in range(weight.shape[0]):
            out[:, t * rows : t * rows + rows] = weight[t].T

    for j in range(4):
        landed(W1.at[:, 32 * j : 32 * j + 32, :], b1 + j)
    transposed(W1, m["W1T"], 128)
    twin_in.wait_recv()
    X = m["X"]

    def input_block(i):
        return IN[lax.div(i, 2), lax.rem(i, 2)].reshape(128, 128)

    def middle_block(i):
        return A1[:, :, span(i, 128)].reshape(128, 128)

    patches(input_block, X)
    P1, P1b, R1, A1 = m["P1"], m["P1b"], m["R1"], m["A1"]

    def conv_one(n, carry):
        cols = span(n, 512)
        total = dot_nn(m["W1T"][...], X[:, cols]).reshape(4, 32, 512)
        P1[:, :, cols] = total
        P1b[:, :, cols] = total.astype(BF)
        return carry

    lax.fori_loop(0, 4, conv_one, 0)

    def to_plane(d):
        there = lax.rem(q + d, 4)
        return there, ha(z, lax.rem(there, 2), e), lax.div(there, 2)

    def scatter(source, slots):
        copies = []
        for d in range(1, 4):
            there, h2, y2 = to_plane(d)
            copies.append(push(source.at[there], slots.at[d - 1], h2, y2))
        return copies

    def gather_four(buf):
        copies = []
        for d in range(1, 4):
            _, h2, y2 = to_plane(d)
            copies.append(push(buf.at[q], buf.at[q], h2, y2))
        return copies

    def gather_plane(buf):
        copies = []
        for d in range(1, 4):
            _, h2, y2 = to_plane(d)
            copies.append(push(buf.at[s], buf.at[s], h2, y2))
        last = [push(buf.at[s], buf.at[s], twin, y)]
        for d in range(1, 4):
            copies[d - 1].wait_recv()
            came = 2 * lax.rem(q + 4 - d, 4) + e
            last.append(push(buf.at[came], buf.at[came], twin, y))
        return last

    def arrive(copies):
        for copy in copies:
            copy.wait_recv()

    arrive(scatter(P1b, R1))

    def act_one(n, carry):
        cols = span(n, 512)
        total = P1[q, :, cols] + R1[0, :, cols].astype(F32)
        total = total + R1[1, :, cols].astype(F32) + R1[2, :, cols].astype(F32)
        P1[q, :, cols] = total
        A1[q, :, cols] = gelu_value(total).astype(BF)
        return carry

    lax.fori_loop(0, 4, act_one, 0)
    wait_one = gather_four(A1)
    for j in range(2):
        landed(W2.at[:, 64 * j : 64 * j + 64, :], b2 + j)
    transposed(W2, m["W2T"], 128)
    arrive(wait_one)

    patches(middle_block, X)
    Z, P2b, T2, S2b, R2 = m["Z"], m["P2b"], m["T2"], m["S2b"], m["R2"]

    def conv_two(n, carry):
        cols = span(n, 512)
        Z[0:256, cols] = dot_nn(m["W2T"][...], X[:, cols])
        P2b[:, cols] = Z[span(1 - e, 128), cols].astype(BF)
        return carry

    lax.fori_loop(0, 4, conv_two, 0)
    arrive([push(P2b, T2, twin, y)])

    def pair_two(n, carry):
        cols = span(n, 512)
        total = Z[span(e, 128), cols] + T2[:, cols].astype(F32)
        Z[span(e, 128), cols] = total
        S2b[n] = total.astype(BF)
        return carry

    lax.fori_loop(0, 4, pair_two, 0)
    two = []
    for d in range(1, 4):
        zt = lax.rem(z + d, 4)
        two.append(push(S2b.at[zt], R2.at[d - 1], ha(zt, x, e), y))
    for d in range(1, 16):
        bu_copies[d - 1].wait_recv()
    for t in range(8):
        m["WUT"][:, t * 128 : t * 128 + 128] = WU[2 * t : 2 * t + 2].reshape(128, 256).T
    arrive(two)
    pre2, A2 = m["pre2"], m["A2"]
    total = Z[span(e, 128), span(z, 512)] + R2[0].astype(F32)
    total = total + R2[1].astype(F32) + R2[2].astype(F32)
    pre2[...] = total
    A2[s] = gelu_value(total).astype(BF)
    wait_two = gather_plane(A2)
    for copy in sk_copies:
        copy.wait_recv()
    for a in range(2):
        for b in range(2):
            p = 2 * a + b
            for i in range(4):
                J[a, 1 + b, 64:128, 128 + 128 * i : 256 + 128 * i] = SK[i, :, p * 128 : p * 128 + 128]
    arrive(wait_two)

    for p in range(4):
        plane = dot_nn(m["WUT"][p * 64 : p * 64 + 64, :], A2[...].reshape(1024, 512))
        J[p // 2, 1 + p % 2, 0:64, 128:640] = plane.astype(BF)

    def fringe(part, up, down, send_down, keep_down, send_up, keep_up):
        below = remote(send_down, keep_down, lax.rem(h + 4, 16), y, down, down)
        above = remote(send_up, keep_up, lax.rem(h + 12, 16), y, up, up)

        @pl.when(z < 3)
        def _():
            below.start()

        @pl.when(z > 0)
        def _():
            above.start()

        started.append((below, z < 3))
        started.append((above, z > 0))

        def wait():
            @pl.when(z > 0)
            def _():
                below.wait_recv()

            @pl.when(z < 3)
            def _():
                above.wait_recv()

        return wait

    bj = reserve(2)
    fringe(
        None,
        bj,
        bj + 1,
        J.at[1, 1:3, :, 512:640],
        J.at[1, 1:3, :, 0:128],
        J.at[0, 1:3, :, 128:256],
        J.at[0, 1:3, :, 640:768],
    )()
    for a in range(2):
        for i in range(1 - a, 6 - a):
            at = slice(i * 128, i * 128 + 128)
            J[a, 0, :, at] = from_left(J[a, 2, :, at].astype(F32)).astype(BF)
            J[a, 3, :, at] = from_right(J[a, 1, :, at].astype(F32)).astype(BF)
    for a in range(2):
        for b in range(2):
            p = 2 * a + b
            for da in range(3):
                up, di = (a + da - 1) % 2, (a + da - 1) // 2
                for db in range(3):
                    tap = da * 3 + db
                    X[tap * 128 : tap * 128 + 128, p * 512 : p * 512 + 512] = J[
                        up, b + db, :, (1 + di) * 128 : (5 + di) * 128
                    ]

    for j in range(4):
        t, half = j // 2, j % 2
        landed(W3.at[:, 64 * t : 64 * t + 64, 256 * half : 256 * half + 256], b3 + j)
    transposed(W3, m["W3T"], 128)
    P3b, T3, S3b, R3 = m["P3b"], m["T3"], m["S3b"], m["R3"]

    def conv_three(n, carry):
        cols = span(n, 256)
        Z[0:512, cols] = dot_nn(m["W3T"][...], X[:, cols])
        for k in range(4):
            P3b[k, :, cols] = Z[span(2 * k + 1 - e, 64), cols].astype(BF)
        return carry

    lax.fori_loop(0, 8, conv_three, 0)
    arrive([push(P3b, T3, twin, y)])

    def pair_three(n, carry):
        cols = span(n, 512)
        for k in range(4):
            total = Z[span(2 * k + e, 64), cols] + T3[k, :, cols].astype(F32)
            Z[span(2 * k + e, 64), cols] = total
            S3b[k, :, cols] = total.astype(BF)
        return carry

    lax.fori_loop(0, 4, pair_three, 0)
    arrive(scatter(S3b, R3))
    pre3, act3, LG = m["pre3"], m["act3"], m["LG"]
    wide = (64, LANE)
    head = fh[span(slot, 64), :].astype(BF).astype(F32)
    h0 = jnp.broadcast_to(head[:, 0:1], wide)
    h1 = jnp.broadcast_to(head[:, 1:2], wide)
    for b in range(16):
        cols = slice(b * 128, b * 128 + 128)
        total = Z[span(s, 64), cols] + R3[0, :, cols].astype(F32)
        total = total + R3[1, :, cols].astype(F32) + R3[2, :, cols].astype(F32)
        pre3[:, cols] = total
        act = gelu_value(total).astype(BF)
        act3[:, cols] = act
        act = act.astype(F32)
        LG[s, b : b + 1, :] = jnp.sum(act * h0, axis=0, keepdims=True)
        LG[s, 16 + b : 17 + b, :] = jnp.sum(act * h1, axis=0, keepdims=True)
    wait_logits = gather_plane(LG)
    for copy in lab_copies:
        copy.wait_recv()
    LBL = m["LBL"]
    for p in range(4):
        for i in range(4):
            LBL[p * 4 + i : p * 4 + i + 1, :] = LB[4 * z + i, p : p + 1, :]
            LBL[16 + p * 4 + i : 17 + p * 4 + i, :] = LB[4 * z + i, 4 + p : 5 + p, :]
    every = jnp.sum(LB[...], axis=0)
    labelled = jnp.sum(jnp.sum(every[4:8, :], axis=0, keepdims=True), axis=1, keepdims=True)
    arrive(wait_logits)

    logits = LG[0]
    for k in range(1, 8):
        logits = logits + LG[k]
    zero, one = logits[0:16, :], logits[16:32, :]
    picks, usable = LBL[0:16, :] > 0.5, LBL[16:32, :]
    top = jnp.maximum(zero, one)
    lse = top + jnp.log(jnp.exp(zero - top) + jnp.exp(one - top))
    logp = jnp.where(picks, one, zero) - lse
    rest = jnp.exp(jnp.where(picks, zero, one) - lse)
    chance = jnp.exp(logp)
    gap = 1.0 - chance
    terms = usable * (-(gap * gap) * logp)
    slope = (2.0 * gap * chance * logp - gap * gap) * usable / labelled
    own, other = slope * gap, -slope * rest
    DL = m["DL"]
    DL[0:16, :] = jnp.where(picks, other, own).astype(BF).astype(F32)
    DL[16:32, :] = jnp.where(picks, own, other).astype(BF).astype(F32)
    loss = jnp.sum(jnp.sum(terms, axis=0, keepdims=True), axis=1, keepdims=True)
    G3, HD = m["G3"], m["HD"]
    sum0 = jnp.zeros(wide, F32)
    sum1 = jnp.zeros(wide, F32)
    for b in range(16):
        cols = slice(b * 128, b * 128 + 128)
        d0 = jnp.broadcast_to(DL[b : b + 1, :], wide)
        d1 = jnp.broadcast_to(DL[16 + b : 17 + b, :], wide)
        G3[s, :, cols] = ((h0 * d0 + h1 * d1) * gelu_slope(pre3[:, cols])).astype(BF)
        act = act3[:, cols].astype(F32)
        sum0 = sum0 + act * d0
        sum1 = sum1 + act * d1
    wait_g3 = gather_plane(G3)
    side = lax.broadcasted_iota(jnp.int32, wide, 1)
    sum0 = jnp.sum(sum0, axis=1, keepdims=True)
    sum1 = jnp.sum(sum1, axis=1, keepdims=True)
    tile = jnp.where(side == 0, sum0, jnp.where(side == 1, sum1, 0.0))
    HD[h, 0:8, 0:64] = tile.T[0:8, :]
    HD[h, 2:3, 0:64] = jnp.broadcast_to(loss, (1, 64))
    hd_copies = []
    for d in range(1, 16):
        hd_copies.append(push(HD.at[h], HD.at[h], lax.rem(h + d, 16), y))
    arrive(wait_g3)

    HS, DB, DR = m["HS"], m["DB"], m["DR"]

    def back_three(n, carry):
        cols = span(n, 256)
        Z[0:576, cols] = dot_nn(
            W3[:, 0:64, :].reshape(576, 512), G3[:, :, cols].reshape(512, 256)
        )
        return carry

    lax.fori_loop(0, 8, back_three, 0)
    ways = (((0, 0, 0), (1, -1, 0), (1, 1, 1)), ((0, -1, -1), (0, 1, 0), (1, 0, 0)))

    def raised_block(a, b, i):
        straight, bent = [], []
        for ao, da, di in ways[a]:
            io = i - di
            if io < 0 or io > 3 or (i < 0 or i > 3) and di == 0:
                continue
            for bo, db, dj in ways[b]:
                tap = (da + 1) * 3 + db + 1
                at = ((2 * ao + bo) * 4 + io) * 128
                (straight if dj == 0 else bent).append(Z[tap * 64 : tap * 64 + 64, at : at + 128])
        turned = sum(bent[1:], bent[0])
        turned = from_left(turned) if b == 0 else from_right(turned)
        return sum(straight, turned)

    for b in range(2):
        HS[0, b] = raised_block(0, b, 4)
        HS[1, b] = raised_block(1, b, -1)
    bh = reserve(2)
    wait_fringe = fringe(None, bh, bh + 1, HS.at[0], HR.at[0], HS.at[1], HR.at[1])
    for a in range(2):
        for b in range(2):
            p = 2 * a + b
            for i in range(4):
                block = raised_block(a, b, i)
                if i == 3 * a:
                    DB[p] = block
                else:
                    DR[p * 64 : p * 64 + 64, i * 128 : i * 128 + 128] = block.astype(BF)
    wait_fringe()
    for a in range(2):
        for b in range(2):
            p = 2 * a + b
            DR[p * 64 : p * 64 + 64, a * 384 : a * 384 + 128] = (DB[p] + HR[a, b]).astype(BF)

    P7b, T7, S7b, R7 = m["P7b"], m["T7"], m["S7b"], m["R7"]

    def back_up(k, carry):
        Z[span(k, 128), 0:512] = dot_nn(WU[pl.ds(2 * k, 2)].reshape(128, 256), DR[...])
        return carry

    lax.fori_loop(0, 8, back_up, 0)
    for k in range(4):
        P7b[k] = Z[span(2 * k + 1 - e, 128), 0:512].astype(BF)
    wait_pair = push(P7b, T7, twin, y)

    GW3, GWU, GW2, GW1 = m["GW3"], m["GWU"], m["GW2"], m["GW1"]
    RG3, RGU, RG2, RG1 = m["RG3"], m["RGU"], m["RG2"], m["RG1"]

    def pair_seven():
        for k in range(4):
            total = Z[span(2 * k + e, 128), 0:512] + T7[k].astype(F32)
            Z[span(2 * k + e, 128), 0:512] = total
            S7b[k] = total.astype(BF)

    wait_pair.wait_recv()
    pair_seven()
    wait_seven = scatter(S7b, R7)

    def grad_three(t, carry):
        GW3[t] = dot_nt(X[span(t, 128), :], G3[...].reshape(512, 2048)).astype(BF)
        return carry

    lax.fori_loop(0, 9, grad_three, 0)

    def grad_up(k, carry):
        GWU[pl.ds(2 * k, 2)] = dot_nt(A2[k], DR[...]).astype(BF).reshape(2, 64, 256)
        return carry

    lax.fori_loop(0, 8, grad_up, 0)
    arrive(wait_seven)
    G2 = m["G2"]
    total = Z[span(s, 128), 0:512] + R7[0].astype(F32)
    total = total + R7[1].astype(F32) + R7[2].astype(F32)
    G2[e, :, span(z, 512)] = (total * gelu_slope(pre2[...])).astype(BF)
    mine = G2.at[e, :, span(z, 512)]
    g2_copies = []
    for d in range(1, 4):
        zt = lax.rem(z + d, 4)
        g2_copies.append(push(mine, mine, ha(zt, x, e), y))
    g2_last = [push(mine, mine, twin, y)]
    for d in range(1, 4):
        g2_copies[d - 1].wait_recv()
        came = G2.at[e, :, span(lax.rem(z + 4 - d, 4), 512)]
        g2_last.append(push(came, came, twin, y))

    bg3 = reserve(4)
    for j in range(4):
        t, half = j // 2, j % 2
        hand(
            GW3.at[:, 64 * t : 64 * t + 64, 256 * half : 256 * half + 256],
            RG3.at[z],
            ha(2 * t + y, x, e),
            half,
            bg3 + j,
            bg3 + z,
        )
    gu_copies = []
    for d in range(1, 16):
        ht = lax.rem(h + d, 16)
        gu_copies.append(push(GWU.at[ht], RGU.at[h], ht, y))
    RGU[h] = GWU[h]
    patches(middle_block, X)
    arrive(g2_last)

    def back_two(n, carry):
        cols = span(n, 256)
        Z[:, cols] = dot_nn(W2[...].reshape(1152, 256), G2[:, :, cols].reshape(256, 256))
        return carry

    lax.fori_loop(0, 8, back_two, 0)
    P8b, R8, G1 = m["P8b"], m["R8"], m["G1"]
    P8 = m["P8"]

    def fold(i, carry):
        sums = []
        for dj in range(3):
            part = None
            for di in range(3):
                row = i - (di - 1)
                inside = jnp.logical_and(row >= 0, row <= 15)
                row = jnp.clip(row, 0, 15)
                tap = di * 3 + dj
                block = jnp.where(inside, Z[tap * 128 : tap * 128 + 128, span(row, 128)], 0.0)
                part = block if part is None else part + block
            sums.append(part)
        total = sums[1] + from_right(sums[0]) + from_left(sums[2])
        P8[:, span(i, 128)] = total
        P8b[:, :, span(i, 128)] = total.reshape(4, 32, 128).astype(BF)
        return carry

    lax.fori_loop(0, 16, fold, 0)
    wait_eight = scatter(P8b, R8)

    def grad_two(t, carry):
        GW2[t] = dot_nt(X[span(t, 128), :], G2[...].reshape(256, 2048)).astype(BF)
        return carry

    lax.fori_loop(0, 9, grad_two, 0)
    arrive(wait_eight)

    def act_back(n, carry):
        cols = span(n, 512)
        total = P8[span(q, 32), cols] + R8[0, :, cols].astype(F32)
        total = total + R8[1, :, cols].astype(F32) + R8[2, :, cols].astype(F32)
        G1[q, :, cols] = (total * gelu_slope(P1[q, :, cols])).astype(BF)
        return carry

    lax.fori_loop(0, 4, act_back, 0)
    wait_g1 = gather_four(G1)
    bg2 = reserve(2)
    for j in range(2):
        hand(
            GW2.at[:, 64 * j : 64 * j + 64, :],
            RG2.at[:, :, span(x, 256)],
            ha(z, e, j),
            y,
            bg2 + j,
            bg2 + x,
        )
    patches(input_block, X)
    arrive(wait_g1)

    def grad_one(t, carry):
        GW1[t] = dot_nt(X[span(t, 128), :], G1[...].reshape(128, 2048)).astype(BF)
        return carry

    lax.fori_loop(0, 9, grad_one, 0)
    bg1 = reserve(4)
    r_low = 2 * lax.rem(z, 2) + e
    for j in range(4):
        hand(
            GW1.at[:, 32 * j : 32 * j + 32, :],
            RG1.at[:, :, span(r_low, 128)],
            ha(j, x, y),
            lax.div(z, 2),
            bg1 + j,
            bg1 + r_low,
        )

    for copy in hd_copies:
        copy.wait_recv()
    for j in range(4):
        hdo[j] = HD[j] + HD[4 + j] + HD[8 + j] + HD[12 + j]
    hdo[4] = jnp.broadcast_to(labelled, (8, 128))
    for k in range(4):
        landed(RG3.at[k], bg3 + k)
    for t in range(9):
        g3o[t] = (RG3[0, t].astype(F32) + RG3[1, t].astype(F32)) + (
            RG3[2, t].astype(F32) + RG3[3, t].astype(F32)
        )
    for copy in gu_copies:
        copy.wait_recv()
    sums = []
    for k in range(4):
        sums.append(
            (RGU[k].astype(F32) + RGU[4 + k].astype(F32))
            + (RGU[8 + k].astype(F32) + RGU[12 + k].astype(F32))
        )
    for p in range(4):
        guo[p] = jnp.concatenate([part[:, p * 64 : p * 64 + 64] for part in sums], axis=1)
    for k in range(2):
        landed(RG2.at[:, :, 256 * k : 256 * k + 256], bg2 + k)
    g2o[...] = RG2[...]
    for k in range(4):
        landed(RG1.at[:, :, 128 * k : 128 * k + 128], bg1 + k)
    g1o[...] = RG1[...]
    for copy, when in started:
        if when is None:
            copy.wait_send()
        else:
            pl.when(when)(copy.wait_send)


def resident_body(
    input_a,
    input_b,
    skip_a,
    skip_b,
    labels_a,
    labels_b,
    valid_a,
    valid_b,
    w_enter,
    moment_enter,
    square_enter,
    w_middle,
    moment_middle,
    square_middle,
    w_upward,
    moment_upward,
    square_upward,
    w_merge,
    moment_merge,
    square_merge,
    w_head,
    moment_head,
    square_head,
):
    marks = [
        jnp.pad(jnp.concatenate([label[0], usable[0]]), ((0, 4), (0, 0)))
        for label, usable in ((labels_a, valid_a), (labels_b, valid_b))
    ]
    vmem = pl.BlockSpec(memory_space=pltpu.VMEM)
    g1, g2, gu, g3, hd = pl.pallas_call(
        lambda *refs: fused((input_a.shape[2], input_b.shape[2]), *refs),
        out_shape=(
            jax.ShapeDtypeStruct((9, 32, 512), BF),
            jax.ShapeDtypeStruct((9, 64, 512), BF),
            jax.ShapeDtypeStruct((4, 64, 256), F32),
            jax.ShapeDtypeStruct((9, 64, 256), F32),
            jax.ShapeDtypeStruct((5, 8, 128), F32),
        ),
        in_specs=[vmem] * 11,
        out_specs=[vmem] * 5,
        scratch_shapes=[pltpu.VMEM(shape, kind) for _, shape, kind in SCRATCH]
        + [pltpu.SemaphoreType.DMA((COPIES,)), pltpu.SemaphoreType.DMA((COPIES,))],
        compiler_params=pltpu.CompilerParams(
            has_side_effects=True, vmem_limit_bytes=56 * 1024 * 1024
        ),
    )(
        input_a[0, 0],
        input_b[0, 0],
        skip_a[0],
        skip_b[0],
        *marks,
        w_enter.reshape(9, 32, 512),
        w_middle.reshape(9, 64, 512),
        w_upward.reshape(4, 64, 256),
        w_merge.reshape(9, 64, 256),
        w_head,
    )
    grad_enter = g1.astype(F32).reshape(w_enter.shape)
    grad_middle = g2.astype(F32).reshape(w_middle.shape)
    grad_upward = gu.reshape(w_upward.shape)
    grad_merge = g3.reshape(w_merge.shape)
    grad_head = hd[0:4, 0:2, 0:64].transpose(0, 2, 1).reshape(w_head.shape)
    return (
        *adamw(w_enter, moment_enter, square_enter, grad_enter),
        *adamw(w_middle, moment_middle, square_middle, grad_middle),
        *adamw(w_upward, moment_upward, square_upward, grad_upward),
        *adamw(w_merge, moment_merge, square_merge, grad_merge),
        *adamw(w_head, moment_head, square_head, grad_head),
        hd[0, 2, 0],
        hd[4, 0, 0],
    )


def chosen(*args):
    input_a, input_b, skip_a = args[0], args[1], args[2]
    w_enter, w_middle, w_upward, w_merge = args[8], args[11], args[14], args[17]
    fits = (
        lax.axis_size("ha") == 16
        and lax.axis_size("col") == 2
        and input_a.shape[:2] == (1, 1)
        and input_b.shape[:2] == (1, 1)
        and input_a.shape[3] == 256
        and skip_a.shape[3] == 256
        and input_a.shape[2] + input_b.shape[2] <= LANE
        and w_enter.shape == (3, 3, 32, 512)
        and w_middle.shape == (3, 3, 64, 512)
        and w_upward.shape == (2, 2, 64, 256)
        and w_merge.shape == (3, 3, 64, 256)
    )
    return resident_body(*args) if fits else body(*args)


def solution(mesh):
    placed = (
        P(None, "ha", None, "col"),
        P(None, "ha", None, "col"),
        P(None, "ha", None, "col"),
        P(None, "ha", None, "col"),
        P(None, "ha", None),
        P(None, "ha", None),
        P(None, "ha", None),
        P(None, "ha", None),
        P(None, None, "ha", "col"),
        P(None, None, "ha", "col"),
        P(None, None, "ha", "col"),
        P(None, None, "ha", "col"),
        P(None, None, "ha", "col"),
        P(None, None, "ha", "col"),
        P(None, None, "ha", "col"),
        P(None, None, "ha", "col"),
        P(None, None, "ha", "col"),
        P(None, None, "ha", "col"),
        P(None, None, "ha", "col"),
        P(None, None, "ha", "col"),
        P("col", None),
        P("col", None),
        P("col", None),
    )
    return jax.shard_map(
        chosen,
        mesh=mesh,
        in_specs=placed,
        out_specs=(
            P(None, None, "ha", "col"),
            P(None, None, "ha", "col"),
            P(None, None, "ha", "col"),
            P(None, None, "ha", "col"),
            P(None, None, "ha", "col"),
            P(None, None, "ha", "col"),
            P(None, None, "ha", "col"),
            P(None, None, "ha", "col"),
            P(None, None, "ha", "col"),
            P(None, None, "ha", "col"),
            P(None, None, "ha", "col"),
            P(None, None, "ha", "col"),
            P(None, None, "ha", "col"),
            P(None, None, "ha", "col"),
            P(None, None, "ha", "col"),
            P(None, None, "ha", "col"),
            P("col", None),
            P("col", None),
            P("col", None),
            P("col", None),
            P(),
            P(),
        ),
        check_vma=False,
    )
```

```python
import jax
import jax.numpy as jnp
from jax import lax
from jax.experimental import pallas as pl
from jax.experimental.pallas import tpu as pltpu
from jax.sharding import PartitionSpec as P

STEP = 10


NUMBERS = ("NHWC", "HWIO", "NHWC")
BETA_ONE = 0.9
BETA_TWO = 0.95
RATE = 0.08
DECAY = 0.1
EPSILON = 1e-08


def extended(cells, sides, width):
    for axis, dim in sides:
        count = lax.axis_size(axis)
        ends = count - 1
        head = lax.slice_in_dim(cells, 0, width, axis=dim)
        tail = lax.slice_in_dim(cells, cells.shape[dim] - width, cells.shape[dim], axis=dim)
        cells = jnp.concatenate(
            [
                lax.ppermute(tail, axis, [(i, (i + 1) % count) for i in range(ends)]),
                cells,
                lax.ppermute(head, axis, [((i + 1) % count, i) for i in range(ends)]),
            ],
            axis=dim,
        )
    return cells


def shortened(value):

    def short(part):
        return part.astype(jnp.bfloat16) if part.dtype == jnp.float32 else part

    return jax.tree.map(short, value)


def convolve_rows(padded, weight):
    return lax.conv_general_dilated(
        padded,
        weight,
        (1, 1),
        ((0, 0), (1, 1)),
        dimension_numbers=NUMBERS,
        preferred_element_type=jnp.float32,
    )


def flipped(weight):
    return jnp.transpose(weight[::-1, ::-1], (0, 1, 3, 2))


def upsample(values, weight):
    product = jnp.einsum("nhwc,abcd->nhawbd", values, weight, preferred_element_type=jnp.float32)
    return product.reshape(
        product.shape[0], 2 * product.shape[1], 2 * product.shape[3], product.shape[5]
    )


def split_pixels(upstream):
    return upstream.reshape(
        upstream.shape[0], upstream.shape[1] // 2, 2, upstream.shape[2] // 2, 2, upstream.shape[3]
    )


def upsample_back(upstream, weight):
    return jnp.einsum(
        "nhawbd,abcd->nhwc", split_pixels(upstream), weight, preferred_element_type=jnp.float32
    )


def upsample_weight(values, upstream):
    return jnp.einsum(
        "nhwc,nhawbd->abcd", values, split_pixels(upstream), preferred_element_type=jnp.float32
    )


def tap_grads(padded, upstream):
    wide = jnp.pad(padded, ((0, 0), (0, 0), (1, 1), (0, 0)))
    height, across = (upstream.shape[1], upstream.shape[2])
    stacked = []
    for row_tap in range(3):
        tapline = []
        for col_tap in range(3):
            window = wide[:, row_tap : row_tap + height, col_tap : col_tap + across, :]
            tapline.append(
                jnp.einsum("nhwc,nhwd->cd", window, upstream, preferred_element_type=jnp.float32)
            )
        stacked.append(jnp.stack(tapline))
    return jnp.stack(stacked)


def alternate(weight, groups):
    dims = weight.shape
    shaped = weight.reshape(dims[0], dims[1], 2, groups, dims[2] // (2 * groups), dims[3])
    return shaped.transpose(0, 1, 3, 2, 4, 5).reshape(dims)


def deinterleave(weight, groups):
    dims = weight.shape
    shaped = weight.reshape(dims[0], dims[1], groups, 2, dims[2] // (2 * groups), dims[3])
    return shaped.transpose(0, 1, 3, 2, 4, 5).reshape(dims)


def gelu_back(pre_act, upstream):
    return jax.vjp(jax.nn.gelu, pre_act)[1](upstream)[0]


def focal(logits, labels, usable):
    logprob = jax.nn.log_softmax(logits, axis=-1)
    picked = jnp.where(labels == 1, logprob[..., 1], logprob[..., 0])
    chance = jnp.exp(picked)
    return jnp.sum(usable.astype(jnp.float32) * (-((1.0 - chance) ** 2) * picked))


def loss_terms(logits, labels, usable, labelled):
    running, pull = jax.vjp(lambda values: focal(values, labels, usable), logits)
    return (running, pull(1.0 / labelled)[0])


def gather_channels(values):
    return lax.all_gather(values, "col", axis=3, tiled=True)


def spread_back(partial_value):
    return lax.psum_scatter(partial_value, "col", scatter_dimension=3, tiled=True)


def conv_forward(local, weight):
    padded = extended(local, (("ha", 1),), 1)
    whole = gather_channels(padded)
    return (convolve_rows(whole, weight), whole)


def up_forward(local, weight):
    whole = gather_channels(local)
    return (upsample(whole, weight), whole)


def conv_weight_grad(kept, upstream):
    return tap_grads(kept, upstream)


def up_weight_grad(kept, upstream):
    return upsample_weight(kept, upstream)


def backward_weights(merge_up, upward, middle):
    return (flipped(merge_up), upward, flipped(middle))


def conv_input_grad(back_weight, upstream):
    padded = extended(shortened(upstream), (("ha", 1),), 1).astype(upstream.dtype)
    return spread_back(convolve_rows(padded, back_weight))


def up_input_grad(back_weight, upstream):
    return spread_back(upsample_back(upstream, back_weight))


def forward_pass(picture, skipped, copies):
    enter, middle, upward, merge_mixed, back_merge, back_upward, back_middle, head_copy = copies
    pre_one, kept_one = conv_forward(picture, enter)
    act_one = jax.nn.gelu(pre_one).astype(jnp.bfloat16)
    pre_two, kept_two = conv_forward(act_one, middle)
    act_two = jax.nn.gelu(pre_two).astype(jnp.bfloat16)
    raised, kept_up = up_forward(act_two, upward)
    joined = jnp.concatenate([raised.astype(jnp.bfloat16), skipped], axis=3)
    pre_three, kept_three = conv_forward(joined, merge_mixed)
    act_three = jax.nn.gelu(pre_three).astype(jnp.bfloat16)
    partial_value = jnp.einsum(
        "nhwc,ck->nhwk", act_three, head_copy, preferred_element_type=jnp.float32
    )
    return (
        partial_value,
        (pre_one, kept_one, pre_two, kept_two, kept_up, pre_three, kept_three, act_three),
    )


def backward_pass(saved, dlogits, copies):
    enter, middle, upward, merge_mixed, back_merge, back_upward, back_middle, head_copy = copies
    pre_one, kept_one, pre_two, kept_two, kept_up, pre_three, kept_three, act_three = saved
    back_three = jnp.einsum("nhwk,ck->nhwc", dlogits, head_copy, preferred_element_type=jnp.float32)
    grad_head = jnp.einsum("nhwc,nhwk->ck", act_three, dlogits, preferred_element_type=jnp.float32)
    grad_three = gelu_back(pre_three, back_three).astype(jnp.bfloat16)
    grad_merge = conv_weight_grad(kept_three, grad_three)
    d_raised = conv_input_grad(back_merge, grad_three).astype(jnp.bfloat16)
    grad_upward = up_weight_grad(kept_up, d_raised)
    back_two = up_input_grad(back_upward, d_raised)
    grad_two = gelu_back(pre_two, back_two).astype(jnp.bfloat16)
    grad_middle = conv_weight_grad(kept_two, grad_two)
    back_one = conv_input_grad(back_middle, grad_two)
    grad_one = gelu_back(pre_one, back_one).astype(jnp.bfloat16)
    grad_enter = conv_weight_grad(kept_one, grad_one)
    return (grad_enter, grad_middle, grad_upward, grad_merge, grad_head)


def adamw(master, moment, square, gradient):
    moment_new = BETA_ONE * moment + (1.0 - BETA_ONE) * gradient
    square_new = BETA_TWO * square + (1.0 - BETA_TWO) * gradient * gradient
    fixed_moment = moment_new / (1.0 - BETA_ONE**STEP)
    fixed_square = square_new / (1.0 - BETA_TWO**STEP)
    master_new = master - RATE * (
        fixed_moment / (jnp.sqrt(fixed_square) + EPSILON) + DECAY * master
    )
    return (master_new, moment_new, square_new, master_new.astype(jnp.bfloat16))


def own_rows(summed, local):
    return lax.dynamic_slice_in_dim(
        summed, lax.axis_index("ha") * local.shape[2], local.shape[2], 2
    )


def body(
    input_a,
    input_b,
    skip_a,
    skip_b,
    labels_a,
    labels_b,
    valid_a,
    valid_b,
    w_enter,
    moment_enter,
    square_enter,
    w_middle,
    moment_middle,
    square_middle,
    w_upward,
    moment_upward,
    square_upward,
    w_merge,
    moment_merge,
    square_merge,
    w_head,
    moment_head,
    square_head,
):
    groups = lax.axis_size("col")
    enter, middle, upward, merge = (
        lax.all_gather(w_enter.astype(jnp.bfloat16), "ha", axis=2, tiled=True),
        lax.all_gather(w_middle.astype(jnp.bfloat16), "ha", axis=2, tiled=True),
        lax.all_gather(w_upward.astype(jnp.bfloat16), "ha", axis=2, tiled=True),
        lax.all_gather(w_merge.astype(jnp.bfloat16), "ha", axis=2, tiled=True),
    )
    head_low = w_head.astype(jnp.bfloat16)
    merge_up = merge[:, :, : merge.shape[2] // 2]
    back_merge, back_upward, back_middle = backward_weights(merge_up, upward, middle)
    copies = (
        enter,
        middle,
        upward,
        alternate(merge, groups),
        back_merge,
        back_upward,
        back_middle,
        head_low,
    )
    labelled = lax.psum(
        jnp.sum(valid_a.astype(jnp.float32)) + jnp.sum(valid_b.astype(jnp.float32)), "ha"
    )
    partial_a, saved_a = forward_pass(input_a, skip_a, copies)
    partial_b, saved_b = forward_pass(input_b, skip_b, copies)
    logits_a, logits_b = lax.psum((partial_a, partial_b), "col")
    loss_a, dlogits_a = loss_terms(logits_a, labels_a, valid_a, labelled)
    loss_b, dlogits_b = loss_terms(logits_b, labels_b, valid_b, labelled)
    grads_a = backward_pass(saved_a, dlogits_a.astype(jnp.bfloat16), copies)
    grads_b = backward_pass(saved_b, dlogits_b.astype(jnp.bfloat16), copies)
    local_enter = grads_a[0] + grads_b[0]
    local_middle = grads_a[1] + grads_b[1]
    local_upward = grads_a[2] + grads_b[2]
    local_merge = deinterleave(grads_a[3] + grads_b[3], groups)
    local_head = grads_a[4] + grads_b[4]
    local_loss = loss_a + loss_b
    full_enter, full_middle, full_upward, full_merge, head_total, loss_total = (
        lax.psum(local_enter.astype(jnp.bfloat16), "ha").astype(jnp.float32),
        lax.psum(local_middle.astype(jnp.bfloat16), "ha").astype(jnp.float32),
        lax.psum(local_upward.astype(jnp.bfloat16), "ha").astype(jnp.float32),
        lax.psum(local_merge.astype(jnp.bfloat16), "ha").astype(jnp.float32),
        lax.psum(local_head.astype(jnp.bfloat16), "ha").astype(jnp.float32),
        lax.psum(local_loss.astype(jnp.bfloat16), "ha").astype(jnp.float32),
    )
    grad_enter = own_rows(full_enter, w_enter)
    grad_middle = own_rows(full_middle, w_middle)
    grad_upward = own_rows(full_upward, w_upward)
    grad_merge = own_rows(full_merge, w_merge)
    enter_out = adamw(w_enter, moment_enter, square_enter, grad_enter)
    middle_out = adamw(w_middle, moment_middle, square_middle, grad_middle)
    upward_out = adamw(w_upward, moment_upward, square_upward, grad_upward)
    merge_out = adamw(w_merge, moment_merge, square_merge, grad_merge)
    head_out = adamw(w_head, moment_head, square_head, head_total)
    return (
        enter_out[0],
        enter_out[1],
        enter_out[2],
        enter_out[3],
        middle_out[0],
        middle_out[1],
        middle_out[2],
        middle_out[3],
        upward_out[0],
        upward_out[1],
        upward_out[2],
        upward_out[3],
        merge_out[0],
        merge_out[1],
        merge_out[2],
        merge_out[3],
        head_out[0],
        head_out[1],
        head_out[2],
        head_out[3],
        loss_total,
        labelled,
    )


BF = jnp.bfloat16
F32 = jnp.float32
MESH = pl.DeviceIdType.MESH
LANE = 128
PI_PART = 0.7978845608028654
CUBE = 0.044715


def gelu_value(v):
    return 0.5 * v * (1.0 + jnp.tanh(PI_PART * (v + CUBE * (v * v * v))))


def gelu_slope(v):
    bent = jnp.tanh(PI_PART * (v + CUBE * (v * v * v)))
    inner = PI_PART * (1.0 + 3.0 * CUBE * (v * v))
    return 0.5 * (1.0 + bent) + 0.5 * v * (1.0 - bent * bent) * inner


def dot_nn(lhs, rhs):
    return lax.dot_general(lhs, rhs, (((1,), (0,)), ((), ())), preferred_element_type=F32)


def dot_nt(lhs, rhs):
    return lax.dot_general(lhs, rhs, (((1,), (1,)), ((), ())), preferred_element_type=F32)


def span(at, size):
    return pl.ds(pl.multiple_of(at * size, size), size)


SCRATCH = (
    ("inT", (2, 4, 32, 128), BF),
    ("skT", (4, 64, 512), BF),
    ("lab", (8, 128), F32),
    ("flat", (4, 256, 128), F32),
    ("w1", (9, 32, 512), BF),
    ("w2", (9, 64, 512), BF),
    ("wu", (4, 64, 256), BF),
    ("w3", (9, 64, 256), BF),
    ("IN", (8, 2, 4, 32, 128), BF),
    ("SK", (4, 64, 512), BF),
    ("LB", (16, 8, 128), F32),
    ("W1", (9, 128, 128), BF),
    ("W2", (9, 128, 256), BF),
    ("WU", (16, 64, 256), BF),
    ("W3", (9, 128, 512), BF),
    ("W1T", (128, 1152), BF),
    ("W2T", (256, 1152), BF),
    ("WUT", (256, 1024), BF),
    ("W3T", (512, 1152), BF),
    ("X", (1152, 2304), BF),
    ("P1", (4, 32, 2048), F32),
    ("P1b", (4, 32, 2048), BF),
    ("R1", (3, 32, 2048), BF),
    ("A1", (4, 32, 2048), BF),
    ("P2b", (4, 128, 512), BF),
    ("T2", (4, 128, 512), BF),
    ("S2b", (3, 128, 512), BF),
    ("R2", (3, 128, 512), BF),
    ("pre2", (128, 512), F32),
    ("A2", (8, 128, 512), BF),
    ("J", (2, 4, 128, 768), BF),
    ("P3b", (4, 4, 64, 512), BF),
    ("T3", (4, 4, 64, 512), BF),
    ("S3b", (4, 4, 64, 512), BF),
    ("R3", (4, 3, 64, 512), BF),
    ("pre3", (64, 2048), F32),
    ("act3", (64, 2048), BF),
    ("LG", (8, 32, 128), F32),
    ("LBL", (32, 128), F32),
    ("DL", (32, 128), F32),
    ("G3", (4, 8, 64, 512), BF),
    ("Z", (1152, 2048), F32),
    ("HS", (2, 2, 64, 128), F32),
    ("HR", (2, 2, 64, 128), F32),
    ("DB", (4, 64, 128), F32),
    ("DR", (256, 512), BF),
    ("P8", (128, 2048), F32),
    ("P7b", (4, 128, 512), BF),
    ("T7", (4, 128, 512), BF),
    ("S7b", (4, 128, 512), BF),
    ("R7", (3, 128, 512), BF),
    ("G2", (2, 128, 2048), BF),
    ("P8b", (4, 32, 2048), BF),
    ("R8", (3, 32, 2048), BF),
    ("G1", (4, 32, 2048), BF),
    ("GW3", (9, 128, 512), BF),
    ("GWU", (16, 64, 256), BF),
    ("GW2", (9, 128, 256), BF),
    ("GW1", (9, 128, 128), BF),
    ("RG3", (4, 9, 64, 256), BF),
    ("Y3", (2, 9, 64, 256), BF),
    ("RGU", (16, 64, 256), BF),
    ("RG2", (9, 64, 512), BF),
    ("RG1", (9, 32, 512), BF),
    ("HD", (16, 8, 128), F32),
)
COPIES = 216


def fused(widths, *refs):
    wa, wb = widths
    rows_a, rows_b, skip_a, skip_b, la, lb, va, vb, f1, f2, fu, f3, fh = refs[:13]
    g1o, g2o, guo, g3o, hdo = refs[13:18]
    m = {name: ref for (name, _, _), ref in zip(SCRATCH, refs[18:-2])}
    send_sem, recv_sem = refs[-2:]
    h, y = lax.axis_index("ha"), lax.axis_index("col")
    z, x, e = lax.div(h, 4), lax.rem(lax.div(h, 2), 2), lax.rem(h, 2)
    q = 2 * y + x
    s = 2 * q + e
    twin = h + 1 - 2 * e
    started = []
    count = [0]

    def ha(z_, x_, e_):
        return 4 * z_ + 2 * x_ + e_

    def remote(src, dst, h2, y2, sem_s, sem_r):
        return pltpu.make_async_remote_copy(
            src_ref=src,
            dst_ref=dst,
            send_sem=send_sem.at[sem_s],
            recv_sem=recv_sem.at[sem_r],
            device_id={"ha": h2, "col": y2},
            device_id_type=MESH,
        )

    def push(src, dst, h2, y2):
        n = count[0]
        count[0] += 1
        copy = remote(src, dst, h2, y2, n, n)
        copy.start()
        started.append((copy, None))
        return copy

    def reserve(n):
        base = count[0]
        count[0] += n
        return base

    def hand(src, dst, h2, y2, sem_s, sem_r):
        same = jnp.logical_and(h2 == h, y2 == y)
        away = jnp.logical_not(same)
        copy = remote(src, dst, h2, y2, sem_s, sem_r)

        @pl.when(same)
        def _():
            pltpu.make_async_copy(src, dst, recv_sem.at[sem_r]).start()

        @pl.when(away)
        def _():
            copy.start()

        started.append((copy, away))

    def landed(dst, sem_r):
        remote(dst, dst, twin, y, sem_r, sem_r).wait_recv()

    lanes = lax.broadcasted_iota(jnp.int32, (1, LANE), 1)
    left_ok = jnp.logical_and(jnp.logical_and(lanes != 0, lanes != wa), lanes < wa + wb)
    right_ok = jnp.logical_and(lanes != wa - 1, lanes < wa + wb - 1)

    def from_left(v):
        return jnp.where(left_ok, pltpu.roll(v, 1, 1), 0.0)

    def from_right(v):
        return jnp.where(right_ok, pltpu.roll(v, LANE - 1, 1), 0.0)

    J, HR = m["J"], m["HR"]

    @pl.when(z == 0)
    def _():
        J[1, 1:3, :, 0:128] = jnp.zeros((2, 128, 128), BF)
        HR[0] = jnp.zeros((2, 64, 128), F32)

    @pl.when(z == 3)
    def _():
        J[0, 1:3, :, 640:768] = jnp.zeros((2, 128, 128), BF)
        HR[1] = jnp.zeros((2, 64, 128), F32)

    inT, skT, lab, flat = m["inT"], m["skT"], m["lab"], m["flat"]
    w1, w2, wu, w3 = m["w1"], m["w2"], m["wu"], m["w3"]
    wide_a, wide_b = 2 * wa, 2 * wb
    for c in range(2):
        half = slice(c * 128, c * 128 + 128)
        flat[c, 96:128, :] = jnp.zeros((32, 128), F32)
        flat[c, 0:wa, :] = rows_a[:, half].astype(F32)
        flat[c, wa : wa + wb, :] = rows_b[:, half].astype(F32)
        inT[c] = flat[c, 0:128, :].T.astype(BF).reshape(4, 32, 128)
    w1[...] = f1[...].astype(BF)
    place = lax.broadcasted_iota(jnp.int32, (256, LANE), 0)
    lane = lax.broadcasted_iota(jnp.int32, (256, LANE), 1)
    spread = jnp.concatenate(
        [
            jnp.concatenate([first[...], second[...]], axis=1).astype(F32)
            for first, second in ((la, lb), (va, vb))
        ],
        axis=0,
    )
    spread = jnp.pad(spread, ((0, 4), (0, 256 - wide_a - wide_b)))
    for b in range(2):
        pick = jnp.where(place == 2 * lane + b, 1.0, 0.0)
        planes = dot_nn(spread.astype(BF), pick.astype(BF))
        for a in range(2):
            lab[2 * a + b : 2 * a + b + 1, :] = planes[a : a + 1, :]
            lab[4 + 2 * a + b : 5 + 2 * a + b, :] = planes[2 + a : 3 + a, :]

    IN, LB = m["IN"], m["LB"]
    in_copies = []
    for dz in range(4):
        zt = lax.rem(z + dz, 4)
        for d in range(4):
            if dz == 0 and d == 0:
                continue
            there = lax.rem(2 * x + y + d, 4)
            in_copies.append(
                push(
                    inT.at[:, there],
                    IN.at[2 * z + x, e, pl.ds(2 * y, 2)],
                    ha(zt, lax.div(there, 2), e),
                    lax.rem(there, 2),
                )
            )
    IN[2 * z + x, e, pl.ds(2 * y, 2)] = inT[:, 2 * x + y]

    W1, W2, WU, W3 = m["W1"], m["W2"], m["WU"], m["W3"]
    b1 = reserve(4)
    for i in range(4):
        hand(
            w1.at[:, :, i * 128 : i * 128 + 128],
            W1.at[:, span(z, 32), :],
            ha(2 * y + i // 2, x, i % 2),
            e,
            b1 + i,
            b1 + z,
        )
    lab_copies = []
    LB[h] = lab[...]
    for d in range(1, 16):
        lab_copies.append(push(lab, LB.at[h], lax.rem(h + d, 16), y))

    for copy in in_copies:
        copy.wait_recv()
    twin_in = push(IN.at[:, e], IN.at[:, e], twin, y)

    w2[...] = f2[...].astype(BF)
    w3[...] = f3[...].astype(BF)
    for k in range(4):
        wu[k] = jnp.concatenate([fu[p, :, k * 64 : k * 64 + 64] for p in range(4)], axis=1).astype(BF)
    for a in range(2):
        for c in range(2):
            half = slice(c * 128, c * 128 + 128)
            buf = flat.at[2 * a + c]
            buf[224:256, :] = jnp.zeros((32, 128), F32)
            buf[0:wide_a, :] = skip_a[a, :, half].astype(F32)
            buf[wide_a : wide_a + wide_b, :] = skip_b[a, :, half].astype(F32)
            for b in range(2):
                p = 2 * a + b
                plane = buf[pl.ds(b, 128, stride=2), :]
                skT[2 * c : 2 * c + 2, :, p * 128 : p * 128 + 128] = plane.T.astype(BF).reshape(2, 64, 128)
    b2 = reserve(2)
    for i in range(2):
        hand(
            w2.at[:, :, i * 256 : i * 256 + 256],
            W2.at[:, span(e, 64), :],
            ha(z, i, x),
            y,
            b2 + i,
            b2 + e,
        )
    SK = m["SK"]
    sk_copies = []
    slot = 2 * x + e
    for d in range(1, 4):
        other = lax.rem(slot + d, 4)
        sk_copies.append(push(skT.at[other], SK.at[slot], 4 * z + other, y))
    SK[slot] = skT[slot]
    bu_copies = []
    for d in range(1, 16):
        ht = lax.rem(h + d, 16)
        bu_copies.append(push(wu.at[lax.rem(ht, 4)], WU.at[h], ht, y))
    WU[h] = wu[slot]
    b3 = reserve(4)
    for i in range(4):
        hand(
            w3,
            W3.at[:, span(lax.div(z, 2), 64), span(y, 256)],
            ha(i, x, e),
            lax.rem(z, 2),
            b3 + i,
            b3 + 2 * lax.div(z, 2) + y,
        )

    X = m["X"]

    def patch_edges():
        zero = jnp.zeros((384, 128), BF)
        X[0:384, 128:256] = zero
        X[768:1152, 2048:2176] = zero

    def patches(block, first, last):
        def one(i, carry):
            low = block(i)
            v = low.astype(F32)
            kinds = (from_left(v).astype(BF), low, from_right(v).astype(BF))
            for di in (-1, 0, 1):
                for dj in range(3):
                    tap = (di + 1) * 3 + dj
                    X[tap * 128 : tap * 128 + 128, span(i - di + 1, 128)] = kinds[dj]
            return carry

        lax.fori_loop(first, last, one, 0)

    def patch_cols(at, size):
        return pl.ds(pl.multiple_of(at * size + 128, 128), size)

    def transposed(weight, out, rows):
        for t in range(weight.shape[0]):
            out[:, t * rows : t * rows + rows] = weight[t].T

    for j in range(4):
        landed(W1.at[:, 32 * j : 32 * j + 32, :], b1 + j)
    transposed(W1, m["W1T"], 128)
    twin_in.wait_recv()

    def input_block(i):
        return IN[lax.div(i, 2), lax.rem(i, 2)].reshape(128, 128)

    def middle_block(i):
        return A1[:, :, span(i, 128)].reshape(128, 128)

    patches(input_block, 0, 16)
    patch_edges()
    P1, P1b, R1, A1 = m["P1"], m["P1b"], m["R1"], m["A1"]

    def conv_one(n, carry):
        cols = span(n, 512)
        total = dot_nn(m["W1T"][...], X[:, patch_cols(n, 512)]).reshape(4, 32, 512)
        P1[:, :, cols] = total
        P1b[:, :, cols] = total.astype(BF)
        return carry

    def to_plane(d):
        there = lax.rem(q + d, 4)
        return there, ha(z, lax.rem(there, 2), e), lax.div(there, 2)

    def scatter(source, slots, cols=slice(None)):
        copies = []
        for d in range(1, 4):
            there, h2, y2 = to_plane(d)
            copies.append(push(source.at[there, :, cols], slots.at[d - 1, :, cols], h2, y2))
        return copies

    def gather_four(buf, cols):
        copies = []
        for d in range(1, 4):
            _, h2, y2 = to_plane(d)
            copies.append(push(buf.at[q, :, cols], buf.at[q, :, cols], h2, y2))
        return copies

    halves = (slice(0, 1024), slice(1024, 2048))

    def plane_sends(buf):
        copies = []
        for d in range(1, 4):
            _, h2, y2 = to_plane(d)
            copies.append(push(buf.at[s], buf.at[s], h2, y2))
        return copies, push(buf.at[s], buf.at[s], twin, y)

    def plane_passes(buf, sends):
        copies, own = sends
        last = [own]
        for d in range(1, 4):
            copies[d - 1].wait_recv()
            came = 2 * lax.rem(q + 4 - d, 4) + e
            last.append(push(buf.at[came], buf.at[came], twin, y))
        return last

    def gather_plane(buf):
        return plane_passes(buf, plane_sends(buf))

    def arrive(copies):
        for copy in copies:
            copy.wait_recv()

    one_out = []
    for c in range(2):
        lax.fori_loop(2 * c, 2 * c + 2, conv_one, 0)
        one_out.append(scatter(P1b, R1, halves[c]))

    def act_one(n, carry):
        cols = span(n, 512)
        total = P1[q, :, cols] + R1[0, :, cols].astype(F32)
        total = total + R1[1, :, cols].astype(F32) + R1[2, :, cols].astype(F32)
        P1[q, :, cols] = total
        A1[q, :, cols] = gelu_value(total).astype(BF)
        return carry

    wait_one = []
    for c in range(2):
        arrive(one_out[c])
        lax.fori_loop(2 * c, 2 * c + 2, act_one, 0)
        wait_one.append(gather_four(A1, halves[c]))
    for j in range(2):
        landed(W2.at[:, 64 * j : 64 * j + 64, :], b2 + j)
    transposed(W2, m["W2T"], 128)

    for c in range(2):
        arrive(wait_one[c])
        patches(middle_block, 8 * c, 8 * c + 8)
    patch_edges()
    Z, P2b, T2, S2b, R2 = m["Z"], m["P2b"], m["T2"], m["S2b"], m["R2"]

    def band_two(k):
        zt = lax.rem(z + 1 + k, 4)
        Z[0:256, span(zt, 512)] = dot_nn(m["W2T"][...], X[:, patch_cols(zt, 512)])
        P2b[k] = Z[span(1 - e, 128), span(zt, 512)].astype(BF)
        return push(P2b.at[k], T2.at[k], twin, y)

    def pair_two(k):
        zt = lax.rem(z + 1 + k, 4)
        pairs[k].wait_recv()
        S2b[k] = (Z[span(e, 128), span(zt, 512)] + T2[k].astype(F32)).astype(BF)
        two.append(push(S2b.at[k], R2.at[k], ha(zt, x, e), y))

    pairs, two = [], []
    for k in range(4):
        pairs.append(band_two(k))
        if k >= 1:
            pair_two(k - 1)
    for d in range(1, 16):
        bu_copies[d - 1].wait_recv()
    for t in range(8):
        m["WUT"][:, t * 128 : t * 128 + 128] = WU[2 * t : 2 * t + 2].reshape(128, 256).T
    arrive(two)
    pre2, A2 = m["pre2"], m["A2"]
    pairs[3].wait_recv()
    total = Z[span(e, 128), span(z, 512)] + T2[3].astype(F32) + R2[0].astype(F32)
    total = total + R2[1].astype(F32) + R2[2].astype(F32)
    pre2[...] = total
    A2[s] = gelu_value(total).astype(BF)
    wait_two = gather_plane(A2)
    for copy in sk_copies:
        copy.wait_recv()
    for a in range(2):
        for b in range(2):
            p = 2 * a + b
            for i in range(4):
                J[a, 1 + b, 64:128, 128 + 128 * i : 256 + 128 * i] = SK[i, :, p * 128 : p * 128 + 128]
    arrive(wait_two)

    for p in range(4):
        plane = dot_nn(m["WUT"][p * 64 : p * 64 + 64, :], A2[...].reshape(1024, 512))
        J[p // 2, 1 + p % 2, 0:64, 128:640] = plane.astype(BF)

    def fringe(up, down, send_down, keep_down, send_up, keep_up):
        below = remote(send_down, keep_down, lax.rem(h + 4, 16), y, down, down)
        above = remote(send_up, keep_up, lax.rem(h + 12, 16), y, up, up)

        @pl.when(z < 3)
        def _():
            below.start()

        @pl.when(z > 0)
        def _():
            above.start()

        started.append((below, z < 3))
        started.append((above, z > 0))

        def wait():
            @pl.when(z > 0)
            def _():
                below.wait_recv()

            @pl.when(z < 3)
            def _():
                above.wait_recv()

        return wait

    bj = reserve(2)
    wait_rows = fringe(
        bj,
        bj + 1,
        J.at[1, 1:3, :, 512:640],
        J.at[1, 1:3, :, 0:128],
        J.at[0, 1:3, :, 128:256],
        J.at[0, 1:3, :, 640:768],
    )

    def beside(a, i):
        at = slice(i * 128, i * 128 + 128)
        J[a, 0, :, at] = from_left(J[a, 2, :, at].astype(F32)).astype(BF)
        J[a, 3, :, at] = from_right(J[a, 1, :, at].astype(F32)).astype(BF)

    def joined_patches(outer):
        for a in range(2):
            for da in range(3):
                up, di = (a + da - 1) % 2, (a + da - 1) // 2
                first, last = 0, 4
                if di != 0:
                    edge = 0 if di < 0 else 3
                    first, last = (edge, edge + 1) if outer else (1, 4) if di < 0 else (0, 3)
                elif outer:
                    continue
                for b in range(2):
                    for db in range(3):
                        tap = da * 3 + db
                        at = 128 + (2 * a + b) * 512
                        X[tap * 128 : tap * 128 + 128, at + first * 128 : at + last * 128] = J[
                            up, b + db, :, (1 + di + first) * 128 : (1 + di + last) * 128
                        ]

    for a in range(2):
        for i in range(1, 5):
            beside(a, i)
    joined_patches(False)
    wait_rows()
    beside(1, 0)
    beside(0, 5)
    joined_patches(True)

    for j in range(4):
        t, half = j // 2, j % 2
        landed(W3.at[:, 64 * t : 64 * t + 64, 256 * half : 256 * half + 256], b3 + j)
    transposed(W3, m["W3T"], 128)
    P3b, T3, S3b, R3 = m["P3b"], m["T3"], m["S3b"], m["R3"]

    def plane_three(p):
        def step(n, carry):
            Z[0:512, span(n, 256)] = dot_nn(m["W3T"][...], X[:, patch_cols(n, 256)])
            return carry

        lax.fori_loop(2 * p, 2 * p + 2, step, 0)
        cols = slice(p * 512, p * 512 + 512)
        for k in range(4):
            P3b[p, k] = Z[span(2 * k + 1 - e, 64), cols].astype(BF)
        return push(P3b.at[p], T3.at[p], twin, y)

    def pair_three(p):
        pairs[p].wait_recv()
        cols = slice(p * 512, p * 512 + 512)
        for k in range(4):
            total = Z[span(2 * k + e, 64), cols] + T3[p, k].astype(F32)
            Z[span(2 * k + e, 64), cols] = total
            S3b[p, k] = total.astype(BF)
        three.append(scatter(S3b.at[p], R3.at[p]))

    pairs, three = [], []
    for p in range(4):
        pairs.append(plane_three(p))
        if p >= 1:
            pair_three(p - 1)
    pair_three(3)
    pre3, act3, LG = m["pre3"], m["act3"], m["LG"]
    wide = (64, LANE)
    head = fh[span(slot, 64), :].astype(BF).astype(F32)
    h0 = jnp.broadcast_to(head[:, 0:1], wide)
    h1 = jnp.broadcast_to(head[:, 1:2], wide)
    for b in range(16):
        if b % 4 == 0:
            arrive(three[b // 4])
        cols = slice(b * 128, b * 128 + 128)
        part = slice(b % 4 * 128, b % 4 * 128 + 128)
        total = Z[span(s, 64), cols] + R3[b // 4, 0, :, part].astype(F32)
        total = total + R3[b // 4, 1, :, part].astype(F32) + R3[b // 4, 2, :, part].astype(F32)
        pre3[:, cols] = total
        act = gelu_value(total).astype(BF)
        act3[:, cols] = act
        act = act.astype(F32)
        LG[s, b : b + 1, :] = jnp.sum(act * h0, axis=0, keepdims=True)
        LG[s, 16 + b : 17 + b, :] = jnp.sum(act * h1, axis=0, keepdims=True)
    wait_logits = []
    for d in range(1, 8):
        there = lax.rem(s + d, 8)
        half = lax.div(there, 4)
        wait_logits.append(push(LG.at[s], LG.at[s], 4 * z + there - 4 * half, half))
    for copy in lab_copies:
        copy.wait_recv()
    LBL = m["LBL"]
    for p in range(4):
        for i in range(4):
            LBL[p * 4 + i : p * 4 + i + 1, :] = LB[4 * z + i, p : p + 1, :]
            LBL[16 + p * 4 + i : 17 + p * 4 + i, :] = LB[4 * z + i, 4 + p : 5 + p, :]
    every = jnp.sum(LB[...], axis=0)
    labelled = jnp.sum(jnp.sum(every[4:8, :], axis=0, keepdims=True), axis=1, keepdims=True)
    arrive(wait_logits)

    logits = LG[0]
    for k in range(1, 8):
        logits = logits + LG[k]
    zero, one = logits[0:16, :], logits[16:32, :]
    picks, usable = LBL[0:16, :] > 0.5, LBL[16:32, :]
    top = jnp.maximum(zero, one)
    lse = top + jnp.log(jnp.exp(zero - top) + jnp.exp(one - top))
    logp = jnp.where(picks, one, zero) - lse
    rest = jnp.exp(jnp.where(picks, zero, one) - lse)
    chance = jnp.exp(logp)
    gap = 1.0 - chance
    terms = usable * (-(gap * gap) * logp)
    slope = (2.0 * gap * chance * logp - gap * gap) * usable / labelled
    own, other = slope * gap, -slope * rest
    DL = m["DL"]
    DL[0:16, :] = jnp.where(picks, other, own).astype(BF).astype(F32)
    DL[16:32, :] = jnp.where(picks, own, other).astype(BF).astype(F32)
    loss = jnp.sum(jnp.sum(terms, axis=0, keepdims=True), axis=1, keepdims=True)
    G3, HD = m["G3"], m["HD"]
    planes = []
    sum0 = jnp.zeros(wide, F32)
    sum1 = jnp.zeros(wide, F32)
    for b in range(16):
        cols = slice(b * 128, b * 128 + 128)
        d0 = jnp.broadcast_to(DL[b : b + 1, :], wide)
        d1 = jnp.broadcast_to(DL[16 + b : 17 + b, :], wide)
        part = slice(b % 4 * 128, b % 4 * 128 + 128)
        G3[b // 4, s, :, part] = ((h0 * d0 + h1 * d1) * gelu_slope(pre3[:, cols])).astype(BF)
        act = act3[:, cols].astype(F32)
        sum0 = sum0 + act * d0
        sum1 = sum1 + act * d1
        if b % 4 == 3:
            planes.append(plane_sends(G3.at[b // 4]))
    side = lax.broadcasted_iota(jnp.int32, wide, 1)
    sum0 = jnp.sum(sum0, axis=1, keepdims=True)
    sum1 = jnp.sum(sum1, axis=1, keepdims=True)
    tile = jnp.where(side == 0, sum0, jnp.where(side == 1, sum1, 0.0))
    HD[h, 0:8, 0:64] = tile.T[0:8, :]
    HD[h, 2:3, 0:64] = jnp.broadcast_to(loss, (1, 64))
    hd_copies = []
    for d in range(1, 16):
        hd_copies.append(push(HD.at[h], HD.at[h], lax.rem(h + d, 16), y))

    HS, DB, DR = m["HS"], m["DB"], m["DR"]

    def back_three(p):
        grads = G3[p].reshape(512, 512)
        Z[0:576, p * 512 : p * 512 + 512] = dot_nn(W3[:, 0:64, :].reshape(576, 512), grads)

    passes = [plane_passes(G3.at[0], planes[0])]
    for p in range(4):
        if p < 3:
            passes.append(plane_passes(G3.at[p + 1], planes[p + 1]))
        arrive(passes[p])
        back_three(p)
    ways = (((0, 0, 0), (1, -1, 0), (1, 1, 1)), ((0, -1, -1), (0, 1, 0), (1, 0, 0)))

    def raised_block(a, b, i):
        straight, bent = [], []
        for ao, da, di in ways[a]:
            io = i - di
            if io < 0 or io > 3 or (i < 0 or i > 3) and di == 0:
                continue
            for bo, db, dj in ways[b]:
                tap = (da + 1) * 3 + db + 1
                at = ((2 * ao + bo) * 4 + io) * 128
                (straight if dj == 0 else bent).append(Z[tap * 64 : tap * 64 + 64, at : at + 128])
        turned = sum(bent[1:], bent[0])
        turned = from_left(turned) if b == 0 else from_right(turned)
        return sum(straight, turned)

    for b in range(2):
        HS[0, b] = raised_block(0, b, 4)
        HS[1, b] = raised_block(1, b, -1)
    bh = reserve(2)
    wait_fringe = fringe(bh, bh + 1, HS.at[0], HR.at[0], HS.at[1], HR.at[1])
    for a in range(2):
        for b in range(2):
            p = 2 * a + b
            for i in range(4):
                block = raised_block(a, b, i)
                if i == 3 * a:
                    DB[p] = block
                else:
                    DR[p * 64 : p * 64 + 64, i * 128 : i * 128 + 128] = block.astype(BF)
    GW3, GWU, GW2, GW1 = m["GW3"], m["GWU"], m["GW2"], m["GW1"]
    RG3, RGU, RG2, RG1 = m["RG3"], m["RGU"], m["RG2"], m["RG1"]

    def grad_three(t, carry):
        total = None
        for p in range(4):
            part = dot_nt(X[span(t, 128), 128 + p * 512 : 640 + p * 512], G3[p].reshape(512, 512))
            total = part if total is None else total + part
        GW3[t] = total.astype(BF)
        return carry

    lax.fori_loop(0, 3, grad_three, 0)
    wait_fringe()
    for a in range(2):
        for b in range(2):
            p = 2 * a + b
            DR[p * 64 : p * 64 + 64, a * 384 : a * 384 + 128] = (DB[p] + HR[a, b]).astype(BF)

    P7b, T7, S7b, R7 = m["P7b"], m["T7"], m["S7b"], m["R7"]

    def back_up(k, carry):
        Z[span(k, 128), 0:512] = dot_nn(WU[pl.ds(2 * k, 2)].reshape(128, 256), DR[...])
        return carry

    lax.fori_loop(0, 8, back_up, 0)
    for k in range(4):
        P7b[k] = Z[span(2 * k + 1 - e, 128), 0:512].astype(BF)
    wait_pair = push(P7b, T7, twin, y)

    def pair_seven():
        for k in range(4):
            total = Z[span(2 * k + e, 128), 0:512] + T7[k].astype(F32)
            Z[span(2 * k + e, 128), 0:512] = total
            S7b[k] = total.astype(BF)

    lax.fori_loop(3, 5, grad_three, 0)
    wait_pair.wait_recv()
    pair_seven()
    wait_seven = scatter(S7b, R7)
    lax.fori_loop(5, 9, grad_three, 0)

    def grad_up(k, carry):
        GWU[pl.ds(2 * k, 2)] = dot_nt(A2[k], DR[...]).astype(BF).reshape(2, 64, 256)
        return carry

    lax.fori_loop(0, 8, grad_up, 0)
    arrive(wait_seven)
    G2 = m["G2"]
    total = Z[span(s, 128), 0:512] + R7[0].astype(F32)
    total = total + R7[1].astype(F32) + R7[2].astype(F32)
    G2[e, :, span(z, 512)] = (total * gelu_slope(pre2[...])).astype(BF)
    mine = G2.at[e, :, span(z, 512)]
    g2_copies = []
    for d in range(1, 4):
        zt = lax.rem(z + d, 4)
        g2_copies.append(push(mine, mine, ha(zt, x, e), y))
    own_pair = push(mine, mine, twin, y)
    Y3 = m["Y3"]
    other = 1 - y
    across = []
    for t in range(2):
        across.append(
            push(
                GW3.at[:, 64 * t : 64 * t + 64, span(other, 256)],
                Y3.at[t],
                h,
                other,
            )
        )
    patches(middle_block, 0, 16)
    patch_edges()

    def back_two(zs):
        for k in range(2):
            cols = pl.ds(pl.multiple_of(zs * 512 + k * 256, 256), 256)
            Z[:, cols] = dot_nn(W2[...].reshape(1152, 256), G2[:, :, cols].reshape(256, 256))

    def relay(d):
        g2_copies[d - 1].wait_recv()
        zs = lax.rem(z + 4 - d, 4)
        came = G2.at[e, :, span(zs, 512)]
        return zs, push(came, came, twin, y)

    zs, copy = relay(1)
    own_pair.wait_recv()
    back_two(z)
    for d in range(2, 4):
        after = relay(d)
        copy.wait_recv()
        back_two(zs)
        zs, copy = after
    bg3 = reserve(4)
    for t in range(2):
        hand(
            GW3.at[:, 64 * t : 64 * t + 64, span(y, 256)],
            RG3.at[z],
            ha(2 * t + y, x, e),
            y,
            bg3 + t,
            bg3 + z,
        )
    gu_copies = []
    for d in range(1, 16):
        ht = lax.rem(h + d, 16)
        gu_copies.append(push(GWU.at[ht], RGU.at[h], ht, y))
    RGU[h] = GWU[h]
    copy.wait_recv()
    back_two(zs)
    P8b, R8, G1 = m["P8b"], m["R8"], m["G1"]
    P8 = m["P8"]

    def fold(i, carry):
        sums = []
        for dj in range(3):
            part = None
            for di in range(3):
                row = i - (di - 1)
                inside = jnp.logical_and(row >= 0, row <= 15)
                row = jnp.clip(row, 0, 15)
                tap = di * 3 + dj
                block = jnp.where(inside, Z[tap * 128 : tap * 128 + 128, span(row, 128)], 0.0)
                part = block if part is None else part + block
            sums.append(part)
        total = sums[1] + from_right(sums[0]) + from_left(sums[2])
        P8[:, span(i, 128)] = total
        P8b[:, :, span(i, 128)] = total.reshape(4, 32, 128).astype(BF)
        return carry

    wait_eight = []
    for c in range(2):
        lax.fori_loop(8 * c, 8 * c + 8, fold, 0)
        wait_eight.append(scatter(P8b, R8, halves[c]))
    arrive(across)
    for t in range(2):
        hand(
            Y3.at[t],
            RG3.at[z],
            ha(2 * t + other, x, e),
            y,
            bg3 + 2 + t,
            bg3 + z,
        )

    def grad_two(t, carry):
        GW2[t] = dot_nt(X[span(t, 128), 128:2176], G2[...].reshape(256, 2048)).astype(BF)
        return carry

    lax.fori_loop(0, 9, grad_two, 0)

    def act_back(n, carry):
        cols = span(n, 512)
        total = P8[span(q, 32), cols] + R8[0, :, cols].astype(F32)
        total = total + R8[1, :, cols].astype(F32) + R8[2, :, cols].astype(F32)
        G1[q, :, cols] = (total * gelu_slope(P1[q, :, cols])).astype(BF)
        return carry

    wait_g1 = []
    for c in range(2):
        arrive(wait_eight[c])
        lax.fori_loop(2 * c, 2 * c + 2, act_back, 0)
        wait_g1 += gather_four(G1, halves[c])
    bg2 = reserve(2)
    for j in range(2):
        hand(
            GW2.at[:, 64 * j : 64 * j + 64, :],
            RG2.at[:, :, span(x, 256)],
            ha(z, e, j),
            y,
            bg2 + j,
            bg2 + x,
        )
    patches(input_block, 0, 16)
    patch_edges()
    arrive(wait_g1)

    def grad_one(t, carry):
        GW1[t] = dot_nt(X[span(t, 128), 128:2176], G1[...].reshape(128, 2048)).astype(BF)
        return carry

    lax.fori_loop(0, 9, grad_one, 0)
    bg1 = reserve(4)
    r_low = 2 * lax.rem(z, 2) + e
    for j in range(4):
        hand(
            GW1.at[:, 32 * j : 32 * j + 32, :],
            RG1.at[:, :, span(r_low, 128)],
            ha(j, x, y),
            lax.div(z, 2),
            bg1 + j,
            bg1 + r_low,
        )

    for copy in hd_copies:
        copy.wait_recv()
    for j in range(4):
        hdo[j] = HD[j] + HD[4 + j] + HD[8 + j] + HD[12 + j]
    hdo[4] = jnp.broadcast_to(labelled, (8, 128))
    for k in range(4):
        landed(RG3.at[k], bg3 + k)
    for t in range(9):
        g3o[t] = (RG3[0, t].astype(F32) + RG3[1, t].astype(F32)) + (
            RG3[2, t].astype(F32) + RG3[3, t].astype(F32)
        )
    for copy in gu_copies:
        copy.wait_recv()
    sums = []
    for k in range(4):
        sums.append(
            (RGU[k].astype(F32) + RGU[4 + k].astype(F32))
            + (RGU[8 + k].astype(F32) + RGU[12 + k].astype(F32))
        )
    for p in range(4):
        guo[p] = jnp.concatenate([part[:, p * 64 : p * 64 + 64] for part in sums], axis=1)
    for k in range(2):
        landed(RG2.at[:, :, 256 * k : 256 * k + 256], bg2 + k)
    g2o[...] = RG2[...]
    for k in range(4):
        landed(RG1.at[:, :, 128 * k : 128 * k + 128], bg1 + k)
    g1o[...] = RG1[...]
    for copy, when in started:
        if when is None:
            copy.wait_send()
        else:
            pl.when(when)(copy.wait_send)


def resident_body(
    input_a,
    input_b,
    skip_a,
    skip_b,
    labels_a,
    labels_b,
    valid_a,
    valid_b,
    w_enter,
    moment_enter,
    square_enter,
    w_middle,
    moment_middle,
    square_middle,
    w_upward,
    moment_upward,
    square_upward,
    w_merge,
    moment_merge,
    square_merge,
    w_head,
    moment_head,
    square_head,
):
    vmem = pl.BlockSpec(memory_space=pltpu.VMEM)
    g1, g2, gu, g3, hd = pl.pallas_call(
        lambda *refs: fused((input_a.shape[2], input_b.shape[2]), *refs),
        out_shape=(
            jax.ShapeDtypeStruct((9, 32, 512), BF),
            jax.ShapeDtypeStruct((9, 64, 512), BF),
            jax.ShapeDtypeStruct((4, 64, 256), F32),
            jax.ShapeDtypeStruct((9, 64, 256), F32),
            jax.ShapeDtypeStruct((5, 8, 128), F32),
        ),
        in_specs=[vmem] * 13,
        out_specs=[vmem] * 5,
        scratch_shapes=[pltpu.VMEM(shape, kind) for _, shape, kind in SCRATCH]
        + [pltpu.SemaphoreType.DMA((COPIES,)), pltpu.SemaphoreType.DMA((COPIES,))],
        compiler_params=pltpu.CompilerParams(
            has_side_effects=True, vmem_limit_bytes=56 * 1024 * 1024
        ),
    )(
        input_a[0, 0],
        input_b[0, 0],
        skip_a[0],
        skip_b[0],
        labels_a[0],
        labels_b[0],
        valid_a[0],
        valid_b[0],
        w_enter.reshape(9, 32, 512),
        w_middle.reshape(9, 64, 512),
        w_upward.reshape(4, 64, 256),
        w_merge.reshape(9, 64, 256),
        w_head,
    )
    grad_enter = g1.astype(F32).reshape(w_enter.shape)
    grad_middle = g2.astype(F32).reshape(w_middle.shape)
    grad_upward = gu.reshape(w_upward.shape)
    grad_merge = g3.reshape(w_merge.shape)
    grad_head = hd[0:4, 0:2, 0:64].transpose(0, 2, 1).reshape(w_head.shape)
    return (
        *adamw(w_enter, moment_enter, square_enter, grad_enter),
        *adamw(w_middle, moment_middle, square_middle, grad_middle),
        *adamw(w_upward, moment_upward, square_upward, grad_upward),
        *adamw(w_merge, moment_merge, square_merge, grad_merge),
        *adamw(w_head, moment_head, square_head, grad_head),
        hd[0, 2, 0],
        hd[4, 0, 0],
    )


def chosen(*args):
    input_a, input_b, skip_a = args[0], args[1], args[2]
    w_enter, w_middle, w_upward, w_merge = args[8], args[11], args[14], args[17]
    fits = (
        lax.axis_size("ha") == 16
        and lax.axis_size("col") == 2
        and input_a.shape[:2] == (1, 1)
        and input_b.shape[:2] == (1, 1)
        and input_a.shape[3] == 256
        and skip_a.shape[3] == 256
        and input_a.shape[2] + input_b.shape[2] <= LANE
        and w_enter.shape == (3, 3, 32, 512)
        and w_middle.shape == (3, 3, 64, 512)
        and w_upward.shape == (2, 2, 64, 256)
        and w_merge.shape == (3, 3, 64, 256)
    )
    return resident_body(*args) if fits else body(*args)


def solution(mesh):
    placed = (
        P(None, "ha", None, "col"),
        P(None, "ha", None, "col"),
        P(None, "ha", None, "col"),
        P(None, "ha", None, "col"),
        P(None, "ha", None),
        P(None, "ha", None),
        P(None, "ha", None),
        P(None, "ha", None),
        P(None, None, "ha", "col"),
        P(None, None, "ha", "col"),
        P(None, None, "ha", "col"),
        P(None, None, "ha", "col"),
        P(None, None, "ha", "col"),
        P(None, None, "ha", "col"),
        P(None, None, "ha", "col"),
        P(None, None, "ha", "col"),
        P(None, None, "ha", "col"),
        P(None, None, "ha", "col"),
        P(None, None, "ha", "col"),
        P(None, None, "ha", "col"),
        P("col", None),
        P("col", None),
        P("col", None),
    )
    return jax.shard_map(
        chosen,
        mesh=mesh,
        in_specs=placed,
        out_specs=(
            P(None, None, "ha", "col"),
            P(None, None, "ha", "col"),
            P(None, None, "ha", "col"),
            P(None, None, "ha", "col"),
            P(None, None, "ha", "col"),
            P(None, None, "ha", "col"),
            P(None, None, "ha", "col"),
            P(None, None, "ha", "col"),
            P(None, None, "ha", "col"),
            P(None, None, "ha", "col"),
            P(None, None, "ha", "col"),
            P(None, None, "ha", "col"),
            P(None, None, "ha", "col"),
            P(None, None, "ha", "col"),
            P(None, None, "ha", "col"),
            P(None, None, "ha", "col"),
            P("col", None),
            P("col", None),
            P("col", None),
            P("col", None),
            P(),
            P(),
        ),
        check_vma=False,
    )
```

```python
import jax
import jax.numpy as jnp
from jax import lax
from jax.experimental import pallas as pl
from jax.experimental.pallas import tpu as pltpu
from jax.sharding import PartitionSpec as P

STEP = 10


NUMBERS = ("NHWC", "HWIO", "NHWC")
BETA_ONE = 0.9
BETA_TWO = 0.95
RATE = 0.08
DECAY = 0.1
EPSILON = 1e-08


def extended(cells, sides, width):
    for axis, dim in sides:
        count = lax.axis_size(axis)
        ends = count - 1
        head = lax.slice_in_dim(cells, 0, width, axis=dim)
        tail = lax.slice_in_dim(cells, cells.shape[dim] - width, cells.shape[dim], axis=dim)
        cells = jnp.concatenate(
            [
                lax.ppermute(tail, axis, [(i, (i + 1) % count) for i in range(ends)]),
                cells,
                lax.ppermute(head, axis, [((i + 1) % count, i) for i in range(ends)]),
            ],
            axis=dim,
        )
    return cells


def shortened(value):

    def short(part):
        return part.astype(jnp.bfloat16) if part.dtype == jnp.float32 else part

    return jax.tree.map(short, value)


def convolve_rows(padded, weight):
    return lax.conv_general_dilated(
        padded,
        weight,
        (1, 1),
        ((0, 0), (1, 1)),
        dimension_numbers=NUMBERS,
        preferred_element_type=jnp.float32,
    )


def flipped(weight):
    return jnp.transpose(weight[::-1, ::-1], (0, 1, 3, 2))


def upsample(values, weight):
    product = jnp.einsum("nhwc,abcd->nhawbd", values, weight, preferred_element_type=jnp.float32)
    return product.reshape(
        product.shape[0], 2 * product.shape[1], 2 * product.shape[3], product.shape[5]
    )


def split_pixels(upstream):
    return upstream.reshape(
        upstream.shape[0], upstream.shape[1] // 2, 2, upstream.shape[2] // 2, 2, upstream.shape[3]
    )


def upsample_back(upstream, weight):
    return jnp.einsum(
        "nhawbd,abcd->nhwc", split_pixels(upstream), weight, preferred_element_type=jnp.float32
    )


def upsample_weight(values, upstream):
    return jnp.einsum(
        "nhwc,nhawbd->abcd", values, split_pixels(upstream), preferred_element_type=jnp.float32
    )


def tap_grads(padded, upstream):
    wide = jnp.pad(padded, ((0, 0), (0, 0), (1, 1), (0, 0)))
    height, across = (upstream.shape[1], upstream.shape[2])
    stacked = []
    for row_tap in range(3):
        tapline = []
        for col_tap in range(3):
            window = wide[:, row_tap : row_tap + height, col_tap : col_tap + across, :]
            tapline.append(
                jnp.einsum("nhwc,nhwd->cd", window, upstream, preferred_element_type=jnp.float32)
            )
        stacked.append(jnp.stack(tapline))
    return jnp.stack(stacked)


def alternate(weight, groups):
    dims = weight.shape
    shaped = weight.reshape(dims[0], dims[1], 2, groups, dims[2] // (2 * groups), dims[3])
    return shaped.transpose(0, 1, 3, 2, 4, 5).reshape(dims)


def deinterleave(weight, groups):
    dims = weight.shape
    shaped = weight.reshape(dims[0], dims[1], groups, 2, dims[2] // (2 * groups), dims[3])
    return shaped.transpose(0, 1, 3, 2, 4, 5).reshape(dims)


def gelu_back(pre_act, upstream):
    return jax.vjp(jax.nn.gelu, pre_act)[1](upstream)[0]


def focal(logits, labels, usable):
    logprob = jax.nn.log_softmax(logits, axis=-1)
    picked = jnp.where(labels == 1, logprob[..., 1], logprob[..., 0])
    chance = jnp.exp(picked)
    return jnp.sum(usable.astype(jnp.float32) * (-((1.0 - chance) ** 2) * picked))


def loss_terms(logits, labels, usable, labelled):
    running, pull = jax.vjp(lambda values: focal(values, labels, usable), logits)
    return (running, pull(1.0 / labelled)[0])


def gather_channels(values):
    return lax.all_gather(values, "col", axis=3, tiled=True)


def spread_back(partial_value):
    return lax.psum_scatter(partial_value, "col", scatter_dimension=3, tiled=True)


def conv_forward(local, weight):
    padded = extended(local, (("ha", 1),), 1)
    whole = gather_channels(padded)
    return (convolve_rows(whole, weight), whole)


def up_forward(local, weight):
    whole = gather_channels(local)
    return (upsample(whole, weight), whole)


def conv_weight_grad(kept, upstream):
    return tap_grads(kept, upstream)


def up_weight_grad(kept, upstream):
    return upsample_weight(kept, upstream)


def backward_weights(merge_up, upward, middle):
    return (flipped(merge_up), upward, flipped(middle))


def conv_input_grad(back_weight, upstream):
    padded = extended(shortened(upstream), (("ha", 1),), 1).astype(upstream.dtype)
    return spread_back(convolve_rows(padded, back_weight))


def up_input_grad(back_weight, upstream):
    return spread_back(upsample_back(upstream, back_weight))


def forward_pass(picture, skipped, copies):
    enter, middle, upward, merge_mixed, back_merge, back_upward, back_middle, head_copy = copies
    pre_one, kept_one = conv_forward(picture, enter)
    act_one = jax.nn.gelu(pre_one).astype(jnp.bfloat16)
    pre_two, kept_two = conv_forward(act_one, middle)
    act_two = jax.nn.gelu(pre_two).astype(jnp.bfloat16)
    raised, kept_up = up_forward(act_two, upward)
    joined = jnp.concatenate([raised.astype(jnp.bfloat16), skipped], axis=3)
    pre_three, kept_three = conv_forward(joined, merge_mixed)
    act_three = jax.nn.gelu(pre_three).astype(jnp.bfloat16)
    partial_value = jnp.einsum(
        "nhwc,ck->nhwk", act_three, head_copy, preferred_element_type=jnp.float32
    )
    return (
        partial_value,
        (pre_one, kept_one, pre_two, kept_two, kept_up, pre_three, kept_three, act_three),
    )


def backward_pass(saved, dlogits, copies):
    enter, middle, upward, merge_mixed, back_merge, back_upward, back_middle, head_copy = copies
    pre_one, kept_one, pre_two, kept_two, kept_up, pre_three, kept_three, act_three = saved
    back_three = jnp.einsum("nhwk,ck->nhwc", dlogits, head_copy, preferred_element_type=jnp.float32)
    grad_head = jnp.einsum("nhwc,nhwk->ck", act_three, dlogits, preferred_element_type=jnp.float32)
    grad_three = gelu_back(pre_three, back_three).astype(jnp.bfloat16)
    grad_merge = conv_weight_grad(kept_three, grad_three)
    d_raised = conv_input_grad(back_merge, grad_three).astype(jnp.bfloat16)
    grad_upward = up_weight_grad(kept_up, d_raised)
    back_two = up_input_grad(back_upward, d_raised)
    grad_two = gelu_back(pre_two, back_two).astype(jnp.bfloat16)
    grad_middle = conv_weight_grad(kept_two, grad_two)
    back_one = conv_input_grad(back_middle, grad_two)
    grad_one = gelu_back(pre_one, back_one).astype(jnp.bfloat16)
    grad_enter = conv_weight_grad(kept_one, grad_one)
    return (grad_enter, grad_middle, grad_upward, grad_merge, grad_head)


def adamw(master, moment, square, gradient):
    moment_new = BETA_ONE * moment + (1.0 - BETA_ONE) * gradient
    square_new = BETA_TWO * square + (1.0 - BETA_TWO) * gradient * gradient
    fixed_moment = moment_new / (1.0 - BETA_ONE**STEP)
    fixed_square = square_new / (1.0 - BETA_TWO**STEP)
    master_new = master - RATE * (
        fixed_moment / (jnp.sqrt(fixed_square) + EPSILON) + DECAY * master
    )
    return (master_new, moment_new, square_new, master_new.astype(jnp.bfloat16))


def own_rows(summed, local):
    return lax.dynamic_slice_in_dim(
        summed, lax.axis_index("ha") * local.shape[2], local.shape[2], 2
    )


def body(
    input_a,
    input_b,
    skip_a,
    skip_b,
    labels_a,
    labels_b,
    valid_a,
    valid_b,
    w_enter,
    moment_enter,
    square_enter,
    w_middle,
    moment_middle,
    square_middle,
    w_upward,
    moment_upward,
    square_upward,
    w_merge,
    moment_merge,
    square_merge,
    w_head,
    moment_head,
    square_head,
):
    groups = lax.axis_size("col")
    enter, middle, upward, merge = (
        lax.all_gather(w_enter.astype(jnp.bfloat16), "ha", axis=2, tiled=True),
        lax.all_gather(w_middle.astype(jnp.bfloat16), "ha", axis=2, tiled=True),
        lax.all_gather(w_upward.astype(jnp.bfloat16), "ha", axis=2, tiled=True),
        lax.all_gather(w_merge.astype(jnp.bfloat16), "ha", axis=2, tiled=True),
    )
    head_low = w_head.astype(jnp.bfloat16)
    merge_up = merge[:, :, : merge.shape[2] // 2]
    back_merge, back_upward, back_middle = backward_weights(merge_up, upward, middle)
    copies = (
        enter,
        middle,
        upward,
        alternate(merge, groups),
        back_merge,
        back_upward,
        back_middle,
        head_low,
    )
    labelled = lax.psum(
        jnp.sum(valid_a.astype(jnp.float32)) + jnp.sum(valid_b.astype(jnp.float32)), "ha"
    )
    partial_a, saved_a = forward_pass(input_a, skip_a, copies)
    partial_b, saved_b = forward_pass(input_b, skip_b, copies)
    logits_a, logits_b = lax.psum((partial_a, partial_b), "col")
    loss_a, dlogits_a = loss_terms(logits_a, labels_a, valid_a, labelled)
    loss_b, dlogits_b = loss_terms(logits_b, labels_b, valid_b, labelled)
    grads_a = backward_pass(saved_a, dlogits_a.astype(jnp.bfloat16), copies)
    grads_b = backward_pass(saved_b, dlogits_b.astype(jnp.bfloat16), copies)
    local_enter = grads_a[0] + grads_b[0]
    local_middle = grads_a[1] + grads_b[1]
    local_upward = grads_a[2] + grads_b[2]
    local_merge = deinterleave(grads_a[3] + grads_b[3], groups)
    local_head = grads_a[4] + grads_b[4]
    local_loss = loss_a + loss_b
    full_enter, full_middle, full_upward, full_merge, head_total, loss_total = (
        lax.psum(local_enter.astype(jnp.bfloat16), "ha").astype(jnp.float32),
        lax.psum(local_middle.astype(jnp.bfloat16), "ha").astype(jnp.float32),
        lax.psum(local_upward.astype(jnp.bfloat16), "ha").astype(jnp.float32),
        lax.psum(local_merge.astype(jnp.bfloat16), "ha").astype(jnp.float32),
        lax.psum(local_head.astype(jnp.bfloat16), "ha").astype(jnp.float32),
        lax.psum(local_loss.astype(jnp.bfloat16), "ha").astype(jnp.float32),
    )
    grad_enter = own_rows(full_enter, w_enter)
    grad_middle = own_rows(full_middle, w_middle)
    grad_upward = own_rows(full_upward, w_upward)
    grad_merge = own_rows(full_merge, w_merge)
    enter_out = adamw(w_enter, moment_enter, square_enter, grad_enter)
    middle_out = adamw(w_middle, moment_middle, square_middle, grad_middle)
    upward_out = adamw(w_upward, moment_upward, square_upward, grad_upward)
    merge_out = adamw(w_merge, moment_merge, square_merge, grad_merge)
    head_out = adamw(w_head, moment_head, square_head, head_total)
    return (
        enter_out[0],
        enter_out[1],
        enter_out[2],
        enter_out[3],
        middle_out[0],
        middle_out[1],
        middle_out[2],
        middle_out[3],
        upward_out[0],
        upward_out[1],
        upward_out[2],
        upward_out[3],
        merge_out[0],
        merge_out[1],
        merge_out[2],
        merge_out[3],
        head_out[0],
        head_out[1],
        head_out[2],
        head_out[3],
        loss_total,
        labelled,
    )


BF = jnp.bfloat16
F32 = jnp.float32
MESH = pl.DeviceIdType.MESH
LANE = 128
PI_PART = 0.7978845608028654
CUBE = 0.044715


def gelu_value(v):
    return 0.5 * v * (1.0 + jnp.tanh(PI_PART * (v + CUBE * (v * v * v))))


def gelu_slope(v):
    bent = jnp.tanh(PI_PART * (v + CUBE * (v * v * v)))
    inner = PI_PART * (1.0 + 3.0 * CUBE * (v * v))
    return 0.5 * (1.0 + bent) + 0.5 * v * (1.0 - bent * bent) * inner


def dot_nn(lhs, rhs):
    return lax.dot_general(lhs, rhs, (((1,), (0,)), ((), ())), preferred_element_type=F32)


def dot_nt(lhs, rhs):
    return lax.dot_general(lhs, rhs, (((1,), (1,)), ((), ())), preferred_element_type=F32)


def span(at, size):
    return pl.ds(pl.multiple_of(at * size, size), size)


SCRATCH = (
    ("inT", (2, 4, 32, 128), BF),
    ("skT", (4, 64, 512), BF),
    ("lab", (8, 128), F32),
    ("flat", (4, 256, 128), F32),
    ("w1", (9, 32, 512), BF),
    ("S1", (9, 32, 512), BF),
    ("w2", (9, 64, 512), BF),
    ("wu", (4, 64, 256), BF),
    ("w3", (9, 64, 256), BF),
    ("IN", (8, 2, 4, 32, 128), BF),
    ("SK", (4, 64, 512), BF),
    ("LB", (16, 8, 128), F32),
    ("W1", (9, 128, 128), BF),
    ("W2", (9, 128, 256), BF),
    ("WU", (16, 64, 256), BF),
    ("W3", (9, 128, 512), BF),
    ("W1T", (128, 1152), BF),
    ("W2T", (256, 1152), BF),
    ("WUT", (256, 1024), BF),
    ("W3T", (512, 1152), BF),
    ("X", (1152, 2304), BF),
    ("P1", (4, 32, 2048), F32),
    ("P1b", (4, 32, 2048), BF),
    ("R1", (3, 32, 2048), BF),
    ("A1", (4, 32, 2048), BF),
    ("P2b", (4, 128, 512), BF),
    ("T2", (4, 128, 512), BF),
    ("S2b", (3, 128, 512), BF),
    ("R2", (3, 128, 512), BF),
    ("pre2", (128, 512), F32),
    ("A2", (8, 128, 512), BF),
    ("J", (2, 4, 128, 768), BF),
    ("P3b", (4, 4, 64, 512), BF),
    ("T3", (4, 4, 64, 512), BF),
    ("S3b", (4, 4, 64, 512), BF),
    ("R3", (4, 3, 64, 512), BF),
    ("pre3", (64, 2048), F32),
    ("act3", (64, 2048), BF),
    ("LG", (8, 32, 128), F32),
    ("LBL", (32, 128), F32),
    ("HT", (256, 8), F32),
    ("DL", (32, 128), F32),
    ("G3", (4, 8, 64, 512), BF),
    ("Z", (1152, 2048), F32),
    ("HS", (2, 2, 64, 128), F32),
    ("HR", (2, 2, 64, 128), F32),
    ("DB", (4, 64, 128), F32),
    ("DR", (256, 512), BF),
    ("P8", (128, 2048), F32),
    ("P7b", (4, 128, 512), BF),
    ("T7", (4, 128, 512), BF),
    ("S7b", (4, 128, 512), BF),
    ("R7", (3, 128, 512), BF),
    ("G2", (2, 128, 2048), BF),
    ("P8b", (4, 32, 2048), BF),
    ("R8", (3, 32, 2048), BF),
    ("G1", (4, 32, 2048), BF),
    ("GW3", (9, 128, 512), BF),
    ("GWU", (16, 64, 256), BF),
    ("GW2", (9, 128, 256), BF),
    ("GW1", (9, 128, 128), BF),
    ("RG3", (4, 9, 64, 256), BF),
    ("Y3", (2, 9, 64, 256), BF),
    ("RGU", (16, 64, 256), BF),
    ("RG2", (9, 64, 512), BF),
    ("RG1", (9, 32, 512), BF),
    ("HD", (16, 8, 128), F32),
)
COPIES = 224


def fused(widths, *refs):
    wa, wb = widths
    rows_a, rows_b, skip_a, skip_b, la, lb, va, vb, f1, f2, fu, f3, fh = refs[:13]
    g1o, g2o, guo, g3o, hdo = refs[13:18]
    m = {name: ref for (name, _, _), ref in zip(SCRATCH, refs[18:-2])}
    send_sem, recv_sem = refs[-2:]
    h, y = lax.axis_index("ha"), lax.axis_index("col")
    z, x, e = lax.div(h, 4), lax.rem(lax.div(h, 2), 2), lax.rem(h, 2)
    q = 2 * y + x
    s = 2 * q + e
    twin = h + 1 - 2 * e
    started = []
    count = [0]

    def ha(z_, x_, e_):
        return 4 * z_ + 2 * x_ + e_

    def remote(src, dst, h2, y2, sem_s, sem_r):
        return pltpu.make_async_remote_copy(
            src_ref=src,
            dst_ref=dst,
            send_sem=send_sem.at[sem_s],
            recv_sem=recv_sem.at[sem_r],
            device_id={"ha": h2, "col": y2},
            device_id_type=MESH,
        )

    def push(src, dst, h2, y2):
        n = count[0]
        count[0] += 1
        copy = remote(src, dst, h2, y2, n, n)
        copy.start()
        started.append((copy, None))
        return copy

    def reserve(n):
        base = count[0]
        count[0] += n
        return base

    def hand(src, dst, h2, y2, sem_s, sem_r, needed=None):
        same = jnp.logical_and(h2 == h, y2 == y)
        away = jnp.logical_not(same)
        if needed is not None:
            same = jnp.logical_and(same, needed)
            away = jnp.logical_and(away, needed)
        copy = remote(src, dst, h2, y2, sem_s, sem_r)

        @pl.when(same)
        def _():
            pltpu.make_async_copy(src, dst, recv_sem.at[sem_r]).start()

        @pl.when(away)
        def _():
            copy.start()

        started.append((copy, away))

    def landed(dst, sem_r):
        remote(dst, dst, twin, y, sem_r, sem_r).wait_recv()

    lanes = lax.broadcasted_iota(jnp.int32, (1, LANE), 1)
    left_ok = jnp.logical_and(jnp.logical_and(lanes != 0, lanes != wa), lanes < wa + wb)
    right_ok = jnp.logical_and(lanes != wa - 1, lanes < wa + wb - 1)

    def from_left(v):
        return jnp.where(left_ok, pltpu.roll(v, 1, 1), 0.0)

    def from_right(v):
        return jnp.where(right_ok, pltpu.roll(v, LANE - 1, 1), 0.0)

    J, HR = m["J"], m["HR"]

    @pl.when(z == 0)
    def _():
        J[1, 1:3, :, 0:128] = jnp.zeros((2, 128, 128), BF)
        HR[0] = jnp.zeros((2, 64, 128), F32)

    @pl.when(z == 3)
    def _():
        J[0, 1:3, :, 640:768] = jnp.zeros((2, 128, 128), BF)
        HR[1] = jnp.zeros((2, 64, 128), F32)

    inT, skT, lab, flat = m["inT"], m["skT"], m["lab"], m["flat"]
    w1, w2, wu, w3 = m["w1"], m["w2"], m["wu"], m["w3"]
    wide_a, wide_b = 2 * wa, 2 * wb
    for c in range(2):
        half = slice(c * 128, c * 128 + 128)
        flat[c, 96:128, :] = jnp.zeros((32, 128), F32)
        flat[c, 0:wa, :] = rows_a[:, half].astype(F32)
        flat[c, wa : wa + wb, :] = rows_b[:, half].astype(F32)
        inT[c] = flat[c, 0:128, :].T.astype(BF).reshape(4, 32, 128)

    IN, LB = m["IN"], m["LB"]
    in_copies = []
    for dz in range(4):
        zt = lax.rem(z + dz, 4)
        for d in range(4):
            if dz == 0 and d == 0:
                continue
            there = lax.rem(2 * x + y + d, 4)
            in_copies.append(
                push(
                    inT.at[:, there],
                    IN.at[2 * z + x, e, pl.ds(2 * y, 2)],
                    ha(zt, lax.div(there, 2), e),
                    lax.rem(there, 2),
                )
            )
    IN[2 * z + x, e, pl.ds(2 * y, 2)] = inT[:, 2 * x + y]

    W1, W2, WU, W3 = m["W1"], m["W2"], m["WU"], m["W3"]
    w1[...] = f1[...].astype(BF)
    S1 = m["S1"]
    near = e == y
    b1 = reserve(4)
    b1s = reserve(5)
    over = remote(w1, S1, h, 1 - y, b1s + 4, b1s + 4)

    @pl.when(jnp.logical_not(near))
    def _():
        over.start()

    started.append((over, jnp.logical_not(near)))

    def spread_first(shard, half, base):
        for k in range(4):
            i = lax.rem(k + 2 * lax.rem(z, 2), 4)
            hand(
                shard.at[:, :, span(i, 128)],
                W1.at[:, span(z, 32), :],
                ha(2 * half + lax.div(i, 2), x, lax.rem(i, 2)),
                e,
                base + k,
                b1 + z,
                near,
            )

    spread_first(w1, y, b1)
    place = lax.broadcasted_iota(jnp.int32, (256, LANE), 0)
    lane = lax.broadcasted_iota(jnp.int32, (256, LANE), 1)
    spread = jnp.concatenate(
        [
            jnp.concatenate([first[...], second[...]], axis=1).astype(F32)
            for first, second in ((la, lb), (va, vb))
        ],
        axis=0,
    )
    spread = jnp.pad(spread, ((0, 4), (0, 256 - wide_a - wide_b)))
    for b in range(2):
        pick = jnp.where(place == 2 * lane + b, 1.0, 0.0)
        planes = dot_nn(spread.astype(BF), pick.astype(BF))
        for a in range(2):
            lab[2 * a + b : 2 * a + b + 1, :] = planes[a : a + 1, :]
            lab[4 + 2 * a + b : 5 + 2 * a + b, :] = planes[2 + a : 3 + a, :]
    lab_copies = []
    LB[h] = lab[...]
    for d in range(1, 16):
        lab_copies.append(push(lab, LB.at[h], lax.rem(h + d, 16), y))


    @pl.when(near)
    def _():
        over.wait_recv()

    spread_first(S1, 1 - y, b1s)
    for copy in in_copies:
        copy.wait_recv()
    twin_in = push(IN.at[:, e], IN.at[:, e], twin, y)

    w2[...] = f2[...].astype(BF)
    w3[...] = f3[...].astype(BF)
    for k in range(4):
        wu[k] = jnp.concatenate([fu[p, :, k * 64 : k * 64 + 64] for p in range(4)], axis=1).astype(BF)
    for a in range(2):
        for c in range(2):
            half = slice(c * 128, c * 128 + 128)
            buf = flat.at[2 * a + c]
            buf[224:256, :] = jnp.zeros((32, 128), F32)
            buf[0:wide_a, :] = skip_a[a, :, half].astype(F32)
            buf[wide_a : wide_a + wide_b, :] = skip_b[a, :, half].astype(F32)
            for b in range(2):
                p = 2 * a + b
                plane = buf[pl.ds(b, 128, stride=2), :]
                skT[2 * c : 2 * c + 2, :, p * 128 : p * 128 + 128] = plane.T.astype(BF).reshape(2, 64, 128)
    b2 = reserve(2)
    for i in range(2):
        hand(
            w2.at[:, :, i * 256 : i * 256 + 256],
            W2.at[:, span(e, 64), :],
            ha(z, i, x),
            y,
            b2 + i,
            b2 + e,
        )
    SK = m["SK"]
    sk_copies = []
    slot = 2 * x + e
    for d in range(1, 4):
        other = lax.rem(slot + d, 4)
        sk_copies.append(push(skT.at[other], SK.at[slot], 4 * z + other, y))
    SK[slot] = skT[slot]
    bu_copies = []
    for d in range(1, 16):
        ht = lax.rem(h + d, 16)
        bu_copies.append(push(wu.at[lax.rem(ht, 4)], WU.at[h], ht, y))
    WU[h] = wu[slot]
    b3 = reserve(4)
    for i in range(4):
        hand(
            w3,
            W3.at[:, span(lax.div(z, 2), 64), span(y, 256)],
            ha(lax.rem(z + i, 4), x, e),
            lax.rem(z, 2),
            b3 + i,
            b3 + 2 * lax.div(z, 2) + y,
        )

    X = m["X"]

    def patch_edges():
        zero = jnp.zeros((384, 128), BF)
        X[0:384, 128:256] = zero
        X[768:1152, 2048:2176] = zero

    def patches(block, first, last):
        def one(i, carry):
            low = block(i)
            v = low.astype(F32)
            kinds = (from_left(v).astype(BF), low, from_right(v).astype(BF))
            for di in (-1, 0, 1):
                for dj in range(3):
                    tap = (di + 1) * 3 + dj
                    X[tap * 128 : tap * 128 + 128, span(i - di + 1, 128)] = kinds[dj]
            return carry

        lax.fori_loop(first, last, one, 0)

    def patch_cols(at, size):
        return pl.ds(pl.multiple_of(at * size + 128, 128), size)

    def transposed(weight, out, rows):
        for t in range(weight.shape[0]):
            out[:, t * rows : t * rows + rows] = weight[t].T

    for j in range(4):
        landed(W1.at[:, 32 * j : 32 * j + 32, :], b1 + j)
    transposed(W1, m["W1T"], 128)
    twin_in.wait_recv()

    def input_block(i):
        return IN[lax.div(i, 2), lax.rem(i, 2)].reshape(128, 128)

    def middle_block(i):
        return A1[:, :, span(i, 128)].reshape(128, 128)

    patches(input_block, 0, 16)
    patch_edges()
    P1, P1b, R1, A1 = m["P1"], m["P1b"], m["R1"], m["A1"]

    def conv_one(n, carry):
        cols = span(n, 512)
        total = dot_nn(m["W1T"][...], X[:, patch_cols(n, 512)]).reshape(4, 32, 512)
        P1[:, :, cols] = total
        P1b[:, :, cols] = total.astype(BF)
        return carry

    def to_plane(d):
        there = lax.rem(q + d, 4)
        return there, ha(z, lax.rem(there, 2), e), lax.div(there, 2)

    def scatter(source, slots, cols=slice(None)):
        copies = []
        for d in range(1, 4):
            there, h2, y2 = to_plane(d)
            copies.append(push(source.at[there, :, cols], slots.at[d - 1, :, cols], h2, y2))
        return copies

    def gather_four(buf, cols):
        copies = []
        for d in range(1, 4):
            _, h2, y2 = to_plane(d)
            copies.append(push(buf.at[q, :, cols], buf.at[q, :, cols], h2, y2))
        return copies

    halves = (slice(0, 1024), slice(1024, 2048))

    def plane_sends(buf):
        copies = []
        for d in range(1, 4):
            _, h2, y2 = to_plane(d)
            copies.append(push(buf.at[s], buf.at[s], h2, y2))
        return copies, push(buf.at[s], buf.at[s], twin, y)

    def plane_passes(buf, sends):
        copies, own = sends
        last = [own]
        for d in range(1, 4):
            copies[d - 1].wait_recv()
            came = 2 * lax.rem(q + 4 - d, 4) + e
            last.append(push(buf.at[came], buf.at[came], twin, y))
        return last

    def gather_plane(buf):
        return plane_passes(buf, plane_sends(buf))

    def arrive(copies):
        for copy in copies:
            copy.wait_recv()

    one_out = []
    for c in range(2):
        lax.fori_loop(2 * c, 2 * c + 2, conv_one, 0)
        one_out.append(scatter(P1b, R1, halves[c]))

    def act_one(n, carry):
        cols = span(n, 512)
        total = P1[q, :, cols] + R1[0, :, cols].astype(F32)
        total = total + R1[1, :, cols].astype(F32) + R1[2, :, cols].astype(F32)
        P1[q, :, cols] = total
        A1[q, :, cols] = gelu_value(total).astype(BF)
        return carry

    wait_one = []
    for c in range(2):
        arrive(one_out[c])
        lax.fori_loop(2 * c, 2 * c + 2, act_one, 0)
        wait_one.append(gather_four(A1, halves[c]))
    for j in range(2):
        landed(W2.at[:, 64 * j : 64 * j + 64, :], b2 + j)
    transposed(W2, m["W2T"], 128)

    for c in range(2):
        arrive(wait_one[c])
        patches(middle_block, 8 * c, 8 * c + 8)
    patch_edges()
    Z, P2b, T2, S2b, R2 = m["Z"], m["P2b"], m["T2"], m["S2b"], m["R2"]

    def band_two(k):
        zt = lax.rem(z + 1 + k, 4)
        Z[0:256, span(zt, 512)] = dot_nn(m["W2T"][...], X[:, patch_cols(zt, 512)])
        P2b[k] = Z[span(1 - e, 128), span(zt, 512)].astype(BF)
        return push(P2b.at[k], T2.at[k], twin, y)

    def pair_two(k):
        zt = lax.rem(z + 1 + k, 4)
        pairs[k].wait_recv()
        S2b[k] = (Z[span(e, 128), span(zt, 512)] + T2[k].astype(F32)).astype(BF)
        two.append(push(S2b.at[k], R2.at[k], ha(zt, x, e), y))

    pairs, two = [], []
    for k in range(4):
        pairs.append(band_two(k))
        if k >= 1:
            pair_two(k - 1)
    for d in range(1, 16):
        bu_copies[d - 1].wait_recv()
    for t in range(8):
        m["WUT"][:, t * 128 : t * 128 + 128] = WU[2 * t : 2 * t + 2].reshape(128, 256).T
    arrive(two)
    pre2, A2 = m["pre2"], m["A2"]
    pairs[3].wait_recv()
    total = Z[span(e, 128), span(z, 512)] + T2[3].astype(F32) + R2[0].astype(F32)
    total = total + R2[1].astype(F32) + R2[2].astype(F32)
    pre2[...] = total
    A2[s] = gelu_value(total).astype(BF)
    wait_two = gather_plane(A2)
    for copy in sk_copies:
        copy.wait_recv()
    for a in range(2):
        for b in range(2):
            p = 2 * a + b
            for i in range(4):
                J[a, 1 + b, 64:128, 128 + 128 * i : 256 + 128 * i] = SK[i, :, p * 128 : p * 128 + 128]
    arrive(wait_two)

    for p in range(4):
        plane = dot_nn(m["WUT"][p * 64 : p * 64 + 64, :], A2[...].reshape(1024, 512))
        J[p // 2, 1 + p % 2, 0:64, 128:640] = plane.astype(BF)

    def fringe(up, down, send_down, keep_down, send_up, keep_up):
        below = remote(send_down, keep_down, lax.rem(h + 4, 16), y, down, down)
        above = remote(send_up, keep_up, lax.rem(h + 12, 16), y, up, up)

        @pl.when(z < 3)
        def _():
            below.start()

        @pl.when(z > 0)
        def _():
            above.start()

        started.append((below, z < 3))
        started.append((above, z > 0))

        def wait():
            @pl.when(z > 0)
            def _():
                below.wait_recv()

            @pl.when(z < 3)
            def _():
                above.wait_recv()

        return wait

    bj = reserve(2)
    wait_rows = fringe(
        bj,
        bj + 1,
        J.at[1, 1:3, :, 512:640],
        J.at[1, 1:3, :, 0:128],
        J.at[0, 1:3, :, 128:256],
        J.at[0, 1:3, :, 640:768],
    )

    def beside(a, i):
        at = slice(i * 128, i * 128 + 128)
        J[a, 0, :, at] = from_left(J[a, 2, :, at].astype(F32)).astype(BF)
        J[a, 3, :, at] = from_right(J[a, 1, :, at].astype(F32)).astype(BF)

    def joined_patches(outer):
        for a in range(2):
            for da in range(3):
                up, di = (a + da - 1) % 2, (a + da - 1) // 2
                first, last = 0, 4
                if di != 0:
                    edge = 0 if di < 0 else 3
                    first, last = (edge, edge + 1) if outer else (1, 4) if di < 0 else (0, 3)
                elif outer:
                    continue
                for b in range(2):
                    for db in range(3):
                        tap = da * 3 + db
                        at = 128 + (2 * a + b) * 512
                        X[tap * 128 : tap * 128 + 128, at + first * 128 : at + last * 128] = J[
                            up, b + db, :, (1 + di + first) * 128 : (1 + di + last) * 128
                        ]

    for a in range(2):
        for i in range(1, 5):
            beside(a, i)
    joined_patches(False)
    wait_rows()
    beside(1, 0)
    beside(0, 5)
    joined_patches(True)

    for j in range(4):
        t, half = j // 2, j % 2
        landed(W3.at[:, 64 * t : 64 * t + 64, 256 * half : 256 * half + 256], b3 + j)
    transposed(W3, m["W3T"], 128)
    P3b, T3, S3b, R3 = m["P3b"], m["T3"], m["S3b"], m["R3"]

    def plane_three(p):
        def step(n, carry):
            Z[0:512, span(n, 256)] = dot_nn(m["W3T"][...], X[:, patch_cols(n, 256)])
            return carry

        lax.fori_loop(2 * p, 2 * p + 2, step, 0)
        cols = slice(p * 512, p * 512 + 512)
        for k in range(4):
            P3b[p, k] = Z[span(2 * k + 1 - e, 64), cols].astype(BF)
        return push(P3b.at[p], T3.at[p], twin, y)

    def pair_three(p):
        pairs[p].wait_recv()
        cols = slice(p * 512, p * 512 + 512)
        for k in range(4):
            total = Z[span(2 * k + e, 64), cols] + T3[p, k].astype(F32)
            Z[span(2 * k + e, 64), cols] = total
            S3b[p, k] = total.astype(BF)
        three.append(scatter(S3b.at[p], R3.at[p]))

    pairs, three = [], []
    for p in range(4):
        pairs.append(plane_three(p))
        if p >= 1:
            pair_three(p - 1)
    pair_three(3)
    pre3, act3, LG = m["pre3"], m["act3"], m["LG"]
    wide = (64, LANE)
    turned = jnp.concatenate([fh[...], jnp.zeros((6, fh.shape[1]), F32)], axis=0).T
    m["HT"][...] = turned.astype(BF).astype(F32)
    head = m["HT"][span(slot, 64), :]
    h0 = jnp.broadcast_to(head[:, 0:1], wide)
    h1 = jnp.broadcast_to(head[:, 1:2], wide)
    for b in range(16):
        if b % 4 == 0:
            arrive(three[b // 4])
        cols = slice(b * 128, b * 128 + 128)
        part = slice(b % 4 * 128, b % 4 * 128 + 128)
        total = Z[span(s, 64), cols] + R3[b // 4, 0, :, part].astype(F32)
        total = total + R3[b // 4, 1, :, part].astype(F32) + R3[b // 4, 2, :, part].astype(F32)
        pre3[:, cols] = total
        act = gelu_value(total).astype(BF)
        act3[:, cols] = act
        act = act.astype(F32)
        LG[s, b : b + 1, :] = jnp.sum(act * h0, axis=0, keepdims=True)
        LG[s, 16 + b : 17 + b, :] = jnp.sum(act * h1, axis=0, keepdims=True)
    wait_logits = []
    for d in range(1, 8):
        there = lax.rem(s + d, 8)
        half = lax.div(there, 4)
        wait_logits.append(push(LG.at[s], LG.at[s], 4 * z + there - 4 * half, half))
    for copy in lab_copies:
        copy.wait_recv()
    LBL = m["LBL"]
    for p in range(4):
        for i in range(4):
            LBL[p * 4 + i : p * 4 + i + 1, :] = LB[4 * z + i, p : p + 1, :]
            LBL[16 + p * 4 + i : 17 + p * 4 + i, :] = LB[4 * z + i, 4 + p : 5 + p, :]
    every = jnp.sum(LB[...], axis=0)
    labelled = jnp.sum(jnp.sum(every[4:8, :], axis=0, keepdims=True), axis=1, keepdims=True)
    arrive(wait_logits)

    logits = LG[0]
    for k in range(1, 8):
        logits = logits + LG[k]
    zero, one = logits[0:16, :], logits[16:32, :]
    picks, usable = LBL[0:16, :] > 0.5, LBL[16:32, :]
    top = jnp.maximum(zero, one)
    lse = top + jnp.log(jnp.exp(zero - top) + jnp.exp(one - top))
    logp = jnp.where(picks, one, zero) - lse
    rest = jnp.exp(jnp.where(picks, zero, one) - lse)
    chance = jnp.exp(logp)
    gap = 1.0 - chance
    terms = usable * (-(gap * gap) * logp)
    slope = (2.0 * gap * chance * logp - gap * gap) * usable / labelled
    own, other = slope * gap, -slope * rest
    DL = m["DL"]
    DL[0:16, :] = jnp.where(picks, other, own).astype(BF).astype(F32)
    DL[16:32, :] = jnp.where(picks, own, other).astype(BF).astype(F32)
    loss = jnp.sum(jnp.sum(terms, axis=0, keepdims=True), axis=1, keepdims=True)
    G3, HD = m["G3"], m["HD"]
    planes = []
    sum0 = jnp.zeros(wide, F32)
    sum1 = jnp.zeros(wide, F32)
    for b in range(16):
        cols = slice(b * 128, b * 128 + 128)
        d0 = jnp.broadcast_to(DL[b : b + 1, :], wide)
        d1 = jnp.broadcast_to(DL[16 + b : 17 + b, :], wide)
        part = slice(b % 4 * 128, b % 4 * 128 + 128)
        G3[b // 4, s, :, part] = ((h0 * d0 + h1 * d1) * gelu_slope(pre3[:, cols])).astype(BF)
        act = act3[:, cols].astype(F32)
        sum0 = sum0 + act * d0
        sum1 = sum1 + act * d1
        if b % 4 == 3:
            planes.append(plane_sends(G3.at[b // 4]))
    side = lax.broadcasted_iota(jnp.int32, wide, 1)
    sum0 = jnp.sum(sum0, axis=1, keepdims=True)
    sum1 = jnp.sum(sum1, axis=1, keepdims=True)
    tile = jnp.where(side == 0, sum0, jnp.where(side == 1, sum1, 0.0))
    HD[h, 0:8, 0:64] = tile.T[0:8, :]
    HD[h, 2:3, 0:64] = jnp.broadcast_to(loss, (1, 64))
    hd_copies = []
    for d in range(1, 16):
        hd_copies.append(push(HD.at[h], HD.at[h], lax.rem(h + d, 16), y))

    HS, DB, DR = m["HS"], m["DB"], m["DR"]

    def back_three(p):
        grads = G3[p].reshape(512, 512)
        Z[0:576, p * 512 : p * 512 + 512] = dot_nn(W3[:, 0:64, :].reshape(576, 512), grads)

    GW3, GWU, GW2, GW1 = m["GW3"], m["GWU"], m["GW2"], m["GW1"]
    RG3, RGU, RG2, RG1 = m["RG3"], m["RGU"], m["RG2"], m["RG1"]

    def grad_three(p):
        def step(t, carry):
            part = dot_nt(X[span(t, 128), 128 + p * 512 : 640 + p * 512], G3[p].reshape(512, 512))
            rows = pl.ds(pl.multiple_of(576 + 128 * lax.div(t, 4), 64), 128)
            cols = span(lax.rem(t, 4), 512)
            if p > 0:
                part = part + Z[rows, cols]
            if p < 3:
                Z[rows, cols] = part
            else:
                GW3[t] = part.astype(BF)
            return carry

        lax.fori_loop(0, 9, step, 0)

    passes = plane_passes(G3.at[0], planes[0])
    for p in range(4):
        arrive(passes)
        back_three(p)
        if p < 3:
            passes = plane_passes(G3.at[p + 1], planes[p + 1])
            grad_three(p)
    def merge_home(first, last):
        for k in range(first, last):
            half, own = lax.rem(y + k // 2, 2), k < 2
            t = lax.rem(lax.div(z, 2) + 1 + k, 2)
            hand(
                GW3.at[:, span(t, 64), span(y, 256)] if own else m["Y3"].at[t],
                RG3.at[z],
                ha(2 * t + half, x, e),
                y,
                bg3 + k,
                bg3 + z,
            )

    ways = (((0, 0, 0), (1, -1, 0), (1, 1, 1)), ((0, -1, -1), (0, 1, 0), (1, 0, 0)))

    def raised_block(a, b, i):
        straight, bent = [], []
        for ao, da, di in ways[a]:
            io = i - di
            if io < 0 or io > 3 or (i < 0 or i > 3) and di == 0:
                continue
            for bo, db, dj in ways[b]:
                tap = (da + 1) * 3 + db + 1
                at = ((2 * ao + bo) * 4 + io) * 128
                (straight if dj == 0 else bent).append(Z[tap * 64 : tap * 64 + 64, at : at + 128])
        turned = sum(bent[1:], bent[0])
        turned = from_left(turned) if b == 0 else from_right(turned)
        return sum(straight, turned)

    for b in range(2):
        HS[0, b] = raised_block(0, b, 4)
        HS[1, b] = raised_block(1, b, -1)
    bh = reserve(2)
    wait_fringe = fringe(bh, bh + 1, HS.at[0], HR.at[0], HS.at[1], HR.at[1])
    for a in range(2):
        for b in range(2):
            p = 2 * a + b
            for i in range(4):
                block = raised_block(a, b, i)
                if i == 3 * a:
                    DB[p] = block
                else:
                    DR[p * 64 : p * 64 + 64, i * 128 : i * 128 + 128] = block.astype(BF)
    grad_three(3)
    bg3 = reserve(4)
    merge_home(0, 2)
    wait_fringe()
    for a in range(2):
        for b in range(2):
            p = 2 * a + b
            DR[p * 64 : p * 64 + 64, a * 384 : a * 384 + 128] = (DB[p] + HR[a, b]).astype(BF)

    P7b, T7, S7b, R7 = m["P7b"], m["T7"], m["S7b"], m["R7"]

    def back_up(k, carry):
        Z[span(k, 128), 0:512] = dot_nn(WU[pl.ds(2 * k, 2)].reshape(128, 256), DR[...])
        return carry

    lax.fori_loop(0, 8, back_up, 0)
    for k in range(4):
        P7b[k] = Z[span(2 * k + 1 - e, 128), 0:512].astype(BF)
    wait_pair = push(P7b, T7, twin, y)

    def pair_seven():
        for k in range(4):
            total = Z[span(2 * k + e, 128), 0:512] + T7[k].astype(F32)
            Z[span(2 * k + e, 128), 0:512] = total
            S7b[k] = total.astype(BF)

    wait_pair.wait_recv()
    pair_seven()
    wait_seven = scatter(S7b, R7)

    def grad_up(k, carry):
        GWU[pl.ds(2 * k, 2)] = dot_nt(A2[k], DR[...]).astype(BF).reshape(2, 64, 256)
        return carry

    Y3 = m["Y3"]
    other = 1 - y
    across = []
    for t in range(2):
        across.append(
            push(
                GW3.at[:, 64 * t : 64 * t + 64, span(other, 256)],
                Y3.at[t],
                h,
                other,
            )
        )

    lax.fori_loop(0, 8, grad_up, 0)
    patches(middle_block, 0, 16)
    patch_edges()
    gu_copies = []
    for d in range(1, 16):
        ht = lax.rem(h + d, 16)
        gu_copies.append(push(GWU.at[ht], RGU.at[h], ht, y))
    RGU[h] = GWU[h]
    arrive(wait_seven)
    G2 = m["G2"]
    total = Z[span(s, 128), 0:512] + R7[0].astype(F32)
    total = total + R7[1].astype(F32) + R7[2].astype(F32)
    G2[e, :, span(z, 512)] = (total * gelu_slope(pre2[...])).astype(BF)
    mine = G2.at[e, :, span(z, 512)]
    g2_copies = []
    for d in range(1, 4):
        zt = lax.rem(z + d, 4)
        g2_copies.append(push(mine, mine, ha(zt, x, e), y))
    own_pair = push(mine, mine, twin, y)

    def back_two(zs):
        for k in range(2):
            cols = pl.ds(pl.multiple_of(zs * 512 + k * 256, 256), 256)
            Z[:, cols] = dot_nn(W2[...].reshape(1152, 256), G2[:, :, cols].reshape(256, 256))

    def relay(d):
        g2_copies[d - 1].wait_recv()
        zs = lax.rem(z + 4 - d, 4)
        came = G2.at[e, :, span(zs, 512)]
        return zs, push(came, came, twin, y)

    arrive(across)
    merge_home(2, 4)
    zs, copy = relay(1)
    own_pair.wait_recv()
    back_two(z)
    for d in range(2, 4):
        after = relay(d)
        copy.wait_recv()
        back_two(zs)
        zs, copy = after
    copy.wait_recv()
    back_two(zs)
    P8b, R8, G1 = m["P8b"], m["R8"], m["G1"]
    P8 = m["P8"]

    def fold(i, carry):
        sums = []
        for dj in range(3):
            part = None
            for di in range(3):
                row = i - (di - 1)
                inside = jnp.logical_and(row >= 0, row <= 15)
                row = jnp.clip(row, 0, 15)
                tap = di * 3 + dj
                block = jnp.where(inside, Z[tap * 128 : tap * 128 + 128, span(row, 128)], 0.0)
                part = block if part is None else part + block
            sums.append(part)
        total = sums[1] + from_right(sums[0]) + from_left(sums[2])
        P8[:, span(i, 128)] = total
        P8b[:, :, span(i, 128)] = total.reshape(4, 32, 128).astype(BF)
        return carry

    wait_eight = []
    for c in range(2):
        lax.fori_loop(8 * c, 8 * c + 8, fold, 0)
        wait_eight.append(scatter(P8b, R8, halves[c]))

    def grad_two(t, carry):
        GW2[t] = dot_nt(X[span(t, 128), 128:2176], G2[...].reshape(256, 2048)).astype(BF)
        return carry

    lax.fori_loop(0, 9, grad_two, 0)

    def act_back(n, carry):
        cols = span(n, 512)
        total = P8[span(q, 32), cols] + R8[0, :, cols].astype(F32)
        total = total + R8[1, :, cols].astype(F32) + R8[2, :, cols].astype(F32)
        G1[q, :, cols] = (total * gelu_slope(P1[q, :, cols])).astype(BF)
        return carry

    wait_g1 = []
    for c in range(2):
        arrive(wait_eight[c])
        lax.fori_loop(2 * c, 2 * c + 2, act_back, 0)
        wait_g1 += gather_four(G1, halves[c])
    bg2 = reserve(2)
    for j in range(2):
        hand(
            GW2.at[:, 64 * j : 64 * j + 64, :],
            RG2.at[:, :, span(x, 256)],
            ha(z, e, j),
            y,
            bg2 + j,
            bg2 + x,
        )
    patches(input_block, 0, 16)
    patch_edges()
    arrive(wait_g1)

    def grad_one(t, carry):
        GW1[t] = dot_nt(X[span(t, 128), 128:2176], G1[...].reshape(128, 2048)).astype(BF)
        return carry

    lax.fori_loop(0, 9, grad_one, 0)
    bg1 = reserve(4)
    r_low = 2 * lax.rem(z, 2) + e
    for k in range(4):
        j = lax.rem(z + 1 + k, 4)
        hand(
            GW1.at[:, span(j, 32), :],
            RG1.at[:, :, span(r_low, 128)],
            ha(j, x, y),
            lax.div(z, 2),
            bg1 + k,
            bg1 + r_low,
        )

    for copy in hd_copies:
        copy.wait_recv()
    for j in range(4):
        hdo[j] = HD[j] + HD[4 + j] + HD[8 + j] + HD[12 + j]
    hdo[4] = jnp.broadcast_to(labelled, (8, 128))
    for k in range(4):
        landed(RG3.at[k], bg3 + k)
    for t in range(9):
        g3o[t] = (RG3[0, t].astype(F32) + RG3[1, t].astype(F32)) + (
            RG3[2, t].astype(F32) + RG3[3, t].astype(F32)
        )
    for copy in gu_copies:
        copy.wait_recv()
    sums = []
    for k in range(4):
        sums.append(
            (RGU[k].astype(F32) + RGU[4 + k].astype(F32))
            + (RGU[8 + k].astype(F32) + RGU[12 + k].astype(F32))
        )
    for p in range(4):
        guo[p] = jnp.concatenate([part[:, p * 64 : p * 64 + 64] for part in sums], axis=1)
    for k in range(2):
        landed(RG2.at[:, :, 256 * k : 256 * k + 256], bg2 + k)
    g2o[...] = RG2[...]
    for k in range(4):
        landed(RG1.at[:, :, 128 * k : 128 * k + 128], bg1 + k)
    g1o[...] = RG1[...]
    for copy, when in started:
        if when is None:
            copy.wait_send()
        else:
            pl.when(when)(copy.wait_send)


def resident_body(
    input_a,
    input_b,
    skip_a,
    skip_b,
    labels_a,
    labels_b,
    valid_a,
    valid_b,
    w_enter,
    moment_enter,
    square_enter,
    w_middle,
    moment_middle,
    square_middle,
    w_upward,
    moment_upward,
    square_upward,
    w_merge,
    moment_merge,
    square_merge,
    w_head,
    moment_head,
    square_head,
):
    vmem = pl.BlockSpec(memory_space=pltpu.VMEM)
    g1, g2, gu, g3, hd = pl.pallas_call(
        lambda *refs: fused((input_a.shape[2], input_b.shape[2]), *refs),
        out_shape=(
            jax.ShapeDtypeStruct((9, 32, 512), BF),
            jax.ShapeDtypeStruct((9, 64, 512), BF),
            jax.ShapeDtypeStruct((4, 64, 256), F32),
            jax.ShapeDtypeStruct((9, 64, 256), F32),
            jax.ShapeDtypeStruct((5, 8, 128), F32),
        ),
        in_specs=[vmem] * 13,
        out_specs=[vmem] * 5,
        scratch_shapes=[pltpu.VMEM(shape, kind) for _, shape, kind in SCRATCH]
        + [pltpu.SemaphoreType.DMA((COPIES,)), pltpu.SemaphoreType.DMA((COPIES,))],
        compiler_params=pltpu.CompilerParams(
            has_side_effects=True, vmem_limit_bytes=56 * 1024 * 1024
        ),
    )(
        input_a[0, 0],
        input_b[0, 0],
        skip_a[0],
        skip_b[0],
        labels_a[0],
        labels_b[0],
        valid_a[0],
        valid_b[0],
        w_enter.reshape(9, 32, 512),
        w_middle.reshape(9, 64, 512),
        w_upward.reshape(4, 64, 256),
        w_merge.reshape(9, 64, 256),
        w_head.T,
    )
    states = (
        (w_enter, moment_enter, square_enter),
        (w_middle, moment_middle, square_middle),
        (w_upward, moment_upward, square_upward),
        (w_merge, moment_merge, square_merge),
    )
    dims = tuple(g.shape for g in (g1, g2, gu, g3))
    flat = [part.reshape(dim) for dim, state in zip(dims, states) for part in state]
    anywhere = pl.BlockSpec(memory_space=pltpu.HBM)
    rows = w_head.T.shape
    new = pl.pallas_call(
        updates,
        out_shape=tuple(
            jax.ShapeDtypeStruct(dim, kind) for dim in (*dims, rows) for kind in (F32, F32, F32, BF)
        ),
        in_specs=[anywhere] * 16 + [vmem] * 4,
        out_specs=[anywhere] * 16 + [vmem] * 4,
        scratch_shapes=[
            pltpu.VMEM(dim, kind)
            for dim, g in zip(dims, (g1, g2, gu, g3))
            for kind in (g.dtype, F32, F32, F32, F32, F32, F32, BF)
        ]
        + [pltpu.SemaphoreType.DMA((len(PIECES), 8))],
        compiler_params=pltpu.CompilerParams(vmem_limit_bytes=62 * 1024 * 1024),
    )(g1, g2, gu, g3, *flat, hd, w_head.T, moment_head.T, square_head.T)
    shapes = (w_enter.shape, w_middle.shape, w_upward.shape, w_merge.shape)
    return (
        *[new[k].reshape(shapes[k // 4]) for k in range(16)],
        *[part.T for part in new[16:]],
        hd[0, 2, 0],
        hd[4, 0, 0],
    )


PIECES = ((3, 0, 5), (3, 5, 9), (2, 0, 4), (1, 0, 3), (1, 3, 6), (1, 6, 9), (0, 0, 5), (0, 5, 9))


def adamw_step(master, moment, square, gradient):
    moment_new = BETA_ONE * moment + (1.0 - BETA_ONE) * gradient
    square_new = BETA_TWO * square + (1.0 - BETA_TWO) * gradient * gradient
    fixed_moment = moment_new * (RATE / (1.0 - BETA_ONE**STEP))
    fixed_square = square_new * (1.0 / (1.0 - BETA_TWO**STEP))
    master_new = (1.0 - RATE * DECAY) * master - fixed_moment / (jnp.sqrt(fixed_square) + EPSILON)
    return (master_new, moment_new, square_new, master_new.astype(BF))


def updates(*refs):
    grads, states = refs[0:4], refs[4:16]
    hd, head, moment, square = refs[16:20]
    outs, tiny = refs[20:36], refs[36:40]
    held, sems = refs[40:72], refs[72]

    def copies(piece):
        k, first, last = PIECES[piece]
        at = slice(first, last)
        inward = [
            pltpu.make_async_copy(source.at[at], held[8 * k + j].at[at], sems.at[piece, j])
            for j, source in enumerate((grads[k], *states[3 * k : 3 * k + 3]))
        ]
        outward = [
            pltpu.make_async_copy(held[8 * k + 4 + j].at[at], outs[4 * k + j].at[at], sems.at[piece, 4 + j])
            for j in range(4)
        ]
        return inward, outward

    every = [copies(piece) for piece in range(len(PIECES))]
    for inward, _ in every:
        for copy in inward:
            copy.start()
    gradient = jnp.concatenate([hd[j, 0:2, 0:64] for j in range(4)], axis=1)
    for ref, value in zip(tiny, adamw_step(head[...], moment[...], square[...], gradient)):
        ref[...] = value
    for (k, first, last), (inward, outward) in zip(PIECES, every):
        for copy in inward:
            copy.wait()
        own = held[8 * k : 8 * k + 8]

        def step(i, carry, own=own):
            made = adamw_step(own[1][i], own[2][i], own[3][i], own[0][i].astype(F32))
            for ref, value in zip(own[4:], made):
                ref[i] = value
            return carry

        lax.fori_loop(first, last, step, 0)
        for copy in outward:
            copy.start()
    for _, outward in every:
        for copy in outward:
            copy.wait()


def chosen(*args):
    input_a, input_b, skip_a = args[0], args[1], args[2]
    w_enter, w_middle, w_upward, w_merge = args[8], args[11], args[14], args[17]
    fits = (
        lax.axis_size("ha") == 16
        and lax.axis_size("col") == 2
        and input_a.shape[:2] == (1, 1)
        and input_b.shape[:2] == (1, 1)
        and input_a.shape[3] == 256
        and skip_a.shape[3] == 256
        and input_a.shape[2] + input_b.shape[2] <= LANE
        and w_enter.shape == (3, 3, 32, 512)
        and w_middle.shape == (3, 3, 64, 512)
        and w_upward.shape == (2, 2, 64, 256)
        and w_merge.shape == (3, 3, 64, 256)
    )
    return resident_body(*args) if fits else body(*args)


def solution(mesh):
    placed = (
        P(None, "ha", None, "col"),
        P(None, "ha", None, "col"),
        P(None, "ha", None, "col"),
        P(None, "ha", None, "col"),
        P(None, "ha", None),
        P(None, "ha", None),
        P(None, "ha", None),
        P(None, "ha", None),
        P(None, None, "ha", "col"),
        P(None, None, "ha", "col"),
        P(None, None, "ha", "col"),
        P(None, None, "ha", "col"),
        P(None, None, "ha", "col"),
        P(None, None, "ha", "col"),
        P(None, None, "ha", "col"),
        P(None, None, "ha", "col"),
        P(None, None, "ha", "col"),
        P(None, None, "ha", "col"),
        P(None, None, "ha", "col"),
        P(None, None, "ha", "col"),
        P("col", None),
        P("col", None),
        P("col", None),
    )
    return jax.shard_map(
        chosen,
        mesh=mesh,
        in_specs=placed,
        out_specs=(
            P(None, None, "ha", "col"),
            P(None, None, "ha", "col"),
            P(None, None, "ha", "col"),
            P(None, None, "ha", "col"),
            P(None, None, "ha", "col"),
            P(None, None, "ha", "col"),
            P(None, None, "ha", "col"),
            P(None, None, "ha", "col"),
            P(None, None, "ha", "col"),
            P(None, None, "ha", "col"),
            P(None, None, "ha", "col"),
            P(None, None, "ha", "col"),
            P(None, None, "ha", "col"),
            P(None, None, "ha", "col"),
            P(None, None, "ha", "col"),
            P(None, None, "ha", "col"),
            P("col", None),
            P("col", None),
            P("col", None),
            P("col", None),
            P(),
            P(),
        ),
        check_vma=False,
    )
```

```python
import jax
import jax.numpy as jnp
from jax import lax
from jax.experimental import pallas as pl
from jax.experimental.pallas import tpu as pltpu
from jax.sharding import PartitionSpec as P

STEP = 10


NUMBERS = ("NHWC", "HWIO", "NHWC")
BETA_ONE = 0.9
BETA_TWO = 0.95
RATE = 0.08
DECAY = 0.1
EPSILON = 1e-08


def extended(cells, sides, width):
    for axis, dim in sides:
        count = lax.axis_size(axis)
        ends = count - 1
        head = lax.slice_in_dim(cells, 0, width, axis=dim)
        tail = lax.slice_in_dim(cells, cells.shape[dim] - width, cells.shape[dim], axis=dim)
        cells = jnp.concatenate(
            [
                lax.ppermute(tail, axis, [(i, (i + 1) % count) for i in range(ends)]),
                cells,
                lax.ppermute(head, axis, [((i + 1) % count, i) for i in range(ends)]),
            ],
            axis=dim,
        )
    return cells


def shortened(value):

    def short(part):
        return part.astype(jnp.bfloat16) if part.dtype == jnp.float32 else part

    return jax.tree.map(short, value)


def convolve_rows(padded, weight):
    return lax.conv_general_dilated(
        padded,
        weight,
        (1, 1),
        ((0, 0), (1, 1)),
        dimension_numbers=NUMBERS,
        preferred_element_type=jnp.float32,
    )


def flipped(weight):
    return jnp.transpose(weight[::-1, ::-1], (0, 1, 3, 2))


def upsample(values, weight):
    product = jnp.einsum("nhwc,abcd->nhawbd", values, weight, preferred_element_type=jnp.float32)
    return product.reshape(
        product.shape[0], 2 * product.shape[1], 2 * product.shape[3], product.shape[5]
    )


def split_pixels(upstream):
    return upstream.reshape(
        upstream.shape[0], upstream.shape[1] // 2, 2, upstream.shape[2] // 2, 2, upstream.shape[3]
    )


def upsample_back(upstream, weight):
    return jnp.einsum(
        "nhawbd,abcd->nhwc", split_pixels(upstream), weight, preferred_element_type=jnp.float32
    )


def upsample_weight(values, upstream):
    return jnp.einsum(
        "nhwc,nhawbd->abcd", values, split_pixels(upstream), preferred_element_type=jnp.float32
    )


def tap_grads(padded, upstream):
    wide = jnp.pad(padded, ((0, 0), (0, 0), (1, 1), (0, 0)))
    height, across = (upstream.shape[1], upstream.shape[2])
    stacked = []
    for row_tap in range(3):
        tapline = []
        for col_tap in range(3):
            window = wide[:, row_tap : row_tap + height, col_tap : col_tap + across, :]
            tapline.append(
                jnp.einsum("nhwc,nhwd->cd", window, upstream, preferred_element_type=jnp.float32)
            )
        stacked.append(jnp.stack(tapline))
    return jnp.stack(stacked)


def alternate(weight, groups):
    dims = weight.shape
    shaped = weight.reshape(dims[0], dims[1], 2, groups, dims[2] // (2 * groups), dims[3])
    return shaped.transpose(0, 1, 3, 2, 4, 5).reshape(dims)


def deinterleave(weight, groups):
    dims = weight.shape
    shaped = weight.reshape(dims[0], dims[1], groups, 2, dims[2] // (2 * groups), dims[3])
    return shaped.transpose(0, 1, 3, 2, 4, 5).reshape(dims)


def gelu_back(pre_act, upstream):
    return jax.vjp(jax.nn.gelu, pre_act)[1](upstream)[0]


def focal(logits, labels, usable):
    logprob = jax.nn.log_softmax(logits, axis=-1)
    picked = jnp.where(labels == 1, logprob[..., 1], logprob[..., 0])
    chance = jnp.exp(picked)
    return jnp.sum(usable.astype(jnp.float32) * (-((1.0 - chance) ** 2) * picked))


def loss_terms(logits, labels, usable, labelled):
    running, pull = jax.vjp(lambda values: focal(values, labels, usable), logits)
    return (running, pull(1.0 / labelled)[0])


def gather_channels(values):
    return lax.all_gather(values, "col", axis=3, tiled=True)


def spread_back(partial_value):
    return lax.psum_scatter(partial_value, "col", scatter_dimension=3, tiled=True)


def conv_forward(local, weight):
    padded = extended(local, (("ha", 1),), 1)
    whole = gather_channels(padded)
    return (convolve_rows(whole, weight), whole)


def up_forward(local, weight):
    whole = gather_channels(local)
    return (upsample(whole, weight), whole)


def conv_weight_grad(kept, upstream):
    return tap_grads(kept, upstream)


def up_weight_grad(kept, upstream):
    return upsample_weight(kept, upstream)


def backward_weights(merge_up, upward, middle):
    return (flipped(merge_up), upward, flipped(middle))


def conv_input_grad(back_weight, upstream):
    padded = extended(shortened(upstream), (("ha", 1),), 1).astype(upstream.dtype)
    return spread_back(convolve_rows(padded, back_weight))


def up_input_grad(back_weight, upstream):
    return spread_back(upsample_back(upstream, back_weight))


def forward_pass(picture, skipped, copies):
    enter, middle, upward, merge_mixed, back_merge, back_upward, back_middle, head_copy = copies
    pre_one, kept_one = conv_forward(picture, enter)
    act_one = jax.nn.gelu(pre_one).astype(jnp.bfloat16)
    pre_two, kept_two = conv_forward(act_one, middle)
    act_two = jax.nn.gelu(pre_two).astype(jnp.bfloat16)
    raised, kept_up = up_forward(act_two, upward)
    joined = jnp.concatenate([raised.astype(jnp.bfloat16), skipped], axis=3)
    pre_three, kept_three = conv_forward(joined, merge_mixed)
    act_three = jax.nn.gelu(pre_three).astype(jnp.bfloat16)
    partial_value = jnp.einsum(
        "nhwc,ck->nhwk", act_three, head_copy, preferred_element_type=jnp.float32
    )
    return (
        partial_value,
        (pre_one, kept_one, pre_two, kept_two, kept_up, pre_three, kept_three, act_three),
    )


def backward_pass(saved, dlogits, copies):
    enter, middle, upward, merge_mixed, back_merge, back_upward, back_middle, head_copy = copies
    pre_one, kept_one, pre_two, kept_two, kept_up, pre_three, kept_three, act_three = saved
    back_three = jnp.einsum("nhwk,ck->nhwc", dlogits, head_copy, preferred_element_type=jnp.float32)
    grad_head = jnp.einsum("nhwc,nhwk->ck", act_three, dlogits, preferred_element_type=jnp.float32)
    grad_three = gelu_back(pre_three, back_three).astype(jnp.bfloat16)
    grad_merge = conv_weight_grad(kept_three, grad_three)
    d_raised = conv_input_grad(back_merge, grad_three).astype(jnp.bfloat16)
    grad_upward = up_weight_grad(kept_up, d_raised)
    back_two = up_input_grad(back_upward, d_raised)
    grad_two = gelu_back(pre_two, back_two).astype(jnp.bfloat16)
    grad_middle = conv_weight_grad(kept_two, grad_two)
    back_one = conv_input_grad(back_middle, grad_two)
    grad_one = gelu_back(pre_one, back_one).astype(jnp.bfloat16)
    grad_enter = conv_weight_grad(kept_one, grad_one)
    return (grad_enter, grad_middle, grad_upward, grad_merge, grad_head)


def adamw(master, moment, square, gradient):
    moment_new = BETA_ONE * moment + (1.0 - BETA_ONE) * gradient
    square_new = BETA_TWO * square + (1.0 - BETA_TWO) * gradient * gradient
    fixed_moment = moment_new / (1.0 - BETA_ONE**STEP)
    fixed_square = square_new / (1.0 - BETA_TWO**STEP)
    master_new = master - RATE * (
        fixed_moment / (jnp.sqrt(fixed_square) + EPSILON) + DECAY * master
    )
    return (master_new, moment_new, square_new, master_new.astype(jnp.bfloat16))


def own_rows(summed, local):
    return lax.dynamic_slice_in_dim(
        summed, lax.axis_index("ha") * local.shape[2], local.shape[2], 2
    )


def body(
    input_a,
    input_b,
    skip_a,
    skip_b,
    labels_a,
    labels_b,
    valid_a,
    valid_b,
    w_enter,
    moment_enter,
    square_enter,
    w_middle,
    moment_middle,
    square_middle,
    w_upward,
    moment_upward,
    square_upward,
    w_merge,
    moment_merge,
    square_merge,
    w_head,
    moment_head,
    square_head,
):
    groups = lax.axis_size("col")
    enter, middle, upward, merge = (
        lax.all_gather(w_enter.astype(jnp.bfloat16), "ha", axis=2, tiled=True),
        lax.all_gather(w_middle.astype(jnp.bfloat16), "ha", axis=2, tiled=True),
        lax.all_gather(w_upward.astype(jnp.bfloat16), "ha", axis=2, tiled=True),
        lax.all_gather(w_merge.astype(jnp.bfloat16), "ha", axis=2, tiled=True),
    )
    head_low = w_head.astype(jnp.bfloat16)
    merge_up = merge[:, :, : merge.shape[2] // 2]
    back_merge, back_upward, back_middle = backward_weights(merge_up, upward, middle)
    copies = (
        enter,
        middle,
        upward,
        alternate(merge, groups),
        back_merge,
        back_upward,
        back_middle,
        head_low,
    )
    labelled = lax.psum(
        jnp.sum(valid_a.astype(jnp.float32)) + jnp.sum(valid_b.astype(jnp.float32)), "ha"
    )
    partial_a, saved_a = forward_pass(input_a, skip_a, copies)
    partial_b, saved_b = forward_pass(input_b, skip_b, copies)
    logits_a, logits_b = lax.psum((partial_a, partial_b), "col")
    loss_a, dlogits_a = loss_terms(logits_a, labels_a, valid_a, labelled)
    loss_b, dlogits_b = loss_terms(logits_b, labels_b, valid_b, labelled)
    grads_a = backward_pass(saved_a, dlogits_a.astype(jnp.bfloat16), copies)
    grads_b = backward_pass(saved_b, dlogits_b.astype(jnp.bfloat16), copies)
    local_enter = grads_a[0] + grads_b[0]
    local_middle = grads_a[1] + grads_b[1]
    local_upward = grads_a[2] + grads_b[2]
    local_merge = deinterleave(grads_a[3] + grads_b[3], groups)
    local_head = grads_a[4] + grads_b[4]
    local_loss = loss_a + loss_b
    full_enter, full_middle, full_upward, full_merge, head_total, loss_total = (
        lax.psum(local_enter.astype(jnp.bfloat16), "ha").astype(jnp.float32),
        lax.psum(local_middle.astype(jnp.bfloat16), "ha").astype(jnp.float32),
        lax.psum(local_upward.astype(jnp.bfloat16), "ha").astype(jnp.float32),
        lax.psum(local_merge.astype(jnp.bfloat16), "ha").astype(jnp.float32),
        lax.psum(local_head.astype(jnp.bfloat16), "ha").astype(jnp.float32),
        lax.psum(local_loss.astype(jnp.bfloat16), "ha").astype(jnp.float32),
    )
    grad_enter = own_rows(full_enter, w_enter)
    grad_middle = own_rows(full_middle, w_middle)
    grad_upward = own_rows(full_upward, w_upward)
    grad_merge = own_rows(full_merge, w_merge)
    enter_out = adamw(w_enter, moment_enter, square_enter, grad_enter)
    middle_out = adamw(w_middle, moment_middle, square_middle, grad_middle)
    upward_out = adamw(w_upward, moment_upward, square_upward, grad_upward)
    merge_out = adamw(w_merge, moment_merge, square_merge, grad_merge)
    head_out = adamw(w_head, moment_head, square_head, head_total)
    return (
        enter_out[0],
        enter_out[1],
        enter_out[2],
        enter_out[3],
        middle_out[0],
        middle_out[1],
        middle_out[2],
        middle_out[3],
        upward_out[0],
        upward_out[1],
        upward_out[2],
        upward_out[3],
        merge_out[0],
        merge_out[1],
        merge_out[2],
        merge_out[3],
        head_out[0],
        head_out[1],
        head_out[2],
        head_out[3],
        loss_total,
        labelled,
    )


BF = jnp.bfloat16
F32 = jnp.float32
MESH = pl.DeviceIdType.MESH
LANE = 128
PI_PART = 0.7978845608028654
CUBE = 0.044715


def gelu_value(v):
    return 0.5 * v * (1.0 + jnp.tanh(PI_PART * (v + CUBE * (v * v * v))))


def gelu_slope(v):
    bent = jnp.tanh(PI_PART * (v + CUBE * (v * v * v)))
    inner = PI_PART * (1.0 + 3.0 * CUBE * (v * v))
    return 0.5 * (1.0 + bent) + 0.5 * v * (1.0 - bent * bent) * inner


def dot_nn(lhs, rhs):
    return lax.dot_general(lhs, rhs, (((1,), (0,)), ((), ())), preferred_element_type=F32)


def dot_nt(lhs, rhs):
    return lax.dot_general(lhs, rhs, (((1,), (1,)), ((), ())), preferred_element_type=F32)


def span(at, size):
    return pl.ds(pl.multiple_of(at * size, size), size)


SCRATCH = (
    ("inT", (2, 4, 32, 128), BF),
    ("skT", (4, 64, 512), BF),
    ("lab", (8, 128), F32),
    ("flat", (4, 256, 128), F32),
    ("w1", (9, 32, 512), BF),
    ("S1", (9, 32, 512), BF),
    ("w2", (9, 64, 512), BF),
    ("wu", (4, 64, 256), BF),
    ("w3", (9, 64, 256), BF),
    ("IN", (8, 2, 4, 32, 128), BF),
    ("SK", (4, 64, 512), BF),
    ("LB", (16, 8, 128), F32),
    ("W1", (9, 128, 128), BF),
    ("W2", (9, 128, 256), BF),
    ("WU", (16, 64, 256), BF),
    ("W3", (9, 128, 512), BF),
    ("W1T", (128, 1152), BF),
    ("W2T", (256, 1152), BF),
    ("WUT", (256, 1024), BF),
    ("W3T", (512, 1152), BF),
    ("X", (1152, 2304), BF),
    ("P1", (4, 32, 2048), F32),
    ("P1b", (4, 32, 2048), BF),
    ("R1", (3, 32, 2048), BF),
    ("A1", (4, 32, 2048), BF),
    ("P2b", (4, 128, 512), BF),
    ("T2", (4, 128, 512), BF),
    ("S2b", (3, 128, 512), BF),
    ("R2", (3, 128, 512), BF),
    ("pre2", (128, 512), F32),
    ("A2", (8, 128, 512), BF),
    ("J", (2, 4, 128, 768), BF),
    ("P3b", (4, 4, 64, 512), BF),
    ("T3", (4, 4, 64, 512), BF),
    ("S3b", (4, 4, 64, 512), BF),
    ("R3", (4, 3, 64, 512), BF),
    ("pre3", (64, 2048), F32),
    ("act3", (64, 2048), BF),
    ("LG", (8, 32, 128), F32),
    ("LBL", (32, 128), F32),
    ("HT", (256, 8), F32),
    ("DL", (32, 128), F32),
    ("G3", (4, 8, 64, 512), BF),
    ("Z", (1152, 2048), F32),
    ("HS", (2, 2, 64, 128), F32),
    ("HR", (2, 2, 64, 128), F32),
    ("DB", (4, 64, 128), F32),
    ("DR", (256, 512), BF),
    ("P8", (128, 2048), F32),
    ("P7b", (4, 128, 512), BF),
    ("T7", (4, 128, 512), BF),
    ("S7b", (4, 128, 512), BF),
    ("R7", (3, 128, 512), BF),
    ("G2", (2, 128, 2048), BF),
    ("P8b", (4, 32, 2048), BF),
    ("R8", (3, 32, 2048), BF),
    ("G1", (4, 32, 2048), BF),
    ("GW3", (9, 128, 512), BF),
    ("GWU", (16, 64, 256), BF),
    ("GW2", (9, 128, 256), BF),
    ("GW1", (9, 128, 128), BF),
    ("RG3", (4, 9, 64, 256), BF),
    ("Y3", (2, 9, 64, 256), BF),
    ("RGU", (16, 64, 256), BF),
    ("RG2", (9, 64, 512), BF),
    ("RG1", (9, 32, 512), BF),
    ("HD", (16, 8, 128), F32),
)
COPIES = 224


def fused(widths, *refs):
    wa, wb = widths
    rows_a, rows_b, skip_a, skip_b, la, lb, va, vb, f1, f2, fu, f3, fh = refs[:13]
    g1o, g2o, guo, g3o, hdo = refs[13:18]
    m = {name: ref for (name, _, _), ref in zip(SCRATCH, refs[18:-2])}
    send_sem, recv_sem = refs[-2:]
    h, y = lax.axis_index("ha"), lax.axis_index("col")
    z, x, e = lax.div(h, 4), lax.rem(lax.div(h, 2), 2), lax.rem(h, 2)
    q = 2 * y + x
    s = 2 * q + e
    twin = h + 1 - 2 * e
    entered = pltpu.get_barrier_semaphore()
    for d in range(16):
        for side in (y, 1 - y)[0 if d else 1 :]:
            pl.semaphore_signal(
                entered,
                inc=1,
                device_id={"ha": lax.rem(h + d, 16), "col": side},
                device_id_type=MESH,
            )
    started = []
    count = [0]

    def ha(z_, x_, e_):
        return 4 * z_ + 2 * x_ + e_

    def remote(src, dst, h2, y2, sem_s, sem_r):
        return pltpu.make_async_remote_copy(
            src_ref=src,
            dst_ref=dst,
            send_sem=send_sem.at[sem_s],
            recv_sem=recv_sem.at[sem_r],
            device_id={"ha": h2, "col": y2},
            device_id_type=MESH,
        )

    def push(src, dst, h2, y2):
        n = count[0]
        count[0] += 1
        copy = remote(src, dst, h2, y2, n, n)
        copy.start()
        started.append((copy, None))
        return copy

    def reserve(n):
        base = count[0]
        count[0] += n
        return base

    def hand(src, dst, h2, y2, sem_s, sem_r, needed=None):
        same = jnp.logical_and(h2 == h, y2 == y)
        away = jnp.logical_not(same)
        if needed is not None:
            same = jnp.logical_and(same, needed)
            away = jnp.logical_and(away, needed)
        copy = remote(src, dst, h2, y2, sem_s, sem_r)

        @pl.when(same)
        def _():
            pltpu.make_async_copy(src, dst, recv_sem.at[sem_r]).start()

        @pl.when(away)
        def _():
            copy.start()

        started.append((copy, away))

    def landed(dst, sem_r):
        remote(dst, dst, twin, y, sem_r, sem_r).wait_recv()

    lanes = lax.broadcasted_iota(jnp.int32, (1, LANE), 1)
    left_ok = jnp.logical_and(jnp.logical_and(lanes != 0, lanes != wa), lanes < wa + wb)
    right_ok = jnp.logical_and(lanes != wa - 1, lanes < wa + wb - 1)

    def from_left(v):
        return jnp.where(left_ok, pltpu.roll(v, 1, 1), 0.0)

    def from_right(v):
        return jnp.where(right_ok, pltpu.roll(v, LANE - 1, 1), 0.0)

    J, HR = m["J"], m["HR"]

    @pl.when(z == 0)
    def _():
        J[1, 1:3, :, 0:128] = jnp.zeros((2, 128, 128), BF)
        HR[0] = jnp.zeros((2, 64, 128), F32)

    @pl.when(z == 3)
    def _():
        J[0, 1:3, :, 640:768] = jnp.zeros((2, 128, 128), BF)
        HR[1] = jnp.zeros((2, 64, 128), F32)

    inT, skT, lab, flat = m["inT"], m["skT"], m["lab"], m["flat"]
    w1, w2, wu, w3 = m["w1"], m["w2"], m["wu"], m["w3"]
    wide_a, wide_b = 2 * wa, 2 * wb
    for c in range(2):
        half = slice(c * 128, c * 128 + 128)
        flat[c, 96:128, :] = jnp.zeros((32, 128), F32)
        flat[c, 0:wa, :] = rows_a[:, half].astype(F32)
        flat[c, wa : wa + wb, :] = rows_b[:, half].astype(F32)
        inT[c] = flat[c, 0:128, :].T.astype(BF).reshape(4, 32, 128)

    w1[...] = f1[...].astype(BF)
    pl.semaphore_wait(entered, 31)

    IN, LB = m["IN"], m["LB"]
    in_copies = []
    for dz in range(4):
        zt = lax.rem(z + dz, 4)
        for d in range(4):
            if dz == 0 and d == 0:
                continue
            there = lax.rem(2 * x + y + d, 4)
            in_copies.append(
                push(
                    inT.at[:, there],
                    IN.at[2 * z + x, e, pl.ds(2 * y, 2)],
                    ha(zt, lax.div(there, 2), e),
                    lax.rem(there, 2),
                )
            )
    IN[2 * z + x, e, pl.ds(2 * y, 2)] = inT[:, 2 * x + y]

    W1, W2, WU, W3 = m["W1"], m["W2"], m["WU"], m["W3"]
    S1 = m["S1"]
    near = e == y
    b1 = reserve(4)
    b1s = reserve(5)
    over = remote(w1, S1, h, 1 - y, b1s + 4, b1s + 4)

    @pl.when(jnp.logical_not(near))
    def _():
        over.start()

    started.append((over, jnp.logical_not(near)))

    def spread_first(shard, half, base):
        for k in range(4):
            i = lax.rem(k + 2 * lax.rem(z, 2), 4)
            hand(
                shard.at[:, :, span(i, 128)],
                W1.at[:, span(z, 32), :],
                ha(2 * half + lax.div(i, 2), x, lax.rem(i, 2)),
                e,
                base + k,
                b1 + z,
                near,
            )

    spread_first(w1, y, b1)
    place = lax.broadcasted_iota(jnp.int32, (256, LANE), 0)
    lane = lax.broadcasted_iota(jnp.int32, (256, LANE), 1)
    spread = jnp.concatenate(
        [
            jnp.concatenate([first[...], second[...]], axis=1).astype(F32)
            for first, second in ((la, lb), (va, vb))
        ],
        axis=0,
    )
    spread = jnp.pad(spread, ((0, 4), (0, 256 - wide_a - wide_b)))
    for b in range(2):
        pick = jnp.where(place == 2 * lane + b, 1.0, 0.0)
        planes = dot_nn(spread.astype(BF), pick.astype(BF))
        for a in range(2):
            lab[2 * a + b : 2 * a + b + 1, :] = planes[a : a + 1, :]
            lab[4 + 2 * a + b : 5 + 2 * a + b, :] = planes[2 + a : 3 + a, :]
    lab_copies = []
    LB[h] = lab[...]
    for d in range(1, 16):
        lab_copies.append(push(lab, LB.at[h], lax.rem(h + d, 16), y))


    @pl.when(near)
    def _():
        over.wait_recv()

    spread_first(S1, 1 - y, b1s)
    for copy in in_copies:
        copy.wait_recv()
    twin_in = push(IN.at[:, e], IN.at[:, e], twin, y)

    w2[...] = f2[...].astype(BF)
    w3[...] = f3[...].astype(BF)
    for k in range(4):
        wu[k] = jnp.concatenate([fu[p, :, k * 64 : k * 64 + 64] for p in range(4)], axis=1).astype(BF)
    for a in range(2):
        for c in range(2):
            half = slice(c * 128, c * 128 + 128)
            buf = flat.at[2 * a + c]
            buf[224:256, :] = jnp.zeros((32, 128), F32)
            buf[0:wide_a, :] = skip_a[a, :, half].astype(F32)
            buf[wide_a : wide_a + wide_b, :] = skip_b[a, :, half].astype(F32)
            for b in range(2):
                p = 2 * a + b
                plane = buf[pl.ds(b, 128, stride=2), :]
                skT[2 * c : 2 * c + 2, :, p * 128 : p * 128 + 128] = plane.T.astype(BF).reshape(2, 64, 128)
    b2 = reserve(2)
    for i in range(2):
        hand(
            w2.at[:, :, i * 256 : i * 256 + 256],
            W2.at[:, span(e, 64), :],
            ha(z, i, x),
            y,
            b2 + i,
            b2 + e,
        )
    SK = m["SK"]
    sk_copies = []
    slot = 2 * x + e
    for d in range(1, 4):
        other = lax.rem(slot + d, 4)
        sk_copies.append(push(skT.at[other], SK.at[slot], 4 * z + other, y))
    SK[slot] = skT[slot]
    bu_copies = []
    for d in range(1, 16):
        ht = lax.rem(h + d, 16)
        bu_copies.append(push(wu.at[lax.rem(ht, 4)], WU.at[h], ht, y))
    WU[h] = wu[slot]
    b3 = reserve(4)
    for i in range(4):
        hand(
            w3,
            W3.at[:, span(lax.div(z, 2), 64), span(y, 256)],
            ha(lax.rem(z + i, 4), x, e),
            lax.rem(z, 2),
            b3 + i,
            b3 + 2 * lax.div(z, 2) + y,
        )

    X = m["X"]

    def patch_edges():
        zero = jnp.zeros((384, 128), BF)
        X[0:384, 128:256] = zero
        X[768:1152, 2048:2176] = zero

    def patches(block, first, last):
        def one(i, carry):
            low = block(i)
            v = low.astype(F32)
            kinds = (from_left(v).astype(BF), low, from_right(v).astype(BF))
            for di in (-1, 0, 1):
                for dj in range(3):
                    tap = (di + 1) * 3 + dj
                    X[tap * 128 : tap * 128 + 128, span(i - di + 1, 128)] = kinds[dj]
            return carry

        lax.fori_loop(first, last, one, 0)

    def patch_cols(at, size):
        return pl.ds(pl.multiple_of(at * size + 128, 128), size)

    def transposed(weight, out, rows):
        for t in range(weight.shape[0]):
            out[:, t * rows : t * rows + rows] = weight[t].T

    for j in range(4):
        landed(W1.at[:, 32 * j : 32 * j + 32, :], b1 + j)
    transposed(W1, m["W1T"], 128)
    twin_in.wait_recv()

    def input_block(i):
        return IN[lax.div(i, 2), lax.rem(i, 2)].reshape(128, 128)

    def middle_block(i):
        return A1[:, :, span(i, 128)].reshape(128, 128)

    patches(input_block, 0, 16)
    patch_edges()
    P1, P1b, R1, A1 = m["P1"], m["P1b"], m["R1"], m["A1"]

    def conv_one(n, carry):
        cols = span(n, 512)
        total = dot_nn(m["W1T"][...], X[:, patch_cols(n, 512)]).reshape(4, 32, 512)
        P1[:, :, cols] = total
        P1b[:, :, cols] = total.astype(BF)
        return carry

    def to_plane(d):
        there = lax.rem(q + d, 4)
        return there, ha(z, lax.rem(there, 2), e), lax.div(there, 2)

    def scatter(source, slots, cols=slice(None)):
        copies = []
        for d in range(1, 4):
            there, h2, y2 = to_plane(d)
            copies.append(push(source.at[there, :, cols], slots.at[d - 1, :, cols], h2, y2))
        return copies

    def gather_four(buf, cols):
        copies = []
        for d in range(1, 4):
            _, h2, y2 = to_plane(d)
            copies.append(push(buf.at[q, :, cols], buf.at[q, :, cols], h2, y2))
        return copies

    halves = (slice(0, 1024), slice(1024, 2048))

    def plane_sends(buf):
        copies = []
        for d in range(1, 4):
            _, h2, y2 = to_plane(d)
            copies.append(push(buf.at[s], buf.at[s], h2, y2))
        return copies, push(buf.at[s], buf.at[s], twin, y)

    def plane_passes(buf, sends):
        copies, own = sends
        last = [own]
        for d in range(1, 4):
            copies[d - 1].wait_recv()
            came = 2 * lax.rem(q + 4 - d, 4) + e
            last.append(push(buf.at[came], buf.at[came], twin, y))
        return last

    def gather_plane(buf):
        return plane_passes(buf, plane_sends(buf))

    def arrive(copies):
        for copy in copies:
            copy.wait_recv()

    one_out = []
    for c in range(2):
        lax.fori_loop(2 * c, 2 * c + 2, conv_one, 0)
        one_out.append(scatter(P1b, R1, halves[c]))

    def act_one(n, carry):
        cols = span(n, 512)
        total = P1[q, :, cols] + R1[0, :, cols].astype(F32)
        total = total + R1[1, :, cols].astype(F32) + R1[2, :, cols].astype(F32)
        P1[q, :, cols] = total
        A1[q, :, cols] = gelu_value(total).astype(BF)
        return carry

    wait_one = []
    for c in range(2):
        arrive(one_out[c])
        lax.fori_loop(2 * c, 2 * c + 2, act_one, 0)
        wait_one.append(gather_four(A1, halves[c]))
    for j in range(2):
        landed(W2.at[:, 64 * j : 64 * j + 64, :], b2 + j)
    transposed(W2, m["W2T"], 128)

    for c in range(2):
        arrive(wait_one[c])
        patches(middle_block, 8 * c, 8 * c + 8)
    patch_edges()
    Z, P2b, T2, S2b, R2 = m["Z"], m["P2b"], m["T2"], m["S2b"], m["R2"]

    def band_two(k):
        zt = lax.rem(z + 1 + k, 4)
        Z[0:256, span(zt, 512)] = dot_nn(m["W2T"][...], X[:, patch_cols(zt, 512)])
        P2b[k] = Z[span(1 - e, 128), span(zt, 512)].astype(BF)
        return push(P2b.at[k], T2.at[k], twin, y)

    def pair_two(k):
        zt = lax.rem(z + 1 + k, 4)
        pairs[k].wait_recv()
        S2b[k] = (Z[span(e, 128), span(zt, 512)] + T2[k].astype(F32)).astype(BF)
        two.append(push(S2b.at[k], R2.at[k], ha(zt, x, e), y))

    pairs, two = [], []
    for k in range(4):
        pairs.append(band_two(k))
        if k >= 1:
            pair_two(k - 1)
    for d in range(1, 16):
        bu_copies[d - 1].wait_recv()
    for t in range(8):
        m["WUT"][:, t * 128 : t * 128 + 128] = WU[2 * t : 2 * t + 2].reshape(128, 256).T
    arrive(two)
    pre2, A2 = m["pre2"], m["A2"]
    pairs[3].wait_recv()
    total = Z[span(e, 128), span(z, 512)] + T2[3].astype(F32) + R2[0].astype(F32)
    total = total + R2[1].astype(F32) + R2[2].astype(F32)
    pre2[...] = total
    A2[s] = gelu_value(total).astype(BF)
    wait_two = gather_plane(A2)
    for copy in sk_copies:
        copy.wait_recv()
    for a in range(2):
        for b in range(2):
            p = 2 * a + b
            for i in range(4):
                J[a, 1 + b, 64:128, 128 + 128 * i : 256 + 128 * i] = SK[i, :, p * 128 : p * 128 + 128]
    arrive(wait_two)

    for p in range(4):
        plane = dot_nn(m["WUT"][p * 64 : p * 64 + 64, :], A2[...].reshape(1024, 512))
        J[p // 2, 1 + p % 2, 0:64, 128:640] = plane.astype(BF)

    def fringe(up, down, send_down, keep_down, send_up, keep_up):
        below = remote(send_down, keep_down, lax.rem(h + 4, 16), y, down, down)
        above = remote(send_up, keep_up, lax.rem(h + 12, 16), y, up, up)

        @pl.when(z < 3)
        def _():
            below.start()

        @pl.when(z > 0)
        def _():
            above.start()

        started.append((below, z < 3))
        started.append((above, z > 0))

        def wait():
            @pl.when(z > 0)
            def _():
                below.wait_recv()

            @pl.when(z < 3)
            def _():
                above.wait_recv()

        return wait

    bj = reserve(2)
    wait_rows = fringe(
        bj,
        bj + 1,
        J.at[1, 1:3, :, 512:640],
        J.at[1, 1:3, :, 0:128],
        J.at[0, 1:3, :, 128:256],
        J.at[0, 1:3, :, 640:768],
    )

    def beside(a, i):
        at = slice(i * 128, i * 128 + 128)
        J[a, 0, :, at] = from_left(J[a, 2, :, at].astype(F32)).astype(BF)
        J[a, 3, :, at] = from_right(J[a, 1, :, at].astype(F32)).astype(BF)

    def joined_patches(outer):
        for a in range(2):
            for da in range(3):
                up, di = (a + da - 1) % 2, (a + da - 1) // 2
                first, last = 0, 4
                if di != 0:
                    edge = 0 if di < 0 else 3
                    first, last = (edge, edge + 1) if outer else (1, 4) if di < 0 else (0, 3)
                elif outer:
                    continue
                for b in range(2):
                    for db in range(3):
                        tap = da * 3 + db
                        at = 128 + (2 * a + b) * 512
                        X[tap * 128 : tap * 128 + 128, at + first * 128 : at + last * 128] = J[
                            up, b + db, :, (1 + di + first) * 128 : (1 + di + last) * 128
                        ]

    for a in range(2):
        for i in range(1, 5):
            beside(a, i)
    joined_patches(False)
    wait_rows()
    beside(1, 0)
    beside(0, 5)
    joined_patches(True)

    for j in range(4):
        t, half = j // 2, j % 2
        landed(W3.at[:, 64 * t : 64 * t + 64, 256 * half : 256 * half + 256], b3 + j)
    transposed(W3, m["W3T"], 128)
    P3b, T3, S3b, R3 = m["P3b"], m["T3"], m["S3b"], m["R3"]

    def plane_three(p):
        def step(n, carry):
            Z[0:512, span(n, 256)] = dot_nn(m["W3T"][...], X[:, patch_cols(n, 256)])
            return carry

        lax.fori_loop(2 * p, 2 * p + 2, step, 0)
        cols = slice(p * 512, p * 512 + 512)
        for k in range(4):
            P3b[p, k] = Z[span(2 * k + 1 - e, 64), cols].astype(BF)
        return push(P3b.at[p], T3.at[p], twin, y)

    def pair_three(p):
        pairs[p].wait_recv()
        cols = slice(p * 512, p * 512 + 512)
        for k in range(4):
            total = Z[span(2 * k + e, 64), cols] + T3[p, k].astype(F32)
            Z[span(2 * k + e, 64), cols] = total
            S3b[p, k] = total.astype(BF)
        three.append(scatter(S3b.at[p], R3.at[p]))

    pairs, three = [], []
    for p in range(4):
        pairs.append(plane_three(p))
        if p >= 1:
            pair_three(p - 1)
    pair_three(3)
    pre3, act3, LG = m["pre3"], m["act3"], m["LG"]
    wide = (64, LANE)
    turned = jnp.concatenate([fh[...], jnp.zeros((6, fh.shape[1]), F32)], axis=0).T
    m["HT"][...] = turned.astype(BF).astype(F32)
    head = m["HT"][span(slot, 64), :]
    h0 = jnp.broadcast_to(head[:, 0:1], wide)
    h1 = jnp.broadcast_to(head[:, 1:2], wide)
    for b in range(16):
        if b % 4 == 0:
            arrive(three[b // 4])
        cols = slice(b * 128, b * 128 + 128)
        part = slice(b % 4 * 128, b % 4 * 128 + 128)
        total = Z[span(s, 64), cols] + R3[b // 4, 0, :, part].astype(F32)
        total = total + R3[b // 4, 1, :, part].astype(F32) + R3[b // 4, 2, :, part].astype(F32)
        pre3[:, cols] = total
        act = gelu_value(total).astype(BF)
        act3[:, cols] = act
        act = act.astype(F32)
        LG[s, b : b + 1, :] = jnp.sum(act * h0, axis=0, keepdims=True)
        LG[s, 16 + b : 17 + b, :] = jnp.sum(act * h1, axis=0, keepdims=True)
    wait_logits = []
    for d in range(1, 8):
        there = lax.rem(s + d, 8)
        half = lax.div(there, 4)
        wait_logits.append(push(LG.at[s], LG.at[s], 4 * z + there - 4 * half, half))
    for copy in lab_copies:
        copy.wait_recv()
    LBL = m["LBL"]
    for p in range(4):
        for i in range(4):
            LBL[p * 4 + i : p * 4 + i + 1, :] = LB[4 * z + i, p : p + 1, :]
            LBL[16 + p * 4 + i : 17 + p * 4 + i, :] = LB[4 * z + i, 4 + p : 5 + p, :]
    every = jnp.sum(LB[...], axis=0)
    labelled = jnp.sum(jnp.sum(every[4:8, :], axis=0, keepdims=True), axis=1, keepdims=True)
    arrive(wait_logits)

    logits = LG[0]
    for k in range(1, 8):
        logits = logits + LG[k]
    zero, one = logits[0:16, :], logits[16:32, :]
    picks, usable = LBL[0:16, :] > 0.5, LBL[16:32, :]
    top = jnp.maximum(zero, one)
    lse = top + jnp.log(jnp.exp(zero - top) + jnp.exp(one - top))
    logp = jnp.where(picks, one, zero) - lse
    rest = jnp.exp(jnp.where(picks, zero, one) - lse)
    chance = jnp.exp(logp)
    gap = 1.0 - chance
    terms = usable * (-(gap * gap) * logp)
    slope = (2.0 * gap * chance * logp - gap * gap) * usable / labelled
    own, other = slope * gap, -slope * rest
    DL = m["DL"]
    DL[0:16, :] = jnp.where(picks, other, own).astype(BF).astype(F32)
    DL[16:32, :] = jnp.where(picks, own, other).astype(BF).astype(F32)
    loss = jnp.sum(jnp.sum(terms, axis=0, keepdims=True), axis=1, keepdims=True)
    G3, HD = m["G3"], m["HD"]
    planes = []
    sum0 = jnp.zeros(wide, F32)
    sum1 = jnp.zeros(wide, F32)
    for b in range(16):
        cols = slice(b * 128, b * 128 + 128)
        d0 = jnp.broadcast_to(DL[b : b + 1, :], wide)
        d1 = jnp.broadcast_to(DL[16 + b : 17 + b, :], wide)
        part = slice(b % 4 * 128, b % 4 * 128 + 128)
        G3[b // 4, s, :, part] = ((h0 * d0 + h1 * d1) * gelu_slope(pre3[:, cols])).astype(BF)
        act = act3[:, cols].astype(F32)
        sum0 = sum0 + act * d0
        sum1 = sum1 + act * d1
        if b % 4 == 3:
            planes.append(plane_sends(G3.at[b // 4]))
    side = lax.broadcasted_iota(jnp.int32, wide, 1)
    sum0 = jnp.sum(sum0, axis=1, keepdims=True)
    sum1 = jnp.sum(sum1, axis=1, keepdims=True)
    tile = jnp.where(side == 0, sum0, jnp.where(side == 1, sum1, 0.0))
    HD[h, 0:8, 0:64] = tile.T[0:8, :]
    HD[h, 2:3, 0:64] = jnp.broadcast_to(loss, (1, 64))
    hd_copies = []
    for d in range(1, 16):
        hd_copies.append(push(HD.at[h], HD.at[h], lax.rem(h + d, 16), y))

    HS, DB, DR = m["HS"], m["DB"], m["DR"]

    def back_three(p):
        grads = G3[p].reshape(512, 512)
        Z[0:576, p * 512 : p * 512 + 512] = dot_nn(W3[:, 0:64, :].reshape(576, 512), grads)

    GW3, GWU, GW2, GW1 = m["GW3"], m["GWU"], m["GW2"], m["GW1"]
    RG3, RGU, RG2, RG1 = m["RG3"], m["RGU"], m["RG2"], m["RG1"]

    def grad_three(p):
        def step(t, carry):
            part = dot_nt(X[span(t, 128), 128 + p * 512 : 640 + p * 512], G3[p].reshape(512, 512))
            rows = pl.ds(pl.multiple_of(576 + 128 * lax.div(t, 4), 64), 128)
            cols = span(lax.rem(t, 4), 512)
            if p > 0:
                part = part + Z[rows, cols]
            if p < 3:
                Z[rows, cols] = part
            else:
                GW3[t] = part.astype(BF)
            return carry

        lax.fori_loop(0, 9, step, 0)

    passes = plane_passes(G3.at[0], planes[0])
    for p in range(4):
        arrive(passes)
        back_three(p)
        if p < 3:
            passes = plane_passes(G3.at[p + 1], planes[p + 1])
            grad_three(p)
    def merge_home(first, last):
        for k in range(first, last):
            half, own = lax.rem(y + k // 2, 2), k < 2
            t = lax.rem(lax.div(z, 2) + 1 + k, 2)
            hand(
                GW3.at[:, span(t, 64), span(y, 256)] if own else m["Y3"].at[t],
                RG3.at[z],
                ha(2 * t + half, x, e),
                y,
                bg3 + k,
                bg3 + z,
            )

    ways = (((0, 0, 0), (1, -1, 0), (1, 1, 1)), ((0, -1, -1), (0, 1, 0), (1, 0, 0)))

    def raised_block(a, b, i):
        straight, bent = [], []
        for ao, da, di in ways[a]:
            io = i - di
            if io < 0 or io > 3 or (i < 0 or i > 3) and di == 0:
                continue
            for bo, db, dj in ways[b]:
                tap = (da + 1) * 3 + db + 1
                at = ((2 * ao + bo) * 4 + io) * 128
                (straight if dj == 0 else bent).append(Z[tap * 64 : tap * 64 + 64, at : at + 128])
        turned = sum(bent[1:], bent[0])
        turned = from_left(turned) if b == 0 else from_right(turned)
        return sum(straight, turned)

    for b in range(2):
        HS[0, b] = raised_block(0, b, 4)
        HS[1, b] = raised_block(1, b, -1)
    bh = reserve(2)
    wait_fringe = fringe(bh, bh + 1, HS.at[0], HR.at[0], HS.at[1], HR.at[1])
    for a in range(2):
        for b in range(2):
            p = 2 * a + b
            for i in range(4):
                block = raised_block(a, b, i)
                if i == 3 * a:
                    DB[p] = block
                else:
                    DR[p * 64 : p * 64 + 64, i * 128 : i * 128 + 128] = block.astype(BF)
    grad_three(3)
    bg3 = reserve(4)
    merge_home(0, 2)
    wait_fringe()
    for a in range(2):
        for b in range(2):
            p = 2 * a + b
            DR[p * 64 : p * 64 + 64, a * 384 : a * 384 + 128] = (DB[p] + HR[a, b]).astype(BF)

    P7b, T7, S7b, R7 = m["P7b"], m["T7"], m["S7b"], m["R7"]

    def back_up(k, carry):
        Z[span(k, 128), 0:512] = dot_nn(WU[pl.ds(2 * k, 2)].reshape(128, 256), DR[...])
        return carry

    lax.fori_loop(0, 8, back_up, 0)
    for k in range(4):
        P7b[k] = Z[span(2 * k + 1 - e, 128), 0:512].astype(BF)
    wait_pair = push(P7b, T7, twin, y)

    def pair_seven():
        for k in range(4):
            total = Z[span(2 * k + e, 128), 0:512] + T7[k].astype(F32)
            Z[span(2 * k + e, 128), 0:512] = total
            S7b[k] = total.astype(BF)

    wait_pair.wait_recv()
    pair_seven()
    wait_seven = scatter(S7b, R7)

    def grad_up(k, carry):
        GWU[pl.ds(2 * k, 2)] = dot_nt(A2[k], DR[...]).astype(BF).reshape(2, 64, 256)
        return carry

    Y3 = m["Y3"]
    other = 1 - y
    across = []
    for t in range(2):
        across.append(
            push(
                GW3.at[:, 64 * t : 64 * t + 64, span(other, 256)],
                Y3.at[t],
                h,
                other,
            )
        )

    lax.fori_loop(0, 8, grad_up, 0)
    patches(middle_block, 0, 16)
    patch_edges()
    gu_copies = []
    for d in range(1, 16):
        ht = lax.rem(h + d, 16)
        gu_copies.append(push(GWU.at[ht], RGU.at[h], ht, y))
    RGU[h] = GWU[h]
    arrive(wait_seven)
    G2 = m["G2"]
    total = Z[span(s, 128), 0:512] + R7[0].astype(F32)
    total = total + R7[1].astype(F32) + R7[2].astype(F32)
    G2[e, :, span(z, 512)] = (total * gelu_slope(pre2[...])).astype(BF)
    mine = G2.at[e, :, span(z, 512)]
    g2_copies = []
    for d in range(1, 4):
        zt = lax.rem(z + d, 4)
        g2_copies.append(push(mine, mine, ha(zt, x, e), y))
    own_pair = push(mine, mine, twin, y)

    def back_two(zs):
        for k in range(2):
            cols = pl.ds(pl.multiple_of(zs * 512 + k * 256, 256), 256)
            Z[:, cols] = dot_nn(W2[...].reshape(1152, 256), G2[:, :, cols].reshape(256, 256))

    def relay(d):
        g2_copies[d - 1].wait_recv()
        zs = lax.rem(z + 4 - d, 4)
        came = G2.at[e, :, span(zs, 512)]
        return zs, push(came, came, twin, y)

    arrive(across)
    merge_home(2, 4)
    zs, copy = relay(1)
    own_pair.wait_recv()
    back_two(z)
    for d in range(2, 4):
        after = relay(d)
        copy.wait_recv()
        back_two(zs)
        zs, copy = after
    copy.wait_recv()
    back_two(zs)
    P8b, R8, G1 = m["P8b"], m["R8"], m["G1"]
    P8 = m["P8"]

    def fold(i, carry):
        sums = []
        for dj in range(3):
            part = None
            for di in range(3):
                row = i - (di - 1)
                inside = jnp.logical_and(row >= 0, row <= 15)
                row = jnp.clip(row, 0, 15)
                tap = di * 3 + dj
                block = jnp.where(inside, Z[tap * 128 : tap * 128 + 128, span(row, 128)], 0.0)
                part = block if part is None else part + block
            sums.append(part)
        total = sums[1] + from_right(sums[0]) + from_left(sums[2])
        P8[:, span(i, 128)] = total
        P8b[:, :, span(i, 128)] = total.reshape(4, 32, 128).astype(BF)
        return carry

    wait_eight = []
    for c in range(2):
        lax.fori_loop(8 * c, 8 * c + 8, fold, 0)
        wait_eight.append(scatter(P8b, R8, halves[c]))

    def grad_two(t, carry):
        GW2[t] = dot_nt(X[span(t, 128), 128:2176], G2[...].reshape(256, 2048)).astype(BF)
        return carry

    lax.fori_loop(0, 9, grad_two, 0)

    def act_back(n, carry):
        cols = span(n, 512)
        total = P8[span(q, 32), cols] + R8[0, :, cols].astype(F32)
        total = total + R8[1, :, cols].astype(F32) + R8[2, :, cols].astype(F32)
        G1[q, :, cols] = (total * gelu_slope(P1[q, :, cols])).astype(BF)
        return carry

    wait_g1 = []
    for c in range(2):
        arrive(wait_eight[c])
        lax.fori_loop(2 * c, 2 * c + 2, act_back, 0)
        wait_g1 += gather_four(G1, halves[c])
    bg2 = reserve(2)
    for j in range(2):
        hand(
            GW2.at[:, 64 * j : 64 * j + 64, :],
            RG2.at[:, :, span(x, 256)],
            ha(z, e, j),
            y,
            bg2 + j,
            bg2 + x,
        )
    patches(input_block, 0, 16)
    patch_edges()
    arrive(wait_g1)

    def grad_one(t, carry):
        GW1[t] = dot_nt(X[span(t, 128), 128:2176], G1[...].reshape(128, 2048)).astype(BF)
        return carry

    lax.fori_loop(0, 9, grad_one, 0)
    bg1 = reserve(4)
    r_low = 2 * lax.rem(z, 2) + e
    for k in range(4):
        j = lax.rem(z + 1 + k, 4)
        hand(
            GW1.at[:, span(j, 32), :],
            RG1.at[:, :, span(r_low, 128)],
            ha(j, x, y),
            lax.div(z, 2),
            bg1 + k,
            bg1 + r_low,
        )

    for copy in hd_copies:
        copy.wait_recv()
    for j in range(4):
        hdo[j] = HD[j] + HD[4 + j] + HD[8 + j] + HD[12 + j]
    hdo[4] = jnp.broadcast_to(labelled, (8, 128))
    for k in range(4):
        landed(RG3.at[k], bg3 + k)
    for t in range(9):
        g3o[t] = (RG3[0, t].astype(F32) + RG3[1, t].astype(F32)) + (
            RG3[2, t].astype(F32) + RG3[3, t].astype(F32)
        )
    for copy in gu_copies:
        copy.wait_recv()
    sums = []
    for k in range(4):
        sums.append(
            (RGU[k].astype(F32) + RGU[4 + k].astype(F32))
            + (RGU[8 + k].astype(F32) + RGU[12 + k].astype(F32))
        )
    for p in range(4):
        guo[p] = jnp.concatenate([part[:, p * 64 : p * 64 + 64] for part in sums], axis=1)
    for k in range(2):
        landed(RG2.at[:, :, 256 * k : 256 * k + 256], bg2 + k)
    g2o[...] = RG2[...]
    for k in range(4):
        landed(RG1.at[:, :, 128 * k : 128 * k + 128], bg1 + k)
    g1o[...] = RG1[...]
    for copy, when in started:
        if when is None:
            copy.wait_send()
        else:
            pl.when(when)(copy.wait_send)


def resident_body(
    input_a,
    input_b,
    skip_a,
    skip_b,
    labels_a,
    labels_b,
    valid_a,
    valid_b,
    w_enter,
    moment_enter,
    square_enter,
    w_middle,
    moment_middle,
    square_middle,
    w_upward,
    moment_upward,
    square_upward,
    w_merge,
    moment_merge,
    square_merge,
    w_head,
    moment_head,
    square_head,
):
    vmem = pl.BlockSpec(memory_space=pltpu.VMEM)
    g1, g2, gu, g3, hd = pl.pallas_call(
        lambda *refs: fused((input_a.shape[2], input_b.shape[2]), *refs),
        out_shape=(
            jax.ShapeDtypeStruct((9, 32, 512), BF),
            jax.ShapeDtypeStruct((9, 64, 512), BF),
            jax.ShapeDtypeStruct((4, 64, 256), F32),
            jax.ShapeDtypeStruct((9, 64, 256), F32),
            jax.ShapeDtypeStruct((5, 8, 128), F32),
        ),
        in_specs=[vmem] * 13,
        out_specs=[vmem] * 5,
        scratch_shapes=[pltpu.VMEM(shape, kind) for _, shape, kind in SCRATCH]
        + [pltpu.SemaphoreType.DMA((COPIES,)), pltpu.SemaphoreType.DMA((COPIES,))],
        compiler_params=pltpu.CompilerParams(
            collective_id=0, has_side_effects=True, vmem_limit_bytes=56 * 1024 * 1024
        ),
    )(
        input_a[0, 0],
        input_b[0, 0],
        skip_a[0],
        skip_b[0],
        labels_a[0],
        labels_b[0],
        valid_a[0],
        valid_b[0],
        w_enter.reshape(9, 32, 512),
        w_middle.reshape(9, 64, 512),
        w_upward.reshape(4, 64, 256),
        w_merge.reshape(9, 64, 256),
        w_head.T,
    )
    states = (
        (w_enter, moment_enter, square_enter),
        (w_middle, moment_middle, square_middle),
        (w_upward, moment_upward, square_upward),
        (w_merge, moment_merge, square_merge),
    )
    dims = tuple(g.shape for g in (g1, g2, gu, g3))
    flat = [part.reshape(dim) for dim, state in zip(dims, states) for part in state]
    anywhere = pl.BlockSpec(memory_space=pltpu.HBM)
    rows = w_head.T.shape
    new = pl.pallas_call(
        updates,
        out_shape=tuple(
            jax.ShapeDtypeStruct(dim, kind) for dim in (*dims, rows) for kind in (F32, F32, F32, BF)
        ),
        in_specs=[anywhere] * 16 + [vmem] * 4,
        out_specs=[anywhere] * 16 + [vmem] * 4,
        scratch_shapes=[
            pltpu.VMEM(dim, kind)
            for dim, g in zip(dims, (g1, g2, gu, g3))
            for kind in (g.dtype, F32, F32, F32, F32, F32, F32, BF)
        ]
        + [pltpu.SemaphoreType.DMA((len(PIECES), 8))],
        compiler_params=pltpu.CompilerParams(vmem_limit_bytes=62 * 1024 * 1024),
    )(g1, g2, gu, g3, *flat, hd, w_head.T, moment_head.T, square_head.T)
    shapes = (w_enter.shape, w_middle.shape, w_upward.shape, w_merge.shape)
    return (
        *[new[k].reshape(shapes[k // 4]) for k in range(16)],
        *[part.T for part in new[16:]],
        hd[0, 2, 0],
        hd[4, 0, 0],
    )


PIECES = ((3, 0, 5), (3, 5, 9), (2, 0, 4), (1, 0, 3), (1, 3, 6), (1, 6, 9), (0, 0, 5), (0, 5, 9))


def adamw_step(master, moment, square, gradient):
    moment_new = BETA_ONE * moment + (1.0 - BETA_ONE) * gradient
    square_new = BETA_TWO * square + (1.0 - BETA_TWO) * gradient * gradient
    fixed_moment = moment_new * (RATE / (1.0 - BETA_ONE**STEP))
    fixed_square = square_new * (1.0 / (1.0 - BETA_TWO**STEP))
    master_new = (1.0 - RATE * DECAY) * master - fixed_moment / (jnp.sqrt(fixed_square) + EPSILON)
    return (master_new, moment_new, square_new, master_new.astype(BF))


def updates(*refs):
    grads, states = refs[0:4], refs[4:16]
    hd, head, moment, square = refs[16:20]
    outs, tiny = refs[20:36], refs[36:40]
    held, sems = refs[40:72], refs[72]

    def copies(piece):
        k, first, last = PIECES[piece]
        at = slice(first, last)
        inward = [
            pltpu.make_async_copy(source.at[at], held[8 * k + j].at[at], sems.at[piece, j])
            for j, source in enumerate((grads[k], *states[3 * k : 3 * k + 3]))
        ]
        outward = [
            pltpu.make_async_copy(held[8 * k + 4 + j].at[at], outs[4 * k + j].at[at], sems.at[piece, 4 + j])
            for j in range(4)
        ]
        return inward, outward

    every = [copies(piece) for piece in range(len(PIECES))]
    for inward, _ in every:
        for copy in inward:
            copy.start()
    gradient = jnp.concatenate([hd[j, 0:2, 0:64] for j in range(4)], axis=1)
    for ref, value in zip(tiny, adamw_step(head[...], moment[...], square[...], gradient)):
        ref[...] = value
    for (k, first, last), (inward, outward) in zip(PIECES, every):
        for copy in inward:
            copy.wait()
        own = held[8 * k : 8 * k + 8]

        def step(i, carry, own=own):
            made = adamw_step(own[1][i], own[2][i], own[3][i], own[0][i].astype(F32))
            for ref, value in zip(own[4:], made):
                ref[i] = value
            return carry

        lax.fori_loop(first, last, step, 0)
        for copy in outward:
            copy.start()
    for _, outward in every:
        for copy in outward:
            copy.wait()


def chosen(*args):
    input_a, input_b, skip_a = args[0], args[1], args[2]
    w_enter, w_middle, w_upward, w_merge = args[8], args[11], args[14], args[17]
    fits = (
        lax.axis_size("ha") == 16
        and lax.axis_size("col") == 2
        and input_a.shape[:2] == (1, 1)
        and input_b.shape[:2] == (1, 1)
        and input_a.shape[3] == 256
        and skip_a.shape[3] == 256
        and input_a.shape[2] + input_b.shape[2] <= LANE
        and w_enter.shape == (3, 3, 32, 512)
        and w_middle.shape == (3, 3, 64, 512)
        and w_upward.shape == (2, 2, 64, 256)
        and w_merge.shape == (3, 3, 64, 256)
    )
    return resident_body(*args) if fits else body(*args)


def solution(mesh):
    placed = (
        P(None, "ha", None, "col"),
        P(None, "ha", None, "col"),
        P(None, "ha", None, "col"),
        P(None, "ha", None, "col"),
        P(None, "ha", None),
        P(None, "ha", None),
        P(None, "ha", None),
        P(None, "ha", None),
        P(None, None, "ha", "col"),
        P(None, None, "ha", "col"),
        P(None, None, "ha", "col"),
        P(None, None, "ha", "col"),
        P(None, None, "ha", "col"),
        P(None, None, "ha", "col"),
        P(None, None, "ha", "col"),
        P(None, None, "ha", "col"),
        P(None, None, "ha", "col"),
        P(None, None, "ha", "col"),
        P(None, None, "ha", "col"),
        P(None, None, "ha", "col"),
        P("col", None),
        P("col", None),
        P("col", None),
    )
    return jax.shard_map(
        chosen,
        mesh=mesh,
        in_specs=placed,
        out_specs=(
            P(None, None, "ha", "col"),
            P(None, None, "ha", "col"),
            P(None, None, "ha", "col"),
            P(None, None, "ha", "col"),
            P(None, None, "ha", "col"),
            P(None, None, "ha", "col"),
            P(None, None, "ha", "col"),
            P(None, None, "ha", "col"),
            P(None, None, "ha", "col"),
            P(None, None, "ha", "col"),
            P(None, None, "ha", "col"),
            P(None, None, "ha", "col"),
            P(None, None, "ha", "col"),
            P(None, None, "ha", "col"),
            P(None, None, "ha", "col"),
            P(None, None, "ha", "col"),
            P("col", None),
            P("col", None),
            P("col", None),
            P("col", None),
            P(),
            P(),
        ),
        check_vma=False,
    )
```

```python
import jax
import jax.numpy as jnp
from jax import lax
from jax.experimental import pallas as pl
from jax.experimental.pallas import tpu as pltpu
from jax.sharding import PartitionSpec as P

STEP = 10


NUMBERS = ("NHWC", "HWIO", "NHWC")
BETA_ONE = 0.9
BETA_TWO = 0.95
RATE = 0.08
DECAY = 0.1
EPSILON = 1e-08


def extended(cells, sides, width):
    for axis, dim in sides:
        count = lax.axis_size(axis)
        ends = count - 1
        head = lax.slice_in_dim(cells, 0, width, axis=dim)
        tail = lax.slice_in_dim(cells, cells.shape[dim] - width, cells.shape[dim], axis=dim)
        cells = jnp.concatenate(
            [
                lax.ppermute(tail, axis, [(i, (i + 1) % count) for i in range(ends)]),
                cells,
                lax.ppermute(head, axis, [((i + 1) % count, i) for i in range(ends)]),
            ],
            axis=dim,
        )
    return cells


def shortened(value):

    def short(part):
        return part.astype(jnp.bfloat16) if part.dtype == jnp.float32 else part

    return jax.tree.map(short, value)


def convolve_rows(padded, weight):
    return lax.conv_general_dilated(
        padded,
        weight,
        (1, 1),
        ((0, 0), (1, 1)),
        dimension_numbers=NUMBERS,
        preferred_element_type=jnp.float32,
    )


def flipped(weight):
    return jnp.transpose(weight[::-1, ::-1], (0, 1, 3, 2))


def upsample(values, weight):
    product = jnp.einsum("nhwc,abcd->nhawbd", values, weight, preferred_element_type=jnp.float32)
    return product.reshape(
        product.shape[0], 2 * product.shape[1], 2 * product.shape[3], product.shape[5]
    )


def split_pixels(upstream):
    return upstream.reshape(
        upstream.shape[0], upstream.shape[1] // 2, 2, upstream.shape[2] // 2, 2, upstream.shape[3]
    )


def upsample_back(upstream, weight):
    return jnp.einsum(
        "nhawbd,abcd->nhwc", split_pixels(upstream), weight, preferred_element_type=jnp.float32
    )


def upsample_weight(values, upstream):
    return jnp.einsum(
        "nhwc,nhawbd->abcd", values, split_pixels(upstream), preferred_element_type=jnp.float32
    )


def tap_grads(padded, upstream):
    wide = jnp.pad(padded, ((0, 0), (0, 0), (1, 1), (0, 0)))
    height, across = (upstream.shape[1], upstream.shape[2])
    stacked = []
    for row_tap in range(3):
        tapline = []
        for col_tap in range(3):
            window = wide[:, row_tap : row_tap + height, col_tap : col_tap + across, :]
            tapline.append(
                jnp.einsum("nhwc,nhwd->cd", window, upstream, preferred_element_type=jnp.float32)
            )
        stacked.append(jnp.stack(tapline))
    return jnp.stack(stacked)


def alternate(weight, groups):
    dims = weight.shape
    shaped = weight.reshape(dims[0], dims[1], 2, groups, dims[2] // (2 * groups), dims[3])
    return shaped.transpose(0, 1, 3, 2, 4, 5).reshape(dims)


def deinterleave(weight, groups):
    dims = weight.shape
    shaped = weight.reshape(dims[0], dims[1], groups, 2, dims[2] // (2 * groups), dims[3])
    return shaped.transpose(0, 1, 3, 2, 4, 5).reshape(dims)


def gelu_back(pre_act, upstream):
    return jax.vjp(jax.nn.gelu, pre_act)[1](upstream)[0]


def focal(logits, labels, usable):
    logprob = jax.nn.log_softmax(logits, axis=-1)
    picked = jnp.where(labels == 1, logprob[..., 1], logprob[..., 0])
    chance = jnp.exp(picked)
    return jnp.sum(usable.astype(jnp.float32) * (-((1.0 - chance) ** 2) * picked))


def loss_terms(logits, labels, usable, labelled):
    running, pull = jax.vjp(lambda values: focal(values, labels, usable), logits)
    return (running, pull(1.0 / labelled)[0])


def gather_channels(values):
    return lax.all_gather(values, "col", axis=3, tiled=True)


def spread_back(partial_value):
    return lax.psum_scatter(partial_value, "col", scatter_dimension=3, tiled=True)


def conv_forward(local, weight):
    padded = extended(local, (("ha", 1),), 1)
    whole = gather_channels(padded)
    return (convolve_rows(whole, weight), whole)


def up_forward(local, weight):
    whole = gather_channels(local)
    return (upsample(whole, weight), whole)


def conv_weight_grad(kept, upstream):
    return tap_grads(kept, upstream)


def up_weight_grad(kept, upstream):
    return upsample_weight(kept, upstream)


def backward_weights(merge_up, upward, middle):
    return (flipped(merge_up), upward, flipped(middle))


def conv_input_grad(back_weight, upstream):
    padded = extended(shortened(upstream), (("ha", 1),), 1).astype(upstream.dtype)
    return spread_back(convolve_rows(padded, back_weight))


def up_input_grad(back_weight, upstream):
    return spread_back(upsample_back(upstream, back_weight))


def forward_pass(picture, skipped, copies):
    enter, middle, upward, merge_mixed, back_merge, back_upward, back_middle, head_copy = copies
    pre_one, kept_one = conv_forward(picture, enter)
    act_one = jax.nn.gelu(pre_one).astype(jnp.bfloat16)
    pre_two, kept_two = conv_forward(act_one, middle)
    act_two = jax.nn.gelu(pre_two).astype(jnp.bfloat16)
    raised, kept_up = up_forward(act_two, upward)
    joined = jnp.concatenate([raised.astype(jnp.bfloat16), skipped], axis=3)
    pre_three, kept_three = conv_forward(joined, merge_mixed)
    act_three = jax.nn.gelu(pre_three).astype(jnp.bfloat16)
    partial_value = jnp.einsum(
        "nhwc,ck->nhwk", act_three, head_copy, preferred_element_type=jnp.float32
    )
    return (
        partial_value,
        (pre_one, kept_one, pre_two, kept_two, kept_up, pre_three, kept_three, act_three),
    )


def backward_pass(saved, dlogits, copies):
    enter, middle, upward, merge_mixed, back_merge, back_upward, back_middle, head_copy = copies
    pre_one, kept_one, pre_two, kept_two, kept_up, pre_three, kept_three, act_three = saved
    back_three = jnp.einsum("nhwk,ck->nhwc", dlogits, head_copy, preferred_element_type=jnp.float32)
    grad_head = jnp.einsum("nhwc,nhwk->ck", act_three, dlogits, preferred_element_type=jnp.float32)
    grad_three = gelu_back(pre_three, back_three).astype(jnp.bfloat16)
    grad_merge = conv_weight_grad(kept_three, grad_three)
    d_raised = conv_input_grad(back_merge, grad_three).astype(jnp.bfloat16)
    grad_upward = up_weight_grad(kept_up, d_raised)
    back_two = up_input_grad(back_upward, d_raised)
    grad_two = gelu_back(pre_two, back_two).astype(jnp.bfloat16)
    grad_middle = conv_weight_grad(kept_two, grad_two)
    back_one = conv_input_grad(back_middle, grad_two)
    grad_one = gelu_back(pre_one, back_one).astype(jnp.bfloat16)
    grad_enter = conv_weight_grad(kept_one, grad_one)
    return (grad_enter, grad_middle, grad_upward, grad_merge, grad_head)


def adamw(master, moment, square, gradient):
    moment_new = BETA_ONE * moment + (1.0 - BETA_ONE) * gradient
    square_new = BETA_TWO * square + (1.0 - BETA_TWO) * gradient * gradient
    fixed_moment = moment_new / (1.0 - BETA_ONE**STEP)
    fixed_square = square_new / (1.0 - BETA_TWO**STEP)
    master_new = master - RATE * (
        fixed_moment / (jnp.sqrt(fixed_square) + EPSILON) + DECAY * master
    )
    return (master_new, moment_new, square_new, master_new.astype(jnp.bfloat16))


def own_rows(summed, local):
    return lax.dynamic_slice_in_dim(
        summed, lax.axis_index("ha") * local.shape[2], local.shape[2], 2
    )


def body(
    input_a,
    input_b,
    skip_a,
    skip_b,
    labels_a,
    labels_b,
    valid_a,
    valid_b,
    w_enter,
    moment_enter,
    square_enter,
    w_middle,
    moment_middle,
    square_middle,
    w_upward,
    moment_upward,
    square_upward,
    w_merge,
    moment_merge,
    square_merge,
    w_head,
    moment_head,
    square_head,
):
    groups = lax.axis_size("col")
    enter, middle, upward, merge = (
        lax.all_gather(w_enter.astype(jnp.bfloat16), "ha", axis=2, tiled=True),
        lax.all_gather(w_middle.astype(jnp.bfloat16), "ha", axis=2, tiled=True),
        lax.all_gather(w_upward.astype(jnp.bfloat16), "ha", axis=2, tiled=True),
        lax.all_gather(w_merge.astype(jnp.bfloat16), "ha", axis=2, tiled=True),
    )
    head_low = w_head.astype(jnp.bfloat16)
    merge_up = merge[:, :, : merge.shape[2] // 2]
    back_merge, back_upward, back_middle = backward_weights(merge_up, upward, middle)
    copies = (
        enter,
        middle,
        upward,
        alternate(merge, groups),
        back_merge,
        back_upward,
        back_middle,
        head_low,
    )
    labelled = lax.psum(
        jnp.sum(valid_a.astype(jnp.float32)) + jnp.sum(valid_b.astype(jnp.float32)), "ha"
    )
    partial_a, saved_a = forward_pass(input_a, skip_a, copies)
    partial_b, saved_b = forward_pass(input_b, skip_b, copies)
    logits_a, logits_b = lax.psum((partial_a, partial_b), "col")
    loss_a, dlogits_a = loss_terms(logits_a, labels_a, valid_a, labelled)
    loss_b, dlogits_b = loss_terms(logits_b, labels_b, valid_b, labelled)
    grads_a = backward_pass(saved_a, dlogits_a.astype(jnp.bfloat16), copies)
    grads_b = backward_pass(saved_b, dlogits_b.astype(jnp.bfloat16), copies)
    local_enter = grads_a[0] + grads_b[0]
    local_middle = grads_a[1] + grads_b[1]
    local_upward = grads_a[2] + grads_b[2]
    local_merge = deinterleave(grads_a[3] + grads_b[3], groups)
    local_head = grads_a[4] + grads_b[4]
    local_loss = loss_a + loss_b
    full_enter, full_middle, full_upward, full_merge, head_total, loss_total = (
        lax.psum(local_enter.astype(jnp.bfloat16), "ha").astype(jnp.float32),
        lax.psum(local_middle.astype(jnp.bfloat16), "ha").astype(jnp.float32),
        lax.psum(local_upward.astype(jnp.bfloat16), "ha").astype(jnp.float32),
        lax.psum(local_merge.astype(jnp.bfloat16), "ha").astype(jnp.float32),
        lax.psum(local_head.astype(jnp.bfloat16), "ha").astype(jnp.float32),
        lax.psum(local_loss.astype(jnp.bfloat16), "ha").astype(jnp.float32),
    )
    grad_enter = own_rows(full_enter, w_enter)
    grad_middle = own_rows(full_middle, w_middle)
    grad_upward = own_rows(full_upward, w_upward)
    grad_merge = own_rows(full_merge, w_merge)
    enter_out = adamw(w_enter, moment_enter, square_enter, grad_enter)
    middle_out = adamw(w_middle, moment_middle, square_middle, grad_middle)
    upward_out = adamw(w_upward, moment_upward, square_upward, grad_upward)
    merge_out = adamw(w_merge, moment_merge, square_merge, grad_merge)
    head_out = adamw(w_head, moment_head, square_head, head_total)
    return (
        enter_out[0],
        enter_out[1],
        enter_out[2],
        enter_out[3],
        middle_out[0],
        middle_out[1],
        middle_out[2],
        middle_out[3],
        upward_out[0],
        upward_out[1],
        upward_out[2],
        upward_out[3],
        merge_out[0],
        merge_out[1],
        merge_out[2],
        merge_out[3],
        head_out[0],
        head_out[1],
        head_out[2],
        head_out[3],
        loss_total,
        labelled,
    )


BF = jnp.bfloat16
F32 = jnp.float32
MESH = pl.DeviceIdType.MESH
LANE = 128
PI_PART = 0.7978845608028654
CUBE = 0.044715


def gelu_value(v):
    return 0.5 * v * (1.0 + jnp.tanh(PI_PART * (v + CUBE * (v * v * v))))


def gelu_slope(v):
    bent = jnp.tanh(PI_PART * (v + CUBE * (v * v * v)))
    inner = PI_PART * (1.0 + 3.0 * CUBE * (v * v))
    return 0.5 * (1.0 + bent) + 0.5 * v * (1.0 - bent * bent) * inner


def dot_nn(lhs, rhs):
    return lax.dot_general(lhs, rhs, (((1,), (0,)), ((), ())), preferred_element_type=F32)


def dot_nt(lhs, rhs):
    return lax.dot_general(lhs, rhs, (((1,), (1,)), ((), ())), preferred_element_type=F32)


def span(at, size):
    return pl.ds(pl.multiple_of(at * size, size), size)


SCRATCH = (
    ("inT", (2, 4, 32, 128), BF),
    ("skT", (4, 64, 512), BF),
    ("lab", (8, 128), F32),
    ("F2", (9, 64, 512), F32),
    ("F3", (9, 64, 256), F32),
    ("FU", (4, 64, 256), F32),
    ("flat", (4, 256, 128), F32),
    ("w1", (9, 32, 512), BF),
    ("S1", (9, 32, 512), BF),
    ("w2", (9, 64, 512), BF),
    ("wu", (4, 64, 256), BF),
    ("w3", (9, 64, 256), BF),
    ("IN", (8, 2, 4, 32, 128), BF),
    ("SK", (4, 64, 512), BF),
    ("LB", (16, 8, 128), F32),
    ("W1", (9, 128, 128), BF),
    ("W2", (9, 128, 256), BF),
    ("WU", (16, 64, 256), BF),
    ("W3", (9, 128, 512), BF),
    ("W1T", (128, 1152), BF),
    ("W2T", (256, 1152), BF),
    ("WUT", (256, 1024), BF),
    ("W3T", (512, 1152), BF),
    ("X", (1152, 2304), BF),
    ("P1", (4, 32, 2048), F32),
    ("P1b", (4, 32, 2048), BF),
    ("R1", (3, 32, 2048), BF),
    ("A1", (4, 32, 2048), BF),
    ("P2b", (4, 128, 512), BF),
    ("T2", (4, 128, 512), BF),
    ("S2b", (3, 128, 512), BF),
    ("R2", (3, 128, 512), BF),
    ("pre2", (128, 512), F32),
    ("A2", (8, 128, 512), BF),
    ("J", (2, 4, 128, 768), BF),
    ("P3b", (4, 4, 64, 512), BF),
    ("T3", (4, 4, 64, 512), BF),
    ("S3b", (4, 4, 64, 512), BF),
    ("R3", (4, 3, 64, 512), BF),
    ("pre3", (64, 2048), F32),
    ("act3", (64, 2048), BF),
    ("LG", (8, 32, 128), F32),
    ("LBL", (32, 128), F32),
    ("HT", (256, 8), F32),
    ("DL", (32, 128), F32),
    ("G3", (4, 8, 64, 512), BF),
    ("Z", (1152, 2048), F32),
    ("HS", (2, 2, 64, 128), F32),
    ("HR", (2, 2, 64, 128), F32),
    ("DB", (4, 64, 128), F32),
    ("DR", (256, 512), BF),
    ("P8", (128, 2048), F32),
    ("P7b", (4, 128, 512), BF),
    ("T7", (4, 128, 512), BF),
    ("S7b", (4, 128, 512), BF),
    ("R7", (3, 128, 512), BF),
    ("G2", (2, 128, 2048), BF),
    ("P8b", (4, 32, 2048), BF),
    ("R8", (3, 32, 2048), BF),
    ("G1", (4, 32, 2048), BF),
    ("GW3", (9, 128, 512), BF),
    ("GWU", (16, 64, 256), BF),
    ("GW2", (9, 128, 256), BF),
    ("GW1", (9, 128, 128), BF),
    ("RG3", (4, 9, 64, 256), BF),
    ("Y3", (2, 9, 64, 256), BF),
    ("RGU", (16, 64, 256), BF),
    ("RG2", (9, 64, 512), BF),
    ("RG1", (9, 32, 512), BF),
    ("HD", (16, 8, 128), F32),
)
COPIES = 224


def fused(widths, *refs):
    wa, wb = widths
    rows_a, rows_b, skip_a, skip_b, la, lb, va, vb, f1, f2, fu, f3, fh = refs[:13]
    g1o, g2o, guo, g3o, hdo = refs[13:18]
    m = {name: ref for (name, _, _), ref in zip(SCRATCH, refs[18:-3])}
    send_sem, recv_sem, load_sem = refs[-3:]
    loads = [
        pltpu.make_async_copy(source, m[name], load_sem.at[n])
        for n, (source, name) in enumerate(((f2, "F2"), (f3, "F3"), (fu, "FU")))
    ]
    for load in loads:
        load.start()
    f2, f3, fu = m["F2"], m["F3"], m["FU"]
    h, y = lax.axis_index("ha"), lax.axis_index("col")
    z, x, e = lax.div(h, 4), lax.rem(lax.div(h, 2), 2), lax.rem(h, 2)
    q = 2 * y + x
    s = 2 * q + e
    twin = h + 1 - 2 * e
    entered = pltpu.get_barrier_semaphore()
    for d in range(16):
        for side in (y, 1 - y)[0 if d else 1 :]:
            pl.semaphore_signal(
                entered,
                inc=1,
                device_id={"ha": lax.rem(h + d, 16), "col": side},
                device_id_type=MESH,
            )
    started = []
    count = [0]

    def ha(z_, x_, e_):
        return 4 * z_ + 2 * x_ + e_

    def remote(src, dst, h2, y2, sem_s, sem_r):
        return pltpu.make_async_remote_copy(
            src_ref=src,
            dst_ref=dst,
            send_sem=send_sem.at[sem_s],
            recv_sem=recv_sem.at[sem_r],
            device_id={"ha": h2, "col": y2},
            device_id_type=MESH,
        )

    def push(src, dst, h2, y2):
        n = count[0]
        count[0] += 1
        copy = remote(src, dst, h2, y2, n, n)
        copy.start()
        started.append((copy, None))
        return copy

    def reserve(n):
        base = count[0]
        count[0] += n
        return base

    def hand(src, dst, h2, y2, sem_s, sem_r, needed=None):
        same = jnp.logical_and(h2 == h, y2 == y)
        away = jnp.logical_not(same)
        if needed is not None:
            same = jnp.logical_and(same, needed)
            away = jnp.logical_and(away, needed)
        copy = remote(src, dst, h2, y2, sem_s, sem_r)

        @pl.when(same)
        def _():
            pltpu.make_async_copy(src, dst, recv_sem.at[sem_r]).start()

        @pl.when(away)
        def _():
            copy.start()

        started.append((copy, away))

    def landed(dst, sem_r):
        remote(dst, dst, twin, y, sem_r, sem_r).wait_recv()

    lanes = lax.broadcasted_iota(jnp.int32, (1, LANE), 1)
    left_ok = jnp.logical_and(jnp.logical_and(lanes != 0, lanes != wa), lanes < wa + wb)
    right_ok = jnp.logical_and(lanes != wa - 1, lanes < wa + wb - 1)

    def from_left(v):
        return jnp.where(left_ok, pltpu.roll(v, 1, 1), 0.0)

    def from_right(v):
        return jnp.where(right_ok, pltpu.roll(v, LANE - 1, 1), 0.0)

    J, HR = m["J"], m["HR"]

    @pl.when(z == 0)
    def _():
        J[1, 1:3, :, 0:128] = jnp.zeros((2, 128, 128), BF)
        HR[0] = jnp.zeros((2, 64, 128), F32)

    @pl.when(z == 3)
    def _():
        J[0, 1:3, :, 640:768] = jnp.zeros((2, 128, 128), BF)
        HR[1] = jnp.zeros((2, 64, 128), F32)

    inT, skT, lab, flat = m["inT"], m["skT"], m["lab"], m["flat"]
    w1, w2, wu, w3 = m["w1"], m["w2"], m["wu"], m["w3"]
    wide_a, wide_b = 2 * wa, 2 * wb
    for c in range(2):
        half = slice(c * 128, c * 128 + 128)
        flat[c, 96:128, :] = jnp.zeros((32, 128), F32)
        flat[c, 0:wa, :] = rows_a[:, half].astype(F32)
        flat[c, wa : wa + wb, :] = rows_b[:, half].astype(F32)
        inT[c] = flat[c, 0:128, :].T.astype(BF).reshape(4, 32, 128)

    w1[...] = f1[...].astype(BF)
    pl.semaphore_wait(entered, 31)

    IN, LB = m["IN"], m["LB"]
    W1, W2, WU, W3 = m["W1"], m["W2"], m["WU"], m["W3"]
    S1 = m["S1"]
    near = e == y
    b1 = reserve(4)
    b1s = reserve(5)
    over = remote(w1, S1, h, 1 - y, b1s + 4, b1s + 4)

    @pl.when(jnp.logical_not(near))
    def _():
        over.start()

    started.append((over, jnp.logical_not(near)))

    def spread_first(shard, half, base):
        for k in range(4):
            i = lax.rem(k + 2 * lax.rem(z, 2), 4)
            hand(
                shard.at[:, :, span(i, 128)],
                W1.at[:, span(z, 32), :],
                ha(2 * half + lax.div(i, 2), x, lax.rem(i, 2)),
                e,
                base + k,
                b1 + z,
                near,
            )

    in_copies = []
    for dz in range(4):
        zt = lax.rem(z + dz, 4)
        for d in range(4):
            if dz == 0 and d == 0:
                continue
            there = lax.rem(2 * x + y + d, 4)
            in_copies.append(
                push(
                    inT.at[:, there],
                    IN.at[2 * z + x, e, pl.ds(2 * y, 2)],
                    ha(zt, lax.div(there, 2), e),
                    lax.rem(there, 2),
                )
            )
    IN[2 * z + x, e, pl.ds(2 * y, 2)] = inT[:, 2 * x + y]

    spread_first(w1, y, b1)
    place = lax.broadcasted_iota(jnp.int32, (256, LANE), 0)
    lane = lax.broadcasted_iota(jnp.int32, (256, LANE), 1)
    spread = jnp.concatenate(
        [
            jnp.concatenate([first[...], second[...]], axis=1).astype(F32)
            for first, second in ((la, lb), (va, vb))
        ],
        axis=0,
    )
    spread = jnp.pad(spread, ((0, 4), (0, 256 - wide_a - wide_b)))
    for b in range(2):
        pick = jnp.where(place == 2 * lane + b, 1.0, 0.0)
        planes = dot_nn(spread.astype(BF), pick.astype(BF))
        for a in range(2):
            lab[2 * a + b : 2 * a + b + 1, :] = planes[a : a + 1, :]
            lab[4 + 2 * a + b : 5 + 2 * a + b, :] = planes[2 + a : 3 + a, :]
    lab_copies = []
    LB[h] = lab[...]
    for d in range(1, 16):
        lab_copies.append(push(lab, LB.at[h], lax.rem(h + d, 16), y))


    @pl.when(near)
    def _():
        over.wait_recv()

    spread_first(S1, 1 - y, b1s)
    for copy in in_copies:
        copy.wait_recv()
    twin_in = push(IN.at[:, e], IN.at[:, e], twin, y)

    for load in loads:
        load.wait()
    w2[...] = f2[...].astype(BF)
    w3[...] = f3[...].astype(BF)
    for k in range(4):
        wu[k] = jnp.concatenate([fu[p, :, k * 64 : k * 64 + 64] for p in range(4)], axis=1).astype(BF)
    for a in range(2):
        for c in range(2):
            half = slice(c * 128, c * 128 + 128)
            buf = flat.at[2 * a + c]
            buf[224:256, :] = jnp.zeros((32, 128), F32)
            buf[0:wide_a, :] = skip_a[a, :, half].astype(F32)
            buf[wide_a : wide_a + wide_b, :] = skip_b[a, :, half].astype(F32)
            for b in range(2):
                p = 2 * a + b
                plane = buf[pl.ds(b, 128, stride=2), :]
                skT[2 * c : 2 * c + 2, :, p * 128 : p * 128 + 128] = plane.T.astype(BF).reshape(2, 64, 128)
    b2 = reserve(2)
    for i in range(2):
        hand(
            w2.at[:, :, i * 256 : i * 256 + 256],
            W2.at[:, span(e, 64), :],
            ha(z, i, x),
            y,
            b2 + i,
            b2 + e,
        )
    SK = m["SK"]
    sk_copies = []
    slot = 2 * x + e
    for d in range(1, 4):
        other = lax.rem(slot + d, 4)
        sk_copies.append(push(skT.at[other], SK.at[slot], 4 * z + other, y))
    SK[slot] = skT[slot]
    bu_copies = []
    for d in range(1, 16):
        ht = lax.rem(h + d, 16)
        bu_copies.append(push(wu.at[lax.rem(ht, 4)], WU.at[h], ht, y))
    WU[h] = wu[slot]
    b3 = reserve(4)
    for i in range(4):
        hand(
            w3,
            W3.at[:, span(lax.div(z, 2), 64), span(y, 256)],
            ha(lax.rem(z + i, 4), x, e),
            lax.rem(z, 2),
            b3 + i,
            b3 + 2 * lax.div(z, 2) + y,
        )

    X = m["X"]

    def patch_edges():
        zero = jnp.zeros((384, 128), BF)
        X[0:384, 128:256] = zero
        X[768:1152, 2048:2176] = zero

    def patches(block, first, last):
        def one(i, carry):
            low = block(i)
            v = low.astype(F32)
            kinds = (from_left(v).astype(BF), low, from_right(v).astype(BF))
            for di in (-1, 0, 1):
                for dj in range(3):
                    tap = (di + 1) * 3 + dj
                    X[tap * 128 : tap * 128 + 128, span(i - di + 1, 128)] = kinds[dj]
            return carry

        lax.fori_loop(first, last, one, 0)

    def patch_cols(at, size):
        return pl.ds(pl.multiple_of(at * size + 128, 128), size)

    def transposed(weight, out, rows):
        for t in range(weight.shape[0]):
            out[:, t * rows : t * rows + rows] = weight[t].T

    for j in range(4):
        landed(W1.at[:, 32 * j : 32 * j + 32, :], b1 + j)
    transposed(W1, m["W1T"], 128)
    twin_in.wait_recv()

    def input_block(i):
        return IN[lax.div(i, 2), lax.rem(i, 2)].reshape(128, 128)

    def middle_block(i):
        return A1[:, :, span(i, 128)].reshape(128, 128)

    patches(input_block, 0, 16)
    patch_edges()
    P1, P1b, R1, A1 = m["P1"], m["P1b"], m["R1"], m["A1"]

    def conv_one(n, carry):
        cols = span(n, 512)
        total = dot_nn(m["W1T"][...], X[:, patch_cols(n, 512)]).reshape(4, 32, 512)
        P1[:, :, cols] = total
        P1b[:, :, cols] = total.astype(BF)
        return carry

    def to_plane(d):
        there = lax.rem(q + d, 4)
        return there, ha(z, lax.rem(there, 2), e), lax.div(there, 2)

    def scatter(source, slots, cols=slice(None)):
        copies = []
        for d in range(1, 4):
            there, h2, y2 = to_plane(d)
            copies.append(push(source.at[there, :, cols], slots.at[d - 1, :, cols], h2, y2))
        return copies

    def gather_four(buf, cols):
        copies = []
        for d in range(1, 4):
            _, h2, y2 = to_plane(d)
            copies.append(push(buf.at[q, :, cols], buf.at[q, :, cols], h2, y2))
        return copies

    halves = (slice(0, 1024), slice(1024, 2048))

    def plane_sends(buf):
        copies = []
        for d in range(1, 4):
            _, h2, y2 = to_plane(d)
            copies.append(push(buf.at[s], buf.at[s], h2, y2))
        return copies, push(buf.at[s], buf.at[s], twin, y)

    def plane_passes(buf, sends):
        copies, own = sends
        last = [own]
        for d in range(1, 4):
            copies[d - 1].wait_recv()
            came = 2 * lax.rem(q + 4 - d, 4) + e
            last.append(push(buf.at[came], buf.at[came], twin, y))
        return last

    def gather_plane(buf):
        return plane_passes(buf, plane_sends(buf))

    def arrive(copies):
        for copy in copies:
            copy.wait_recv()

    one_out = []
    for c in range(2):
        lax.fori_loop(2 * c, 2 * c + 2, conv_one, 0)
        one_out.append(scatter(P1b, R1, halves[c]))

    def act_one(n, carry):
        cols = span(n, 512)
        total = P1[q, :, cols] + R1[0, :, cols].astype(F32)
        total = total + R1[1, :, cols].astype(F32) + R1[2, :, cols].astype(F32)
        P1[q, :, cols] = total
        A1[q, :, cols] = gelu_value(total).astype(BF)
        return carry

    wait_one = []
    for c in range(2):
        arrive(one_out[c])
        lax.fori_loop(2 * c, 2 * c + 2, act_one, 0)
        wait_one.append(gather_four(A1, halves[c]))
    for j in range(2):
        landed(W2.at[:, 64 * j : 64 * j + 64, :], b2 + j)
    transposed(W2, m["W2T"], 128)

    for c in range(2):
        arrive(wait_one[c])
        patches(middle_block, 8 * c, 8 * c + 8)
    patch_edges()
    Z, P2b, T2, S2b, R2 = m["Z"], m["P2b"], m["T2"], m["S2b"], m["R2"]

    def band_two(k):
        zt = lax.rem(z + 1 + k, 4)
        Z[0:256, span(zt, 512)] = dot_nn(m["W2T"][...], X[:, patch_cols(zt, 512)])
        P2b[k] = Z[span(1 - e, 128), span(zt, 512)].astype(BF)
        return push(P2b.at[k], T2.at[k], twin, y)

    def pair_two(k):
        zt = lax.rem(z + 1 + k, 4)
        pairs[k].wait_recv()
        S2b[k] = (Z[span(e, 128), span(zt, 512)] + T2[k].astype(F32)).astype(BF)
        two.append(push(S2b.at[k], R2.at[k], ha(zt, x, e), y))

    pairs, two = [], []
    for k in range(4):
        pairs.append(band_two(k))
        if k >= 1:
            pair_two(k - 1)
    for d in range(1, 16):
        bu_copies[d - 1].wait_recv()
    for t in range(8):
        m["WUT"][:, t * 128 : t * 128 + 128] = WU[2 * t : 2 * t + 2].reshape(128, 256).T
    arrive(two)
    pre2, A2 = m["pre2"], m["A2"]
    pairs[3].wait_recv()
    total = Z[span(e, 128), span(z, 512)] + T2[3].astype(F32) + R2[0].astype(F32)
    total = total + R2[1].astype(F32) + R2[2].astype(F32)
    pre2[...] = total
    A2[s] = gelu_value(total).astype(BF)
    wait_two = gather_plane(A2)
    for copy in sk_copies:
        copy.wait_recv()
    for a in range(2):
        for b in range(2):
            p = 2 * a + b
            for i in range(4):
                J[a, 1 + b, 64:128, 128 + 128 * i : 256 + 128 * i] = SK[i, :, p * 128 : p * 128 + 128]
    arrive(wait_two)

    for p in range(4):
        plane = dot_nn(m["WUT"][p * 64 : p * 64 + 64, :], A2[...].reshape(1024, 512))
        J[p // 2, 1 + p % 2, 0:64, 128:640] = plane.astype(BF)

    def fringe(up, down, send_down, keep_down, send_up, keep_up):
        below = remote(send_down, keep_down, lax.rem(h + 4, 16), y, down, down)
        above = remote(send_up, keep_up, lax.rem(h + 12, 16), y, up, up)

        @pl.when(z < 3)
        def _():
            below.start()

        @pl.when(z > 0)
        def _():
            above.start()

        started.append((below, z < 3))
        started.append((above, z > 0))

        def wait():
            @pl.when(z > 0)
            def _():
                below.wait_recv()

            @pl.when(z < 3)
            def _():
                above.wait_recv()

        return wait

    bj = reserve(2)
    wait_rows = fringe(
        bj,
        bj + 1,
        J.at[1, 1:3, :, 512:640],
        J.at[1, 1:3, :, 0:128],
        J.at[0, 1:3, :, 128:256],
        J.at[0, 1:3, :, 640:768],
    )

    def beside(a, i):
        at = slice(i * 128, i * 128 + 128)
        J[a, 0, :, at] = from_left(J[a, 2, :, at].astype(F32)).astype(BF)
        J[a, 3, :, at] = from_right(J[a, 1, :, at].astype(F32)).astype(BF)

    def joined_patches(outer):
        for a in range(2):
            for da in range(3):
                up, di = (a + da - 1) % 2, (a + da - 1) // 2
                first, last = 0, 4
                if di != 0:
                    edge = 0 if di < 0 else 3
                    first, last = (edge, edge + 1) if outer else (1, 4) if di < 0 else (0, 3)
                elif outer:
                    continue
                for b in range(2):
                    for db in range(3):
                        tap = da * 3 + db
                        at = 128 + (2 * a + b) * 512
                        X[tap * 128 : tap * 128 + 128, at + first * 128 : at + last * 128] = J[
                            up, b + db, :, (1 + di + first) * 128 : (1 + di + last) * 128
                        ]

    for a in range(2):
        for i in range(1, 5):
            beside(a, i)
    joined_patches(False)
    wait_rows()
    beside(1, 0)
    beside(0, 5)
    joined_patches(True)

    for j in range(4):
        t, half = j // 2, j % 2
        landed(W3.at[:, 64 * t : 64 * t + 64, 256 * half : 256 * half + 256], b3 + j)
    transposed(W3, m["W3T"], 128)
    P3b, T3, S3b, R3 = m["P3b"], m["T3"], m["S3b"], m["R3"]

    def plane_three(p):
        def step(n, carry):
            Z[0:512, span(n, 256)] = dot_nn(m["W3T"][...], X[:, patch_cols(n, 256)])
            return carry

        lax.fori_loop(2 * p, 2 * p + 2, step, 0)
        cols = slice(p * 512, p * 512 + 512)
        for k in range(4):
            P3b[p, k] = Z[span(2 * k + 1 - e, 64), cols].astype(BF)
        return push(P3b.at[p], T3.at[p], twin, y)

    def pair_three(p):
        pairs[p].wait_recv()
        cols = slice(p * 512, p * 512 + 512)
        for k in range(4):
            total = Z[span(2 * k + e, 64), cols] + T3[p, k].astype(F32)
            Z[span(2 * k + e, 64), cols] = total
            S3b[p, k] = total.astype(BF)
        three.append(scatter(S3b.at[p], R3.at[p]))

    pairs, three = [], []
    for p in range(4):
        pairs.append(plane_three(p))
        if p >= 1:
            pair_three(p - 1)
    pair_three(3)
    pre3, act3, LG = m["pre3"], m["act3"], m["LG"]
    wide = (64, LANE)
    turned = jnp.concatenate([fh[...], jnp.zeros((6, fh.shape[1]), F32)], axis=0).T
    m["HT"][...] = turned.astype(BF).astype(F32)
    head = m["HT"][span(slot, 64), :]
    h0 = jnp.broadcast_to(head[:, 0:1], wide)
    h1 = jnp.broadcast_to(head[:, 1:2], wide)
    for b in range(16):
        if b % 4 == 0:
            arrive(three[b // 4])
        cols = slice(b * 128, b * 128 + 128)
        part = slice(b % 4 * 128, b % 4 * 128 + 128)
        total = Z[span(s, 64), cols] + R3[b // 4, 0, :, part].astype(F32)
        total = total + R3[b // 4, 1, :, part].astype(F32) + R3[b // 4, 2, :, part].astype(F32)
        pre3[:, cols] = total
        act = gelu_value(total).astype(BF)
        act3[:, cols] = act
        act = act.astype(F32)
        LG[s, b : b + 1, :] = jnp.sum(act * h0, axis=0, keepdims=True)
        LG[s, 16 + b : 17 + b, :] = jnp.sum(act * h1, axis=0, keepdims=True)
    wait_logits = []
    for d in range(1, 8):
        there = lax.rem(s + d, 8)
        half = lax.div(there, 4)
        wait_logits.append(push(LG.at[s], LG.at[s], 4 * z + there - 4 * half, half))
    for copy in lab_copies:
        copy.wait_recv()
    LBL = m["LBL"]
    for p in range(4):
        for i in range(4):
            LBL[p * 4 + i : p * 4 + i + 1, :] = LB[4 * z + i, p : p + 1, :]
            LBL[16 + p * 4 + i : 17 + p * 4 + i, :] = LB[4 * z + i, 4 + p : 5 + p, :]
    every = jnp.sum(LB[...], axis=0)
    labelled = jnp.sum(jnp.sum(every[4:8, :], axis=0, keepdims=True), axis=1, keepdims=True)
    arrive(wait_logits)

    logits = LG[0]
    for k in range(1, 8):
        logits = logits + LG[k]
    zero, one = logits[0:16, :], logits[16:32, :]
    picks, usable = LBL[0:16, :] > 0.5, LBL[16:32, :]
    top = jnp.maximum(zero, one)
    lse = top + jnp.log(jnp.exp(zero - top) + jnp.exp(one - top))
    logp = jnp.where(picks, one, zero) - lse
    rest = jnp.exp(jnp.where(picks, zero, one) - lse)
    chance = jnp.exp(logp)
    gap = 1.0 - chance
    terms = usable * (-(gap * gap) * logp)
    slope = (2.0 * gap * chance * logp - gap * gap) * usable / labelled
    own, other = slope * gap, -slope * rest
    DL = m["DL"]
    DL[0:16, :] = jnp.where(picks, other, own).astype(BF).astype(F32)
    DL[16:32, :] = jnp.where(picks, own, other).astype(BF).astype(F32)
    loss = jnp.sum(jnp.sum(terms, axis=0, keepdims=True), axis=1, keepdims=True)
    G3, HD = m["G3"], m["HD"]
    planes = []
    sum0 = jnp.zeros(wide, F32)
    sum1 = jnp.zeros(wide, F32)
    for b in range(16):
        cols = slice(b * 128, b * 128 + 128)
        d0 = jnp.broadcast_to(DL[b : b + 1, :], wide)
        d1 = jnp.broadcast_to(DL[16 + b : 17 + b, :], wide)
        part = slice(b % 4 * 128, b % 4 * 128 + 128)
        G3[b // 4, s, :, part] = ((h0 * d0 + h1 * d1) * gelu_slope(pre3[:, cols])).astype(BF)
        act = act3[:, cols].astype(F32)
        sum0 = sum0 + act * d0
        sum1 = sum1 + act * d1
        if b % 4 == 3:
            planes.append(plane_sends(G3.at[b // 4]))
    side = lax.broadcasted_iota(jnp.int32, wide, 1)
    sum0 = jnp.sum(sum0, axis=1, keepdims=True)
    sum1 = jnp.sum(sum1, axis=1, keepdims=True)
    tile = jnp.where(side == 0, sum0, jnp.where(side == 1, sum1, 0.0))
    HD[h, 0:8, 0:64] = tile.T[0:8, :]
    HD[h, 2:3, 0:64] = jnp.broadcast_to(loss, (1, 64))
    hd_copies = []
    for d in range(1, 16):
        hd_copies.append(push(HD.at[h], HD.at[h], lax.rem(h + d, 16), y))

    HS, DB, DR = m["HS"], m["DB"], m["DR"]

    def back_three(p):
        grads = G3[p].reshape(512, 512)
        Z[0:576, p * 512 : p * 512 + 512] = dot_nn(W3[:, 0:64, :].reshape(576, 512), grads)

    GW3, GWU, GW2, GW1 = m["GW3"], m["GWU"], m["GW2"], m["GW1"]
    RG3, RGU, RG2, RG1 = m["RG3"], m["RGU"], m["RG2"], m["RG1"]

    def grad_three(p):
        def step(t, carry):
            part = dot_nt(X[span(t, 128), 128 + p * 512 : 640 + p * 512], G3[p].reshape(512, 512))
            rows = pl.ds(pl.multiple_of(576 + 128 * lax.div(t, 4), 64), 128)
            cols = span(lax.rem(t, 4), 512)
            if p > 0:
                part = part + Z[rows, cols]
            if p < 3:
                Z[rows, cols] = part
            else:
                GW3[t] = part.astype(BF)
            return carry

        lax.fori_loop(0, 9, step, 0)

    passes = plane_passes(G3.at[0], planes[0])
    for p in range(4):
        arrive(passes)
        back_three(p)
        if p < 3:
            passes = plane_passes(G3.at[p + 1], planes[p + 1])
            grad_three(p)
    def merge_home(first, last):
        for k in range(first, last):
            half, own = lax.rem(y + k // 2, 2), k < 2
            t = lax.rem(lax.div(z, 2) + 1 + k, 2)
            hand(
                GW3.at[:, span(t, 64), span(y, 256)] if own else m["Y3"].at[t],
                RG3.at[z],
                ha(2 * t + half, x, e),
                y,
                bg3 + k,
                bg3 + z,
            )

    ways = (((0, 0, 0), (1, -1, 0), (1, 1, 1)), ((0, -1, -1), (0, 1, 0), (1, 0, 0)))

    def raised_block(a, b, i):
        straight, bent = [], []
        for ao, da, di in ways[a]:
            io = i - di
            if io < 0 or io > 3 or (i < 0 or i > 3) and di == 0:
                continue
            for bo, db, dj in ways[b]:
                tap = (da + 1) * 3 + db + 1
                at = ((2 * ao + bo) * 4 + io) * 128
                (straight if dj == 0 else bent).append(Z[tap * 64 : tap * 64 + 64, at : at + 128])
        turned = sum(bent[1:], bent[0])
        turned = from_left(turned) if b == 0 else from_right(turned)
        return sum(straight, turned)

    for b in range(2):
        HS[0, b] = raised_block(0, b, 4)
        HS[1, b] = raised_block(1, b, -1)
    bh = reserve(2)
    wait_fringe = fringe(bh, bh + 1, HS.at[0], HR.at[0], HS.at[1], HR.at[1])
    for a in range(2):
        for b in range(2):
            p = 2 * a + b
            for i in range(4):
                block = raised_block(a, b, i)
                if i == 3 * a:
                    DB[p] = block
                else:
                    DR[p * 64 : p * 64 + 64, i * 128 : i * 128 + 128] = block.astype(BF)
    grad_three(3)
    bg3 = reserve(4)
    merge_home(0, 2)
    wait_fringe()
    for a in range(2):
        for b in range(2):
            p = 2 * a + b
            DR[p * 64 : p * 64 + 64, a * 384 : a * 384 + 128] = (DB[p] + HR[a, b]).astype(BF)

    P7b, T7, S7b, R7 = m["P7b"], m["T7"], m["S7b"], m["R7"]

    def back_up(k, carry):
        Z[span(k, 128), 0:512] = dot_nn(WU[pl.ds(2 * k, 2)].reshape(128, 256), DR[...])
        return carry

    lax.fori_loop(0, 8, back_up, 0)
    for k in range(4):
        P7b[k] = Z[span(2 * k + 1 - e, 128), 0:512].astype(BF)
    wait_pair = push(P7b, T7, twin, y)

    def pair_seven():
        for k in range(4):
            total = Z[span(2 * k + e, 128), 0:512] + T7[k].astype(F32)
            Z[span(2 * k + e, 128), 0:512] = total
            S7b[k] = total.astype(BF)

    wait_pair.wait_recv()
    pair_seven()
    wait_seven = scatter(S7b, R7)

    def grad_up(k, carry):
        GWU[pl.ds(2 * k, 2)] = dot_nt(A2[k], DR[...]).astype(BF).reshape(2, 64, 256)
        return carry

    Y3 = m["Y3"]
    other = 1 - y
    across = []
    for t in range(2):
        across.append(
            push(
                GW3.at[:, 64 * t : 64 * t + 64, span(other, 256)],
                Y3.at[t],
                h,
                other,
            )
        )

    lax.fori_loop(0, 8, grad_up, 0)
    patches(middle_block, 0, 16)
    patch_edges()
    gu_copies = []
    for d in range(1, 16):
        ht = lax.rem(h + d, 16)
        gu_copies.append(push(GWU.at[ht], RGU.at[h], ht, y))
    RGU[h] = GWU[h]
    arrive(wait_seven)
    G2 = m["G2"]
    total = Z[span(s, 128), 0:512] + R7[0].astype(F32)
    total = total + R7[1].astype(F32) + R7[2].astype(F32)
    G2[e, :, span(z, 512)] = (total * gelu_slope(pre2[...])).astype(BF)
    mine = G2.at[e, :, span(z, 512)]
    g2_copies = []
    for d in range(1, 4):
        zt = lax.rem(z + d, 4)
        g2_copies.append(push(mine, mine, ha(zt, x, e), y))
    own_pair = push(mine, mine, twin, y)

    def back_two(zs):
        for k in range(2):
            cols = pl.ds(pl.multiple_of(zs * 512 + k * 256, 256), 256)
            Z[:, cols] = dot_nn(W2[...].reshape(1152, 256), G2[:, :, cols].reshape(256, 256))

    def relay(d):
        g2_copies[d - 1].wait_recv()
        zs = lax.rem(z + 4 - d, 4)
        came = G2.at[e, :, span(zs, 512)]
        return zs, push(came, came, twin, y)

    arrive(across)
    merge_home(2, 4)
    zs, copy = relay(1)
    own_pair.wait_recv()
    back_two(z)
    for d in range(2, 4):
        after = relay(d)
        copy.wait_recv()
        back_two(zs)
        zs, copy = after
    copy.wait_recv()
    back_two(zs)
    P8b, R8, G1 = m["P8b"], m["R8"], m["G1"]
    P8 = m["P8"]

    def fold(i, carry):
        sums = []
        for dj in range(3):
            part = None
            for di in range(3):
                row = i - (di - 1)
                inside = jnp.logical_and(row >= 0, row <= 15)
                row = jnp.clip(row, 0, 15)
                tap = di * 3 + dj
                block = jnp.where(inside, Z[tap * 128 : tap * 128 + 128, span(row, 128)], 0.0)
                part = block if part is None else part + block
            sums.append(part)
        total = sums[1] + from_right(sums[0]) + from_left(sums[2])
        P8[:, span(i, 128)] = total
        P8b[:, :, span(i, 128)] = total.reshape(4, 32, 128).astype(BF)
        return carry

    wait_eight = []
    for c in range(2):
        lax.fori_loop(8 * c, 8 * c + 8, fold, 0)
        wait_eight.append(scatter(P8b, R8, halves[c]))

    def grad_two(t, carry):
        GW2[t] = dot_nt(X[span(t, 128), 128:2176], G2[...].reshape(256, 2048)).astype(BF)
        return carry

    lax.fori_loop(0, 9, grad_two, 0)

    def act_back(n, carry):
        cols = span(n, 512)
        total = P8[span(q, 32), cols] + R8[0, :, cols].astype(F32)
        total = total + R8[1, :, cols].astype(F32) + R8[2, :, cols].astype(F32)
        G1[q, :, cols] = (total * gelu_slope(P1[q, :, cols])).astype(BF)
        return carry

    wait_g1 = []
    for c in range(2):
        arrive(wait_eight[c])
        lax.fori_loop(2 * c, 2 * c + 2, act_back, 0)
        wait_g1 += gather_four(G1, halves[c])
    bg2 = reserve(2)
    for j in range(2):
        hand(
            GW2.at[:, 64 * j : 64 * j + 64, :],
            RG2.at[:, :, span(x, 256)],
            ha(z, e, j),
            y,
            bg2 + j,
            bg2 + x,
        )
    patches(input_block, 0, 16)
    patch_edges()
    arrive(wait_g1)

    def grad_one(t, carry):
        GW1[t] = dot_nt(X[span(t, 128), 128:2176], G1[...].reshape(128, 2048)).astype(BF)
        return carry

    lax.fori_loop(0, 9, grad_one, 0)
    bg1 = reserve(4)
    r_low = 2 * lax.rem(z, 2) + e
    for k in range(4):
        j = lax.rem(z + 1 + k, 4)
        hand(
            GW1.at[:, span(j, 32), :],
            RG1.at[:, :, span(r_low, 128)],
            ha(j, x, y),
            lax.div(z, 2),
            bg1 + k,
            bg1 + r_low,
        )

    for copy in hd_copies:
        copy.wait_recv()
    for j in range(4):
        hdo[j] = HD[j] + HD[4 + j] + HD[8 + j] + HD[12 + j]
    hdo[4] = jnp.broadcast_to(labelled, (8, 128))
    for k in range(4):
        landed(RG3.at[k], bg3 + k)
    for t in range(9):
        g3o[t] = (RG3[0, t].astype(F32) + RG3[1, t].astype(F32)) + (
            RG3[2, t].astype(F32) + RG3[3, t].astype(F32)
        )
    for copy in gu_copies:
        copy.wait_recv()
    sums = []
    for k in range(4):
        sums.append(
            (RGU[k].astype(F32) + RGU[4 + k].astype(F32))
            + (RGU[8 + k].astype(F32) + RGU[12 + k].astype(F32))
        )
    for p in range(4):
        guo[p] = jnp.concatenate([part[:, p * 64 : p * 64 + 64] for part in sums], axis=1)
    for k in range(2):
        landed(RG2.at[:, :, 256 * k : 256 * k + 256], bg2 + k)
    g2o[...] = RG2[...]
    for k in range(4):
        landed(RG1.at[:, :, 128 * k : 128 * k + 128], bg1 + k)
    g1o[...] = RG1[...]
    for copy, when in started:
        if when is None:
            copy.wait_send()
        else:
            pl.when(when)(copy.wait_send)


def resident_body(
    input_a,
    input_b,
    skip_a,
    skip_b,
    labels_a,
    labels_b,
    valid_a,
    valid_b,
    w_enter,
    moment_enter,
    square_enter,
    w_middle,
    moment_middle,
    square_middle,
    w_upward,
    moment_upward,
    square_upward,
    w_merge,
    moment_merge,
    square_merge,
    w_head,
    moment_head,
    square_head,
):
    vmem = pl.BlockSpec(memory_space=pltpu.VMEM)
    anywhere = pl.BlockSpec(memory_space=pl.ANY)
    g1, g2, gu, g3, hd = pl.pallas_call(
        lambda *refs: fused((input_a.shape[2], input_b.shape[2]), *refs),
        out_shape=(
            jax.ShapeDtypeStruct((9, 32, 512), BF),
            jax.ShapeDtypeStruct((9, 64, 512), BF),
            jax.ShapeDtypeStruct((4, 64, 256), F32),
            jax.ShapeDtypeStruct((9, 64, 256), F32),
            jax.ShapeDtypeStruct((5, 8, 128), F32),
        ),
        in_specs=[vmem] * 9 + [anywhere] * 3 + [vmem],
        out_specs=[vmem] * 5,
        scratch_shapes=[pltpu.VMEM(shape, kind) for _, shape, kind in SCRATCH]
        + [pltpu.SemaphoreType.DMA((COPIES,)), pltpu.SemaphoreType.DMA((COPIES,)), pltpu.SemaphoreType.DMA((3,))],
        compiler_params=pltpu.CompilerParams(
            collective_id=0, has_side_effects=True, vmem_limit_bytes=61 * 1024 * 1024
        ),
    )(
        input_a[0, 0],
        input_b[0, 0],
        skip_a[0],
        skip_b[0],
        labels_a[0],
        labels_b[0],
        valid_a[0],
        valid_b[0],
        w_enter.reshape(9, 32, 512),
        w_middle.reshape(9, 64, 512),
        w_upward.reshape(4, 64, 256),
        w_merge.reshape(9, 64, 256),
        w_head.T,
    )
    states = (
        (w_enter, moment_enter, square_enter),
        (w_middle, moment_middle, square_middle),
        (w_upward, moment_upward, square_upward),
        (w_merge, moment_merge, square_merge),
    )
    dims = tuple(g.shape for g in (g1, g2, gu, g3))
    flat = [part.reshape(dim) for dim, state in zip(dims, states) for part in state]
    rows = w_head.T.shape
    new = pl.pallas_call(
        updates,
        out_shape=tuple(
            jax.ShapeDtypeStruct(dim, kind) for dim in (*dims, rows) for kind in (F32, F32, F32, BF)
        )
        + (jax.ShapeDtypeStruct((1, 1), F32),) * 2,
        in_specs=[anywhere] * 16 + [vmem] * 4,
        out_specs=[anywhere] * 16 + [vmem] * 6,
        scratch_shapes=[
            pltpu.VMEM(dim, kind)
            for dim, g in zip(dims, (g1, g2, gu, g3))
            for kind in (g.dtype, F32, F32, F32, F32, F32, F32, BF)
        ]
        + [pltpu.SemaphoreType.DMA((len(PIECES), 8))],
        compiler_params=pltpu.CompilerParams(vmem_limit_bytes=62 * 1024 * 1024),
    )(g1, g2, gu, g3, *flat, hd, w_head.T, moment_head.T, square_head.T)
    shapes = (w_enter.shape, w_middle.shape, w_upward.shape, w_merge.shape)
    return (
        *[new[k].reshape(shapes[k // 4]) for k in range(16)],
        *[part.T for part in new[16:20]],
        new[20].reshape(()),
        new[21].reshape(()),
    )


PIECES = ((3, 0, 5), (3, 5, 9), (2, 0, 4), (1, 0, 3), (1, 3, 6), (1, 6, 9), (0, 0, 5), (0, 5, 9))


def adamw_step(master, moment, square, gradient):
    moment_new = BETA_ONE * moment + (1.0 - BETA_ONE) * gradient
    square_new = BETA_TWO * square + (1.0 - BETA_TWO) * gradient * gradient
    fixed_moment = moment_new * (RATE / (1.0 - BETA_ONE**STEP))
    fixed_square = square_new * (1.0 / (1.0 - BETA_TWO**STEP))
    master_new = (1.0 - RATE * DECAY) * master - fixed_moment / (jnp.sqrt(fixed_square) + EPSILON)
    return (master_new, moment_new, square_new, master_new.astype(BF))


def updates(*refs):
    grads, states = refs[0:4], refs[4:16]
    hd, head, moment, square = refs[16:20]
    outs, tiny, loss, labelled = refs[20:36], refs[36:40], refs[40], refs[41]
    held, sems = refs[42:74], refs[74]

    def copies(piece):
        k, first, last = PIECES[piece]
        at = slice(first, last)
        inward = [
            pltpu.make_async_copy(source.at[at], held[8 * k + j].at[at], sems.at[piece, j])
            for j, source in enumerate((grads[k], *states[3 * k : 3 * k + 3]))
        ]
        outward = [
            pltpu.make_async_copy(held[8 * k + 4 + j].at[at], outs[4 * k + j].at[at], sems.at[piece, 4 + j])
            for j in range(4)
        ]
        return inward, outward

    every = [copies(piece) for piece in range(len(PIECES))]
    for inward, _ in every:
        for copy in inward:
            copy.start()
    loss[...] = hd[0, 2:3, 0:1]
    labelled[...] = hd[4, 0:1, 0:1]
    gradient = jnp.concatenate([hd[j, 0:2, 0:64] for j in range(4)], axis=1)
    for ref, value in zip(tiny, adamw_step(head[...], moment[...], square[...], gradient)):
        ref[...] = value
    for (k, first, last), (inward, outward) in zip(PIECES, every):
        for copy in inward:
            copy.wait()
        own = held[8 * k : 8 * k + 8]

        def step(i, carry, own=own):
            made = adamw_step(own[1][i], own[2][i], own[3][i], own[0][i].astype(F32))
            for ref, value in zip(own[4:], made):
                ref[i] = value
            return carry

        lax.fori_loop(first, last, step, 0)
        for copy in outward:
            copy.start()
    for _, outward in every:
        for copy in outward:
            copy.wait()


def chosen(*args):
    input_a, input_b, skip_a = args[0], args[1], args[2]
    w_enter, w_middle, w_upward, w_merge = args[8], args[11], args[14], args[17]
    fits = (
        lax.axis_size("ha") == 16
        and lax.axis_size("col") == 2
        and input_a.shape[:2] == (1, 1)
        and input_b.shape[:2] == (1, 1)
        and input_a.shape[3] == 256
        and skip_a.shape[3] == 256
        and input_a.shape[2] + input_b.shape[2] <= LANE
        and w_enter.shape == (3, 3, 32, 512)
        and w_middle.shape == (3, 3, 64, 512)
        and w_upward.shape == (2, 2, 64, 256)
        and w_merge.shape == (3, 3, 64, 256)
    )
    return resident_body(*args) if fits else body(*args)


def solution(mesh):
    placed = (
        P(None, "ha", None, "col"),
        P(None, "ha", None, "col"),
        P(None, "ha", None, "col"),
        P(None, "ha", None, "col"),
        P(None, "ha", None),
        P(None, "ha", None),
        P(None, "ha", None),
        P(None, "ha", None),
        P(None, None, "ha", "col"),
        P(None, None, "ha", "col"),
        P(None, None, "ha", "col"),
        P(None, None, "ha", "col"),
        P(None, None, "ha", "col"),
        P(None, None, "ha", "col"),
        P(None, None, "ha", "col"),
        P(None, None, "ha", "col"),
        P(None, None, "ha", "col"),
        P(None, None, "ha", "col"),
        P(None, None, "ha", "col"),
        P(None, None, "ha", "col"),
        P("col", None),
        P("col", None),
        P("col", None),
    )
    return jax.shard_map(
        chosen,
        mesh=mesh,
        in_specs=placed,
        out_specs=(
            P(None, None, "ha", "col"),
            P(None, None, "ha", "col"),
            P(None, None, "ha", "col"),
            P(None, None, "ha", "col"),
            P(None, None, "ha", "col"),
            P(None, None, "ha", "col"),
            P(None, None, "ha", "col"),
            P(None, None, "ha", "col"),
            P(None, None, "ha", "col"),
            P(None, None, "ha", "col"),
            P(None, None, "ha", "col"),
            P(None, None, "ha", "col"),
            P(None, None, "ha", "col"),
            P(None, None, "ha", "col"),
            P(None, None, "ha", "col"),
            P(None, None, "ha", "col"),
            P("col", None),
            P("col", None),
            P("col", None),
            P("col", None),
            P(),
            P(),
        ),
        check_vma=False,
    )
```

```python
import jax
import jax.numpy as jnp
from jax import lax
from jax.experimental import pallas as pl
from jax.experimental.pallas import tpu as pltpu
from jax.sharding import PartitionSpec as P

STEP = 10


NUMBERS = ("NHWC", "HWIO", "NHWC")
BETA_ONE = 0.9
BETA_TWO = 0.95
RATE = 0.08
DECAY = 0.1
EPSILON = 1e-08


def extended(cells, sides, width):
    for axis, dim in sides:
        count = lax.axis_size(axis)
        ends = count - 1
        head = lax.slice_in_dim(cells, 0, width, axis=dim)
        tail = lax.slice_in_dim(cells, cells.shape[dim] - width, cells.shape[dim], axis=dim)
        cells = jnp.concatenate(
            [
                lax.ppermute(tail, axis, [(i, (i + 1) % count) for i in range(ends)]),
                cells,
                lax.ppermute(head, axis, [((i + 1) % count, i) for i in range(ends)]),
            ],
            axis=dim,
        )
    return cells


def shortened(value):

    def short(part):
        return part.astype(jnp.bfloat16) if part.dtype == jnp.float32 else part

    return jax.tree.map(short, value)


def convolve_rows(padded, weight):
    return lax.conv_general_dilated(
        padded,
        weight,
        (1, 1),
        ((0, 0), (1, 1)),
        dimension_numbers=NUMBERS,
        preferred_element_type=jnp.float32,
    )


def flipped(weight):
    return jnp.transpose(weight[::-1, ::-1], (0, 1, 3, 2))


def upsample(values, weight):
    product = jnp.einsum("nhwc,abcd->nhawbd", values, weight, preferred_element_type=jnp.float32)
    return product.reshape(
        product.shape[0], 2 * product.shape[1], 2 * product.shape[3], product.shape[5]
    )


def split_pixels(upstream):
    return upstream.reshape(
        upstream.shape[0], upstream.shape[1] // 2, 2, upstream.shape[2] // 2, 2, upstream.shape[3]
    )


def upsample_back(upstream, weight):
    return jnp.einsum(
        "nhawbd,abcd->nhwc", split_pixels(upstream), weight, preferred_element_type=jnp.float32
    )


def upsample_weight(values, upstream):
    return jnp.einsum(
        "nhwc,nhawbd->abcd", values, split_pixels(upstream), preferred_element_type=jnp.float32
    )


def tap_grads(padded, upstream):
    wide = jnp.pad(padded, ((0, 0), (0, 0), (1, 1), (0, 0)))
    height, across = (upstream.shape[1], upstream.shape[2])
    stacked = []
    for row_tap in range(3):
        tapline = []
        for col_tap in range(3):
            window = wide[:, row_tap : row_tap + height, col_tap : col_tap + across, :]
            tapline.append(
                jnp.einsum("nhwc,nhwd->cd", window, upstream, preferred_element_type=jnp.float32)
            )
        stacked.append(jnp.stack(tapline))
    return jnp.stack(stacked)


def alternate(weight, groups):
    dims = weight.shape
    shaped = weight.reshape(dims[0], dims[1], 2, groups, dims[2] // (2 * groups), dims[3])
    return shaped.transpose(0, 1, 3, 2, 4, 5).reshape(dims)


def deinterleave(weight, groups):
    dims = weight.shape
    shaped = weight.reshape(dims[0], dims[1], groups, 2, dims[2] // (2 * groups), dims[3])
    return shaped.transpose(0, 1, 3, 2, 4, 5).reshape(dims)


def gelu_back(pre_act, upstream):
    return jax.vjp(jax.nn.gelu, pre_act)[1](upstream)[0]


def focal(logits, labels, usable):
    logprob = jax.nn.log_softmax(logits, axis=-1)
    picked = jnp.where(labels == 1, logprob[..., 1], logprob[..., 0])
    chance = jnp.exp(picked)
    return jnp.sum(usable.astype(jnp.float32) * (-((1.0 - chance) ** 2) * picked))


def loss_terms(logits, labels, usable, labelled):
    running, pull = jax.vjp(lambda values: focal(values, labels, usable), logits)
    return (running, pull(1.0 / labelled)[0])


def gather_channels(values):
    return lax.all_gather(values, "col", axis=3, tiled=True)


def spread_back(partial_value):
    return lax.psum_scatter(partial_value, "col", scatter_dimension=3, tiled=True)


def conv_forward(local, weight):
    padded = extended(local, (("ha", 1),), 1)
    whole = gather_channels(padded)
    return (convolve_rows(whole, weight), whole)


def up_forward(local, weight):
    whole = gather_channels(local)
    return (upsample(whole, weight), whole)


def conv_weight_grad(kept, upstream):
    return tap_grads(kept, upstream)


def up_weight_grad(kept, upstream):
    return upsample_weight(kept, upstream)


def backward_weights(merge_up, upward, middle):
    return (flipped(merge_up), upward, flipped(middle))


def conv_input_grad(back_weight, upstream):
    padded = extended(shortened(upstream), (("ha", 1),), 1).astype(upstream.dtype)
    return spread_back(convolve_rows(padded, back_weight))


def up_input_grad(back_weight, upstream):
    return spread_back(upsample_back(upstream, back_weight))


def forward_pass(picture, skipped, copies):
    enter, middle, upward, merge_mixed, back_merge, back_upward, back_middle, head_copy = copies
    pre_one, kept_one = conv_forward(picture, enter)
    act_one = jax.nn.gelu(pre_one).astype(jnp.bfloat16)
    pre_two, kept_two = conv_forward(act_one, middle)
    act_two = jax.nn.gelu(pre_two).astype(jnp.bfloat16)
    raised, kept_up = up_forward(act_two, upward)
    joined = jnp.concatenate([raised.astype(jnp.bfloat16), skipped], axis=3)
    pre_three, kept_three = conv_forward(joined, merge_mixed)
    act_three = jax.nn.gelu(pre_three).astype(jnp.bfloat16)
    partial_value = jnp.einsum(
        "nhwc,ck->nhwk", act_three, head_copy, preferred_element_type=jnp.float32
    )
    return (
        partial_value,
        (pre_one, kept_one, pre_two, kept_two, kept_up, pre_three, kept_three, act_three),
    )


def backward_pass(saved, dlogits, copies):
    enter, middle, upward, merge_mixed, back_merge, back_upward, back_middle, head_copy = copies
    pre_one, kept_one, pre_two, kept_two, kept_up, pre_three, kept_three, act_three = saved
    back_three = jnp.einsum("nhwk,ck->nhwc", dlogits, head_copy, preferred_element_type=jnp.float32)
    grad_head = jnp.einsum("nhwc,nhwk->ck", act_three, dlogits, preferred_element_type=jnp.float32)
    grad_three = gelu_back(pre_three, back_three).astype(jnp.bfloat16)
    grad_merge = conv_weight_grad(kept_three, grad_three)
    d_raised = conv_input_grad(back_merge, grad_three).astype(jnp.bfloat16)
    grad_upward = up_weight_grad(kept_up, d_raised)
    back_two = up_input_grad(back_upward, d_raised)
    grad_two = gelu_back(pre_two, back_two).astype(jnp.bfloat16)
    grad_middle = conv_weight_grad(kept_two, grad_two)
    back_one = conv_input_grad(back_middle, grad_two)
    grad_one = gelu_back(pre_one, back_one).astype(jnp.bfloat16)
    grad_enter = conv_weight_grad(kept_one, grad_one)
    return (grad_enter, grad_middle, grad_upward, grad_merge, grad_head)


def adamw(master, moment, square, gradient):
    moment_new = BETA_ONE * moment + (1.0 - BETA_ONE) * gradient
    square_new = BETA_TWO * square + (1.0 - BETA_TWO) * gradient * gradient
    fixed_moment = moment_new / (1.0 - BETA_ONE**STEP)
    fixed_square = square_new / (1.0 - BETA_TWO**STEP)
    master_new = master - RATE * (
        fixed_moment / (jnp.sqrt(fixed_square) + EPSILON) + DECAY * master
    )
    return (master_new, moment_new, square_new, master_new.astype(jnp.bfloat16))


def own_rows(summed, local):
    return lax.dynamic_slice_in_dim(
        summed, lax.axis_index("ha") * local.shape[2], local.shape[2], 2
    )


def body(
    input_a,
    input_b,
    skip_a,
    skip_b,
    labels_a,
    labels_b,
    valid_a,
    valid_b,
    w_enter,
    moment_enter,
    square_enter,
    w_middle,
    moment_middle,
    square_middle,
    w_upward,
    moment_upward,
    square_upward,
    w_merge,
    moment_merge,
    square_merge,
    w_head,
    moment_head,
    square_head,
):
    groups = lax.axis_size("col")
    enter, middle, upward, merge = (
        lax.all_gather(w_enter.astype(jnp.bfloat16), "ha", axis=2, tiled=True),
        lax.all_gather(w_middle.astype(jnp.bfloat16), "ha", axis=2, tiled=True),
        lax.all_gather(w_upward.astype(jnp.bfloat16), "ha", axis=2, tiled=True),
        lax.all_gather(w_merge.astype(jnp.bfloat16), "ha", axis=2, tiled=True),
    )
    head_low = w_head.astype(jnp.bfloat16)
    merge_up = merge[:, :, : merge.shape[2] // 2]
    back_merge, back_upward, back_middle = backward_weights(merge_up, upward, middle)
    copies = (
        enter,
        middle,
        upward,
        alternate(merge, groups),
        back_merge,
        back_upward,
        back_middle,
        head_low,
    )
    labelled = lax.psum(
        jnp.sum(valid_a.astype(jnp.float32)) + jnp.sum(valid_b.astype(jnp.float32)), "ha"
    )
    partial_a, saved_a = forward_pass(input_a, skip_a, copies)
    partial_b, saved_b = forward_pass(input_b, skip_b, copies)
    logits_a, logits_b = lax.psum((partial_a, partial_b), "col")
    loss_a, dlogits_a = loss_terms(logits_a, labels_a, valid_a, labelled)
    loss_b, dlogits_b = loss_terms(logits_b, labels_b, valid_b, labelled)
    grads_a = backward_pass(saved_a, dlogits_a.astype(jnp.bfloat16), copies)
    grads_b = backward_pass(saved_b, dlogits_b.astype(jnp.bfloat16), copies)
    local_enter = grads_a[0] + grads_b[0]
    local_middle = grads_a[1] + grads_b[1]
    local_upward = grads_a[2] + grads_b[2]
    local_merge = deinterleave(grads_a[3] + grads_b[3], groups)
    local_head = grads_a[4] + grads_b[4]
    local_loss = loss_a + loss_b
    full_enter, full_middle, full_upward, full_merge, head_total, loss_total = (
        lax.psum(local_enter.astype(jnp.bfloat16), "ha").astype(jnp.float32),
        lax.psum(local_middle.astype(jnp.bfloat16), "ha").astype(jnp.float32),
        lax.psum(local_upward.astype(jnp.bfloat16), "ha").astype(jnp.float32),
        lax.psum(local_merge.astype(jnp.bfloat16), "ha").astype(jnp.float32),
        lax.psum(local_head.astype(jnp.bfloat16), "ha").astype(jnp.float32),
        lax.psum(local_loss.astype(jnp.bfloat16), "ha").astype(jnp.float32),
    )
    grad_enter = own_rows(full_enter, w_enter)
    grad_middle = own_rows(full_middle, w_middle)
    grad_upward = own_rows(full_upward, w_upward)
    grad_merge = own_rows(full_merge, w_merge)
    enter_out = adamw(w_enter, moment_enter, square_enter, grad_enter)
    middle_out = adamw(w_middle, moment_middle, square_middle, grad_middle)
    upward_out = adamw(w_upward, moment_upward, square_upward, grad_upward)
    merge_out = adamw(w_merge, moment_merge, square_merge, grad_merge)
    head_out = adamw(w_head, moment_head, square_head, head_total)
    return (
        enter_out[0],
        enter_out[1],
        enter_out[2],
        enter_out[3],
        middle_out[0],
        middle_out[1],
        middle_out[2],
        middle_out[3],
        upward_out[0],
        upward_out[1],
        upward_out[2],
        upward_out[3],
        merge_out[0],
        merge_out[1],
        merge_out[2],
        merge_out[3],
        head_out[0],
        head_out[1],
        head_out[2],
        head_out[3],
        loss_total,
        labelled,
    )


BF = jnp.bfloat16
F32 = jnp.float32
MESH = pl.DeviceIdType.MESH
LANE = 128
PI_PART = 0.7978845608028654
CUBE = 0.044715


def gelu_value(v):
    return 0.5 * v * (1.0 + jnp.tanh(PI_PART * (v + CUBE * (v * v * v))))


def gelu_slope(v):
    bent = jnp.tanh(PI_PART * (v + CUBE * (v * v * v)))
    inner = PI_PART * (1.0 + 3.0 * CUBE * (v * v))
    return 0.5 * (1.0 + bent) + 0.5 * v * (1.0 - bent * bent) * inner


def dot_nn(lhs, rhs):
    return lax.dot_general(lhs, rhs, (((1,), (0,)), ((), ())), preferred_element_type=F32)


def dot_nt(lhs, rhs):
    return lax.dot_general(lhs, rhs, (((1,), (1,)), ((), ())), preferred_element_type=F32)


def span(at, size):
    return pl.ds(pl.multiple_of(at * size, size), size)


SCRATCH = (
    ("inT", (2, 4, 32, 128), BF),
    ("skT", (4, 64, 512), BF),
    ("lab", (8, 128), F32),
    ("F2", (9, 64, 512), F32),
    ("F3", (9, 64, 256), F32),
    ("FU", (4, 64, 256), F32),
    ("flat", (4, 256, 128), F32),
    ("w1", (9, 32, 512), BF),
    ("S1", (9, 32, 512), BF),
    ("w2", (9, 64, 512), BF),
    ("wu", (4, 64, 256), BF),
    ("w3", (9, 64, 256), BF),
    ("IN", (8, 2, 4, 32, 128), BF),
    ("SK", (4, 64, 512), BF),
    ("LB", (16, 8, 128), F32),
    ("W1", (9, 128, 128), BF),
    ("W2", (9, 128, 256), BF),
    ("WU", (16, 64, 256), BF),
    ("W3", (9, 128, 512), BF),
    ("W1T", (128, 1152), BF),
    ("W2T", (256, 1152), BF),
    ("WUT", (256, 1024), BF),
    ("W3T", (512, 1152), BF),
    ("X", (1152, 2304), BF),
    ("P1", (4, 32, 2048), F32),
    ("P1b", (4, 32, 2048), BF),
    ("R1", (3, 32, 2048), BF),
    ("A1", (4, 32, 2048), BF),
    ("P2b", (4, 128, 512), BF),
    ("T2", (4, 128, 512), BF),
    ("S2b", (3, 128, 512), BF),
    ("R2", (3, 128, 512), BF),
    ("pre2", (128, 512), F32),
    ("A2", (8, 128, 512), BF),
    ("J", (2, 4, 128, 768), BF),
    ("P3b", (4, 4, 64, 512), BF),
    ("T3", (4, 4, 64, 512), BF),
    ("S3b", (4, 4, 64, 512), BF),
    ("R3", (4, 3, 64, 512), BF),
    ("pre3", (64, 2048), F32),
    ("act3", (64, 2048), BF),
    ("LG", (8, 32, 128), F32),
    ("LBL", (32, 128), F32),
    ("HT", (256, 8), F32),
    ("DL", (32, 128), F32),
    ("G3", (4, 8, 64, 512), BF),
    ("Z", (1152, 2048), F32),
    ("HS", (2, 2, 64, 128), F32),
    ("HR", (2, 2, 64, 128), F32),
    ("DB", (4, 64, 128), F32),
    ("DR", (256, 512), BF),
    ("P8", (128, 2048), F32),
    ("P7b", (4, 128, 512), BF),
    ("T7", (4, 128, 512), BF),
    ("S7b", (4, 128, 512), BF),
    ("R7", (3, 128, 512), BF),
    ("G2", (2, 128, 2048), BF),
    ("P8b", (4, 32, 2048), BF),
    ("R8", (3, 32, 2048), BF),
    ("G1", (4, 32, 2048), BF),
    ("GW3", (9, 128, 512), BF),
    ("GWU", (16, 64, 256), BF),
    ("GW2", (9, 128, 256), BF),
    ("GW1", (9, 128, 128), BF),
    ("RG3", (4, 9, 64, 256), BF),
    ("Y3", (2, 9, 64, 256), BF),
    ("RGU", (16, 64, 256), BF),
    ("RG2", (9, 64, 512), BF),
    ("RG1", (9, 32, 512), BF),
    ("HD", (16, 8, 128), F32),
)
COPIES = 224


def fused(widths, *refs):
    wa, wb = widths
    rows_a, rows_b, skip_a, skip_b, la, lb, va, vb, f1, f2, fu, f3, fh = refs[:13]
    g1o, g2o, guo, g3o, hdo = refs[13:18]
    m = {name: ref for (name, _, _), ref in zip(SCRATCH, refs[18:-3])}
    send_sem, recv_sem, load_sem = refs[-3:]
    loads = [
        pltpu.make_async_copy(source, m[name], load_sem.at[n])
        for n, (source, name) in enumerate(((f2, "F2"), (f3, "F3"), (fu, "FU")))
    ]
    for load in loads:
        load.start()
    f2, f3, fu = m["F2"], m["F3"], m["FU"]
    h, y = lax.axis_index("ha"), lax.axis_index("col")
    z, x, e = lax.div(h, 4), lax.rem(lax.div(h, 2), 2), lax.rem(h, 2)
    q = 2 * y + x
    s = 2 * q + e
    twin = h + 1 - 2 * e
    entered = pltpu.get_barrier_semaphore()
    for d in range(16):
        for side in (y, 1 - y)[0 if d else 1 :]:
            pl.semaphore_signal(
                entered,
                inc=1,
                device_id={"ha": lax.rem(h + d, 16), "col": side},
                device_id_type=MESH,
            )
    started = []
    count = [0]

    def ha(z_, x_, e_):
        return 4 * z_ + 2 * x_ + e_

    def remote(src, dst, h2, y2, sem_s, sem_r):
        return pltpu.make_async_remote_copy(
            src_ref=src,
            dst_ref=dst,
            send_sem=send_sem.at[sem_s],
            recv_sem=recv_sem.at[sem_r],
            device_id={"ha": h2, "col": y2},
            device_id_type=MESH,
        )

    def push(src, dst, h2, y2):
        n = count[0]
        count[0] += 1
        copy = remote(src, dst, h2, y2, n, n)
        copy.start()
        started.append((copy, None))
        return copy

    def reserve(n):
        base = count[0]
        count[0] += n
        return base

    def hand(src, dst, h2, y2, sem_s, sem_r, needed=None):
        same = jnp.logical_and(h2 == h, y2 == y)
        away = jnp.logical_not(same)
        if needed is not None:
            same = jnp.logical_and(same, needed)
            away = jnp.logical_and(away, needed)
        copy = remote(src, dst, h2, y2, sem_s, sem_r)

        @pl.when(same)
        def _():
            pltpu.make_async_copy(src, dst, recv_sem.at[sem_r]).start()

        @pl.when(away)
        def _():
            copy.start()

        started.append((copy, away))

    def landed(dst, sem_r):
        remote(dst, dst, twin, y, sem_r, sem_r).wait_recv()

    lanes = lax.broadcasted_iota(jnp.int32, (1, LANE), 1)
    left_ok = jnp.logical_and(jnp.logical_and(lanes != 0, lanes != wa), lanes < wa + wb)
    right_ok = jnp.logical_and(lanes != wa - 1, lanes < wa + wb - 1)

    def from_left(v):
        return jnp.where(left_ok, pltpu.roll(v, 1, 1), 0.0)

    def from_right(v):
        return jnp.where(right_ok, pltpu.roll(v, LANE - 1, 1), 0.0)

    J, HR = m["J"], m["HR"]

    @pl.when(z == 0)
    def _():
        J[1, 1:3, :, 0:128] = jnp.zeros((2, 128, 128), BF)
        HR[0] = jnp.zeros((2, 64, 128), F32)

    @pl.when(z == 3)
    def _():
        J[0, 1:3, :, 640:768] = jnp.zeros((2, 128, 128), BF)
        HR[1] = jnp.zeros((2, 64, 128), F32)

    inT, skT, lab, flat = m["inT"], m["skT"], m["lab"], m["flat"]
    w1, w2, wu, w3 = m["w1"], m["w2"], m["wu"], m["w3"]
    wide_a, wide_b = 2 * wa, 2 * wb
    for c in range(2):
        half = slice(c * 128, c * 128 + 128)
        flat[c, 96:128, :] = jnp.zeros((32, 128), F32)
        flat[c, 0:wa, :] = rows_a[:, half].astype(F32)
        flat[c, wa : wa + wb, :] = rows_b[:, half].astype(F32)
        inT[c] = flat[c, 0:128, :].T.astype(BF).reshape(4, 32, 128)

    w1[...] = f1[...].astype(BF)
    pl.semaphore_wait(entered, 31)

    IN, LB = m["IN"], m["LB"]
    W1, W2, WU, W3 = m["W1"], m["W2"], m["WU"], m["W3"]
    S1 = m["S1"]
    near = e == y
    b1 = reserve(4)
    b1s = reserve(5)
    over = remote(w1, S1, h, 1 - y, b1s + 4, b1s + 4)

    @pl.when(jnp.logical_not(near))
    def _():
        over.start()

    started.append((over, jnp.logical_not(near)))

    def spread_first(shard, half, base):
        for k in range(4):
            i = lax.rem(k + 2 * lax.rem(z, 2), 4)
            hand(
                shard.at[:, :, span(i, 128)],
                W1.at[:, span(z, 32), :],
                ha(2 * half + lax.div(i, 2), x, lax.rem(i, 2)),
                e,
                base + k,
                b1 + z,
                near,
            )

    in_copies = []
    for dz in range(4):
        zt = lax.rem(z + dz, 4)
        for d in range(4):
            if dz == 0 and d == 0:
                continue
            there = lax.rem(2 * x + y + d, 4)
            in_copies.append(
                push(
                    inT.at[:, there],
                    IN.at[2 * z + x, e, pl.ds(2 * y, 2)],
                    ha(zt, lax.div(there, 2), e),
                    lax.rem(there, 2),
                )
            )
    IN[2 * z + x, e, pl.ds(2 * y, 2)] = inT[:, 2 * x + y]

    spread_first(w1, y, b1)
    place = lax.broadcasted_iota(jnp.int32, (256, LANE), 0)
    lane = lax.broadcasted_iota(jnp.int32, (256, LANE), 1)
    spread = jnp.concatenate(
        [
            jnp.concatenate([first[...], second[...]], axis=1).astype(F32)
            for first, second in ((la, lb), (va, vb))
        ],
        axis=0,
    )
    spread = jnp.pad(spread, ((0, 4), (0, 256 - wide_a - wide_b)))
    for b in range(2):
        pick = jnp.where(place == 2 * lane + b, 1.0, 0.0)
        planes = dot_nn(spread.astype(BF), pick.astype(BF))
        for a in range(2):
            lab[2 * a + b : 2 * a + b + 1, :] = planes[a : a + 1, :]
            lab[4 + 2 * a + b : 5 + 2 * a + b, :] = planes[2 + a : 3 + a, :]
    lab_copies = []
    LB[h] = lab[...]
    for d in range(1, 16):
        lab_copies.append(push(lab, LB.at[h], lax.rem(h + d, 16), y))


    @pl.when(near)
    def _():
        over.wait_recv()

    spread_first(S1, 1 - y, b1s)
    for copy in in_copies:
        copy.wait_recv()
    twin_in = push(IN.at[:, e], IN.at[:, e], twin, y)

    for load in loads:
        load.wait()
    w2[...] = f2[...].astype(BF)
    w3[...] = f3[...].astype(BF)
    for k in range(4):
        wu[k] = jnp.concatenate([fu[p, :, k * 64 : k * 64 + 64] for p in range(4)], axis=1).astype(BF)
    for a in range(2):
        for c in range(2):
            half = slice(c * 128, c * 128 + 128)
            buf = flat.at[2 * a + c]
            buf[224:256, :] = jnp.zeros((32, 128), F32)
            buf[0:wide_a, :] = skip_a[a, :, half].astype(F32)
            buf[wide_a : wide_a + wide_b, :] = skip_b[a, :, half].astype(F32)
            for b in range(2):
                p = 2 * a + b
                plane = buf[pl.ds(b, 128, stride=2), :]
                skT[2 * c : 2 * c + 2, :, p * 128 : p * 128 + 128] = plane.T.astype(BF).reshape(2, 64, 128)
    b2 = reserve(2)
    for i in range(2):
        hand(
            w2.at[:, :, i * 256 : i * 256 + 256],
            W2.at[:, span(e, 64), :],
            ha(z, i, x),
            y,
            b2 + i,
            b2 + e,
        )
    SK = m["SK"]
    sk_copies = []
    slot = 2 * x + e
    for d in range(1, 4):
        other = lax.rem(slot + d, 4)
        sk_copies.append(push(skT.at[other], SK.at[slot], 4 * z + other, y))
    SK[slot] = skT[slot]
    bu_copies = []
    for d in range(1, 16):
        ht = lax.rem(h + d, 16)
        bu_copies.append(push(wu.at[lax.rem(ht, 4)], WU.at[h], ht, y))
    WU[h] = wu[slot]
    b3 = reserve(4)
    for i in range(4):
        hand(
            w3,
            W3.at[:, span(lax.div(z, 2), 64), span(y, 256)],
            ha(lax.rem(z + i, 4), x, e),
            lax.rem(z, 2),
            b3 + i,
            b3 + 2 * lax.div(z, 2) + y,
        )

    X = m["X"]

    def patch_edges():
        zero = jnp.zeros((384, 128), BF)
        X[0:384, 128:256] = zero
        X[768:1152, 2048:2176] = zero

    def patches(block, first, last):
        def one(i, carry):
            low = block(i)
            v = low.astype(F32)
            kinds = (from_left(v).astype(BF), low, from_right(v).astype(BF))
            for di in (-1, 0, 1):
                for dj in range(3):
                    tap = (di + 1) * 3 + dj
                    X[tap * 128 : tap * 128 + 128, span(i - di + 1, 128)] = kinds[dj]
            return carry

        lax.fori_loop(first, last, one, 0)

    def patch_cols(at, size):
        return pl.ds(pl.multiple_of(at * size + 128, 128), size)

    def transposed(weight, out, rows):
        for t in range(weight.shape[0]):
            out[:, t * rows : t * rows + rows] = weight[t].T

    for j in range(4):
        landed(W1.at[:, 32 * j : 32 * j + 32, :], b1 + j)
    transposed(W1, m["W1T"], 128)
    twin_in.wait_recv()

    def input_block(i):
        return IN[lax.div(i, 2), lax.rem(i, 2)].reshape(128, 128)

    def middle_block(i):
        return A1[:, :, span(i, 128)].reshape(128, 128)

    patches(input_block, 0, 16)
    patch_edges()
    P1, P1b, R1, A1 = m["P1"], m["P1b"], m["R1"], m["A1"]

    def conv_one(n, carry):
        cols = span(n, 512)
        total = dot_nn(m["W1T"][...], X[:, patch_cols(n, 512)]).reshape(4, 32, 512)
        P1[:, :, cols] = total
        P1b[:, :, cols] = total.astype(BF)
        return carry

    def to_plane(d):
        there = lax.rem(q + d, 4)
        return there, ha(z, lax.rem(there, 2), e), lax.div(there, 2)

    def scatter(source, slots, cols=slice(None)):
        copies = []
        for d in range(1, 4):
            there, h2, y2 = to_plane(d)
            copies.append(push(source.at[there, :, cols], slots.at[d - 1, :, cols], h2, y2))
        return copies

    def gather_four(buf, cols):
        copies = []
        for d in range(1, 4):
            _, h2, y2 = to_plane(d)
            copies.append(push(buf.at[q, :, cols], buf.at[q, :, cols], h2, y2))
        return copies

    halves = (slice(0, 1024), slice(1024, 2048))

    def plane_sends(buf):
        copies = []
        for d in range(1, 4):
            _, h2, y2 = to_plane(d)
            copies.append(push(buf.at[s], buf.at[s], h2, y2))
        return copies, push(buf.at[s], buf.at[s], twin, y)

    def plane_passes(buf, sends):
        copies, own = sends
        last = [own]
        for d in range(1, 4):
            copies[d - 1].wait_recv()
            came = 2 * lax.rem(q + 4 - d, 4) + e
            last.append(push(buf.at[came], buf.at[came], twin, y))
        return last

    def gather_plane(buf):
        return plane_passes(buf, plane_sends(buf))

    def arrive(copies):
        for copy in copies:
            copy.wait_recv()

    one_out = []
    for c in range(2):
        lax.fori_loop(2 * c, 2 * c + 2, conv_one, 0)
        one_out.append(scatter(P1b, R1, halves[c]))

    def act_one(n, carry):
        cols = span(n, 512)
        total = P1[q, :, cols] + R1[0, :, cols].astype(F32)
        total = total + R1[1, :, cols].astype(F32) + R1[2, :, cols].astype(F32)
        P1[q, :, cols] = total
        A1[q, :, cols] = gelu_value(total).astype(BF)
        return carry

    wait_one = []
    for c in range(2):
        arrive(one_out[c])
        lax.fori_loop(2 * c, 2 * c + 2, act_one, 0)
        wait_one.append(gather_four(A1, halves[c]))
    for j in range(2):
        landed(W2.at[:, 64 * j : 64 * j + 64, :], b2 + j)
    transposed(W2, m["W2T"], 128)

    for c in range(2):
        arrive(wait_one[c])
        patches(middle_block, 8 * c, 8 * c + 8)
    patch_edges()
    Z, P2b, T2, S2b, R2 = m["Z"], m["P2b"], m["T2"], m["S2b"], m["R2"]

    def band_two(k):
        zt = lax.rem(z + 1 + k, 4)
        Z[0:256, span(zt, 512)] = dot_nn(m["W2T"][...], X[:, patch_cols(zt, 512)])
        P2b[k] = Z[span(1 - e, 128), span(zt, 512)].astype(BF)
        return push(P2b.at[k], T2.at[k], twin, y)

    def pair_two(k):
        zt = lax.rem(z + 1 + k, 4)
        pairs[k].wait_recv()
        S2b[k] = (Z[span(e, 128), span(zt, 512)] + T2[k].astype(F32)).astype(BF)
        two.append(push(S2b.at[k], R2.at[k], ha(zt, x, e), y))

    pairs, two = [], []
    for k in range(4):
        pairs.append(band_two(k))
        if k >= 1:
            pair_two(k - 1)
    for d in range(1, 16):
        bu_copies[d - 1].wait_recv()
    for t in range(8):
        m["WUT"][:, t * 128 : t * 128 + 128] = WU[2 * t : 2 * t + 2].reshape(128, 256).T
    arrive(two)
    pre2, A2 = m["pre2"], m["A2"]
    pairs[3].wait_recv()
    total = Z[span(e, 128), span(z, 512)] + T2[3].astype(F32) + R2[0].astype(F32)
    total = total + R2[1].astype(F32) + R2[2].astype(F32)
    pre2[...] = total
    A2[s] = gelu_value(total).astype(BF)
    wait_two = gather_plane(A2)
    for copy in sk_copies:
        copy.wait_recv()
    for a in range(2):
        for b in range(2):
            p = 2 * a + b
            for i in range(4):
                J[a, 1 + b, 64:128, 128 + 128 * i : 256 + 128 * i] = SK[i, :, p * 128 : p * 128 + 128]
    arrive(wait_two)

    for p in range(4):
        plane = dot_nn(m["WUT"][p * 64 : p * 64 + 64, :], A2[...].reshape(1024, 512))
        J[p // 2, 1 + p % 2, 0:64, 128:640] = plane.astype(BF)

    def fringe(up, down, send_down, keep_down, send_up, keep_up):
        below = remote(send_down, keep_down, lax.rem(h + 4, 16), y, down, down)
        above = remote(send_up, keep_up, lax.rem(h + 12, 16), y, up, up)

        @pl.when(z < 3)
        def _():
            below.start()

        @pl.when(z > 0)
        def _():
            above.start()

        started.append((below, z < 3))
        started.append((above, z > 0))

        def wait():
            @pl.when(z > 0)
            def _():
                below.wait_recv()

            @pl.when(z < 3)
            def _():
                above.wait_recv()

        return wait

    bj = reserve(2)
    wait_rows = fringe(
        bj,
        bj + 1,
        J.at[1, 1:3, :, 512:640],
        J.at[1, 1:3, :, 0:128],
        J.at[0, 1:3, :, 128:256],
        J.at[0, 1:3, :, 640:768],
    )

    def beside(a, i):
        at = slice(i * 128, i * 128 + 128)
        J[a, 0, :, at] = from_left(J[a, 2, :, at].astype(F32)).astype(BF)
        J[a, 3, :, at] = from_right(J[a, 1, :, at].astype(F32)).astype(BF)

    def joined_patches(outer):
        for a in range(2):
            for da in range(3):
                up, di = (a + da - 1) % 2, (a + da - 1) // 2
                first, last = 0, 4
                if di != 0:
                    edge = 0 if di < 0 else 3
                    first, last = (edge, edge + 1) if outer else (1, 4) if di < 0 else (0, 3)
                elif outer:
                    continue
                for b in range(2):
                    for db in range(3):
                        tap = da * 3 + db
                        at = 128 + (2 * a + b) * 512
                        X[tap * 128 : tap * 128 + 128, at + first * 128 : at + last * 128] = J[
                            up, b + db, :, (1 + di + first) * 128 : (1 + di + last) * 128
                        ]

    for a in range(2):
        for i in range(1, 5):
            beside(a, i)
    joined_patches(False)
    wait_rows()
    beside(1, 0)
    beside(0, 5)
    joined_patches(True)

    for j in range(4):
        t, half = j // 2, j % 2
        landed(W3.at[:, 64 * t : 64 * t + 64, 256 * half : 256 * half + 256], b3 + j)
    transposed(W3, m["W3T"], 128)
    P3b, T3, S3b, R3 = m["P3b"], m["T3"], m["S3b"], m["R3"]

    def plane_three(p):
        def step(n, carry):
            Z[0:512, span(n, 256)] = dot_nn(m["W3T"][...], X[:, patch_cols(n, 256)])
            return carry

        lax.fori_loop(2 * p, 2 * p + 2, step, 0)
        cols = slice(p * 512, p * 512 + 512)
        for k in range(4):
            P3b[p, k] = Z[span(2 * k + 1 - e, 64), cols].astype(BF)
        return push(P3b.at[p], T3.at[p], twin, y)

    def pair_three(p):
        pairs[p].wait_recv()
        cols = slice(p * 512, p * 512 + 512)
        for k in range(4):
            total = Z[span(2 * k + e, 64), cols] + T3[p, k].astype(F32)
            Z[span(2 * k + e, 64), cols] = total
            S3b[p, k] = total.astype(BF)
        three.append(scatter(S3b.at[p], R3.at[p]))

    pairs, three = [], []
    for p in range(4):
        pairs.append(plane_three(p))
        if p >= 1:
            pair_three(p - 1)
    pair_three(3)
    pre3, act3, LG = m["pre3"], m["act3"], m["LG"]
    wide = (64, LANE)
    turned = jnp.concatenate([fh[...], jnp.zeros((6, fh.shape[1]), F32)], axis=0).T
    m["HT"][...] = turned.astype(BF).astype(F32)
    head = m["HT"][span(slot, 64), :]
    h0 = jnp.broadcast_to(head[:, 0:1], wide)
    h1 = jnp.broadcast_to(head[:, 1:2], wide)
    for b in range(16):
        if b % 4 == 0:
            arrive(three[b // 4])
        cols = slice(b * 128, b * 128 + 128)
        part = slice(b % 4 * 128, b % 4 * 128 + 128)
        total = Z[span(s, 64), cols] + R3[b // 4, 0, :, part].astype(F32)
        total = total + R3[b // 4, 1, :, part].astype(F32) + R3[b // 4, 2, :, part].astype(F32)
        pre3[:, cols] = total
        act = gelu_value(total).astype(BF)
        act3[:, cols] = act
        act = act.astype(F32)
        LG[s, b : b + 1, :] = jnp.sum(act * h0, axis=0, keepdims=True)
        LG[s, 16 + b : 17 + b, :] = jnp.sum(act * h1, axis=0, keepdims=True)
    wait_logits = []
    for d in range(1, 8):
        there = lax.rem(s + d, 8)
        half = lax.div(there, 4)
        wait_logits.append(push(LG.at[s], LG.at[s], 4 * z + there - 4 * half, half))
    for copy in lab_copies:
        copy.wait_recv()
    LBL = m["LBL"]
    for p in range(4):
        for i in range(4):
            LBL[p * 4 + i : p * 4 + i + 1, :] = LB[4 * z + i, p : p + 1, :]
            LBL[16 + p * 4 + i : 17 + p * 4 + i, :] = LB[4 * z + i, 4 + p : 5 + p, :]
    every = jnp.sum(LB[...], axis=0)
    labelled = jnp.sum(jnp.sum(every[4:8, :], axis=0, keepdims=True), axis=1, keepdims=True)
    arrive(wait_logits)

    logits = LG[0]
    for k in range(1, 8):
        logits = logits + LG[k]
    zero, one = logits[0:16, :], logits[16:32, :]
    picks, usable = LBL[0:16, :] > 0.5, LBL[16:32, :]
    top = jnp.maximum(zero, one)
    lse = top + jnp.log(jnp.exp(zero - top) + jnp.exp(one - top))
    logp = jnp.where(picks, one, zero) - lse
    rest = jnp.exp(jnp.where(picks, zero, one) - lse)
    chance = jnp.exp(logp)
    gap = 1.0 - chance
    terms = usable * (-(gap * gap) * logp)
    slope = (2.0 * gap * chance * logp - gap * gap) * usable / labelled
    own, other = slope * gap, -slope * rest
    DL = m["DL"]
    DL[0:16, :] = jnp.where(picks, other, own).astype(BF).astype(F32)
    DL[16:32, :] = jnp.where(picks, own, other).astype(BF).astype(F32)
    loss = jnp.sum(jnp.sum(terms, axis=0, keepdims=True), axis=1, keepdims=True)
    G3, HD = m["G3"], m["HD"]
    planes = []
    sum0 = jnp.zeros(wide, F32)
    sum1 = jnp.zeros(wide, F32)
    for b in range(16):
        cols = slice(b * 128, b * 128 + 128)
        d0 = jnp.broadcast_to(DL[b : b + 1, :], wide)
        d1 = jnp.broadcast_to(DL[16 + b : 17 + b, :], wide)
        part = slice(b % 4 * 128, b % 4 * 128 + 128)
        G3[b // 4, s, :, part] = ((h0 * d0 + h1 * d1) * gelu_slope(pre3[:, cols])).astype(BF)
        act = act3[:, cols].astype(F32)
        sum0 = sum0 + act * d0
        sum1 = sum1 + act * d1
        if b % 4 == 3:
            planes.append(plane_sends(G3.at[b // 4]))
    side = lax.broadcasted_iota(jnp.int32, wide, 1)
    sum0 = jnp.sum(sum0, axis=1, keepdims=True)
    sum1 = jnp.sum(sum1, axis=1, keepdims=True)
    tile = jnp.where(side == 0, sum0, jnp.where(side == 1, sum1, 0.0))
    HD[h, 0:8, 0:64] = tile.T[0:8, :]
    HD[h, 2:3, 0:64] = jnp.broadcast_to(loss, (1, 64))
    hd_copies = []
    for d in range(1, 16):
        hd_copies.append(push(HD.at[h], HD.at[h], lax.rem(h + d, 16), y))

    HS, DB, DR = m["HS"], m["DB"], m["DR"]

    def back_three(p):
        grads = G3[p].reshape(512, 512)
        Z[0:576, p * 512 : p * 512 + 512] = dot_nn(W3[:, 0:64, :].reshape(576, 512), grads)

    GW3, GWU, GW2, GW1 = m["GW3"], m["GWU"], m["GW2"], m["GW1"]
    RG3, RGU, RG2, RG1 = m["RG3"], m["RGU"], m["RG2"], m["RG1"]

    def grad_three(p):
        def step(t, carry):
            part = dot_nt(X[span(t, 128), 128 + p * 512 : 640 + p * 512], G3[p].reshape(512, 512))
            rows = pl.ds(pl.multiple_of(576 + 128 * lax.div(t, 4), 64), 128)
            cols = span(lax.rem(t, 4), 512)
            if p > 0:
                part = part + Z[rows, cols]
            if p < 3:
                Z[rows, cols] = part
            else:
                GW3[t] = part.astype(BF)
            return carry

        lax.fori_loop(0, 9, step, 0)

    passes = plane_passes(G3.at[0], planes[0])
    for p in range(4):
        arrive(passes)
        back_three(p)
        if p < 3:
            passes = plane_passes(G3.at[p + 1], planes[p + 1])
            grad_three(p)
    def merge_home(first, last):
        for k in range(first, last):
            half, own = lax.rem(y + k // 2, 2), k < 2
            t = lax.rem(lax.div(z, 2) + 1 + k, 2)
            hand(
                GW3.at[:, span(t, 64), span(y, 256)] if own else m["Y3"].at[t],
                RG3.at[z],
                ha(2 * t + half, x, e),
                y,
                bg3 + k,
                bg3 + z,
            )

    ways = (((0, 0, 0), (1, -1, 0), (1, 1, 1)), ((0, -1, -1), (0, 1, 0), (1, 0, 0)))

    def raised_block(a, b, i):
        straight, bent = [], []
        for ao, da, di in ways[a]:
            io = i - di
            if io < 0 or io > 3 or (i < 0 or i > 3) and di == 0:
                continue
            for bo, db, dj in ways[b]:
                tap = (da + 1) * 3 + db + 1
                at = ((2 * ao + bo) * 4 + io) * 128
                (straight if dj == 0 else bent).append(Z[tap * 64 : tap * 64 + 64, at : at + 128])
        turned = sum(bent[1:], bent[0])
        turned = from_left(turned) if b == 0 else from_right(turned)
        return sum(straight, turned)

    for b in range(2):
        HS[0, b] = raised_block(0, b, 4)
        HS[1, b] = raised_block(1, b, -1)
    bh = reserve(2)
    wait_fringe = fringe(bh, bh + 1, HS.at[0], HR.at[0], HS.at[1], HR.at[1])
    for a in range(2):
        for b in range(2):
            p = 2 * a + b
            for i in range(4):
                block = raised_block(a, b, i)
                if i == 3 * a:
                    DB[p] = block
                else:
                    DR[p * 64 : p * 64 + 64, i * 128 : i * 128 + 128] = block.astype(BF)
    grad_three(3)
    bg3 = reserve(4)
    merge_home(0, 2)
    wait_fringe()
    for a in range(2):
        for b in range(2):
            p = 2 * a + b
            DR[p * 64 : p * 64 + 64, a * 384 : a * 384 + 128] = (DB[p] + HR[a, b]).astype(BF)

    P7b, T7, S7b, R7 = m["P7b"], m["T7"], m["S7b"], m["R7"]

    def back_up(k, carry):
        Z[span(k, 128), 0:512] = dot_nn(WU[pl.ds(2 * k, 2)].reshape(128, 256), DR[...])
        return carry

    lax.fori_loop(0, 8, back_up, 0)
    for k in range(4):
        P7b[k] = Z[span(2 * k + 1 - e, 128), 0:512].astype(BF)
    wait_pair = push(P7b, T7, twin, y)

    def pair_seven():
        for k in range(4):
            total = Z[span(2 * k + e, 128), 0:512] + T7[k].astype(F32)
            Z[span(2 * k + e, 128), 0:512] = total
            S7b[k] = total.astype(BF)

    wait_pair.wait_recv()
    pair_seven()
    wait_seven = scatter(S7b, R7)

    def grad_up(k, carry):
        GWU[pl.ds(2 * k, 2)] = dot_nt(A2[k], DR[...]).astype(BF).reshape(2, 64, 256)
        return carry

    Y3 = m["Y3"]
    other = 1 - y
    across = []
    for t in range(2):
        across.append(
            push(
                GW3.at[:, 64 * t : 64 * t + 64, span(other, 256)],
                Y3.at[t],
                h,
                other,
            )
        )

    lax.fori_loop(0, 8, grad_up, 0)
    patches(middle_block, 0, 16)
    patch_edges()
    arrive(wait_seven)
    G2 = m["G2"]
    total = Z[span(s, 128), 0:512] + R7[0].astype(F32)
    total = total + R7[1].astype(F32) + R7[2].astype(F32)
    G2[e, :, span(z, 512)] = (total * gelu_slope(pre2[...])).astype(BF)
    mine = G2.at[e, :, span(z, 512)]
    g2_copies = []
    for d in range(1, 4):
        zt = lax.rem(z + d, 4)
        g2_copies.append(push(mine, mine, ha(zt, x, e), y))
    own_pair = push(mine, mine, twin, y)
    gu_copies = []
    for d in range(1, 16):
        ht = lax.rem(h + d, 16)
        gu_copies.append(push(GWU.at[ht], RGU.at[h], ht, y))
    RGU[h] = GWU[h]

    def back_two(zs):
        for k in range(2):
            cols = pl.ds(pl.multiple_of(zs * 512 + k * 256, 256), 256)
            Z[:, cols] = dot_nn(W2[...].reshape(1152, 256), G2[:, :, cols].reshape(256, 256))

    def relay(d):
        g2_copies[d - 1].wait_recv()
        zs = lax.rem(z + 4 - d, 4)
        came = G2.at[e, :, span(zs, 512)]
        return zs, push(came, came, twin, y)

    arrive(across)
    merge_home(2, 4)
    zs, copy = relay(1)
    own_pair.wait_recv()
    back_two(z)
    for d in range(2, 4):
        after = relay(d)
        copy.wait_recv()
        back_two(zs)
        zs, copy = after
    copy.wait_recv()
    back_two(zs)
    P8b, R8, G1 = m["P8b"], m["R8"], m["G1"]
    P8 = m["P8"]

    def fold(i, carry):
        sums = []
        for dj in range(3):
            part = None
            for di in range(3):
                row = i - (di - 1)
                inside = jnp.logical_and(row >= 0, row <= 15)
                row = jnp.clip(row, 0, 15)
                tap = di * 3 + dj
                block = jnp.where(inside, Z[tap * 128 : tap * 128 + 128, span(row, 128)], 0.0)
                part = block if part is None else part + block
            sums.append(part)
        total = sums[1] + from_right(sums[0]) + from_left(sums[2])
        P8[:, span(i, 128)] = total
        P8b[:, :, span(i, 128)] = total.reshape(4, 32, 128).astype(BF)
        return carry

    wait_eight = []
    for c in range(2):
        lax.fori_loop(8 * c, 8 * c + 8, fold, 0)
        wait_eight.append(scatter(P8b, R8, halves[c]))

    def grad_two(t, carry):
        GW2[t] = dot_nt(X[span(t, 128), 128:2176], G2[...].reshape(256, 2048)).astype(BF)
        return carry

    lax.fori_loop(0, 9, grad_two, 0)

    def act_back(n, carry):
        cols = span(n, 512)
        total = P8[span(q, 32), cols] + R8[0, :, cols].astype(F32)
        total = total + R8[1, :, cols].astype(F32) + R8[2, :, cols].astype(F32)
        G1[q, :, cols] = (total * gelu_slope(P1[q, :, cols])).astype(BF)
        return carry

    wait_g1 = []
    for c in range(2):
        arrive(wait_eight[c])
        lax.fori_loop(2 * c, 2 * c + 2, act_back, 0)
        wait_g1 += gather_four(G1, halves[c])
    bg2 = reserve(2)
    for j in range(2):
        hand(
            GW2.at[:, 64 * j : 64 * j + 64, :],
            RG2.at[:, :, span(x, 256)],
            ha(z, e, j),
            y,
            bg2 + j,
            bg2 + x,
        )
    patches(input_block, 0, 16)
    patch_edges()
    arrive(wait_g1)

    def grad_one(t, carry):
        GW1[t] = dot_nt(X[span(t, 128), 128:2176], G1[...].reshape(128, 2048)).astype(BF)
        return carry

    lax.fori_loop(0, 9, grad_one, 0)
    bg1 = reserve(4)
    r_low = 2 * lax.rem(z, 2) + e
    for k in range(4):
        j = lax.rem(z + 1 + k, 4)
        hand(
            GW1.at[:, span(j, 32), :],
            RG1.at[:, :, span(r_low, 128)],
            ha(j, x, y),
            lax.div(z, 2),
            bg1 + k,
            bg1 + r_low,
        )

    for copy in hd_copies:
        copy.wait_recv()
    for j in range(4):
        hdo[j] = HD[j] + HD[4 + j] + HD[8 + j] + HD[12 + j]
    hdo[4] = jnp.broadcast_to(labelled, (8, 128))
    for k in range(4):
        landed(RG3.at[k], bg3 + k)
    for t in range(9):
        g3o[t] = (RG3[0, t].astype(F32) + RG3[1, t].astype(F32)) + (
            RG3[2, t].astype(F32) + RG3[3, t].astype(F32)
        )
    for copy in gu_copies:
        copy.wait_recv()
    sums = []
    for k in range(4):
        sums.append(
            (RGU[k].astype(F32) + RGU[4 + k].astype(F32))
            + (RGU[8 + k].astype(F32) + RGU[12 + k].astype(F32))
        )
    for p in range(4):
        guo[p] = jnp.concatenate([part[:, p * 64 : p * 64 + 64] for part in sums], axis=1)
    for k in range(2):
        landed(RG2.at[:, :, 256 * k : 256 * k + 256], bg2 + k)
    g2o[...] = RG2[...]
    for k in range(4):
        landed(RG1.at[:, :, 128 * k : 128 * k + 128], bg1 + k)
    g1o[...] = RG1[...]
    for copy, when in started:
        if when is None:
            copy.wait_send()
        else:
            pl.when(when)(copy.wait_send)


def resident_body(
    input_a,
    input_b,
    skip_a,
    skip_b,
    labels_a,
    labels_b,
    valid_a,
    valid_b,
    w_enter,
    moment_enter,
    square_enter,
    w_middle,
    moment_middle,
    square_middle,
    w_upward,
    moment_upward,
    square_upward,
    w_merge,
    moment_merge,
    square_merge,
    w_head,
    moment_head,
    square_head,
):
    vmem = pl.BlockSpec(memory_space=pltpu.VMEM)
    anywhere = pl.BlockSpec(memory_space=pl.ANY)
    g1, g2, gu, g3, hd = pl.pallas_call(
        lambda *refs: fused((input_a.shape[2], input_b.shape[2]), *refs),
        out_shape=(
            jax.ShapeDtypeStruct((9, 32, 512), BF),
            jax.ShapeDtypeStruct((9, 64, 512), BF),
            jax.ShapeDtypeStruct((4, 64, 256), F32),
            jax.ShapeDtypeStruct((9, 64, 256), F32),
            jax.ShapeDtypeStruct((5, 8, 128), F32),
        ),
        in_specs=[vmem] * 9 + [anywhere] * 3 + [vmem],
        out_specs=[vmem] * 5,
        scratch_shapes=[pltpu.VMEM(shape, kind) for _, shape, kind in SCRATCH]
        + [pltpu.SemaphoreType.DMA((COPIES,)), pltpu.SemaphoreType.DMA((COPIES,)), pltpu.SemaphoreType.DMA((3,))],
        compiler_params=pltpu.CompilerParams(
            collective_id=0, has_side_effects=True, vmem_limit_bytes=61 * 1024 * 1024
        ),
    )(
        input_a[0, 0],
        input_b[0, 0],
        skip_a[0],
        skip_b[0],
        labels_a[0],
        labels_b[0],
        valid_a[0],
        valid_b[0],
        w_enter.reshape(9, 32, 512),
        w_middle.reshape(9, 64, 512),
        w_upward.reshape(4, 64, 256),
        w_merge.reshape(9, 64, 256),
        w_head.T,
    )
    states = (
        (w_enter, moment_enter, square_enter),
        (w_middle, moment_middle, square_middle),
        (w_upward, moment_upward, square_upward),
        (w_merge, moment_merge, square_merge),
    )
    dims = tuple(g.shape for g in (g1, g2, gu, g3))
    flat = [part.reshape(dim) for dim, state in zip(dims, states) for part in state]
    rows = w_head.T.shape
    new = pl.pallas_call(
        updates,
        out_shape=tuple(
            jax.ShapeDtypeStruct(dim, kind) for dim in (*dims, rows) for kind in (F32, F32, F32, BF)
        )
        + (jax.ShapeDtypeStruct((1, 1), F32),) * 2,
        in_specs=[anywhere] * 16 + [vmem] * 4,
        out_specs=[anywhere] * 16 + [vmem] * 6,
        scratch_shapes=[
            pltpu.VMEM(dim, kind)
            for dim, g in zip(dims, (g1, g2, gu, g3))
            for kind in (g.dtype, F32, F32, F32, F32, F32, F32, BF)
        ]
        + [pltpu.SemaphoreType.DMA((len(PIECES), 8))],
        compiler_params=pltpu.CompilerParams(vmem_limit_bytes=62 * 1024 * 1024),
    )(g1, g2, gu, g3, *flat, hd, w_head.T, moment_head.T, square_head.T)
    shapes = (w_enter.shape, w_middle.shape, w_upward.shape, w_merge.shape)
    return (
        *[new[k].reshape(shapes[k // 4]) for k in range(16)],
        *[part.T for part in new[16:20]],
        new[20].reshape(()),
        new[21].reshape(()),
    )


PIECES = ((3, 0, 5), (3, 5, 9), (2, 0, 4), (1, 0, 3), (1, 3, 6), (1, 6, 9), (0, 0, 5), (0, 5, 9))


def adamw_step(master, moment, square, gradient):
    moment_new = BETA_ONE * moment + (1.0 - BETA_ONE) * gradient
    square_new = BETA_TWO * square + (1.0 - BETA_TWO) * gradient * gradient
    fixed_moment = moment_new * (RATE / (1.0 - BETA_ONE**STEP))
    fixed_square = square_new * (1.0 / (1.0 - BETA_TWO**STEP))
    master_new = (1.0 - RATE * DECAY) * master - fixed_moment / (jnp.sqrt(fixed_square) + EPSILON)
    return (master_new, moment_new, square_new, master_new.astype(BF))


def updates(*refs):
    grads, states = refs[0:4], refs[4:16]
    hd, head, moment, square = refs[16:20]
    outs, tiny, loss, labelled = refs[20:36], refs[36:40], refs[40], refs[41]
    held, sems = refs[42:74], refs[74]

    def copies(piece):
        k, first, last = PIECES[piece]
        at = slice(first, last)
        inward = [
            pltpu.make_async_copy(source.at[at], held[8 * k + j].at[at], sems.at[piece, j])
            for j, source in enumerate((grads[k], *states[3 * k : 3 * k + 3]))
        ]
        outward = [
            pltpu.make_async_copy(held[8 * k + 4 + j].at[at], outs[4 * k + j].at[at], sems.at[piece, 4 + j])
            for j in range(4)
        ]
        return inward, outward

    every = [copies(piece) for piece in range(len(PIECES))]
    for inward, _ in every:
        for copy in inward:
            copy.start()
    loss[...] = hd[0, 2:3, 0:1]
    labelled[...] = hd[4, 0:1, 0:1]
    gradient = jnp.concatenate([hd[j, 0:2, 0:64] for j in range(4)], axis=1)
    for ref, value in zip(tiny, adamw_step(head[...], moment[...], square[...], gradient)):
        ref[...] = value
    for (k, first, last), (inward, outward) in zip(PIECES, every):
        for copy in inward:
            copy.wait()
        own = held[8 * k : 8 * k + 8]

        def step(i, carry, own=own):
            made = adamw_step(own[1][i], own[2][i], own[3][i], own[0][i].astype(F32))
            for ref, value in zip(own[4:], made):
                ref[i] = value
            return carry

        lax.fori_loop(first, last, step, 0)
        for copy in outward:
            copy.start()
    for _, outward in every:
        for copy in outward:
            copy.wait()


def chosen(*args):
    input_a, input_b, skip_a = args[0], args[1], args[2]
    w_enter, w_middle, w_upward, w_merge = args[8], args[11], args[14], args[17]
    fits = (
        lax.axis_size("ha") == 16
        and lax.axis_size("col") == 2
        and input_a.shape[:2] == (1, 1)
        and input_b.shape[:2] == (1, 1)
        and input_a.shape[3] == 256
        and skip_a.shape[3] == 256
        and input_a.shape[2] + input_b.shape[2] <= LANE
        and w_enter.shape == (3, 3, 32, 512)
        and w_middle.shape == (3, 3, 64, 512)
        and w_upward.shape == (2, 2, 64, 256)
        and w_merge.shape == (3, 3, 64, 256)
    )
    return resident_body(*args) if fits else body(*args)


def solution(mesh):
    placed = (
        P(None, "ha", None, "col"),
        P(None, "ha", None, "col"),
        P(None, "ha", None, "col"),
        P(None, "ha", None, "col"),
        P(None, "ha", None),
        P(None, "ha", None),
        P(None, "ha", None),
        P(None, "ha", None),
        P(None, None, "ha", "col"),
        P(None, None, "ha", "col"),
        P(None, None, "ha", "col"),
        P(None, None, "ha", "col"),
        P(None, None, "ha", "col"),
        P(None, None, "ha", "col"),
        P(None, None, "ha", "col"),
        P(None, None, "ha", "col"),
        P(None, None, "ha", "col"),
        P(None, None, "ha", "col"),
        P(None, None, "ha", "col"),
        P(None, None, "ha", "col"),
        P("col", None),
        P("col", None),
        P("col", None),
    )
    return jax.shard_map(
        chosen,
        mesh=mesh,
        in_specs=placed,
        out_specs=(
            P(None, None, "ha", "col"),
            P(None, None, "ha", "col"),
            P(None, None, "ha", "col"),
            P(None, None, "ha", "col"),
            P(None, None, "ha", "col"),
            P(None, None, "ha", "col"),
            P(None, None, "ha", "col"),
            P(None, None, "ha", "col"),
            P(None, None, "ha", "col"),
            P(None, None, "ha", "col"),
            P(None, None, "ha", "col"),
            P(None, None, "ha", "col"),
            P(None, None, "ha", "col"),
            P(None, None, "ha", "col"),
            P(None, None, "ha", "col"),
            P(None, None, "ha", "col"),
            P("col", None),
            P("col", None),
            P("col", None),
            P("col", None),
            P(),
            P(),
        ),
        check_vma=False,
    )
```

```python
import jax
import jax.numpy as jnp
from jax import lax
from jax.experimental import pallas as pl
from jax.experimental.pallas import tpu as pltpu
from jax.sharding import PartitionSpec as P

STEP = 10


NUMBERS = ("NHWC", "HWIO", "NHWC")
BETA_ONE = 0.9
BETA_TWO = 0.95
RATE = 0.08
DECAY = 0.1
EPSILON = 1e-08


def extended(cells, sides, width):
    for axis, dim in sides:
        count = lax.axis_size(axis)
        ends = count - 1
        head = lax.slice_in_dim(cells, 0, width, axis=dim)
        tail = lax.slice_in_dim(cells, cells.shape[dim] - width, cells.shape[dim], axis=dim)
        cells = jnp.concatenate(
            [
                lax.ppermute(tail, axis, [(i, (i + 1) % count) for i in range(ends)]),
                cells,
                lax.ppermute(head, axis, [((i + 1) % count, i) for i in range(ends)]),
            ],
            axis=dim,
        )
    return cells


def shortened(value):

    def short(part):
        return part.astype(jnp.bfloat16) if part.dtype == jnp.float32 else part

    return jax.tree.map(short, value)


def convolve_rows(padded, weight):
    return lax.conv_general_dilated(
        padded,
        weight,
        (1, 1),
        ((0, 0), (1, 1)),
        dimension_numbers=NUMBERS,
        preferred_element_type=jnp.float32,
    )


def flipped(weight):
    return jnp.transpose(weight[::-1, ::-1], (0, 1, 3, 2))


def upsample(values, weight):
    product = jnp.einsum("nhwc,abcd->nhawbd", values, weight, preferred_element_type=jnp.float32)
    return product.reshape(
        product.shape[0], 2 * product.shape[1], 2 * product.shape[3], product.shape[5]
    )


def split_pixels(upstream):
    return upstream.reshape(
        upstream.shape[0], upstream.shape[1] // 2, 2, upstream.shape[2] // 2, 2, upstream.shape[3]
    )


def upsample_back(upstream, weight):
    return jnp.einsum(
        "nhawbd,abcd->nhwc", split_pixels(upstream), weight, preferred_element_type=jnp.float32
    )


def upsample_weight(values, upstream):
    return jnp.einsum(
        "nhwc,nhawbd->abcd", values, split_pixels(upstream), preferred_element_type=jnp.float32
    )


def tap_grads(padded, upstream):
    wide = jnp.pad(padded, ((0, 0), (0, 0), (1, 1), (0, 0)))
    height, across = (upstream.shape[1], upstream.shape[2])
    stacked = []
    for row_tap in range(3):
        tapline = []
        for col_tap in range(3):
            window = wide[:, row_tap : row_tap + height, col_tap : col_tap + across, :]
            tapline.append(
                jnp.einsum("nhwc,nhwd->cd", window, upstream, preferred_element_type=jnp.float32)
            )
        stacked.append(jnp.stack(tapline))
    return jnp.stack(stacked)


def alternate(weight, groups):
    dims = weight.shape
    shaped = weight.reshape(dims[0], dims[1], 2, groups, dims[2] // (2 * groups), dims[3])
    return shaped.transpose(0, 1, 3, 2, 4, 5).reshape(dims)


def deinterleave(weight, groups):
    dims = weight.shape
    shaped = weight.reshape(dims[0], dims[1], groups, 2, dims[2] // (2 * groups), dims[3])
    return shaped.transpose(0, 1, 3, 2, 4, 5).reshape(dims)


def gelu_back(pre_act, upstream):
    return jax.vjp(jax.nn.gelu, pre_act)[1](upstream)[0]


def focal(logits, labels, usable):
    logprob = jax.nn.log_softmax(logits, axis=-1)
    picked = jnp.where(labels == 1, logprob[..., 1], logprob[..., 0])
    chance = jnp.exp(picked)
    return jnp.sum(usable.astype(jnp.float32) * (-((1.0 - chance) ** 2) * picked))


def loss_terms(logits, labels, usable, labelled):
    running, pull = jax.vjp(lambda values: focal(values, labels, usable), logits)
    return (running, pull(1.0 / labelled)[0])


def gather_channels(values):
    return lax.all_gather(values, "col", axis=3, tiled=True)


def spread_back(partial_value):
    return lax.psum_scatter(partial_value, "col", scatter_dimension=3, tiled=True)


def conv_forward(local, weight):
    padded = extended(local, (("ha", 1),), 1)
    whole = gather_channels(padded)
    return (convolve_rows(whole, weight), whole)


def up_forward(local, weight):
    whole = gather_channels(local)
    return (upsample(whole, weight), whole)


def conv_weight_grad(kept, upstream):
    return tap_grads(kept, upstream)


def up_weight_grad(kept, upstream):
    return upsample_weight(kept, upstream)


def backward_weights(merge_up, upward, middle):
    return (flipped(merge_up), upward, flipped(middle))


def conv_input_grad(back_weight, upstream):
    padded = extended(shortened(upstream), (("ha", 1),), 1).astype(upstream.dtype)
    return spread_back(convolve_rows(padded, back_weight))


def up_input_grad(back_weight, upstream):
    return spread_back(upsample_back(upstream, back_weight))


def forward_pass(picture, skipped, copies):
    enter, middle, upward, merge_mixed, back_merge, back_upward, back_middle, head_copy = copies
    pre_one, kept_one = conv_forward(picture, enter)
    act_one = jax.nn.gelu(pre_one).astype(jnp.bfloat16)
    pre_two, kept_two = conv_forward(act_one, middle)
    act_two = jax.nn.gelu(pre_two).astype(jnp.bfloat16)
    raised, kept_up = up_forward(act_two, upward)
    joined = jnp.concatenate([raised.astype(jnp.bfloat16), skipped], axis=3)
    pre_three, kept_three = conv_forward(joined, merge_mixed)
    act_three = jax.nn.gelu(pre_three).astype(jnp.bfloat16)
    partial_value = jnp.einsum(
        "nhwc,ck->nhwk", act_three, head_copy, preferred_element_type=jnp.float32
    )
    return (
        partial_value,
        (pre_one, kept_one, pre_two, kept_two, kept_up, pre_three, kept_three, act_three),
    )


def backward_pass(saved, dlogits, copies):
    enter, middle, upward, merge_mixed, back_merge, back_upward, back_middle, head_copy = copies
    pre_one, kept_one, pre_two, kept_two, kept_up, pre_three, kept_three, act_three = saved
    back_three = jnp.einsum("nhwk,ck->nhwc", dlogits, head_copy, preferred_element_type=jnp.float32)
    grad_head = jnp.einsum("nhwc,nhwk->ck", act_three, dlogits, preferred_element_type=jnp.float32)
    grad_three = gelu_back(pre_three, back_three).astype(jnp.bfloat16)
    grad_merge = conv_weight_grad(kept_three, grad_three)
    d_raised = conv_input_grad(back_merge, grad_three).astype(jnp.bfloat16)
    grad_upward = up_weight_grad(kept_up, d_raised)
    back_two = up_input_grad(back_upward, d_raised)
    grad_two = gelu_back(pre_two, back_two).astype(jnp.bfloat16)
    grad_middle = conv_weight_grad(kept_two, grad_two)
    back_one = conv_input_grad(back_middle, grad_two)
    grad_one = gelu_back(pre_one, back_one).astype(jnp.bfloat16)
    grad_enter = conv_weight_grad(kept_one, grad_one)
    return (grad_enter, grad_middle, grad_upward, grad_merge, grad_head)


def adamw(master, moment, square, gradient):
    moment_new = BETA_ONE * moment + (1.0 - BETA_ONE) * gradient
    square_new = BETA_TWO * square + (1.0 - BETA_TWO) * gradient * gradient
    fixed_moment = moment_new / (1.0 - BETA_ONE**STEP)
    fixed_square = square_new / (1.0 - BETA_TWO**STEP)
    master_new = master - RATE * (
        fixed_moment / (jnp.sqrt(fixed_square) + EPSILON) + DECAY * master
    )
    return (master_new, moment_new, square_new, master_new.astype(jnp.bfloat16))


def own_rows(summed, local):
    return lax.dynamic_slice_in_dim(
        summed, lax.axis_index("ha") * local.shape[2], local.shape[2], 2
    )


def body(
    input_a,
    input_b,
    skip_a,
    skip_b,
    labels_a,
    labels_b,
    valid_a,
    valid_b,
    w_enter,
    moment_enter,
    square_enter,
    w_middle,
    moment_middle,
    square_middle,
    w_upward,
    moment_upward,
    square_upward,
    w_merge,
    moment_merge,
    square_merge,
    w_head,
    moment_head,
    square_head,
):
    groups = lax.axis_size("col")
    enter, middle, upward, merge = (
        lax.all_gather(w_enter.astype(jnp.bfloat16), "ha", axis=2, tiled=True),
        lax.all_gather(w_middle.astype(jnp.bfloat16), "ha", axis=2, tiled=True),
        lax.all_gather(w_upward.astype(jnp.bfloat16), "ha", axis=2, tiled=True),
        lax.all_gather(w_merge.astype(jnp.bfloat16), "ha", axis=2, tiled=True),
    )
    head_low = w_head.astype(jnp.bfloat16)
    merge_up = merge[:, :, : merge.shape[2] // 2]
    back_merge, back_upward, back_middle = backward_weights(merge_up, upward, middle)
    copies = (
        enter,
        middle,
        upward,
        alternate(merge, groups),
        back_merge,
        back_upward,
        back_middle,
        head_low,
    )
    labelled = lax.psum(
        jnp.sum(valid_a.astype(jnp.float32)) + jnp.sum(valid_b.astype(jnp.float32)), "ha"
    )
    partial_a, saved_a = forward_pass(input_a, skip_a, copies)
    partial_b, saved_b = forward_pass(input_b, skip_b, copies)
    logits_a, logits_b = lax.psum((partial_a, partial_b), "col")
    loss_a, dlogits_a = loss_terms(logits_a, labels_a, valid_a, labelled)
    loss_b, dlogits_b = loss_terms(logits_b, labels_b, valid_b, labelled)
    grads_a = backward_pass(saved_a, dlogits_a.astype(jnp.bfloat16), copies)
    grads_b = backward_pass(saved_b, dlogits_b.astype(jnp.bfloat16), copies)
    local_enter = grads_a[0] + grads_b[0]
    local_middle = grads_a[1] + grads_b[1]
    local_upward = grads_a[2] + grads_b[2]
    local_merge = deinterleave(grads_a[3] + grads_b[3], groups)
    local_head = grads_a[4] + grads_b[4]
    local_loss = loss_a + loss_b
    full_enter, full_middle, full_upward, full_merge, head_total, loss_total = (
        lax.psum(local_enter.astype(jnp.bfloat16), "ha").astype(jnp.float32),
        lax.psum(local_middle.astype(jnp.bfloat16), "ha").astype(jnp.float32),
        lax.psum(local_upward.astype(jnp.bfloat16), "ha").astype(jnp.float32),
        lax.psum(local_merge.astype(jnp.bfloat16), "ha").astype(jnp.float32),
        lax.psum(local_head.astype(jnp.bfloat16), "ha").astype(jnp.float32),
        lax.psum(local_loss.astype(jnp.bfloat16), "ha").astype(jnp.float32),
    )
    grad_enter = own_rows(full_enter, w_enter)
    grad_middle = own_rows(full_middle, w_middle)
    grad_upward = own_rows(full_upward, w_upward)
    grad_merge = own_rows(full_merge, w_merge)
    enter_out = adamw(w_enter, moment_enter, square_enter, grad_enter)
    middle_out = adamw(w_middle, moment_middle, square_middle, grad_middle)
    upward_out = adamw(w_upward, moment_upward, square_upward, grad_upward)
    merge_out = adamw(w_merge, moment_merge, square_merge, grad_merge)
    head_out = adamw(w_head, moment_head, square_head, head_total)
    return (
        enter_out[0],
        enter_out[1],
        enter_out[2],
        enter_out[3],
        middle_out[0],
        middle_out[1],
        middle_out[2],
        middle_out[3],
        upward_out[0],
        upward_out[1],
        upward_out[2],
        upward_out[3],
        merge_out[0],
        merge_out[1],
        merge_out[2],
        merge_out[3],
        head_out[0],
        head_out[1],
        head_out[2],
        head_out[3],
        loss_total,
        labelled,
    )


BF = jnp.bfloat16
F32 = jnp.float32
MESH = pl.DeviceIdType.MESH
LANE = 128
PI_PART = 0.7978845608028654
CUBE = 0.044715


def gelu_value(v):
    return 0.5 * v * (1.0 + jnp.tanh(PI_PART * (v + CUBE * (v * v * v))))


def gelu_slope(v):
    bent = jnp.tanh(PI_PART * (v + CUBE * (v * v * v)))
    inner = PI_PART * (1.0 + 3.0 * CUBE * (v * v))
    return 0.5 * (1.0 + bent) + 0.5 * v * (1.0 - bent * bent) * inner


def dot_nn(lhs, rhs):
    return lax.dot_general(lhs, rhs, (((1,), (0,)), ((), ())), preferred_element_type=F32)


def dot_nt(lhs, rhs):
    return lax.dot_general(lhs, rhs, (((1,), (1,)), ((), ())), preferred_element_type=F32)


def span(at, size):
    return pl.ds(pl.multiple_of(at * size, size), size)


SCRATCH = (
    ("inT", (2, 4, 32, 128), BF),
    ("skT", (4, 64, 512), BF),
    ("lab", (8, 128), F32),
    ("F2", (9, 64, 512), F32),
    ("F3", (9, 64, 256), F32),
    ("FU", (4, 64, 256), F32),
    ("flat", (4, 256, 128), F32),
    ("w1", (9, 32, 512), BF),
    ("S1", (9, 32, 512), BF),
    ("w2", (9, 64, 512), BF),
    ("wu", (4, 64, 256), BF),
    ("w3", (9, 64, 256), BF),
    ("IN", (8, 2, 4, 32, 128), BF),
    ("SK", (4, 64, 512), BF),
    ("LB", (16, 8, 128), F32),
    ("W1", (9, 128, 128), BF),
    ("W2", (9, 128, 256), BF),
    ("WU", (16, 64, 256), BF),
    ("W3", (9, 128, 512), BF),
    ("W1T", (128, 1152), BF),
    ("W2T", (256, 1152), BF),
    ("WUT", (256, 1024), BF),
    ("W3T", (512, 1152), BF),
    ("X", (1152, 2304), BF),
    ("P1", (4, 32, 2048), F32),
    ("P1b", (4, 32, 2048), BF),
    ("R1", (3, 32, 2048), BF),
    ("A1", (4, 32, 2048), BF),
    ("P2b", (4, 128, 512), BF),
    ("T2", (4, 128, 512), BF),
    ("S2b", (3, 128, 512), BF),
    ("R2", (3, 128, 512), BF),
    ("pre2", (128, 512), F32),
    ("A2", (8, 128, 512), BF),
    ("J", (2, 4, 128, 768), BF),
    ("P3b", (4, 4, 64, 512), BF),
    ("T3", (4, 4, 64, 512), BF),
    ("S3b", (4, 4, 64, 512), BF),
    ("R3", (4, 3, 64, 512), BF),
    ("pre3", (64, 2048), F32),
    ("act3", (64, 2048), BF),
    ("LG", (8, 32, 128), F32),
    ("LBL", (32, 128), F32),
    ("HT", (256, 8), F32),
    ("DL", (32, 128), F32),
    ("G3", (4, 8, 64, 512), BF),
    ("Z", (1152, 2048), F32),
    ("HS", (2, 2, 64, 128), F32),
    ("HR", (2, 2, 64, 128), F32),
    ("DB", (4, 64, 128), F32),
    ("DR", (256, 512), BF),
    ("P8", (128, 2048), F32),
    ("P7b", (4, 128, 512), BF),
    ("T7", (4, 128, 512), BF),
    ("S7b", (4, 128, 512), BF),
    ("R7", (3, 128, 512), BF),
    ("G2", (2, 128, 2048), BF),
    ("P8b", (4, 32, 2048), BF),
    ("R8", (3, 32, 2048), BF),
    ("G1", (4, 32, 2048), BF),
    ("GW3", (9, 128, 512), BF),
    ("GWU", (16, 64, 256), BF),
    ("GW2", (9, 128, 256), BF),
    ("GW1", (9, 128, 128), BF),
    ("RG3", (4, 9, 64, 256), BF),
    ("Y3", (2, 9, 64, 256), BF),
    ("RGU", (16, 64, 256), BF),
    ("RG2", (9, 64, 512), BF),
    ("RG1", (9, 32, 512), BF),
    ("HD", (16, 8, 128), F32),
)
COPIES = 224


def fused(widths, *refs):
    wa, wb = widths
    rows_a, rows_b, skip_a, skip_b, la, lb, va, vb, f1, f2, fu, f3, fh = refs[:13]
    g1o, g2o, guo, g3o, hdo = refs[13:18]
    m = {name: ref for (name, _, _), ref in zip(SCRATCH, refs[18:-3])}
    send_sem, recv_sem, load_sem = refs[-3:]
    loads = [
        pltpu.make_async_copy(source, m[name], load_sem.at[n])
        for n, (source, name) in enumerate(((f2, "F2"), (f3, "F3"), (fu, "FU")))
    ]
    for load in loads:
        load.start()
    f2, f3, fu = m["F2"], m["F3"], m["FU"]
    h, y = lax.axis_index("ha"), lax.axis_index("col")
    z, x, e = lax.div(h, 4), lax.rem(lax.div(h, 2), 2), lax.rem(h, 2)
    q = 2 * y + x
    s = 2 * q + e
    twin = h + 1 - 2 * e
    entered = pltpu.get_barrier_semaphore()
    for d in range(16):
        for side in (y, 1 - y)[0 if d else 1 :]:
            pl.semaphore_signal(
                entered,
                inc=1,
                device_id={"ha": lax.rem(h + d, 16), "col": side},
                device_id_type=MESH,
            )
    started = []
    count = [0]

    def ha(z_, x_, e_):
        return 4 * z_ + 2 * x_ + e_

    def remote(src, dst, h2, y2, sem_s, sem_r):
        return pltpu.make_async_remote_copy(
            src_ref=src,
            dst_ref=dst,
            send_sem=send_sem.at[sem_s],
            recv_sem=recv_sem.at[sem_r],
            device_id={"ha": h2, "col": y2},
            device_id_type=MESH,
        )

    def push(src, dst, h2, y2):
        n = count[0]
        count[0] += 1
        copy = remote(src, dst, h2, y2, n, n)
        copy.start()
        started.append((copy, None))
        return copy

    def reserve(n):
        base = count[0]
        count[0] += n
        return base

    def hand(src, dst, h2, y2, sem_s, sem_r, needed=None):
        same = jnp.logical_and(h2 == h, y2 == y)
        away = jnp.logical_not(same)
        if needed is not None:
            same = jnp.logical_and(same, needed)
            away = jnp.logical_and(away, needed)
        copy = remote(src, dst, h2, y2, sem_s, sem_r)

        @pl.when(same)
        def _():
            pltpu.make_async_copy(src, dst, recv_sem.at[sem_r]).start()

        @pl.when(away)
        def _():
            copy.start()

        started.append((copy, away))

    def landed(dst, sem_r):
        remote(dst, dst, twin, y, sem_r, sem_r).wait_recv()

    lanes = lax.broadcasted_iota(jnp.int32, (1, LANE), 1)
    left_ok = jnp.logical_and(jnp.logical_and(lanes != 0, lanes != wa), lanes < wa + wb)
    right_ok = jnp.logical_and(lanes != wa - 1, lanes < wa + wb - 1)

    def from_left(v):
        return jnp.where(left_ok, pltpu.roll(v, 1, 1), 0.0)

    def from_right(v):
        return jnp.where(right_ok, pltpu.roll(v, LANE - 1, 1), 0.0)

    J, HR = m["J"], m["HR"]

    @pl.when(z == 0)
    def _():
        J[1, 1:3, :, 0:128] = jnp.zeros((2, 128, 128), BF)
        HR[0] = jnp.zeros((2, 64, 128), F32)

    @pl.when(z == 3)
    def _():
        J[0, 1:3, :, 640:768] = jnp.zeros((2, 128, 128), BF)
        HR[1] = jnp.zeros((2, 64, 128), F32)

    inT, skT, lab, flat = m["inT"], m["skT"], m["lab"], m["flat"]
    w1, w2, wu, w3 = m["w1"], m["w2"], m["wu"], m["w3"]
    wide_a, wide_b = 2 * wa, 2 * wb
    for c in range(2):
        half = slice(c * 128, c * 128 + 128)
        flat[c, 96:128, :] = jnp.zeros((32, 128), F32)
        flat[c, 0:wa, :] = rows_a[:, half].astype(F32)
        flat[c, wa : wa + wb, :] = rows_b[:, half].astype(F32)
        inT[c] = flat[c, 0:128, :].T.astype(BF).reshape(4, 32, 128)

    w1[...] = f1[...].astype(BF)
    pl.semaphore_wait(entered, 31)

    IN, LB = m["IN"], m["LB"]
    W1, W2, WU, W3 = m["W1"], m["W2"], m["WU"], m["W3"]
    S1 = m["S1"]
    near = e == y
    b1 = reserve(4)
    b1s = reserve(5)
    over = remote(w1, S1, h, 1 - y, b1s + 4, b1s + 4)

    @pl.when(jnp.logical_not(near))
    def _():
        over.start()

    started.append((over, jnp.logical_not(near)))

    def spread_first(shard, half, base):
        for k in range(4):
            i = lax.rem(k + 2 * lax.rem(z, 2), 4)
            hand(
                shard.at[:, :, span(i, 128)],
                W1.at[:, span(z, 32), :],
                ha(2 * half + lax.div(i, 2), x, lax.rem(i, 2)),
                e,
                base + k,
                b1 + z,
                near,
            )

    in_copies = []
    for dz in range(4):
        zt = lax.rem(z + dz, 4)
        for d in range(4):
            if dz == 0 and d == 0:
                continue
            there = lax.rem(2 * x + y + d, 4)
            in_copies.append(
                push(
                    inT.at[:, there],
                    IN.at[2 * z + x, e, pl.ds(2 * y, 2)],
                    ha(zt, lax.div(there, 2), e),
                    lax.rem(there, 2),
                )
            )
    IN[2 * z + x, e, pl.ds(2 * y, 2)] = inT[:, 2 * x + y]

    spread_first(w1, y, b1)
    place = lax.broadcasted_iota(jnp.int32, (256, LANE), 0)
    lane = lax.broadcasted_iota(jnp.int32, (256, LANE), 1)
    spread = jnp.concatenate(
        [
            jnp.concatenate([first[...], second[...]], axis=1).astype(F32)
            for first, second in ((la, lb), (va, vb))
        ],
        axis=0,
    )
    spread = jnp.pad(spread, ((0, 4), (0, 256 - wide_a - wide_b)))
    for b in range(2):
        pick = jnp.where(place == 2 * lane + b, 1.0, 0.0)
        planes = dot_nn(spread.astype(BF), pick.astype(BF))
        for a in range(2):
            lab[2 * a + b : 2 * a + b + 1, :] = planes[a : a + 1, :]
            lab[4 + 2 * a + b : 5 + 2 * a + b, :] = planes[2 + a : 3 + a, :]
    lab_copies = []
    LB[h] = lab[...]
    for d in range(1, 16):
        lab_copies.append(push(lab, LB.at[h], lax.rem(h + d, 16), y))


    @pl.when(near)
    def _():
        over.wait_recv()

    spread_first(S1, 1 - y, b1s)
    for copy in in_copies:
        copy.wait_recv()
    twin_in = push(IN.at[:, e], IN.at[:, e], twin, y)

    for load in loads:
        load.wait()
    w2[...] = f2[...].astype(BF)
    w3[...] = f3[...].astype(BF)
    for k in range(4):
        wu[k] = jnp.concatenate([fu[p, :, k * 64 : k * 64 + 64] for p in range(4)], axis=1).astype(BF)
    for a in range(2):
        for c in range(2):
            half = slice(c * 128, c * 128 + 128)
            buf = flat.at[2 * a + c]
            buf[224:256, :] = jnp.zeros((32, 128), F32)
            buf[0:wide_a, :] = skip_a[a, :, half].astype(F32)
            buf[wide_a : wide_a + wide_b, :] = skip_b[a, :, half].astype(F32)
            for b in range(2):
                p = 2 * a + b
                plane = buf[pl.ds(b, 128, stride=2), :]
                skT[2 * c : 2 * c + 2, :, p * 128 : p * 128 + 128] = plane.T.astype(BF).reshape(2, 64, 128)
    b2 = reserve(2)
    for i in range(2):
        hand(
            w2.at[:, :, i * 256 : i * 256 + 256],
            W2.at[:, span(e, 64), :],
            ha(z, i, x),
            y,
            b2 + i,
            b2 + e,
        )
    SK = m["SK"]
    sk_copies = []
    slot = 2 * x + e
    for d in range(1, 4):
        other = lax.rem(slot + d, 4)
        sk_copies.append(push(skT.at[other], SK.at[slot], 4 * z + other, y))
    SK[slot] = skT[slot]
    bu_copies = []
    for d in range(1, 16):
        ht = lax.rem(h + d, 16)
        bu_copies.append(push(wu.at[lax.rem(ht, 4)], WU.at[h], ht, y))
    WU[h] = wu[slot]
    b3 = reserve(4)
    for i in range(4):
        hand(
            w3,
            W3.at[:, span(lax.div(z, 2), 64), span(y, 256)],
            ha(lax.rem(z + i, 4), x, e),
            lax.rem(z, 2),
            b3 + i,
            b3 + 2 * lax.div(z, 2) + y,
        )

    X = m["X"]

    def patch_edges():
        zero = jnp.zeros((384, 128), BF)
        X[0:384, 128:256] = zero
        X[768:1152, 2048:2176] = zero

    def patches(block, first, last):
        def one(i, carry):
            low = block(i)
            v = low.astype(F32)
            kinds = (from_left(v).astype(BF), low, from_right(v).astype(BF))
            for di in (-1, 0, 1):
                for dj in range(3):
                    tap = (di + 1) * 3 + dj
                    X[tap * 128 : tap * 128 + 128, span(i - di + 1, 128)] = kinds[dj]
            return carry

        lax.fori_loop(first, last, one, 0)

    def patch_cols(at, size):
        return pl.ds(pl.multiple_of(at * size + 128, 128), size)

    def transposed(weight, out, rows):
        for t in range(weight.shape[0]):
            out[:, t * rows : t * rows + rows] = weight[t].T

    for j in range(4):
        landed(W1.at[:, 32 * j : 32 * j + 32, :], b1 + j)
    transposed(W1, m["W1T"], 128)
    twin_in.wait_recv()

    def input_block(i):
        return IN[lax.div(i, 2), lax.rem(i, 2)].reshape(128, 128)

    def middle_block(i):
        return A1[:, :, span(i, 128)].reshape(128, 128)

    patches(input_block, 0, 16)
    patch_edges()
    P1, P1b, R1, A1 = m["P1"], m["P1b"], m["R1"], m["A1"]

    def conv_one(n, carry):
        cols = span(n, 512)
        total = dot_nn(m["W1T"][...], X[:, patch_cols(n, 512)]).reshape(4, 32, 512)
        P1[:, :, cols] = total
        P1b[:, :, cols] = total.astype(BF)
        return carry

    def to_plane(d):
        there = lax.rem(q + d, 4)
        return there, ha(z, lax.rem(there, 2), e), lax.div(there, 2)

    def scatter(source, slots, cols=slice(None)):
        copies = []
        for d in range(1, 4):
            there, h2, y2 = to_plane(d)
            copies.append(push(source.at[there, :, cols], slots.at[d - 1, :, cols], h2, y2))
        return copies

    def gather_four(buf, cols):
        copies = []
        for d in range(1, 4):
            _, h2, y2 = to_plane(d)
            copies.append(push(buf.at[q, :, cols], buf.at[q, :, cols], h2, y2))
        return copies

    halves = (slice(0, 1024), slice(1024, 2048))

    def plane_sends(buf):
        copies = []
        for d in range(1, 4):
            _, h2, y2 = to_plane(d)
            copies.append(push(buf.at[s], buf.at[s], h2, y2))
        return copies, push(buf.at[s], buf.at[s], twin, y)

    def plane_passes(buf, sends):
        copies, own = sends
        last = [own]
        for d in range(1, 4):
            copies[d - 1].wait_recv()
            came = 2 * lax.rem(q + 4 - d, 4) + e
            last.append(push(buf.at[came], buf.at[came], twin, y))
        return last

    def gather_plane(buf):
        return plane_passes(buf, plane_sends(buf))

    def arrive(copies):
        for copy in copies:
            copy.wait_recv()

    one_out = []
    for c in range(2):
        lax.fori_loop(2 * c, 2 * c + 2, conv_one, 0)
        one_out.append(scatter(P1b, R1, halves[c]))

    def act_one(n, carry):
        cols = span(n, 512)
        total = P1[q, :, cols] + R1[0, :, cols].astype(F32)
        total = total + R1[1, :, cols].astype(F32) + R1[2, :, cols].astype(F32)
        P1[q, :, cols] = total
        A1[q, :, cols] = gelu_value(total).astype(BF)
        return carry

    wait_one = []
    for c in range(2):
        arrive(one_out[c])
        lax.fori_loop(2 * c, 2 * c + 2, act_one, 0)
        wait_one.append(gather_four(A1, halves[c]))
    for j in range(2):
        landed(W2.at[:, 64 * j : 64 * j + 64, :], b2 + j)
    transposed(W2, m["W2T"], 128)

    for c in range(2):
        arrive(wait_one[c])
        patches(middle_block, 8 * c, 8 * c + 8)
    patch_edges()
    Z, P2b, T2, S2b, R2 = m["Z"], m["P2b"], m["T2"], m["S2b"], m["R2"]

    def band_two(k):
        zt = lax.rem(z + 1 + k, 4)
        Z[0:256, span(zt, 512)] = dot_nn(m["W2T"][...], X[:, patch_cols(zt, 512)])
        P2b[k] = Z[span(1 - e, 128), span(zt, 512)].astype(BF)
        return push(P2b.at[k], T2.at[k], twin, y)

    def pair_two(k):
        zt = lax.rem(z + 1 + k, 4)
        pairs[k].wait_recv()
        S2b[k] = (Z[span(e, 128), span(zt, 512)] + T2[k].astype(F32)).astype(BF)
        two.append(push(S2b.at[k], R2.at[k], ha(zt, x, e), y))

    pairs, two = [], []
    for k in range(4):
        pairs.append(band_two(k))
        if k >= 1:
            pair_two(k - 1)
    for d in range(1, 16):
        bu_copies[d - 1].wait_recv()
    for t in range(8):
        m["WUT"][:, t * 128 : t * 128 + 128] = WU[2 * t : 2 * t + 2].reshape(128, 256).T
    arrive(two)
    pre2, A2 = m["pre2"], m["A2"]
    pairs[3].wait_recv()
    total = Z[span(e, 128), span(z, 512)] + T2[3].astype(F32) + R2[0].astype(F32)
    total = total + R2[1].astype(F32) + R2[2].astype(F32)
    pre2[...] = total
    A2[s] = gelu_value(total).astype(BF)
    wait_two = gather_plane(A2)
    for copy in sk_copies:
        copy.wait_recv()
    for a in range(2):
        for b in range(2):
            p = 2 * a + b
            for i in range(4):
                J[a, 1 + b, 64:128, 128 + 128 * i : 256 + 128 * i] = SK[i, :, p * 128 : p * 128 + 128]
    arrive(wait_two)

    for p in range(4):
        plane = dot_nn(m["WUT"][p * 64 : p * 64 + 64, :], A2[...].reshape(1024, 512))
        J[p // 2, 1 + p % 2, 0:64, 128:640] = plane.astype(BF)

    def fringe(up, down, send_down, keep_down, send_up, keep_up):
        below = remote(send_down, keep_down, lax.rem(h + 4, 16), y, down, down)
        above = remote(send_up, keep_up, lax.rem(h + 12, 16), y, up, up)

        @pl.when(z < 3)
        def _():
            below.start()

        @pl.when(z > 0)
        def _():
            above.start()

        started.append((below, z < 3))
        started.append((above, z > 0))

        def wait():
            @pl.when(z > 0)
            def _():
                below.wait_recv()

            @pl.when(z < 3)
            def _():
                above.wait_recv()

        return wait

    bj = reserve(2)
    wait_rows = fringe(
        bj,
        bj + 1,
        J.at[1, 1:3, :, 512:640],
        J.at[1, 1:3, :, 0:128],
        J.at[0, 1:3, :, 128:256],
        J.at[0, 1:3, :, 640:768],
    )

    def beside(a, i):
        at = slice(i * 128, i * 128 + 128)
        J[a, 0, :, at] = from_left(J[a, 2, :, at].astype(F32)).astype(BF)
        J[a, 3, :, at] = from_right(J[a, 1, :, at].astype(F32)).astype(BF)

    def joined_patches(outer):
        for a in range(2):
            for da in range(3):
                up, di = (a + da - 1) % 2, (a + da - 1) // 2
                first, last = 0, 4
                if di != 0:
                    edge = 0 if di < 0 else 3
                    first, last = (edge, edge + 1) if outer else (1, 4) if di < 0 else (0, 3)
                elif outer:
                    continue
                for b in range(2):
                    for db in range(3):
                        tap = da * 3 + db
                        at = 128 + (2 * a + b) * 512
                        X[tap * 128 : tap * 128 + 128, at + first * 128 : at + last * 128] = J[
                            up, b + db, :, (1 + di + first) * 128 : (1 + di + last) * 128
                        ]

    for a in range(2):
        for i in range(1, 5):
            beside(a, i)
    joined_patches(False)
    wait_rows()
    beside(1, 0)
    beside(0, 5)
    joined_patches(True)

    for j in range(4):
        t, half = j // 2, j % 2
        landed(W3.at[:, 64 * t : 64 * t + 64, 256 * half : 256 * half + 256], b3 + j)
    transposed(W3, m["W3T"], 128)
    P3b, T3, S3b, R3 = m["P3b"], m["T3"], m["S3b"], m["R3"]

    def plane_three(p):
        def step(n, carry):
            Z[0:512, span(n, 256)] = dot_nn(m["W3T"][...], X[:, patch_cols(n, 256)])
            return carry

        lax.fori_loop(2 * p, 2 * p + 2, step, 0)
        cols = slice(p * 512, p * 512 + 512)
        for k in range(4):
            P3b[p, k] = Z[span(2 * k + 1 - e, 64), cols].astype(BF)
        return push(P3b.at[p], T3.at[p], twin, y)

    def pair_three(p):
        pairs[p].wait_recv()
        cols = slice(p * 512, p * 512 + 512)
        for k in range(4):
            total = Z[span(2 * k + e, 64), cols] + T3[p, k].astype(F32)
            Z[span(2 * k + e, 64), cols] = total
            S3b[p, k] = total.astype(BF)
        three.append(scatter(S3b.at[p], R3.at[p]))

    pairs, three = [], []
    for p in range(4):
        pairs.append(plane_three(p))
        if p >= 1:
            pair_three(p - 1)
    pair_three(3)
    pre3, act3, LG = m["pre3"], m["act3"], m["LG"]
    wide = (64, LANE)
    turned = jnp.concatenate([fh[...], jnp.zeros((6, fh.shape[1]), F32)], axis=0).T
    m["HT"][...] = turned.astype(BF).astype(F32)
    head = m["HT"][span(slot, 64), :]
    h0 = jnp.broadcast_to(head[:, 0:1], wide)
    h1 = jnp.broadcast_to(head[:, 1:2], wide)
    for b in range(16):
        if b % 4 == 0:
            arrive(three[b // 4])
        cols = slice(b * 128, b * 128 + 128)
        part = slice(b % 4 * 128, b % 4 * 128 + 128)
        total = Z[span(s, 64), cols] + R3[b // 4, 0, :, part].astype(F32)
        total = total + R3[b // 4, 1, :, part].astype(F32) + R3[b // 4, 2, :, part].astype(F32)
        pre3[:, cols] = total
        act = gelu_value(total).astype(BF)
        act3[:, cols] = act
        act = act.astype(F32)
        LG[s, b : b + 1, :] = jnp.sum(act * h0, axis=0, keepdims=True)
        LG[s, 16 + b : 17 + b, :] = jnp.sum(act * h1, axis=0, keepdims=True)
    wait_logits = []
    for d in range(1, 8):
        there = lax.rem(s + d, 8)
        half = lax.div(there, 4)
        wait_logits.append(push(LG.at[s], LG.at[s], 4 * z + there - 4 * half, half))
    for copy in lab_copies:
        copy.wait_recv()
    LBL = m["LBL"]
    for p in range(4):
        for i in range(4):
            LBL[p * 4 + i : p * 4 + i + 1, :] = LB[4 * z + i, p : p + 1, :]
            LBL[16 + p * 4 + i : 17 + p * 4 + i, :] = LB[4 * z + i, 4 + p : 5 + p, :]
    every = jnp.sum(LB[...], axis=0)
    labelled = jnp.sum(jnp.sum(every[4:8, :], axis=0, keepdims=True), axis=1, keepdims=True)
    arrive(wait_logits)

    logits = LG[0]
    for k in range(1, 8):
        logits = logits + LG[k]
    zero, one = logits[0:16, :], logits[16:32, :]
    picks, usable = LBL[0:16, :] > 0.5, LBL[16:32, :]
    top = jnp.maximum(zero, one)
    lse = top + jnp.log(jnp.exp(zero - top) + jnp.exp(one - top))
    logp = jnp.where(picks, one, zero) - lse
    rest = jnp.exp(jnp.where(picks, zero, one) - lse)
    chance = jnp.exp(logp)
    gap = 1.0 - chance
    terms = usable * (-(gap * gap) * logp)
    slope = (2.0 * gap * chance * logp - gap * gap) * usable / labelled
    own, other = slope * gap, -slope * rest
    DL = m["DL"]
    DL[0:16, :] = jnp.where(picks, other, own).astype(BF).astype(F32)
    DL[16:32, :] = jnp.where(picks, own, other).astype(BF).astype(F32)
    loss = jnp.sum(jnp.sum(terms, axis=0, keepdims=True), axis=1, keepdims=True)
    G3, HD = m["G3"], m["HD"]
    planes = []
    sum0 = jnp.zeros(wide, F32)
    sum1 = jnp.zeros(wide, F32)
    for b in range(16):
        cols = slice(b * 128, b * 128 + 128)
        d0 = jnp.broadcast_to(DL[b : b + 1, :], wide)
        d1 = jnp.broadcast_to(DL[16 + b : 17 + b, :], wide)
        part = slice(b % 4 * 128, b % 4 * 128 + 128)
        G3[b // 4, s, :, part] = ((h0 * d0 + h1 * d1) * gelu_slope(pre3[:, cols])).astype(BF)
        act = act3[:, cols].astype(F32)
        sum0 = sum0 + act * d0
        sum1 = sum1 + act * d1
        if b % 4 == 3:
            planes.append(plane_sends(G3.at[b // 4]))
    side = lax.broadcasted_iota(jnp.int32, wide, 1)
    sum0 = jnp.sum(sum0, axis=1, keepdims=True)
    sum1 = jnp.sum(sum1, axis=1, keepdims=True)
    tile = jnp.where(side == 0, sum0, jnp.where(side == 1, sum1, 0.0))
    HD[h, 0:8, 0:64] = tile.T[0:8, :]
    HD[h, 2:3, 0:64] = jnp.broadcast_to(loss, (1, 64))
    hd_copies = []
    for d in range(1, 16):
        hd_copies.append(push(HD.at[h], HD.at[h], lax.rem(h + d, 16), y))

    HS, DB, DR = m["HS"], m["DB"], m["DR"]

    def back_three(p):
        grads = G3[p].reshape(512, 512)
        Z[0:576, p * 512 : p * 512 + 512] = dot_nn(W3[:, 0:64, :].reshape(576, 512), grads)

    GW3, GWU, GW2, GW1 = m["GW3"], m["GWU"], m["GW2"], m["GW1"]
    RG3, RGU, RG2, RG1 = m["RG3"], m["RGU"], m["RG2"], m["RG1"]

    def grad_three(p):
        def step(t, carry):
            part = dot_nt(X[span(t, 128), 128 + p * 512 : 640 + p * 512], G3[p].reshape(512, 512))
            rows = pl.ds(pl.multiple_of(576 + 128 * lax.div(t, 4), 64), 128)
            cols = span(lax.rem(t, 4), 512)
            if p > 0:
                part = part + Z[rows, cols]
            if p < 3:
                Z[rows, cols] = part
            else:
                GW3[t] = part.astype(BF)
            return carry

        lax.fori_loop(0, 9, step, 0)

    passes = plane_passes(G3.at[0], planes[0])
    for p in range(4):
        arrive(passes)
        back_three(p)
        if p < 3:
            passes = plane_passes(G3.at[p + 1], planes[p + 1])
            grad_three(p)
    def merge_home(first, last):
        for k in range(first, last):
            half, own = lax.rem(y + k // 2, 2), k < 2
            t = lax.rem(lax.div(z, 2) + 1 + k, 2)
            hand(
                GW3.at[:, span(t, 64), span(y, 256)] if own else m["Y3"].at[t],
                RG3.at[z],
                ha(2 * t + half, x, e),
                y,
                bg3 + k,
                bg3 + z,
            )

    ways = (((0, 0, 0), (1, -1, 0), (1, 1, 1)), ((0, -1, -1), (0, 1, 0), (1, 0, 0)))

    def raised_block(a, b, i):
        straight, bent = [], []
        for ao, da, di in ways[a]:
            io = i - di
            if io < 0 or io > 3 or (i < 0 or i > 3) and di == 0:
                continue
            for bo, db, dj in ways[b]:
                tap = (da + 1) * 3 + db + 1
                at = ((2 * ao + bo) * 4 + io) * 128
                (straight if dj == 0 else bent).append(Z[tap * 64 : tap * 64 + 64, at : at + 128])
        turned = sum(bent[1:], bent[0])
        turned = from_left(turned) if b == 0 else from_right(turned)
        return sum(straight, turned)

    for b in range(2):
        HS[0, b] = raised_block(0, b, 4)
        HS[1, b] = raised_block(1, b, -1)
    bh = reserve(2)
    wait_fringe = fringe(bh, bh + 1, HS.at[0], HR.at[0], HS.at[1], HR.at[1])
    for a in range(2):
        for b in range(2):
            p = 2 * a + b
            for i in range(4):
                block = raised_block(a, b, i)
                if i == 3 * a:
                    DB[p] = block
                else:
                    DR[p * 64 : p * 64 + 64, i * 128 : i * 128 + 128] = block.astype(BF)
    grad_three(3)
    bg3 = reserve(4)
    merge_home(0, 2)
    wait_fringe()
    for a in range(2):
        for b in range(2):
            p = 2 * a + b
            DR[p * 64 : p * 64 + 64, a * 384 : a * 384 + 128] = (DB[p] + HR[a, b]).astype(BF)

    P7b, T7, S7b, R7 = m["P7b"], m["T7"], m["S7b"], m["R7"]

    def back_up(k, carry):
        Z[span(k, 128), 0:512] = dot_nn(WU[pl.ds(2 * k, 2)].reshape(128, 256), DR[...])
        return carry

    lax.fori_loop(0, 8, back_up, 0)
    for k in range(4):
        P7b[k] = Z[span(2 * k + 1 - e, 128), 0:512].astype(BF)
    wait_pair = push(P7b, T7, twin, y)

    def pair_seven():
        for k in range(4):
            total = Z[span(2 * k + e, 128), 0:512] + T7[k].astype(F32)
            Z[span(2 * k + e, 128), 0:512] = total
            S7b[k] = total.astype(BF)

    wait_pair.wait_recv()
    pair_seven()
    wait_seven = scatter(S7b, R7)

    def grad_up(k, carry):
        GWU[pl.ds(2 * k, 2)] = dot_nt(A2[k], DR[...]).astype(BF).reshape(2, 64, 256)
        return carry

    Y3 = m["Y3"]
    other = 1 - y
    across = []
    for t in range(2):
        across.append(
            push(
                GW3.at[:, 64 * t : 64 * t + 64, span(other, 256)],
                Y3.at[t],
                h,
                other,
            )
        )

    lax.fori_loop(0, 8, grad_up, 0)
    patches(middle_block, 0, 16)
    patch_edges()
    arrive(wait_seven)
    G2 = m["G2"]
    total = Z[span(s, 128), 0:512] + R7[0].astype(F32)
    total = total + R7[1].astype(F32) + R7[2].astype(F32)
    G2[e, :, span(z, 512)] = (total * gelu_slope(pre2[...])).astype(BF)
    mine = G2.at[e, :, span(z, 512)]
    g2_copies = []
    for d in range(1, 4):
        zt = lax.rem(z + d, 4)
        g2_copies.append(push(mine, mine, ha(zt, x, e), y))
    own_pair = push(mine, mine, twin, y)
    gu_copies = []
    for d in range(1, 16):
        ht = lax.rem(h + d, 16)
        gu_copies.append(push(GWU.at[ht], RGU.at[h], ht, y))
    RGU[h] = GWU[h]

    def back_two(zs):
        for k in range(2):
            cols = pl.ds(pl.multiple_of(zs * 512 + k * 256, 256), 256)
            Z[:, cols] = dot_nn(W2[...].reshape(1152, 256), G2[:, :, cols].reshape(256, 256))

    def relay(d):
        g2_copies[d - 1].wait_recv()
        zs = lax.rem(z + 4 - d, 4)
        came = G2.at[e, :, span(zs, 512)]
        return zs, push(came, came, twin, y)

    zs, copy = relay(1)
    own_pair.wait_recv()
    back_two(z)
    arrive(across)
    merge_home(2, 4)
    for d in range(2, 4):
        after = relay(d)
        copy.wait_recv()
        back_two(zs)
        zs, copy = after
    copy.wait_recv()
    back_two(zs)
    P8b, R8, G1 = m["P8b"], m["R8"], m["G1"]
    P8 = m["P8"]

    def fold(i, carry):
        sums = []
        for dj in range(3):
            part = None
            for di in range(3):
                row = i - (di - 1)
                inside = jnp.logical_and(row >= 0, row <= 15)
                row = jnp.clip(row, 0, 15)
                tap = di * 3 + dj
                block = jnp.where(inside, Z[tap * 128 : tap * 128 + 128, span(row, 128)], 0.0)
                part = block if part is None else part + block
            sums.append(part)
        total = sums[1] + from_right(sums[0]) + from_left(sums[2])
        P8[:, span(i, 128)] = total
        P8b[:, :, span(i, 128)] = total.reshape(4, 32, 128).astype(BF)
        return carry

    wait_eight = []
    for c in range(2):
        lax.fori_loop(8 * c, 8 * c + 8, fold, 0)
        wait_eight.append(scatter(P8b, R8, halves[c]))

    def grad_two(t, carry):
        GW2[t] = dot_nt(X[span(t, 128), 128:2176], G2[...].reshape(256, 2048)).astype(BF)
        return carry

    lax.fori_loop(0, 9, grad_two, 0)

    def act_back(n, carry):
        cols = span(n, 512)
        total = P8[span(q, 32), cols] + R8[0, :, cols].astype(F32)
        total = total + R8[1, :, cols].astype(F32) + R8[2, :, cols].astype(F32)
        G1[q, :, cols] = (total * gelu_slope(P1[q, :, cols])).astype(BF)
        return carry

    wait_g1 = []
    for c in range(2):
        arrive(wait_eight[c])
        lax.fori_loop(2 * c, 2 * c + 2, act_back, 0)
        wait_g1 += gather_four(G1, halves[c])
    bg2 = reserve(2)
    for j in range(2):
        hand(
            GW2.at[:, 64 * j : 64 * j + 64, :],
            RG2.at[:, :, span(x, 256)],
            ha(z, e, j),
            y,
            bg2 + j,
            bg2 + x,
        )
    patches(input_block, 0, 16)
    patch_edges()
    arrive(wait_g1)

    def grad_one(t, carry):
        GW1[t] = dot_nt(X[span(t, 128), 128:2176], G1[...].reshape(128, 2048)).astype(BF)
        return carry

    lax.fori_loop(0, 9, grad_one, 0)
    bg1 = reserve(4)
    r_low = 2 * lax.rem(z, 2) + e
    for k in range(4):
        j = lax.rem(z + 1 + k, 4)
        hand(
            GW1.at[:, span(j, 32), :],
            RG1.at[:, :, span(r_low, 128)],
            ha(j, x, y),
            lax.div(z, 2),
            bg1 + k,
            bg1 + r_low,
        )

    for copy in hd_copies:
        copy.wait_recv()
    for j in range(4):
        hdo[j] = HD[j] + HD[4 + j] + HD[8 + j] + HD[12 + j]
    hdo[4] = jnp.broadcast_to(labelled, (8, 128))
    for k in range(4):
        landed(RG3.at[k], bg3 + k)
    for t in range(9):
        g3o[t] = (RG3[0, t].astype(F32) + RG3[1, t].astype(F32)) + (
            RG3[2, t].astype(F32) + RG3[3, t].astype(F32)
        )
    for copy in gu_copies:
        copy.wait_recv()
    sums = []
    for k in range(4):
        sums.append(
            (RGU[k].astype(F32) + RGU[4 + k].astype(F32))
            + (RGU[8 + k].astype(F32) + RGU[12 + k].astype(F32))
        )
    for p in range(4):
        guo[p] = jnp.concatenate([part[:, p * 64 : p * 64 + 64] for part in sums], axis=1)
    for k in range(2):
        landed(RG2.at[:, :, 256 * k : 256 * k + 256], bg2 + k)
    g2o[...] = RG2[...]
    for k in range(4):
        landed(RG1.at[:, :, 128 * k : 128 * k + 128], bg1 + k)
    g1o[...] = RG1[...]
    for copy, when in started:
        if when is None:
            copy.wait_send()
        else:
            pl.when(when)(copy.wait_send)


def resident_body(
    input_a,
    input_b,
    skip_a,
    skip_b,
    labels_a,
    labels_b,
    valid_a,
    valid_b,
    w_enter,
    moment_enter,
    square_enter,
    w_middle,
    moment_middle,
    square_middle,
    w_upward,
    moment_upward,
    square_upward,
    w_merge,
    moment_merge,
    square_merge,
    w_head,
    moment_head,
    square_head,
):
    vmem = pl.BlockSpec(memory_space=pltpu.VMEM)
    anywhere = pl.BlockSpec(memory_space=pl.ANY)
    g1, g2, gu, g3, hd = pl.pallas_call(
        lambda *refs: fused((input_a.shape[2], input_b.shape[2]), *refs),
        out_shape=(
            jax.ShapeDtypeStruct((9, 32, 512), BF),
            jax.ShapeDtypeStruct((9, 64, 512), BF),
            jax.ShapeDtypeStruct((4, 64, 256), F32),
            jax.ShapeDtypeStruct((9, 64, 256), F32),
            jax.ShapeDtypeStruct((5, 8, 128), F32),
        ),
        in_specs=[vmem] * 9 + [anywhere] * 3 + [vmem],
        out_specs=[vmem] * 5,
        scratch_shapes=[pltpu.VMEM(shape, kind) for _, shape, kind in SCRATCH]
        + [pltpu.SemaphoreType.DMA((COPIES,)), pltpu.SemaphoreType.DMA((COPIES,)), pltpu.SemaphoreType.DMA((3,))],
        compiler_params=pltpu.CompilerParams(
            collective_id=0, has_side_effects=True, vmem_limit_bytes=61 * 1024 * 1024
        ),
    )(
        input_a[0, 0],
        input_b[0, 0],
        skip_a[0],
        skip_b[0],
        labels_a[0],
        labels_b[0],
        valid_a[0],
        valid_b[0],
        w_enter.reshape(9, 32, 512),
        w_middle.reshape(9, 64, 512),
        w_upward.reshape(4, 64, 256),
        w_merge.reshape(9, 64, 256),
        w_head.T,
    )
    states = (
        (w_enter, moment_enter, square_enter),
        (w_middle, moment_middle, square_middle),
        (w_upward, moment_upward, square_upward),
        (w_merge, moment_merge, square_merge),
    )
    dims = tuple(g.shape for g in (g1, g2, gu, g3))
    flat = [part.reshape(dim) for dim, state in zip(dims, states) for part in state]
    rows = w_head.T.shape
    new = pl.pallas_call(
        updates,
        out_shape=tuple(
            jax.ShapeDtypeStruct(dim, kind) for dim in (*dims, rows) for kind in (F32, F32, F32, BF)
        )
        + (jax.ShapeDtypeStruct((1, 1), F32),) * 2,
        in_specs=[anywhere] * 16 + [vmem] * 4,
        out_specs=[anywhere] * 16 + [vmem] * 6,
        scratch_shapes=[
            pltpu.VMEM(dim, kind)
            for dim, g in zip(dims, (g1, g2, gu, g3))
            for kind in (g.dtype, F32, F32, F32, F32, F32, F32, BF)
        ]
        + [pltpu.SemaphoreType.DMA((len(PIECES), 8))],
        compiler_params=pltpu.CompilerParams(vmem_limit_bytes=62 * 1024 * 1024),
    )(g1, g2, gu, g3, *flat, hd, w_head.T, moment_head.T, square_head.T)
    shapes = (w_enter.shape, w_middle.shape, w_upward.shape, w_merge.shape)
    return (
        *[new[k].reshape(shapes[k // 4]) for k in range(16)],
        *[part.T for part in new[16:20]],
        new[20].reshape(()),
        new[21].reshape(()),
    )


PIECES = ((3, 0, 5), (3, 5, 9), (2, 0, 4), (1, 0, 3), (1, 3, 6), (1, 6, 9), (0, 0, 5), (0, 5, 9))


def adamw_step(master, moment, square, gradient):
    moment_new = BETA_ONE * moment + (1.0 - BETA_ONE) * gradient
    square_new = BETA_TWO * square + (1.0 - BETA_TWO) * gradient * gradient
    fixed_moment = moment_new * (RATE / (1.0 - BETA_ONE**STEP))
    fixed_square = square_new * (1.0 / (1.0 - BETA_TWO**STEP))
    master_new = (1.0 - RATE * DECAY) * master - fixed_moment / (jnp.sqrt(fixed_square) + EPSILON)
    return (master_new, moment_new, square_new, master_new.astype(BF))


def updates(*refs):
    grads, states = refs[0:4], refs[4:16]
    hd, head, moment, square = refs[16:20]
    outs, tiny, loss, labelled = refs[20:36], refs[36:40], refs[40], refs[41]
    held, sems = refs[42:74], refs[74]

    def copies(piece):
        k, first, last = PIECES[piece]
        at = slice(first, last)
        inward = [
            pltpu.make_async_copy(source.at[at], held[8 * k + j].at[at], sems.at[piece, j])
            for j, source in enumerate((grads[k], *states[3 * k : 3 * k + 3]))
        ]
        outward = [
            pltpu.make_async_copy(held[8 * k + 4 + j].at[at], outs[4 * k + j].at[at], sems.at[piece, 4 + j])
            for j in range(4)
        ]
        return inward, outward

    every = [copies(piece) for piece in range(len(PIECES))]
    for inward, _ in every:
        for copy in inward:
            copy.start()
    loss[...] = hd[0, 2:3, 0:1]
    labelled[...] = hd[4, 0:1, 0:1]
    gradient = jnp.concatenate([hd[j, 0:2, 0:64] for j in range(4)], axis=1)
    for ref, value in zip(tiny, adamw_step(head[...], moment[...], square[...], gradient)):
        ref[...] = value
    for (k, first, last), (inward, outward) in zip(PIECES, every):
        for copy in inward:
            copy.wait()
        own = held[8 * k : 8 * k + 8]

        def step(i, carry, own=own):
            made = adamw_step(own[1][i], own[2][i], own[3][i], own[0][i].astype(F32))
            for ref, value in zip(own[4:], made):
                ref[i] = value
            return carry

        lax.fori_loop(first, last, step, 0)
        for copy in outward:
            copy.start()
    for _, outward in every:
        for copy in outward:
            copy.wait()


def chosen(*args):
    input_a, input_b, skip_a = args[0], args[1], args[2]
    w_enter, w_middle, w_upward, w_merge = args[8], args[11], args[14], args[17]
    fits = (
        lax.axis_size("ha") == 16
        and lax.axis_size("col") == 2
        and input_a.shape[:2] == (1, 1)
        and input_b.shape[:2] == (1, 1)
        and input_a.shape[3] == 256
        and skip_a.shape[3] == 256
        and input_a.shape[2] + input_b.shape[2] <= LANE
        and w_enter.shape == (3, 3, 32, 512)
        and w_middle.shape == (3, 3, 64, 512)
        and w_upward.shape == (2, 2, 64, 256)
        and w_merge.shape == (3, 3, 64, 256)
    )
    return resident_body(*args) if fits else body(*args)


def solution(mesh):
    placed = (
        P(None, "ha", None, "col"),
        P(None, "ha", None, "col"),
        P(None, "ha", None, "col"),
        P(None, "ha", None, "col"),
        P(None, "ha", None),
        P(None, "ha", None),
        P(None, "ha", None),
        P(None, "ha", None),
        P(None, None, "ha", "col"),
        P(None, None, "ha", "col"),
        P(None, None, "ha", "col"),
        P(None, None, "ha", "col"),
        P(None, None, "ha", "col"),
        P(None, None, "ha", "col"),
        P(None, None, "ha", "col"),
        P(None, None, "ha", "col"),
        P(None, None, "ha", "col"),
        P(None, None, "ha", "col"),
        P(None, None, "ha", "col"),
        P(None, None, "ha", "col"),
        P("col", None),
        P("col", None),
        P("col", None),
    )
    return jax.shard_map(
        chosen,
        mesh=mesh,
        in_specs=placed,
        out_specs=(
            P(None, None, "ha", "col"),
            P(None, None, "ha", "col"),
            P(None, None, "ha", "col"),
            P(None, None, "ha", "col"),
            P(None, None, "ha", "col"),
            P(None, None, "ha", "col"),
            P(None, None, "ha", "col"),
            P(None, None, "ha", "col"),
            P(None, None, "ha", "col"),
            P(None, None, "ha", "col"),
            P(None, None, "ha", "col"),
            P(None, None, "ha", "col"),
            P(None, None, "ha", "col"),
            P(None, None, "ha", "col"),
            P(None, None, "ha", "col"),
            P(None, None, "ha", "col"),
            P("col", None),
            P("col", None),
            P("col", None),
            P("col", None),
            P(),
            P(),
        ),
        check_vma=False,
    )
```

```python
import jax
import jax.numpy as jnp
from jax import lax
from jax.experimental import pallas as pl
from jax.experimental.pallas import tpu as pltpu
from jax.sharding import PartitionSpec as P

STEP = 10


NUMBERS = ("NHWC", "HWIO", "NHWC")
BETA_ONE = 0.9
BETA_TWO = 0.95
RATE = 0.08
DECAY = 0.1
EPSILON = 1e-08


def extended(cells, sides, width):
    for axis, dim in sides:
        count = lax.axis_size(axis)
        ends = count - 1
        head = lax.slice_in_dim(cells, 0, width, axis=dim)
        tail = lax.slice_in_dim(cells, cells.shape[dim] - width, cells.shape[dim], axis=dim)
        cells = jnp.concatenate(
            [
                lax.ppermute(tail, axis, [(i, (i + 1) % count) for i in range(ends)]),
                cells,
                lax.ppermute(head, axis, [((i + 1) % count, i) for i in range(ends)]),
            ],
            axis=dim,
        )
    return cells


def shortened(value):

    def short(part):
        return part.astype(jnp.bfloat16) if part.dtype == jnp.float32 else part

    return jax.tree.map(short, value)


def convolve_rows(padded, weight):
    return lax.conv_general_dilated(
        padded,
        weight,
        (1, 1),
        ((0, 0), (1, 1)),
        dimension_numbers=NUMBERS,
        preferred_element_type=jnp.float32,
    )


def flipped(weight):
    return jnp.transpose(weight[::-1, ::-1], (0, 1, 3, 2))


def upsample(values, weight):
    product = jnp.einsum("nhwc,abcd->nhawbd", values, weight, preferred_element_type=jnp.float32)
    return product.reshape(
        product.shape[0], 2 * product.shape[1], 2 * product.shape[3], product.shape[5]
    )


def split_pixels(upstream):
    return upstream.reshape(
        upstream.shape[0], upstream.shape[1] // 2, 2, upstream.shape[2] // 2, 2, upstream.shape[3]
    )


def upsample_back(upstream, weight):
    return jnp.einsum(
        "nhawbd,abcd->nhwc", split_pixels(upstream), weight, preferred_element_type=jnp.float32
    )


def upsample_weight(values, upstream):
    return jnp.einsum(
        "nhwc,nhawbd->abcd", values, split_pixels(upstream), preferred_element_type=jnp.float32
    )


def tap_grads(padded, upstream):
    wide = jnp.pad(padded, ((0, 0), (0, 0), (1, 1), (0, 0)))
    height, across = (upstream.shape[1], upstream.shape[2])
    stacked = []
    for row_tap in range(3):
        tapline = []
        for col_tap in range(3):
            window = wide[:, row_tap : row_tap + height, col_tap : col_tap + across, :]
            tapline.append(
                jnp.einsum("nhwc,nhwd->cd", window, upstream, preferred_element_type=jnp.float32)
            )
        stacked.append(jnp.stack(tapline))
    return jnp.stack(stacked)


def alternate(weight, groups):
    dims = weight.shape
    shaped = weight.reshape(dims[0], dims[1], 2, groups, dims[2] // (2 * groups), dims[3])
    return shaped.transpose(0, 1, 3, 2, 4, 5).reshape(dims)


def deinterleave(weight, groups):
    dims = weight.shape
    shaped = weight.reshape(dims[0], dims[1], groups, 2, dims[2] // (2 * groups), dims[3])
    return shaped.transpose(0, 1, 3, 2, 4, 5).reshape(dims)


def gelu_back(pre_act, upstream):
    return jax.vjp(jax.nn.gelu, pre_act)[1](upstream)[0]


def focal(logits, labels, usable):
    logprob = jax.nn.log_softmax(logits, axis=-1)
    picked = jnp.where(labels == 1, logprob[..., 1], logprob[..., 0])
    chance = jnp.exp(picked)
    return jnp.sum(usable.astype(jnp.float32) * (-((1.0 - chance) ** 2) * picked))


def loss_terms(logits, labels, usable, labelled):
    running, pull = jax.vjp(lambda values: focal(values, labels, usable), logits)
    return (running, pull(1.0 / labelled)[0])


def gather_channels(values):
    return lax.all_gather(values, "col", axis=3, tiled=True)


def spread_back(partial_value):
    return lax.psum_scatter(partial_value, "col", scatter_dimension=3, tiled=True)


def conv_forward(local, weight):
    padded = extended(local, (("ha", 1),), 1)
    whole = gather_channels(padded)
    return (convolve_rows(whole, weight), whole)


def up_forward(local, weight):
    whole = gather_channels(local)
    return (upsample(whole, weight), whole)


def conv_weight_grad(kept, upstream):
    return tap_grads(kept, upstream)


def up_weight_grad(kept, upstream):
    return upsample_weight(kept, upstream)


def backward_weights(merge_up, upward, middle):
    return (flipped(merge_up), upward, flipped(middle))


def conv_input_grad(back_weight, upstream):
    padded = extended(shortened(upstream), (("ha", 1),), 1).astype(upstream.dtype)
    return spread_back(convolve_rows(padded, back_weight))


def up_input_grad(back_weight, upstream):
    return spread_back(upsample_back(upstream, back_weight))


def forward_pass(picture, skipped, copies):
    enter, middle, upward, merge_mixed, back_merge, back_upward, back_middle, head_copy = copies
    pre_one, kept_one = conv_forward(picture, enter)
    act_one = jax.nn.gelu(pre_one).astype(jnp.bfloat16)
    pre_two, kept_two = conv_forward(act_one, middle)
    act_two = jax.nn.gelu(pre_two).astype(jnp.bfloat16)
    raised, kept_up = up_forward(act_two, upward)
    joined = jnp.concatenate([raised.astype(jnp.bfloat16), skipped], axis=3)
    pre_three, kept_three = conv_forward(joined, merge_mixed)
    act_three = jax.nn.gelu(pre_three).astype(jnp.bfloat16)
    partial_value = jnp.einsum(
        "nhwc,ck->nhwk", act_three, head_copy, preferred_element_type=jnp.float32
    )
    return (
        partial_value,
        (pre_one, kept_one, pre_two, kept_two, kept_up, pre_three, kept_three, act_three),
    )


def backward_pass(saved, dlogits, copies):
    enter, middle, upward, merge_mixed, back_merge, back_upward, back_middle, head_copy = copies
    pre_one, kept_one, pre_two, kept_two, kept_up, pre_three, kept_three, act_three = saved
    back_three = jnp.einsum("nhwk,ck->nhwc", dlogits, head_copy, preferred_element_type=jnp.float32)
    grad_head = jnp.einsum("nhwc,nhwk->ck", act_three, dlogits, preferred_element_type=jnp.float32)
    grad_three = gelu_back(pre_three, back_three).astype(jnp.bfloat16)
    grad_merge = conv_weight_grad(kept_three, grad_three)
    d_raised = conv_input_grad(back_merge, grad_three).astype(jnp.bfloat16)
    grad_upward = up_weight_grad(kept_up, d_raised)
    back_two = up_input_grad(back_upward, d_raised)
    grad_two = gelu_back(pre_two, back_two).astype(jnp.bfloat16)
    grad_middle = conv_weight_grad(kept_two, grad_two)
    back_one = conv_input_grad(back_middle, grad_two)
    grad_one = gelu_back(pre_one, back_one).astype(jnp.bfloat16)
    grad_enter = conv_weight_grad(kept_one, grad_one)
    return (grad_enter, grad_middle, grad_upward, grad_merge, grad_head)


def adamw(master, moment, square, gradient):
    moment_new = BETA_ONE * moment + (1.0 - BETA_ONE) * gradient
    square_new = BETA_TWO * square + (1.0 - BETA_TWO) * gradient * gradient
    fixed_moment = moment_new / (1.0 - BETA_ONE**STEP)
    fixed_square = square_new / (1.0 - BETA_TWO**STEP)
    master_new = master - RATE * (
        fixed_moment / (jnp.sqrt(fixed_square) + EPSILON) + DECAY * master
    )
    return (master_new, moment_new, square_new, master_new.astype(jnp.bfloat16))


def own_rows(summed, local):
    return lax.dynamic_slice_in_dim(
        summed, lax.axis_index("ha") * local.shape[2], local.shape[2], 2
    )


def body(
    input_a,
    input_b,
    skip_a,
    skip_b,
    labels_a,
    labels_b,
    valid_a,
    valid_b,
    w_enter,
    moment_enter,
    square_enter,
    w_middle,
    moment_middle,
    square_middle,
    w_upward,
    moment_upward,
    square_upward,
    w_merge,
    moment_merge,
    square_merge,
    w_head,
    moment_head,
    square_head,
):
    groups = lax.axis_size("col")
    enter, middle, upward, merge = (
        lax.all_gather(w_enter.astype(jnp.bfloat16), "ha", axis=2, tiled=True),
        lax.all_gather(w_middle.astype(jnp.bfloat16), "ha", axis=2, tiled=True),
        lax.all_gather(w_upward.astype(jnp.bfloat16), "ha", axis=2, tiled=True),
        lax.all_gather(w_merge.astype(jnp.bfloat16), "ha", axis=2, tiled=True),
    )
    head_low = w_head.astype(jnp.bfloat16)
    merge_up = merge[:, :, : merge.shape[2] // 2]
    back_merge, back_upward, back_middle = backward_weights(merge_up, upward, middle)
    copies = (
        enter,
        middle,
        upward,
        alternate(merge, groups),
        back_merge,
        back_upward,
        back_middle,
        head_low,
    )
    labelled = lax.psum(
        jnp.sum(valid_a.astype(jnp.float32)) + jnp.sum(valid_b.astype(jnp.float32)), "ha"
    )
    partial_a, saved_a = forward_pass(input_a, skip_a, copies)
    partial_b, saved_b = forward_pass(input_b, skip_b, copies)
    logits_a, logits_b = lax.psum((partial_a, partial_b), "col")
    loss_a, dlogits_a = loss_terms(logits_a, labels_a, valid_a, labelled)
    loss_b, dlogits_b = loss_terms(logits_b, labels_b, valid_b, labelled)
    grads_a = backward_pass(saved_a, dlogits_a.astype(jnp.bfloat16), copies)
    grads_b = backward_pass(saved_b, dlogits_b.astype(jnp.bfloat16), copies)
    local_enter = grads_a[0] + grads_b[0]
    local_middle = grads_a[1] + grads_b[1]
    local_upward = grads_a[2] + grads_b[2]
    local_merge = deinterleave(grads_a[3] + grads_b[3], groups)
    local_head = grads_a[4] + grads_b[4]
    local_loss = loss_a + loss_b
    full_enter, full_middle, full_upward, full_merge, head_total, loss_total = (
        lax.psum(local_enter.astype(jnp.bfloat16), "ha").astype(jnp.float32),
        lax.psum(local_middle.astype(jnp.bfloat16), "ha").astype(jnp.float32),
        lax.psum(local_upward.astype(jnp.bfloat16), "ha").astype(jnp.float32),
        lax.psum(local_merge.astype(jnp.bfloat16), "ha").astype(jnp.float32),
        lax.psum(local_head.astype(jnp.bfloat16), "ha").astype(jnp.float32),
        lax.psum(local_loss.astype(jnp.bfloat16), "ha").astype(jnp.float32),
    )
    grad_enter = own_rows(full_enter, w_enter)
    grad_middle = own_rows(full_middle, w_middle)
    grad_upward = own_rows(full_upward, w_upward)
    grad_merge = own_rows(full_merge, w_merge)
    enter_out = adamw(w_enter, moment_enter, square_enter, grad_enter)
    middle_out = adamw(w_middle, moment_middle, square_middle, grad_middle)
    upward_out = adamw(w_upward, moment_upward, square_upward, grad_upward)
    merge_out = adamw(w_merge, moment_merge, square_merge, grad_merge)
    head_out = adamw(w_head, moment_head, square_head, head_total)
    return (
        enter_out[0],
        enter_out[1],
        enter_out[2],
        enter_out[3],
        middle_out[0],
        middle_out[1],
        middle_out[2],
        middle_out[3],
        upward_out[0],
        upward_out[1],
        upward_out[2],
        upward_out[3],
        merge_out[0],
        merge_out[1],
        merge_out[2],
        merge_out[3],
        head_out[0],
        head_out[1],
        head_out[2],
        head_out[3],
        loss_total,
        labelled,
    )


BF = jnp.bfloat16
F32 = jnp.float32
MESH = pl.DeviceIdType.MESH
LANE = 128
PI_PART = 0.7978845608028654
CUBE = 0.044715


def gelu_value(v):
    return 0.5 * v * (1.0 + jnp.tanh(PI_PART * (v + CUBE * (v * v * v))))


def gelu_slope(v):
    bent = jnp.tanh(PI_PART * (v + CUBE * (v * v * v)))
    inner = PI_PART * (1.0 + 3.0 * CUBE * (v * v))
    return 0.5 * (1.0 + bent) + 0.5 * v * (1.0 - bent * bent) * inner


def dot_nn(lhs, rhs):
    return lax.dot_general(lhs, rhs, (((1,), (0,)), ((), ())), preferred_element_type=F32)


def dot_nt(lhs, rhs):
    return lax.dot_general(lhs, rhs, (((1,), (1,)), ((), ())), preferred_element_type=F32)


def span(at, size):
    return pl.ds(pl.multiple_of(at * size, size), size)


SCRATCH = (
    ("inT", (2, 4, 32, 128), BF),
    ("skT", (4, 64, 512), BF),
    ("lab", (8, 128), F32),
    ("F2", (9, 64, 512), F32),
    ("F3", (9, 64, 256), F32),
    ("FU", (4, 64, 256), F32),
    ("flat", (4, 256, 128), F32),
    ("w1", (9, 32, 512), BF),
    ("S1", (9, 32, 512), BF),
    ("w2", (9, 64, 512), BF),
    ("wu", (4, 64, 256), BF),
    ("w3", (9, 64, 256), BF),
    ("IN", (8, 2, 4, 32, 128), BF),
    ("SK", (4, 64, 512), BF),
    ("LB", (16, 8, 128), F32),
    ("W1", (9, 128, 128), BF),
    ("W2", (9, 128, 256), BF),
    ("WU", (16, 64, 256), BF),
    ("W3", (9, 128, 512), BF),
    ("W1T", (128, 1152), BF),
    ("W2T", (256, 1152), BF),
    ("WUT", (256, 1024), BF),
    ("W3T", (512, 1152), BF),
    ("X", (1152, 2304), BF),
    ("P1", (4, 32, 2048), F32),
    ("P1b", (4, 32, 2048), BF),
    ("R1", (3, 32, 2048), BF),
    ("A1", (4, 32, 2048), BF),
    ("P2b", (4, 128, 512), BF),
    ("T2", (4, 128, 512), BF),
    ("S2b", (3, 128, 512), BF),
    ("R2", (3, 128, 512), BF),
    ("pre2", (128, 512), F32),
    ("A2", (8, 128, 512), BF),
    ("J", (2, 4, 128, 768), BF),
    ("P3b", (4, 4, 64, 512), BF),
    ("T3", (4, 4, 64, 512), BF),
    ("S3b", (4, 4, 64, 512), BF),
    ("R3", (4, 3, 64, 512), BF),
    ("pre3", (64, 2048), F32),
    ("act3", (64, 2048), BF),
    ("LG", (8, 32, 128), F32),
    ("LBL", (32, 128), F32),
    ("HT", (256, 8), F32),
    ("DL", (32, 128), F32),
    ("G3", (4, 8, 64, 512), BF),
    ("Z", (1152, 2048), F32),
    ("HS", (2, 2, 64, 128), F32),
    ("HR", (2, 2, 64, 128), F32),
    ("DB", (4, 64, 128), F32),
    ("DR", (256, 512), BF),
    ("P8", (128, 2048), F32),
    ("P7b", (4, 128, 512), BF),
    ("T7", (4, 128, 512), BF),
    ("S7b", (4, 128, 512), BF),
    ("R7", (3, 128, 512), BF),
    ("G2", (2, 128, 2048), BF),
    ("P8b", (4, 32, 2048), BF),
    ("R8", (3, 32, 2048), BF),
    ("G1", (4, 32, 2048), BF),
    ("GW3", (9, 128, 512), BF),
    ("GWU", (16, 64, 256), BF),
    ("GW2", (9, 128, 256), BF),
    ("GW1", (9, 128, 128), BF),
    ("RG3", (4, 9, 64, 256), BF),
    ("Y3", (2, 9, 64, 256), BF),
    ("RGU", (16, 64, 256), BF),
    ("RG2", (9, 64, 512), BF),
    ("RG1", (9, 32, 512), BF),
    ("HD", (16, 8, 128), F32),
)
COPIES = 224


def fused(widths, *refs):
    wa, wb = widths
    rows_a, rows_b, skip_a, skip_b, la, lb, va, vb, f1, f2, fu, f3, fh = refs[:13]
    g1o, g2o, guo, g3o, hdo = refs[13:18]
    m = {name: ref for (name, _, _), ref in zip(SCRATCH, refs[18:-3])}
    send_sem, recv_sem, load_sem = refs[-3:]
    loads = [
        pltpu.make_async_copy(source, m[name], load_sem.at[n])
        for n, (source, name) in enumerate(((f2, "F2"), (f3, "F3"), (fu, "FU")))
    ]
    for load in loads:
        load.start()
    f2, f3, fu = m["F2"], m["F3"], m["FU"]
    h, y = lax.axis_index("ha"), lax.axis_index("col")
    z, x, e = lax.div(h, 4), lax.rem(lax.div(h, 2), 2), lax.rem(h, 2)
    q = 2 * y + x
    s = 2 * q + e
    twin = h + 1 - 2 * e
    entered = pltpu.get_barrier_semaphore()
    for d in range(16):
        for side in (y, 1 - y)[0 if d else 1 :]:
            pl.semaphore_signal(
                entered,
                inc=1,
                device_id={"ha": lax.rem(h + d, 16), "col": side},
                device_id_type=MESH,
            )
    started = []
    count = [0]

    def ha(z_, x_, e_):
        return 4 * z_ + 2 * x_ + e_

    def remote(src, dst, h2, y2, sem_s, sem_r):
        return pltpu.make_async_remote_copy(
            src_ref=src,
            dst_ref=dst,
            send_sem=send_sem.at[sem_s],
            recv_sem=recv_sem.at[sem_r],
            device_id={"ha": h2, "col": y2},
            device_id_type=MESH,
        )

    def push(src, dst, h2, y2):
        n = count[0]
        count[0] += 1
        copy = remote(src, dst, h2, y2, n, n)
        copy.start()
        started.append((copy, None))
        return copy

    def reserve(n):
        base = count[0]
        count[0] += n
        return base

    def hand(src, dst, h2, y2, sem_s, sem_r, needed=None):
        same = jnp.logical_and(h2 == h, y2 == y)
        away = jnp.logical_not(same)
        if needed is not None:
            same = jnp.logical_and(same, needed)
            away = jnp.logical_and(away, needed)
        copy = remote(src, dst, h2, y2, sem_s, sem_r)

        @pl.when(same)
        def _():
            pltpu.make_async_copy(src, dst, recv_sem.at[sem_r]).start()

        @pl.when(away)
        def _():
            copy.start()

        started.append((copy, away))

    def landed(dst, sem_r):
        remote(dst, dst, twin, y, sem_r, sem_r).wait_recv()

    lanes = lax.broadcasted_iota(jnp.int32, (1, LANE), 1)
    left_ok = jnp.logical_and(jnp.logical_and(lanes != 0, lanes != wa), lanes < wa + wb)
    right_ok = jnp.logical_and(lanes != wa - 1, lanes < wa + wb - 1)

    def from_left(v):
        return jnp.where(left_ok, pltpu.roll(v, 1, 1), 0.0)

    def from_right(v):
        return jnp.where(right_ok, pltpu.roll(v, LANE - 1, 1), 0.0)

    J, HR = m["J"], m["HR"]

    @pl.when(z == 0)
    def _():
        J[1, 1:3, :, 0:128] = jnp.zeros((2, 128, 128), BF)
        HR[0] = jnp.zeros((2, 64, 128), F32)

    @pl.when(z == 3)
    def _():
        J[0, 1:3, :, 640:768] = jnp.zeros((2, 128, 128), BF)
        HR[1] = jnp.zeros((2, 64, 128), F32)

    inT, skT, lab, flat = m["inT"], m["skT"], m["lab"], m["flat"]
    w1, w2, wu, w3 = m["w1"], m["w2"], m["wu"], m["w3"]
    wide_a, wide_b = 2 * wa, 2 * wb
    for c in range(2):
        half = slice(c * 128, c * 128 + 128)
        flat[c, 96:128, :] = jnp.zeros((32, 128), F32)
        flat[c, 0:wa, :] = rows_a[:, half].astype(F32)
        flat[c, wa : wa + wb, :] = rows_b[:, half].astype(F32)
        inT[c] = flat[c, 0:128, :].T.astype(BF).reshape(4, 32, 128)

    w1[...] = f1[...].astype(BF)
    pl.semaphore_wait(entered, 31)

    IN, LB = m["IN"], m["LB"]
    W1, W2, WU, W3 = m["W1"], m["W2"], m["WU"], m["W3"]
    S1 = m["S1"]
    near = e == y
    b1 = reserve(4)
    b1s = reserve(5)
    over = remote(w1, S1, h, 1 - y, b1s + 4, b1s + 4)

    @pl.when(jnp.logical_not(near))
    def _():
        over.start()

    started.append((over, jnp.logical_not(near)))

    def spread_first(shard, half, base):
        for k in range(4):
            i = lax.rem(k + 2 * lax.rem(z, 2), 4)
            hand(
                shard.at[:, :, span(i, 128)],
                W1.at[:, span(z, 32), :],
                ha(2 * half + lax.div(i, 2), x, lax.rem(i, 2)),
                e,
                base + k,
                b1 + z,
                near,
            )

    in_copies = []
    for dz in range(4):
        zt = lax.rem(z + dz, 4)
        for d in range(4):
            if dz == 0 and d == 0:
                continue
            there = lax.rem(2 * x + y + d, 4)
            in_copies.append(
                push(
                    inT.at[:, there],
                    IN.at[2 * z + x, e, pl.ds(2 * y, 2)],
                    ha(zt, lax.div(there, 2), e),
                    lax.rem(there, 2),
                )
            )
    IN[2 * z + x, e, pl.ds(2 * y, 2)] = inT[:, 2 * x + y]

    spread_first(w1, y, b1)
    place = lax.broadcasted_iota(jnp.int32, (256, LANE), 0)
    lane = lax.broadcasted_iota(jnp.int32, (256, LANE), 1)
    spread = jnp.concatenate(
        [
            jnp.concatenate([first[...], second[...]], axis=1).astype(F32)
            for first, second in ((la, lb), (va, vb))
        ],
        axis=0,
    )
    spread = jnp.pad(spread, ((0, 4), (0, 256 - wide_a - wide_b)))
    for b in range(2):
        pick = jnp.where(place == 2 * lane + b, 1.0, 0.0)
        planes = dot_nn(spread.astype(BF), pick.astype(BF))
        for a in range(2):
            lab[2 * a + b : 2 * a + b + 1, :] = planes[a : a + 1, :]
            lab[4 + 2 * a + b : 5 + 2 * a + b, :] = planes[2 + a : 3 + a, :]
    lab_copies = []
    LB[h] = lab[...]
    for d in range(1, 16):
        lab_copies.append(push(lab, LB.at[h], lax.rem(h + d, 16), y))


    @pl.when(near)
    def _():
        over.wait_recv()

    spread_first(S1, 1 - y, b1s)
    for copy in in_copies:
        copy.wait_recv()
    twin_in = push(IN.at[:, e], IN.at[:, e], twin, y)

    for load in loads:
        load.wait()
    w2[...] = f2[...].astype(BF)
    w3[...] = f3[...].astype(BF)
    for k in range(4):
        wu[k] = jnp.concatenate([fu[p, :, k * 64 : k * 64 + 64] for p in range(4)], axis=1).astype(BF)
    for a in range(2):
        for c in range(2):
            half = slice(c * 128, c * 128 + 128)
            buf = flat.at[2 * a + c]
            buf[224:256, :] = jnp.zeros((32, 128), F32)
            buf[0:wide_a, :] = skip_a[a, :, half].astype(F32)
            buf[wide_a : wide_a + wide_b, :] = skip_b[a, :, half].astype(F32)
            for b in range(2):
                p = 2 * a + b
                plane = buf[pl.ds(b, 128, stride=2), :]
                skT[2 * c : 2 * c + 2, :, p * 128 : p * 128 + 128] = plane.T.astype(BF).reshape(2, 64, 128)
    b2 = reserve(2)
    for i in range(2):
        hand(
            w2.at[:, :, i * 256 : i * 256 + 256],
            W2.at[:, span(e, 64), :],
            ha(z, i, x),
            y,
            b2 + i,
            b2 + e,
        )
    SK = m["SK"]
    sk_copies = []
    slot = 2 * x + e
    for d in range(1, 4):
        other = lax.rem(slot + d, 4)
        sk_copies.append(push(skT.at[other], SK.at[slot], 4 * z + other, y))
    SK[slot] = skT[slot]
    bu_copies = []
    for d in range(1, 16):
        ht = lax.rem(h + d, 16)
        bu_copies.append(push(wu.at[lax.rem(ht, 4)], WU.at[h], ht, y))
    WU[h] = wu[slot]
    b3 = reserve(4)
    for i in range(4):
        hand(
            w3,
            W3.at[:, span(lax.div(z, 2), 64), span(y, 256)],
            ha(lax.rem(z + i, 4), x, e),
            lax.rem(z, 2),
            b3 + i,
            b3 + 2 * lax.div(z, 2) + y,
        )

    X = m["X"]

    def patch_edges():
        zero = jnp.zeros((384, 128), BF)
        X[0:384, 128:256] = zero
        X[768:1152, 2048:2176] = zero

    def patches(block, first, last):
        def one(i, carry):
            low = block(i)
            v = low.astype(F32)
            kinds = (from_left(v).astype(BF), low, from_right(v).astype(BF))
            for di in (-1, 0, 1):
                for dj in range(3):
                    tap = (di + 1) * 3 + dj
                    X[tap * 128 : tap * 128 + 128, span(i - di + 1, 128)] = kinds[dj]
            return carry

        lax.fori_loop(first, last, one, 0)

    def patch_cols(at, size):
        return pl.ds(pl.multiple_of(at * size + 128, 128), size)

    def transposed(weight, out, rows):
        for t in range(weight.shape[0]):
            out[:, t * rows : t * rows + rows] = weight[t].T

    for j in range(4):
        landed(W1.at[:, 32 * j : 32 * j + 32, :], b1 + j)
    transposed(W1, m["W1T"], 128)
    twin_in.wait_recv()

    def input_block(i):
        return IN[lax.div(i, 2), lax.rem(i, 2)].reshape(128, 128)

    def middle_block(i):
        return A1[:, :, span(i, 128)].reshape(128, 128)

    patches(input_block, 0, 16)
    patch_edges()
    P1, P1b, R1, A1 = m["P1"], m["P1b"], m["R1"], m["A1"]

    def conv_one(n, carry):
        cols = span(n, 512)
        total = dot_nn(m["W1T"][...], X[:, patch_cols(n, 512)]).reshape(4, 32, 512)
        P1[:, :, cols] = total
        P1b[:, :, cols] = total.astype(BF)
        return carry

    def to_plane(d):
        there = lax.rem(q + d, 4)
        return there, ha(z, lax.rem(there, 2), e), lax.div(there, 2)

    def scatter(source, slots, cols=slice(None)):
        copies = []
        for d in range(1, 4):
            there, h2, y2 = to_plane(d)
            copies.append(push(source.at[there, :, cols], slots.at[d - 1, :, cols], h2, y2))
        return copies

    def gather_four(buf, cols):
        copies = []
        for d in range(1, 4):
            _, h2, y2 = to_plane(d)
            copies.append(push(buf.at[q, :, cols], buf.at[q, :, cols], h2, y2))
        return copies

    halves = (slice(0, 1024), slice(1024, 2048))

    def plane_sends(buf):
        copies = []
        for d in range(1, 4):
            _, h2, y2 = to_plane(d)
            copies.append(push(buf.at[s], buf.at[s], h2, y2))
        return copies, push(buf.at[s], buf.at[s], twin, y)

    def plane_passes(buf, sends):
        copies, own = sends
        last = [own]
        for d in range(1, 4):
            copies[d - 1].wait_recv()
            came = 2 * lax.rem(q + 4 - d, 4) + e
            last.append(push(buf.at[came], buf.at[came], twin, y))
        return last

    def gather_plane(buf):
        return plane_passes(buf, plane_sends(buf))

    def arrive(copies):
        for copy in copies:
            copy.wait_recv()

    one_out = []
    for c in range(2):
        lax.fori_loop(2 * c, 2 * c + 2, conv_one, 0)
        one_out.append(scatter(P1b, R1, halves[c]))

    def act_one(n, carry):
        cols = span(n, 512)
        total = P1[q, :, cols] + R1[0, :, cols].astype(F32)
        total = total + R1[1, :, cols].astype(F32) + R1[2, :, cols].astype(F32)
        P1[q, :, cols] = total
        A1[q, :, cols] = gelu_value(total).astype(BF)
        return carry

    wait_one = []
    for c in range(2):
        arrive(one_out[c])
        lax.fori_loop(2 * c, 2 * c + 2, act_one, 0)
        wait_one.append(gather_four(A1, halves[c]))
    for j in range(2):
        landed(W2.at[:, 64 * j : 64 * j + 64, :], b2 + j)
    transposed(W2, m["W2T"], 128)

    for c in range(2):
        arrive(wait_one[c])
        patches(middle_block, 8 * c, 8 * c + 8)
    patch_edges()
    Z, P2b, T2, S2b, R2 = m["Z"], m["P2b"], m["T2"], m["S2b"], m["R2"]

    def band_two(k):
        zt = lax.rem(z + 1 + k, 4)
        Z[0:256, span(zt, 512)] = dot_nn(m["W2T"][...], X[:, patch_cols(zt, 512)])
        P2b[k] = Z[span(1 - e, 128), span(zt, 512)].astype(BF)
        return push(P2b.at[k], T2.at[k], twin, y)

    def pair_two(k):
        zt = lax.rem(z + 1 + k, 4)
        pairs[k].wait_recv()
        S2b[k] = (Z[span(e, 128), span(zt, 512)] + T2[k].astype(F32)).astype(BF)
        two.append(push(S2b.at[k], R2.at[k], ha(zt, x, e), y))

    pairs, two = [], []
    for k in range(4):
        pairs.append(band_two(k))
        if k >= 1:
            pair_two(k - 1)
    for d in range(1, 16):
        bu_copies[d - 1].wait_recv()
    for t in range(8):
        m["WUT"][:, t * 128 : t * 128 + 128] = WU[2 * t : 2 * t + 2].reshape(128, 256).T
    arrive(two)
    pre2, A2 = m["pre2"], m["A2"]
    pairs[3].wait_recv()
    total = Z[span(e, 128), span(z, 512)] + T2[3].astype(F32) + R2[0].astype(F32)
    total = total + R2[1].astype(F32) + R2[2].astype(F32)
    pre2[...] = total
    A2[s] = gelu_value(total).astype(BF)
    wait_two = gather_plane(A2)
    for copy in sk_copies:
        copy.wait_recv()
    for a in range(2):
        for b in range(2):
            p = 2 * a + b
            for i in range(4):
                J[a, 1 + b, 64:128, 128 + 128 * i : 256 + 128 * i] = SK[i, :, p * 128 : p * 128 + 128]
    arrive(wait_two)

    for p in range(4):
        plane = dot_nn(m["WUT"][p * 64 : p * 64 + 64, :], A2[...].reshape(1024, 512))
        J[p // 2, 1 + p % 2, 0:64, 128:640] = plane.astype(BF)

    def fringe(up, down, send_down, keep_down, send_up, keep_up):
        below = remote(send_down, keep_down, lax.rem(h + 4, 16), y, down, down)
        above = remote(send_up, keep_up, lax.rem(h + 12, 16), y, up, up)

        @pl.when(z < 3)
        def _():
            below.start()

        @pl.when(z > 0)
        def _():
            above.start()

        started.append((below, z < 3))
        started.append((above, z > 0))

        def wait():
            @pl.when(z > 0)
            def _():
                below.wait_recv()

            @pl.when(z < 3)
            def _():
                above.wait_recv()

        return wait

    bj = reserve(2)
    wait_rows = fringe(
        bj,
        bj + 1,
        J.at[1, 1:3, :, 512:640],
        J.at[1, 1:3, :, 0:128],
        J.at[0, 1:3, :, 128:256],
        J.at[0, 1:3, :, 640:768],
    )

    def beside(a, i):
        at = slice(i * 128, i * 128 + 128)
        J[a, 0, :, at] = from_left(J[a, 2, :, at].astype(F32)).astype(BF)
        J[a, 3, :, at] = from_right(J[a, 1, :, at].astype(F32)).astype(BF)

    def joined_patches(outer):
        for a in range(2):
            for da in range(3):
                up, di = (a + da - 1) % 2, (a + da - 1) // 2
                first, last = 0, 4
                if di != 0:
                    edge = 0 if di < 0 else 3
                    first, last = (edge, edge + 1) if outer else (1, 4) if di < 0 else (0, 3)
                elif outer:
                    continue
                for b in range(2):
                    for db in range(3):
                        tap = da * 3 + db
                        at = 128 + (2 * a + b) * 512
                        X[tap * 128 : tap * 128 + 128, at + first * 128 : at + last * 128] = J[
                            up, b + db, :, (1 + di + first) * 128 : (1 + di + last) * 128
                        ]

    for a in range(2):
        for i in range(1, 5):
            beside(a, i)
    joined_patches(False)
    wait_rows()
    beside(1, 0)
    beside(0, 5)
    joined_patches(True)

    for j in range(4):
        t, half = j // 2, j % 2
        landed(W3.at[:, 64 * t : 64 * t + 64, 256 * half : 256 * half + 256], b3 + j)
    transposed(W3, m["W3T"], 128)
    P3b, T3, S3b, R3 = m["P3b"], m["T3"], m["S3b"], m["R3"]

    def plane_three(p):
        def step(n, carry):
            Z[0:512, span(n, 256)] = dot_nn(m["W3T"][...], X[:, patch_cols(n, 256)])
            return carry

        lax.fori_loop(2 * p, 2 * p + 2, step, 0)
        cols = slice(p * 512, p * 512 + 512)
        for k in range(4):
            P3b[p, k] = Z[span(2 * k + 1 - e, 64), cols].astype(BF)
        return push(P3b.at[p], T3.at[p], twin, y)

    def pair_three(p):
        pairs[p].wait_recv()
        cols = slice(p * 512, p * 512 + 512)
        for k in range(4):
            total = Z[span(2 * k + e, 64), cols] + T3[p, k].astype(F32)
            Z[span(2 * k + e, 64), cols] = total
            S3b[p, k] = total.astype(BF)
        three.append(scatter(S3b.at[p], R3.at[p]))

    pairs, three = [], []
    for p in range(4):
        pairs.append(plane_three(p))
        if p >= 1:
            pair_three(p - 1)
    pair_three(3)
    pre3, act3, LG = m["pre3"], m["act3"], m["LG"]
    wide = (64, LANE)
    turned = jnp.concatenate([fh[...], jnp.zeros((6, fh.shape[1]), F32)], axis=0).T
    m["HT"][...] = turned.astype(BF).astype(F32)
    head = m["HT"][span(slot, 64), :]
    h0 = jnp.broadcast_to(head[:, 0:1], wide)
    h1 = jnp.broadcast_to(head[:, 1:2], wide)
    for b in range(16):
        if b % 4 == 0:
            arrive(three[b // 4])
        cols = slice(b * 128, b * 128 + 128)
        part = slice(b % 4 * 128, b % 4 * 128 + 128)
        total = Z[span(s, 64), cols] + R3[b // 4, 0, :, part].astype(F32)
        total = total + R3[b // 4, 1, :, part].astype(F32) + R3[b // 4, 2, :, part].astype(F32)
        pre3[:, cols] = total
        act = gelu_value(total).astype(BF)
        act3[:, cols] = act
        act = act.astype(F32)
        LG[s, b : b + 1, :] = jnp.sum(act * h0, axis=0, keepdims=True)
        LG[s, 16 + b : 17 + b, :] = jnp.sum(act * h1, axis=0, keepdims=True)
    wait_logits = []
    for d in range(1, 8):
        there = lax.rem(s + d, 8)
        half = lax.div(there, 4)
        wait_logits.append(push(LG.at[s], LG.at[s], 4 * z + there - 4 * half, half))
    for copy in lab_copies:
        copy.wait_recv()
    LBL = m["LBL"]
    for p in range(4):
        for i in range(4):
            LBL[p * 4 + i : p * 4 + i + 1, :] = LB[4 * z + i, p : p + 1, :]
            LBL[16 + p * 4 + i : 17 + p * 4 + i, :] = LB[4 * z + i, 4 + p : 5 + p, :]
    every = jnp.sum(LB[...], axis=0)
    labelled = jnp.sum(jnp.sum(every[4:8, :], axis=0, keepdims=True), axis=1, keepdims=True)
    arrive(wait_logits)

    logits = LG[0]
    for k in range(1, 8):
        logits = logits + LG[k]
    zero, one = logits[0:16, :], logits[16:32, :]
    picks, usable = LBL[0:16, :] > 0.5, LBL[16:32, :]
    top = jnp.maximum(zero, one)
    lse = top + jnp.log(jnp.exp(zero - top) + jnp.exp(one - top))
    logp = jnp.where(picks, one, zero) - lse
    rest = jnp.exp(jnp.where(picks, zero, one) - lse)
    chance = jnp.exp(logp)
    gap = 1.0 - chance
    terms = usable * (-(gap * gap) * logp)
    slope = (2.0 * gap * chance * logp - gap * gap) * usable / labelled
    own, other = slope * gap, -slope * rest
    DL = m["DL"]
    DL[0:16, :] = jnp.where(picks, other, own).astype(BF).astype(F32)
    DL[16:32, :] = jnp.where(picks, own, other).astype(BF).astype(F32)
    loss = jnp.sum(jnp.sum(terms, axis=0, keepdims=True), axis=1, keepdims=True)
    G3, HD = m["G3"], m["HD"]
    planes = []
    sum0 = jnp.zeros(wide, F32)
    sum1 = jnp.zeros(wide, F32)
    for b in range(16):
        cols = slice(b * 128, b * 128 + 128)
        d0 = jnp.broadcast_to(DL[b : b + 1, :], wide)
        d1 = jnp.broadcast_to(DL[16 + b : 17 + b, :], wide)
        part = slice(b % 4 * 128, b % 4 * 128 + 128)
        G3[b // 4, s, :, part] = ((h0 * d0 + h1 * d1) * gelu_slope(pre3[:, cols])).astype(BF)
        act = act3[:, cols].astype(F32)
        sum0 = sum0 + act * d0
        sum1 = sum1 + act * d1
        if b % 4 == 3:
            planes.append(plane_sends(G3.at[b // 4]))
    side = lax.broadcasted_iota(jnp.int32, wide, 1)
    sum0 = jnp.sum(sum0, axis=1, keepdims=True)
    sum1 = jnp.sum(sum1, axis=1, keepdims=True)
    tile = jnp.where(side == 0, sum0, jnp.where(side == 1, sum1, 0.0))
    HD[h, 0:8, 0:64] = tile.T[0:8, :]
    HD[h, 2:3, 0:64] = jnp.broadcast_to(loss, (1, 64))
    hd_copies = []
    for d in range(1, 16):
        hd_copies.append(push(HD.at[h], HD.at[h], lax.rem(h + d, 16), y))

    HS, DB, DR = m["HS"], m["DB"], m["DR"]

    def back_three(p):
        grads = G3[p].reshape(512, 512)
        Z[0:576, p * 512 : p * 512 + 512] = dot_nn(W3[:, 0:64, :].reshape(576, 512), grads)

    GW3, GWU, GW2, GW1 = m["GW3"], m["GWU"], m["GW2"], m["GW1"]
    RG3, RGU, RG2, RG1 = m["RG3"], m["RGU"], m["RG2"], m["RG1"]

    def grad_three(p):
        def step(t, carry):
            part = dot_nt(X[span(t, 128), 128 + p * 512 : 640 + p * 512], G3[p].reshape(512, 512))
            rows = pl.ds(pl.multiple_of(576 + 128 * lax.div(t, 4), 64), 128)
            cols = span(lax.rem(t, 4), 512)
            if p > 0:
                part = part + Z[rows, cols]
            if p < 3:
                Z[rows, cols] = part
            else:
                GW3[t] = part.astype(BF)
            return carry

        lax.fori_loop(0, 9, step, 0)

    passes = plane_passes(G3.at[0], planes[0])
    for p in range(4):
        arrive(passes)
        back_three(p)
        if p < 3:
            passes = plane_passes(G3.at[p + 1], planes[p + 1])
            grad_three(p)
    def merge_home(first, last):
        for k in range(first, last):
            half, own = lax.rem(y + k // 2, 2), k < 2
            t = lax.rem(lax.div(z, 2) + 1 + k, 2)
            hand(
                GW3.at[:, span(t, 64), span(y, 256)] if own else m["Y3"].at[t],
                RG3.at[z],
                ha(2 * t + half, x, e),
                y,
                bg3 + k,
                bg3 + z,
            )

    ways = (((0, 0, 0), (1, -1, 0), (1, 1, 1)), ((0, -1, -1), (0, 1, 0), (1, 0, 0)))

    def raised_block(a, b, i):
        straight, bent = [], []
        for ao, da, di in ways[a]:
            io = i - di
            if io < 0 or io > 3 or (i < 0 or i > 3) and di == 0:
                continue
            for bo, db, dj in ways[b]:
                tap = (da + 1) * 3 + db + 1
                at = ((2 * ao + bo) * 4 + io) * 128
                (straight if dj == 0 else bent).append(Z[tap * 64 : tap * 64 + 64, at : at + 128])
        turned = sum(bent[1:], bent[0])
        turned = from_left(turned) if b == 0 else from_right(turned)
        return sum(straight, turned)

    for b in range(2):
        HS[0, b] = raised_block(0, b, 4)
        HS[1, b] = raised_block(1, b, -1)
    bh = reserve(2)
    wait_fringe = fringe(bh, bh + 1, HS.at[0], HR.at[0], HS.at[1], HR.at[1])
    for a in range(2):
        for b in range(2):
            p = 2 * a + b
            for i in range(4):
                block = raised_block(a, b, i)
                if i == 3 * a:
                    DB[p] = block
                else:
                    DR[p * 64 : p * 64 + 64, i * 128 : i * 128 + 128] = block.astype(BF)
    grad_three(3)
    bg3 = reserve(4)
    merge_home(0, 2)
    wait_fringe()
    for a in range(2):
        for b in range(2):
            p = 2 * a + b
            DR[p * 64 : p * 64 + 64, a * 384 : a * 384 + 128] = (DB[p] + HR[a, b]).astype(BF)

    P7b, T7, S7b, R7 = m["P7b"], m["T7"], m["S7b"], m["R7"]

    def back_up(k, carry):
        Z[span(k, 128), 0:512] = dot_nn(WU[pl.ds(2 * k, 2)].reshape(128, 256), DR[...])
        return carry

    lax.fori_loop(0, 8, back_up, 0)
    for k in range(4):
        P7b[k] = Z[span(2 * k + 1 - e, 128), 0:512].astype(BF)
    wait_pair = push(P7b, T7, twin, y)

    def pair_seven():
        for k in range(4):
            total = Z[span(2 * k + e, 128), 0:512] + T7[k].astype(F32)
            Z[span(2 * k + e, 128), 0:512] = total
            S7b[k] = total.astype(BF)

    wait_pair.wait_recv()
    pair_seven()
    wait_seven = scatter(S7b, R7)

    def grad_up(k, carry):
        GWU[pl.ds(2 * k, 2)] = dot_nt(A2[k], DR[...]).astype(BF).reshape(2, 64, 256)
        return carry

    Y3 = m["Y3"]
    other = 1 - y
    across = []
    for t in range(2):
        across.append(
            push(
                GW3.at[:, 64 * t : 64 * t + 64, span(other, 256)],
                Y3.at[t],
                h,
                other,
            )
        )

    lax.fori_loop(0, 8, grad_up, 0)
    patches(middle_block, 0, 16)
    patch_edges()
    arrive(wait_seven)
    G2 = m["G2"]
    total = Z[span(s, 128), 0:512] + R7[0].astype(F32)
    total = total + R7[1].astype(F32) + R7[2].astype(F32)
    G2[e, :, span(z, 512)] = (total * gelu_slope(pre2[...])).astype(BF)
    mine = G2.at[e, :, span(z, 512)]
    g2_copies = []
    for d in range(1, 4):
        zt = lax.rem(z + d, 4)
        g2_copies.append(push(mine, mine, ha(zt, x, e), y))
    own_pair = push(mine, mine, twin, y)

    def back_two(zs):
        for k in range(2):
            cols = pl.ds(pl.multiple_of(zs * 512 + k * 256, 256), 256)
            Z[:, cols] = dot_nn(W2[...].reshape(1152, 256), G2[:, :, cols].reshape(256, 256))

    def relay(d):
        g2_copies[d - 1].wait_recv()
        zs = lax.rem(z + 4 - d, 4)
        came = G2.at[e, :, span(zs, 512)]
        return zs, push(came, came, twin, y)

    zs, copy = relay(1)
    own_pair.wait_recv()
    back_two(z)
    arrive(across)
    merge_home(2, 4)
    gu_copies = []
    for d in range(1, 16):
        ht = lax.rem(h + d, 16)
        gu_copies.append(push(GWU.at[ht], RGU.at[h], ht, y))
    RGU[h] = GWU[h]
    for d in range(2, 4):
        after = relay(d)
        copy.wait_recv()
        back_two(zs)
        zs, copy = after
    copy.wait_recv()
    back_two(zs)
    P8b, R8, G1 = m["P8b"], m["R8"], m["G1"]
    P8 = m["P8"]

    def fold(i, carry):
        sums = []
        for dj in range(3):
            part = None
            for di in range(3):
                row = i - (di - 1)
                inside = jnp.logical_and(row >= 0, row <= 15)
                row = jnp.clip(row, 0, 15)
                tap = di * 3 + dj
                block = jnp.where(inside, Z[tap * 128 : tap * 128 + 128, span(row, 128)], 0.0)
                part = block if part is None else part + block
            sums.append(part)
        total = sums[1] + from_right(sums[0]) + from_left(sums[2])
        P8[:, span(i, 128)] = total
        P8b[:, :, span(i, 128)] = total.reshape(4, 32, 128).astype(BF)
        return carry

    wait_eight = []
    for c in range(2):
        lax.fori_loop(8 * c, 8 * c + 8, fold, 0)
        wait_eight.append(scatter(P8b, R8, halves[c]))

    def grad_two(t, carry):
        GW2[t] = dot_nt(X[span(t, 128), 128:2176], G2[...].reshape(256, 2048)).astype(BF)
        return carry

    lax.fori_loop(0, 9, grad_two, 0)

    def act_back(n, carry):
        cols = span(n, 512)
        total = P8[span(q, 32), cols] + R8[0, :, cols].astype(F32)
        total = total + R8[1, :, cols].astype(F32) + R8[2, :, cols].astype(F32)
        G1[q, :, cols] = (total * gelu_slope(P1[q, :, cols])).astype(BF)
        return carry

    wait_g1 = []
    for c in range(2):
        arrive(wait_eight[c])
        lax.fori_loop(2 * c, 2 * c + 2, act_back, 0)
        wait_g1 += gather_four(G1, halves[c])
    bg2 = reserve(2)
    for j in range(2):
        hand(
            GW2.at[:, 64 * j : 64 * j + 64, :],
            RG2.at[:, :, span(x, 256)],
            ha(z, e, j),
            y,
            bg2 + j,
            bg2 + x,
        )
    patches(input_block, 0, 16)
    patch_edges()
    arrive(wait_g1)

    def grad_one(t, carry):
        GW1[t] = dot_nt(X[span(t, 128), 128:2176], G1[...].reshape(128, 2048)).astype(BF)
        return carry

    lax.fori_loop(0, 9, grad_one, 0)
    bg1 = reserve(4)
    r_low = 2 * lax.rem(z, 2) + e
    for k in range(4):
        j = lax.rem(z + 1 + k, 4)
        hand(
            GW1.at[:, span(j, 32), :],
            RG1.at[:, :, span(r_low, 128)],
            ha(j, x, y),
            lax.div(z, 2),
            bg1 + k,
            bg1 + r_low,
        )

    for copy in hd_copies:
        copy.wait_recv()
    for j in range(4):
        hdo[j] = HD[j] + HD[4 + j] + HD[8 + j] + HD[12 + j]
    hdo[4] = jnp.broadcast_to(labelled, (8, 128))
    for k in range(4):
        landed(RG3.at[k], bg3 + k)
    for t in range(9):
        g3o[t] = (RG3[0, t].astype(F32) + RG3[1, t].astype(F32)) + (
            RG3[2, t].astype(F32) + RG3[3, t].astype(F32)
        )
    for copy in gu_copies:
        copy.wait_recv()
    sums = []
    for k in range(4):
        sums.append(
            (RGU[k].astype(F32) + RGU[4 + k].astype(F32))
            + (RGU[8 + k].astype(F32) + RGU[12 + k].astype(F32))
        )
    for p in range(4):
        guo[p] = jnp.concatenate([part[:, p * 64 : p * 64 + 64] for part in sums], axis=1)
    for k in range(2):
        landed(RG2.at[:, :, 256 * k : 256 * k + 256], bg2 + k)
    g2o[...] = RG2[...]
    for k in range(4):
        landed(RG1.at[:, :, 128 * k : 128 * k + 128], bg1 + k)
    g1o[...] = RG1[...]
    for copy, when in started:
        if when is None:
            copy.wait_send()
        else:
            pl.when(when)(copy.wait_send)


def resident_body(
    input_a,
    input_b,
    skip_a,
    skip_b,
    labels_a,
    labels_b,
    valid_a,
    valid_b,
    w_enter,
    moment_enter,
    square_enter,
    w_middle,
    moment_middle,
    square_middle,
    w_upward,
    moment_upward,
    square_upward,
    w_merge,
    moment_merge,
    square_merge,
    w_head,
    moment_head,
    square_head,
):
    vmem = pl.BlockSpec(memory_space=pltpu.VMEM)
    anywhere = pl.BlockSpec(memory_space=pl.ANY)
    g1, g2, gu, g3, hd = pl.pallas_call(
        lambda *refs: fused((input_a.shape[2], input_b.shape[2]), *refs),
        out_shape=(
            jax.ShapeDtypeStruct((9, 32, 512), BF),
            jax.ShapeDtypeStruct((9, 64, 512), BF),
            jax.ShapeDtypeStruct((4, 64, 256), F32),
            jax.ShapeDtypeStruct((9, 64, 256), F32),
            jax.ShapeDtypeStruct((5, 8, 128), F32),
        ),
        in_specs=[vmem] * 9 + [anywhere] * 3 + [vmem],
        out_specs=[vmem] * 5,
        scratch_shapes=[pltpu.VMEM(shape, kind) for _, shape, kind in SCRATCH]
        + [pltpu.SemaphoreType.DMA((COPIES,)), pltpu.SemaphoreType.DMA((COPIES,)), pltpu.SemaphoreType.DMA((3,))],
        compiler_params=pltpu.CompilerParams(
            collective_id=0, has_side_effects=True, vmem_limit_bytes=61 * 1024 * 1024
        ),
    )(
        input_a[0, 0],
        input_b[0, 0],
        skip_a[0],
        skip_b[0],
        labels_a[0],
        labels_b[0],
        valid_a[0],
        valid_b[0],
        w_enter.reshape(9, 32, 512),
        w_middle.reshape(9, 64, 512),
        w_upward.reshape(4, 64, 256),
        w_merge.reshape(9, 64, 256),
        w_head.T,
    )
    states = (
        (w_enter, moment_enter, square_enter),
        (w_middle, moment_middle, square_middle),
        (w_upward, moment_upward, square_upward),
        (w_merge, moment_merge, square_merge),
    )
    dims = tuple(g.shape for g in (g1, g2, gu, g3))
    flat = [part.reshape(dim) for dim, state in zip(dims, states) for part in state]
    rows = w_head.T.shape
    new = pl.pallas_call(
        updates,
        out_shape=tuple(
            jax.ShapeDtypeStruct(dim, kind) for dim in (*dims, rows) for kind in (F32, F32, F32, BF)
        )
        + (jax.ShapeDtypeStruct((1, 1), F32),) * 2,
        in_specs=[anywhere] * 16 + [vmem] * 4,
        out_specs=[anywhere] * 16 + [vmem] * 6,
        scratch_shapes=[
            pltpu.VMEM(dim, kind)
            for dim, g in zip(dims, (g1, g2, gu, g3))
            for kind in (g.dtype, F32, F32, F32, F32, F32, F32, BF)
        ]
        + [pltpu.SemaphoreType.DMA((len(PIECES), 8))],
        compiler_params=pltpu.CompilerParams(vmem_limit_bytes=62 * 1024 * 1024),
    )(g1, g2, gu, g3, *flat, hd, w_head.T, moment_head.T, square_head.T)
    shapes = (w_enter.shape, w_middle.shape, w_upward.shape, w_merge.shape)
    return (
        *[new[k].reshape(shapes[k // 4]) for k in range(16)],
        *[part.T for part in new[16:20]],
        new[20].reshape(()),
        new[21].reshape(()),
    )


PIECES = ((3, 0, 5), (3, 5, 9), (2, 0, 4), (1, 0, 3), (1, 3, 6), (1, 6, 9), (0, 0, 5), (0, 5, 9))


def adamw_step(master, moment, square, gradient):
    moment_new = BETA_ONE * moment + (1.0 - BETA_ONE) * gradient
    square_new = BETA_TWO * square + (1.0 - BETA_TWO) * gradient * gradient
    fixed_moment = moment_new * (RATE / (1.0 - BETA_ONE**STEP))
    fixed_square = square_new * (1.0 / (1.0 - BETA_TWO**STEP))
    master_new = (1.0 - RATE * DECAY) * master - fixed_moment / (jnp.sqrt(fixed_square) + EPSILON)
    return (master_new, moment_new, square_new, master_new.astype(BF))


def updates(*refs):
    grads, states = refs[0:4], refs[4:16]
    hd, head, moment, square = refs[16:20]
    outs, tiny, loss, labelled = refs[20:36], refs[36:40], refs[40], refs[41]
    held, sems = refs[42:74], refs[74]

    def copies(piece):
        k, first, last = PIECES[piece]
        at = slice(first, last)
        inward = [
            pltpu.make_async_copy(source.at[at], held[8 * k + j].at[at], sems.at[piece, j])
            for j, source in enumerate((grads[k], *states[3 * k : 3 * k + 3]))
        ]
        outward = [
            pltpu.make_async_copy(held[8 * k + 4 + j].at[at], outs[4 * k + j].at[at], sems.at[piece, 4 + j])
            for j in range(4)
        ]
        return inward, outward

    every = [copies(piece) for piece in range(len(PIECES))]
    for inward, _ in every:
        for copy in inward:
            copy.start()
    loss[...] = hd[0, 2:3, 0:1]
    labelled[...] = hd[4, 0:1, 0:1]
    gradient = jnp.concatenate([hd[j, 0:2, 0:64] for j in range(4)], axis=1)
    for ref, value in zip(tiny, adamw_step(head[...], moment[...], square[...], gradient)):
        ref[...] = value
    for (k, first, last), (inward, outward) in zip(PIECES, every):
        for copy in inward:
            copy.wait()
        own = held[8 * k : 8 * k + 8]

        def step(i, carry, own=own):
            made = adamw_step(own[1][i], own[2][i], own[3][i], own[0][i].astype(F32))
            for ref, value in zip(own[4:], made):
                ref[i] = value
            return carry

        lax.fori_loop(first, last, step, 0)
        for copy in outward:
            copy.start()
    for _, outward in every:
        for copy in outward:
            copy.wait()


def chosen(*args):
    input_a, input_b, skip_a = args[0], args[1], args[2]
    w_enter, w_middle, w_upward, w_merge = args[8], args[11], args[14], args[17]
    fits = (
        lax.axis_size("ha") == 16
        and lax.axis_size("col") == 2
        and input_a.shape[:2] == (1, 1)
        and input_b.shape[:2] == (1, 1)
        and input_a.shape[3] == 256
        and skip_a.shape[3] == 256
        and input_a.shape[2] + input_b.shape[2] <= LANE
        and w_enter.shape == (3, 3, 32, 512)
        and w_middle.shape == (3, 3, 64, 512)
        and w_upward.shape == (2, 2, 64, 256)
        and w_merge.shape == (3, 3, 64, 256)
    )
    return resident_body(*args) if fits else body(*args)


def solution(mesh):
    placed = (
        P(None, "ha", None, "col"),
        P(None, "ha", None, "col"),
        P(None, "ha", None, "col"),
        P(None, "ha", None, "col"),
        P(None, "ha", None),
        P(None, "ha", None),
        P(None, "ha", None),
        P(None, "ha", None),
        P(None, None, "ha", "col"),
        P(None, None, "ha", "col"),
        P(None, None, "ha", "col"),
        P(None, None, "ha", "col"),
        P(None, None, "ha", "col"),
        P(None, None, "ha", "col"),
        P(None, None, "ha", "col"),
        P(None, None, "ha", "col"),
        P(None, None, "ha", "col"),
        P(None, None, "ha", "col"),
        P(None, None, "ha", "col"),
        P(None, None, "ha", "col"),
        P("col", None),
        P("col", None),
        P("col", None),
    )
    return jax.shard_map(
        chosen,
        mesh=mesh,
        in_specs=placed,
        out_specs=(
            P(None, None, "ha", "col"),
            P(None, None, "ha", "col"),
            P(None, None, "ha", "col"),
            P(None, None, "ha", "col"),
            P(None, None, "ha", "col"),
            P(None, None, "ha", "col"),
            P(None, None, "ha", "col"),
            P(None, None, "ha", "col"),
            P(None, None, "ha", "col"),
            P(None, None, "ha", "col"),
            P(None, None, "ha", "col"),
            P(None, None, "ha", "col"),
            P(None, None, "ha", "col"),
            P(None, None, "ha", "col"),
            P(None, None, "ha", "col"),
            P(None, None, "ha", "col"),
            P("col", None),
            P("col", None),
            P("col", None),
            P("col", None),
            P(),
            P(),
        ),
        check_vma=False,
    )
```
